32 devices in a mesh: expert: 16 (over z, y, x), tensor: 2 (over core).
Axes of the slice: x: 2, y: 2, z: 4, core: 2. Of those that a mesh axis runs over, the one named last changes fastest.
Arguments:
- layer_input: bfloat16 [3, 1024, 2048], P(None, 'expert'), may hold values from -6 to 6
- norm_first: float32 [2048], replicated, may hold values from 0.5 to 1.5
- query_weight: bfloat16 [2048, 4096], P(None, 'tensor'), may hold values from -0.125 to 0.125
- key_weight: bfloat16 [2048, 512], P(None, 'tensor'), may hold values from -0.125 to 0.125
- value_weight: bfloat16 [2048, 512], P(None, 'tensor'), may hold values from -0.125 to 0.125
- mixing_weight: bfloat16 [4096, 2048], P('tensor'), may hold values from -2 to 2
- query_gain: float32 [128], replicated, may hold values from 0.5 to 1.5
- key_gain: float32 [128], replicated, may hold values from 0.5 to 1.5
- norm_second: float32 [2048], replicated, may hold values from 0.5 to 1.5
- router_weight: bfloat16 [2048, 16], replicated, may hold values from -0.0625 to 0.0625
- gate_weight: bfloat16 [16, 2048, 768], P('expert', None, 'tensor'), may hold values from -0.125 to 0.125
- up_weight: bfloat16 [16, 2048, 768], P('expert', None, 'tensor'), may hold values from -0.125 to 0.125
- down_weight: bfloat16 [16, 768, 2048], P('expert', 'tensor'), may hold values from -0.625 to 0.625
- routes: int32 [3, 1024, 8], P(None, 'expert'), may hold values from 0 to 15, all different within a row
- fill_order: int32 [3, 1024], P(None, 'expert'), may hold values from 0 to 3071, as said below
- cotangent: bfloat16 [3, 1024, 2048], P(None, 'expert'), may hold values from -6 to 6
Outputs:
- layer_output: bfloat16 [3, 1024, 2048], P(None, 'expert', 'tensor')
- input_grad: float32 [3, 1024, 2048], P(None, 'expert')
- first_grad: float32 [2048], replicated
- query_grad: float32 [2048, 4096], P('expert', 'tensor')
- key_grad: float32 [2048, 512], P('expert', 'tensor')
- value_grad: float32 [2048, 512], P('expert', 'tensor')
- mixing_grad: float32 [4096, 2048], P('tensor', 'expert')
- querygain_grad: float32 [128], replicated
- keygain_grad: float32 [128], replicated
- second_grad: float32 [2048], replicated
- router_grad: float32 [2048, 16], replicated
- gate_grad: float32 [16, 2048, 768], P('expert', None, 'tensor')
- up_grad: float32 [16, 2048, 768], P('expert', None, 'tensor')
- down_grad: float32 [16, 768, 2048], P('expert', 'tensor')
The draws below stay inside these ranges and needn't reach their ends.
Inputs may be any that keep to these rules, and one draw needn't show every extreme that they name: `routes`: each token names 8 different experts. `fill_order`: holds each whole number below 3072 once; a smaller number takes a slot first.
All inputs are finite; a program needn't handle non-finite values.
Results may differ from the reference program's by a relative error of at most 0.023.
Values may be sent and summed in bfloat16 or wider, within the bound.
A program may use at most 320 MiB of HBM per device.

```python
import jax
import jax.numpy as jnp
from jax import lax

D = 2048
HQ = 32
HK = 4
HD = 128
FF = 768
TOPK = 8
SEQS = 3
SEG = 64
BLOCK = 256
EXPERTS = 16
LENGTH = 1024
CAP = 120
N_EXPERT = 16


def draw_fill_order(key, part):
    key = jax.random.fold_in(key, 11)
    return jax.random.permutation(key, SEQS * LENGTH).astype(jnp.int32).reshape(SEQS, LENGTH)


def with_spikes(entries, rng, source, target, shards_of, factor):
    owner, partner = [(jnp.arange(entries.shape[axis_at]) // (entries.shape[axis_at] // shards_of)).reshape([-1 if axis == axis_at else 1 for axis in range(entries.ndim)]) for axis_at in (source, target)]
    chosen = jax.random.permutation(rng, shards_of)[partner]
    strong = (owner == chosen) | (owner == (partner + shards_of // 2) % shards_of)
    return jnp.where(strong, factor * entries, entries)


def block_levels(own_key, dims, shards, least, high):
    def one(dim, shards_of):
        draws = jax.random.uniform(jax.random.fold_in(jax.random.fold_in(own_key, 6), dim), (shards_of,), jnp.float32, least / len(shards), high / len(shards))
        return jnp.repeat(jnp.exp(draws), dims[dim] // shards_of).reshape((-1,) + (1,) * (len(dims) - dim - 1))

    gain = one(*shards[0])
    for cut in shards[1:]:
        gain = gain * one(*cut)
    return gain


def distinct(rng, rows, count, top, lift):
    sequence = jax.random.permutation(jax.random.fold_in(rng, 1), count)
    boost = sequence
    for power in range(3):
        boost = boost * boost // count
    boost = boost * lift // count
    lots = jax.random.randint(jax.random.fold_in(rng, 2), (rows, count), 0, 4096) + boost
    fixed_rows = jax.random.permutation(jax.random.fold_in(rng, 3), rows)[jnp.arange(count) % rows]
    lots = jnp.where(jnp.arange(rows)[:, None] == fixed_rows[None, :], 1 << 14, lots)
    priority = lots * count + jnp.arange(count)
    return lax.top_k(priority.astype(jnp.int32), top)[1].astype(jnp.int32)


def normal_values(stream_key, extent, spread, most, split=(), held_as=jnp.bfloat16):
    factor_of = block_levels(stream_key, extent, split, -0.22, 0.18) if split else 1.0
    values = jax.random.normal(stream_key, extent, jnp.float32) * spread * factor_of
    return jnp.minimum(jnp.maximum(values, -most), most).astype(held_as)


def bell_draw_with(own_key, extent, deviation, limit, split, heavy, kind=jnp.bfloat16):
    drawn = deviation * jax.random.normal(own_key, extent, jnp.float32)
    if split:
        drawn = drawn * block_levels(own_key, extent, split, -0.22, 0.18)
    return jnp.clip(with_spikes(drawn, jax.random.fold_in(own_key, 3), *heavy), -limit, limit).astype(kind)


def setup_inputs(seed: int = 0) -> dict:
    seeds = jax.random.split(jax.random.key(seed), 17)
    return {
        "layer_input": bell_draw_with(seeds[0], (SEQS, LENGTH, D), 1.0, 6.0, ((1, 16),), (1, 2, 16, 2.0)),
        "norm_first": jnp.clip(1.0 + 0.1 * jax.random.normal(seeds[1], (D,), jnp.float32), 0.5, 1.5),
        "query_weight": normal_values(seeds[2], (D, HQ * HD), D ** -0.5, 0.125, ((1, 2),)),
        "key_weight": normal_values(seeds[3], (D, HK * HD), D ** -0.5, 0.125, ((1, 2),)),
        "value_weight": normal_values(seeds[4], (D, HK * HD), D ** -0.5, 0.125, ((1, 2),)),
        "mixing_weight": normal_values(seeds[5], (HQ * HD, D), (max(1, 2 * HQ * HD // LENGTH)) ** -0.5, 2.0, ((0, 2),)),
        "query_gain": jnp.clip(1.0 + 0.1 * jax.random.normal(seeds[6], (HD,), jnp.float32), 0.5, 1.5),
        "key_gain": jnp.clip(1.0 + 0.1 * jax.random.normal(seeds[7], (HD,), jnp.float32), 0.5, 1.5),
        "norm_second": jnp.clip(1.0 + 0.1 * jax.random.normal(seeds[8], (D,), jnp.float32), 0.5, 1.5),
        "router_weight": normal_values(seeds[9], (D, EXPERTS), (4 * D) ** -0.5, 0.0625),
        "gate_weight": normal_values(seeds[10], (EXPERTS, D, FF), D ** -0.5, 0.125, ((0, 16), (2, 2))),
        "up_weight": normal_values(seeds[11], (EXPERTS, D, FF), D ** -0.5, 0.125, ((0, 16), (2, 2))),
        "down_weight": normal_values(seeds[12], (EXPERTS, FF, D), (FF // 8) ** -0.5, 0.625, ((0, 16), (1, 2))),
        "routes": distinct(seeds[13], SEQS * LENGTH, EXPERTS, TOPK, 4096).reshape((SEQS, LENGTH, TOPK)),
        "fill_order": draw_fill_order(jax.random.fold_in(seeds[16], 71), 0),
        "cotangent": normal_values(seeds[15], (SEQS, LENGTH, D), 1.0, 6.0, ((1, 16),)),
    }


epsilon = 1e-06
rope_base = 1000000.0
far_below = -1e+30
highest = lax.Precision.HIGHEST

@jax.custom_vjp
def low(v):
    return lax.optimization_barrier(v.astype(jnp.bfloat16)).astype(jnp.float32)

@jax.custom_vjp
def low_back(v):
    return v

def low_keep(v):
    return (low(v), None)

def low_pass(kept, grad):
    return (grad,)

def back_keep(v):
    return (v, None)

def back_low(kept, grad):
    return (low(grad),)
low.defvjp(low_keep, low_pass)
low_back.defvjp(back_keep, back_low)

def rms_scaled(values, gain_vec):
    return values * lax.rsqrt(lax.optimization_barrier(jnp.mean(values * values, axis=-1, keepdims=True)) + epsilon) * gain_vec

def rotary_tables(positions, head_dim):
    halfway = head_dim // 2
    exponents = jnp.arange(halfway, dtype=jnp.float32) * (2.0 / head_dim)
    inverse = jnp.exp(-exponents * jnp.log(jnp.float32(rope_base)))
    angles = positions.astype(jnp.float32)[:, None] * inverse[None, :]
    return (jnp.cos(angles), jnp.sin(angles))

def rotate(values, cosine, sine_table):
    halfway = values.shape[-1] // 2
    first = values[..., :halfway]
    latter = values[..., halfway:]
    return jnp.concatenate([first * cosine - latter * sine_table, latter * cosine + first * sine_table], axis=-1)

def regroup(values):
    return values.reshape(N_EXPERT, SEQS, SEG, TOPK).transpose(1, 0, 2, 3).reshape(SEQS, LENGTH, TOPK)

def routing(routes, fill_order):
    groups = N_EXPERT
    per_group = SEQS * SEG
    grouped = routes.reshape(SEQS, groups, SEG, TOPK).transpose(1, 0, 2, 3).reshape(groups, per_group, TOPK)
    ranking = fill_order.reshape(SEQS, groups, SEG).transpose(1, 0, 2).reshape(groups, per_group)
    chosen = (grouped[..., None] == jnp.arange(EXPERTS, dtype=jnp.int32)).astype(jnp.int32)
    usages = lax.optimization_barrier(jnp.sum(chosen, axis=2))
    ordering = jnp.argsort(ranking, axis=1, stable=True).astype(jnp.int32)
    inverse_order = jnp.argsort(ordering, axis=1, stable=True).astype(jnp.int32)
    sorted_usage = jnp.take_along_axis(usages, ordering[:, :, None], axis=1)
    running = jnp.cumsum(sorted_usage, axis=1, dtype=jnp.int32) - sorted_usage
    counts = jnp.take_along_axis(running, inverse_order[:, :, None], axis=1).astype(jnp.int32)
    slot_ids = jnp.take_along_axis(counts, grouped, axis=2).astype(jnp.int32)
    kept_mask = slot_ids < CAP
    source = jnp.arange(groups, dtype=jnp.int32)[:, None, None]
    places = (grouped * groups + source) * CAP + slot_ids
    seq_index = jnp.arange(per_group, dtype=jnp.int32) // SEG
    row_index = jnp.arange(per_group, dtype=jnp.int32) % SEG
    token_ids = seq_index[None, :] * LENGTH + source[:, :, 0] * SEG + row_index[None, :]
    buffer_rows = EXPERTS * groups * CAP
    targets = jnp.where(kept_mask, places, buffer_rows).astype(jnp.int32)
    filled = jnp.broadcast_to(token_ids[:, :, None], targets.shape).reshape(-1).astype(jnp.int32)
    row_table = jnp.full((buffer_rows,), -1, dtype=jnp.int32).at[targets.reshape(-1)].set(filled, mode='drop')
    return (row_table.reshape(EXPERTS, groups * CAP), regroup(kept_mask), regroup(jnp.where(kept_mask, places, 0).astype(jnp.int32)))

def expert_rows(flat_inputs, gate_w, up_w, down_w, row_table):

    @jax.checkpoint
    def one_expert(expert_item):
        gate_one, up_one, down_one, indices = expert_item
        live_rows = (indices >= 0).astype(flat_inputs.dtype)
        gathered = low_back(jnp.take(flat_inputs, jnp.maximum(indices, 0), axis=0) * live_rows[:, None])
        gate_act = low_back(jnp.dot(gathered, gate_one, precision=highest))
        up_act = low_back(jnp.dot(gathered, up_one, precision=highest))
        hidden = low(jax.nn.silu(gate_act) * up_act)
        return low(low_back(jnp.dot(hidden, down_one, precision=highest)))
    return lax.map(one_expert, (gate_w, up_w, down_w, row_table))

def attend(queries, key_heads, value_heads):
    block_rows = min(512, LENGTH)
    query_blocks = LENGTH // block_rows
    group_size = HQ // HK
    item_count = SEQS * query_blocks * HK
    stacked = queries.reshape(SEQS, query_blocks, block_rows, HK, group_size, HD)
    stacked = stacked.transpose(0, 1, 3, 2, 4, 5).reshape(item_count, block_rows, group_size, HD)
    key_pos = jnp.arange(LENGTH, dtype=jnp.int32) // BLOCK
    factor = HD ** (-0.5)

    @jax.checkpoint
    def one_block(block_item):
        query_tile, position = block_item
        seq_id = position // (query_blocks * HK)
        block_id = position // HK % query_blocks
        head_id = position % HK
        key_tile = lax.dynamic_index_in_dim(lax.dynamic_index_in_dim(key_heads, seq_id, 0, keepdims=False), head_id, 1, keepdims=False)
        value_tile = lax.dynamic_index_in_dim(lax.dynamic_index_in_dim(value_heads, seq_id, 0, keepdims=False), head_id, 1, keepdims=False)
        raw_scores = jnp.einsum('rgd,kd->grk', query_tile, key_tile, precision=highest)
        scores = low_back(raw_scores * factor)
        query_pos = (block_id * block_rows + jnp.arange(block_rows, dtype=jnp.int32)) // BLOCK
        allowed = key_pos[None, :] <= query_pos[:, None]
        masked = jnp.where(allowed[None, :, :], scores, far_below)
        weights = low(jax.nn.softmax(masked, axis=-1))
        return jnp.einsum('grk,kd->rgd', weights, value_tile, precision=highest)
    mixed_out = lax.map(one_block, (stacked, jnp.arange(item_count, dtype=jnp.int32)))
    mixed_out = mixed_out.reshape(SEQS, query_blocks, HK, block_rows, group_size, HD).transpose(0, 1, 3, 2, 4, 5)
    return mixed_out.reshape(SEQS, LENGTH, HQ * HD)

def reference(layer_input, norm_first, query_weight, key_weight, value_weight, mixing_weight, query_gain, key_gain, norm_second, router_weight, gate_weight, up_weight, down_weight, routes, fill_order, cotangent):
    row_table, kept_mask, places = routing(routes, fill_order)
    cosine, sine_table = rotary_tables(jnp.arange(LENGTH, dtype=jnp.int32), HD)
    cosine = cosine[:, None, :]
    sine_table = sine_table[:, None, :]
    kept_float = kept_mask.astype(jnp.float32)

    def forward(inputs, first_gain, query_w, key_w, value_w, mixing_w, query_scale, key_scale, second_gain, router_w, gate_w, up_w, down_w):
        normed = low(rms_scaled(inputs, first_gain))
        query_raw = low_back(jnp.dot(normed, query_w, precision=highest)).reshape(SEQS, LENGTH, HQ, HD)
        key_raw = low_back(jnp.dot(normed, key_w, precision=highest)).reshape(SEQS, LENGTH, HK, HD)
        value_all = low(low_back(jnp.dot(normed, value_w, precision=highest))).reshape(SEQS, LENGTH, HK, HD)
        query_rot = low(rotate(rms_scaled(query_raw, query_scale), cosine, sine_table))
        key_rot = low(rotate(rms_scaled(key_raw, key_scale), cosine, sine_table))
        context = low(low_back(attend(query_rot, key_rot, value_all)))
        residual = inputs + low_back(jnp.dot(context, mixing_w, precision=highest))
        second = low(rms_scaled(residual, second_gain))
        logits = low_back(jnp.dot(second, router_w, precision=highest))
        gates = jax.nn.softmax(jnp.take_along_axis(logits, routes, axis=-1), axis=-1) * kept_float
        results = expert_rows(second.reshape(SEQS * LENGTH, D), gate_w, up_w, down_w, row_table).reshape(-1, D)
        mixture = residual
        for route_k in range(TOPK):
            mixture = mixture + gates[..., route_k:route_k + 1] * jnp.take(results, places[..., route_k], axis=0)
        return mixture
    floats = [array_in.astype(jnp.float32) for array_in in (layer_input, norm_first, query_weight, key_weight, value_weight, mixing_weight, query_gain, key_gain, norm_second, router_weight, gate_weight, up_weight, down_weight)]
    result, pullback = jax.vjp(forward, *floats)
    gradients = pullback(cotangent.astype(jnp.float32))
    return (result.astype(jnp.bfloat16), gradients[0], gradients[1], gradients[2], gradients[3], gradients[4], gradients[5], gradients[6], gradients[7], gradients[8], gradients[9], gradients[10], gradients[11], gradients[12])
```

```python
import functools

import jax
import jax.numpy as jnp
from jax import lax
from jax.experimental import pallas as pl
from jax.experimental.pallas import tpu as pltpu
from jax.sharding import PartitionSpec as P

BLOCK = 256
MESH = pl.DeviceIdType.MESH
ROOM = 56 * 2**20


class Spot:
    def __init__(self):
        self.e = lax.axis_index("expert")
        self.t = lax.axis_index("tensor")
        self.a = lax.div(self.e, 4)
        y = lax.rem(lax.div(self.e, 2), 2)
        x = lax.rem(self.e, 2)
        self.b = x + self.t * (y - x)
        self.c = y + self.t * (x - y)

    def index(self, a, b, c):
        y = c + self.t * (b - c)
        x = b + self.t * (c - b)
        return a * 4 + y * 2 + x

    def at(self, a, b, c):
        return (self.index(a, b, c), self.t)

    def core(self):
        return (self.e, 1 - self.t)

    def greet(self, planes, chain, flat, share):
        barrier = pltpu.get_barrier_semaphore()
        total = 0

        def call(who):
            pl.semaphore_signal(barrier, inc=1, device_id=who, device_id_type=MESH)

        if share:
            call(self.core())
            total = total + 1
        if flat:
            call(self.at(self.a, 1 - self.b, self.c))
            call(self.at(self.a, self.b, 1 - self.c))
            total = total + 2
        if chain:
            up = self.a + 1 < planes
            down = self.a > 0

            @pl.when(up)
            def _():
                call(self.at(self.a + 1, self.b, self.c))

            @pl.when(down)
            def _():
                call(self.at(self.a - 1, self.b, self.c))

            total = total + up.astype(jnp.int32) + down.astype(jnp.int32)
        pl.semaphore_wait(barrier, total)


def push(src, dst, send_sem, recv_sem, who):
    return pltpu.make_async_remote_copy(
        src_ref=src, dst_ref=dst, send_sem=send_sem, recv_sem=recv_sem, device_id=who, device_id_type=MESH
    )


def offsets(planes):
    out = [0]
    for step in range(1, planes):
        out += [step, -step]
    return out


def gather_kernel(planes, share, x_ref, o_ref, ssem, rsem, csem, lsem):
    me = Spot()
    rows = x_ref.shape[0]
    half = rows // 2 if share else rows
    start = pl.multiple_of(me.t * half, half) if share else 0
    span = pl.ds(start, half)
    own = me.index(me.a, me.b, me.c)

    def copy(idx, kind, src=None):
        who = {
            0: me.at(me.a + 1, me.b, me.c),
            1: me.at(me.a - 1, me.b, me.c),
            2: me.at(me.a, 1 - me.b, me.c),
            3: me.at(me.a, me.b, 1 - me.c),
            4: me.core(),
        }[kind]
        there = o_ref.at[idx, span]
        landed = csem if kind == 4 else rsem
        return push(there if src is None else src, there, ssem.at[idx, kind], landed.at[idx], who)

    local = pltpu.make_async_copy(x_ref, o_ref.at[own], lsem)
    local.start()
    me.greet(planes, True, True, share)

    def each(act):
        for da in offsets(planes):
            sa = me.a + da

            @pl.when((sa >= 0) & (sa < planes))
            def _(da=da, sa=sa):
                idx = me.index(sa, me.b, me.c)
                src = x_ref.at[span] if da == 0 else None
                if da != 0 and act == "start":
                    copy(idx, 2).wait_recv()
                if da <= 0:

                    @pl.when(me.a + 1 < planes)
                    def _():
                        run(copy(idx, 0, src))

                if da >= 0:

                    @pl.when(me.a > 0)
                    def _():
                        run(copy(idx, 1, src))

                run(copy(idx, 3, src))
                run(copy(idx, 2, src))
                if share and da != 0:
                    run(copy(idx, 4))
                idx = me.index(sa, 1 - me.b, me.c)
                if act == "start":
                    copy(idx, 2).wait_recv()
                run(copy(idx, 3))
                if share:
                    run(copy(idx, 4))

        for da in offsets(planes):
            sa = me.a + da

            @pl.when((sa >= 0) & (sa < planes))
            def _(da=da, sa=sa):
                for sb in (me.b, 1 - me.b):
                    idx = me.index(sa, sb, 1 - me.c)
                    if act == "start":
                        copy(idx, 2).wait_recv()
                    if share:
                        run(copy(idx, 4))

    def run(c):
        c.start() if mode[0] == "start" else c.wait_send()

    mode = ["start"]
    each("start")
    mode[0] = "wait"
    each("wait")
    if share:
        other = pl.ds(pl.multiple_of((1 - me.t) * half, half), half)
        for da in offsets(planes):
            sa = me.a + da

            @pl.when((sa >= 0) & (sa < planes))
            def _(da=da, sa=sa):
                for sb in (me.b, 1 - me.b):
                    for sc in (me.c, 1 - me.c):
                        if da == 0 and sb is me.b and sc is me.c:
                            continue
                        idx = me.index(sa, sb, sc)
                        there = o_ref.at[idx, other]
                        push(there, there, ssem.at[idx, 4], csem.at[idx], me.core()).wait_recv()
    local.wait()


def gather_rows(x, planes, share, cid, name):
    count = planes * 4
    return pl.pallas_call(
        functools.partial(gather_kernel, planes, share),
        out_shape=jax.ShapeDtypeStruct((count,) + x.shape, x.dtype),
        in_specs=[pl.BlockSpec(memory_space=pl.ANY)],
        out_specs=pl.BlockSpec(memory_space=pl.ANY),
        scratch_shapes=[
            pltpu.SemaphoreType.DMA((count, 5)),
            pltpu.SemaphoreType.DMA((count,)),
            pltpu.SemaphoreType.DMA((count,)),
            pltpu.SemaphoreType.DMA,
        ],
        compiler_params=pltpu.CompilerParams(collective_id=cid, has_side_effects=True),
        name=name,
    )(x)


def add_rows(target, parts):
    rows = target.shape[0]
    step = 32 if rows % 32 == 0 else 16

    def body(i, carry):
        at = pl.ds(pl.multiple_of(i * step, step), step)
        total = parts[0][at, :].astype(jnp.float32)
        for part in parts[1:]:
            total = total + part[at, :].astype(jnp.float32)
        target[at, :] = total.astype(target.dtype)
        return carry

    lax.fori_loop(0, rows // step, body, 0)


def far_first(a, planes, i):
    last = planes - 1
    low = jnp.where(i < last - a, last - i, jnp.where(i < last, i - (last - a), a))
    high = jnp.where(i < a, i, jnp.where(i < last, last - (i - a), a))
    return jnp.where(2 * a < last, low, high)


def scatter_kernel(
    planes, flat, share, p_ref, o_ref, mine, land0, landc, landb, landa, lsem, csem, rsem, ssem, esem
):
    me = Spot()
    rows = p_ref.shape[1]
    half = rows // 2 if share else rows
    ours = pl.ds(pl.multiple_of(me.t * half, half), half) if share else pl.ds(0, half)
    other = pl.ds(pl.multiple_of((1 - me.t) * half, half), half)
    order = [far_first(me.a, planes, i) for i in range(planes)]

    def block(sa, sb, sc):
        return me.index(sa, sb, sc) if flat else sa

    def load(idx):
        return pltpu.make_async_copy(p_ref.at[idx, ours], mine.at[idx], lsem.at[idx])

    def trade(idx):
        return push(p_ref.at[idx, other], land0.at[idx], ssem.at[0, idx], csem.at[idx], me.core())

    spots = [(sb, sc) for sc in (1 - me.c, me.c) for sb in (1 - me.b, me.b)] if flat else [(me.b, me.c)]
    for sa in order:
        for sb, sc in spots:
            load(block(sa, sb, sc)).start()
    me.greet(planes, True, flat, share)
    if share:
        for sa in order:
            for sb, sc in spots:
                trade(block(sa, sb, sc)).start()

    def send_c(sa, sb):
        slot = sa * 2 + sb
        return push(
            mine.at[me.index(sa, sb, 1 - me.c)],
            landc.at[slot],
            ssem.at[1, slot],
            rsem.at[0, slot],
            me.at(me.a, me.b, 1 - me.c),
        )

    def send_b(sa):
        return push(
            mine.at[me.index(sa, 1 - me.b, me.c)],
            landb.at[sa],
            ssem.at[2, sa],
            rsem.at[1, sa],
            me.at(me.a, 1 - me.b, me.c),
        )

    def send_a(sa, up):
        arrive = me.a + 1 if up else me.a - 1
        slot = sa if up else jnp.where(sa == arrive, planes, sa)
        return push(
            mine.at[block(sa, me.b, me.c)],
            landa.at[slot],
            ssem.at[3, sa],
            rsem.at[2, slot],
            me.at(arrive, me.b, me.c),
        )

    if flat:
        for sa in order:
            for sb, sc in spots:
                idx = me.index(sa, sb, sc)
                load(idx).wait()
                if share:
                    trade(idx).wait_recv()
                    add_rows(mine.at[idx], [mine.at[idx], land0.at[idx]])
                if sc is spots[0][1]:
                    send_c(sa, sb).start()

    def from_c(sa):
        for sb in (1 - me.b, me.b):
            slot = sa * 2 + sb
            push(landc.at[slot], landc.at[slot], ssem.at[1, slot], rsem.at[0, slot], me.at(me.a, me.b, 1 - me.c)).wait_recv()
            idx = me.index(sa, sb, me.c)
            add_rows(mine.at[idx], [mine.at[idx], landc.at[slot]])
            if sb is not me.b:
                send_b(sa).start()

    def along(i, sa):
        idx = block(sa, me.b, me.c)
        parts = [mine.at[idx]]
        if flat:
            push(landb.at[sa], landb.at[sa], ssem.at[2, sa], rsem.at[1, sa], me.at(me.a, 1 - me.b, me.c)).wait_recv()
            parts = parts + [landb.at[sa]]
        else:
            load(idx).wait()

        def landed(slot):
            push(landa.at[slot], landa.at[slot], ssem.at[3, 0], rsem.at[2, slot], me.at(me.a, me.b, me.c)).wait_recv()

        if i < planes - 1:
            up = sa > me.a
            inner = (up & (me.a > 0)) | (jnp.logical_not(up) & (me.a + 1 < planes))

            @pl.when(inner)
            def _():
                landed(sa)
                add_rows(mine.at[idx], parts + [landa.at[sa]])

            if len(parts) > 1:

                @pl.when(jnp.logical_not(inner))
                def _():
                    add_rows(mine.at[idx], parts)

            @pl.when(up)
            def _():
                send_a(sa, True).start()

            @pl.when(jnp.logical_not(up))
            def _():
                send_a(sa, False).start()

        else:
            target = o_ref.at[ours] if share else o_ref

            @pl.when(me.a > 0)
            def _():
                landed(me.a)

            @pl.when(me.a + 1 < planes)
            def _():
                landed(planes)

            @pl.when((me.a > 0) & (me.a + 1 < planes))
            def _():
                add_rows(target, parts + [landa.at[me.a], landa.at[planes]])

            @pl.when(me.a == 0)
            def _():
                add_rows(target, parts + [landa.at[planes]])

            @pl.when(me.a + 1 == planes)
            def _():
                add_rows(target, parts + [landa.at[me.a]])

    for i in range(planes + 1):
        if flat and i < planes:
            from_c(order[i])
        if i > 0:
            along(i - 1, order[i - 1])
    if share:
        done = push(o_ref.at[ours], o_ref.at[ours], esem.at[0], esem.at[1], me.core())
        done.start()
    for i, sa in enumerate(order):
        if flat:
            for sb, sc in spots:
                if share:
                    trade(me.index(sa, sb, sc)).wait_send()
            for sb in (1 - me.b, me.b):
                send_c(sa, sb).wait_send()
            send_b(sa).wait_send()
        if i < planes - 1:
            send_a(sa, False).wait_send()
    if share:
        done.wait_send()
        push(o_ref.at[other], o_ref.at[other], esem.at[0], esem.at[1], me.core()).wait_recv()


def scatter_sum(p, planes, flat, share, out_type, cid, name):
    count, rows, width = p.shape
    half = rows // 2 if share else rows
    one = (16, width)

    def space(use, slots):
        return pltpu.VMEM((slots, half, width), p.dtype) if use else pltpu.VMEM((1,) + one, p.dtype)

    return pl.pallas_call(
        functools.partial(scatter_kernel, planes, flat, share),
        out_shape=jax.ShapeDtypeStruct((rows, width), out_type),
        in_specs=[pl.BlockSpec(memory_space=pl.ANY)],
        out_specs=pl.BlockSpec(memory_space=pltpu.VMEM),
        scratch_shapes=[
            space(True, count),
            space(share, count),
            space(flat, 2 * planes),
            space(flat, planes),
            space(True, planes + 1),
            pltpu.SemaphoreType.DMA((count,)),
            pltpu.SemaphoreType.DMA((count,)),
            pltpu.SemaphoreType.DMA((3, max(2 * planes, planes + 1))),
            pltpu.SemaphoreType.DMA((4, max(count, 2 * planes))),
            pltpu.SemaphoreType.DMA((2,)),
        ],
        compiler_params=pltpu.CompilerParams(collective_id=cid, has_side_effects=True, vmem_limit_bytes=ROOM),
        name=name,
    )(p)


def swap_kernel(x_ref, o_ref, sems):
    me = Spot()
    me.greet(1, False, False, True)
    c = push(x_ref, o_ref, sems.at[0], sems.at[1], me.core())
    c.start()
    c.wait()


def swap_cores(x, cid, name):
    return pl.pallas_call(
        swap_kernel,
        out_shape=jax.ShapeDtypeStruct(x.shape, x.dtype),
        in_specs=[pl.BlockSpec(memory_space=pl.ANY)],
        out_specs=pl.BlockSpec(memory_space=pl.ANY),
        scratch_shapes=[pltpu.SemaphoreType.DMA((2,))],
        compiler_params=pltpu.CompilerParams(collective_id=cid, has_side_effects=True),
        name=name,
    )(x)


def plane_kernel(g_ref, s_ref, go_ref, so_ref, ssem, rsem, lsem):
    me = Spot()
    q = lax.rem(me.e, 4)
    base = me.e - q

    def spot(b, c):
        return me.index(0, b, c)

    near = [(1 - me.b, me.c), (me.b, 1 - me.c), (1 - me.b, 1 - me.c)]
    barrier = pltpu.get_barrier_semaphore()
    for b, c in near:
        pl.semaphore_signal(barrier, inc=1, device_id=(base + spot(b, c), me.t), device_id_type=MESH)
    keep = [
        pltpu.make_async_copy(g_ref, go_ref.at[q], lsem.at[0]),
        pltpu.make_async_copy(s_ref.at[q], so_ref.at[q], lsem.at[1]),
    ]
    for k in keep:
        k.start()
    pl.semaphore_wait(barrier, 3)
    whole = [
        push(g_ref, go_ref.at[q], ssem.at[i], rsem.at[i], (base + spot(*near[i]), me.t)) for i in range(2)
    ]
    parts = [
        push(s_ref.at[spot(*near[i])], so_ref.at[q], ssem.at[3 + i], rsem.at[3 + i], (base + spot(*near[i]), me.t))
        for i in range(3)
    ]
    for k in whole + parts:
        k.start()
    whole[0].wait_recv()
    source = spot(*near[0])
    relay = push(go_ref.at[source], go_ref.at[source], ssem.at[2], rsem.at[2], (base + spot(*near[1]), me.t))
    relay.start()
    whole[0].wait_send()
    whole[1].wait()
    for k in parts:
        k.wait()
    relay.wait()
    for k in keep:
        k.wait()


def plane_exchange(g, s, cid, name):
    return pl.pallas_call(
        plane_kernel,
        out_shape=[jax.ShapeDtypeStruct((4,) + g.shape, g.dtype), jax.ShapeDtypeStruct(s.shape, s.dtype)],
        in_specs=[pl.BlockSpec(memory_space=pl.ANY)] * 2,
        out_specs=[pl.BlockSpec(memory_space=pl.ANY)] * 2,
        scratch_shapes=[
            pltpu.SemaphoreType.DMA((6,)),
            pltpu.SemaphoreType.DMA((6,)),
            pltpu.SemaphoreType.DMA((2,)),
        ],
        compiler_params=pltpu.CompilerParams(collective_id=cid, has_side_effects=True),
        name=name,
    )(g, s)


def total_kernel(count, x_ref, o_ref, land, send, ssem, rsem):
    me = Spot()
    rows = x_ref.shape[0]
    half = rows // 2
    ours = pl.ds(pl.multiple_of(me.t * half, half), half)
    other = pl.ds(pl.multiple_of((1 - me.t) * half, half), half)
    steps = []
    bit = 1
    while bit < count:
        steps.append(me.e + bit * (1 - 2 * lax.rem(lax.div(me.e, bit), 2)))
        bit *= 2
    barrier = pltpu.get_barrier_semaphore()
    for who in steps:
        pl.semaphore_signal(barrier, inc=1, device_id=(who, me.t), device_id_type=MESH)
    pl.semaphore_signal(barrier, inc=1, device_id=me.core(), device_id_type=MESH)
    pl.semaphore_wait(barrier, len(steps) + 1)
    send[0] = x_ref[ours, :]
    copies = []
    for i, who in enumerate(steps):
        c = push(send.at[i], land.at[i], ssem.at[i], rsem.at[i], (who, me.t))
        c.start()
        copies.append(c)
        c.wait_recv()
        if i + 1 < len(steps):
            send[i + 1] = send[i] + land[i]
        else:
            o_ref[ours, :] = send[i] + land[i]
    last = push(o_ref.at[ours], o_ref.at[ours], ssem.at[len(steps)], rsem.at[len(steps)], me.core())
    last.start()
    for c in copies:
        c.wait_send()
    last.wait_send()
    push(o_ref.at[other], o_ref.at[other], ssem.at[len(steps)], rsem.at[len(steps)], me.core()).wait_recv()


def total_over(x, count, cid, name):
    steps = count.bit_length() - 1
    half = (x.shape[0] // 2, x.shape[1])
    return pl.pallas_call(
        functools.partial(total_kernel, count),
        out_shape=jax.ShapeDtypeStruct(x.shape, x.dtype),
        in_specs=[pl.BlockSpec(memory_space=pltpu.VMEM)],
        out_specs=pl.BlockSpec(memory_space=pltpu.VMEM),
        scratch_shapes=[
            pltpu.VMEM((steps,) + half, x.dtype),
            pltpu.VMEM((steps,) + half, x.dtype),
            pltpu.SemaphoreType.DMA((steps + 1,)),
            pltpu.SemaphoreType.DMA((steps + 1,)),
        ],
        compiler_params=pltpu.CompilerParams(collective_id=cid, has_side_effects=True),
        name=name,
    )(x)


def over(first, second, contract):
    return lax.dot_general(first, second, (contract, ((), ())), preferred_element_type=jnp.float32)


NN = ((1,), (0,))
NT = ((1,), (1,))
TN = ((0,), (0,))


def experts_kernel(
    planes,
    parcel_ref,
    up_ref,
    gate_in,
    lift_in,
    down_in,
    all_ref,
    other_ref,
    share_ref,
    home_ref,
    gate_sum,
    lift_sum,
    down_sum,
    wide,
    down,
    wide_half,
    down_half,
    pbuf,
    ubuf,
    xbuf,
    gbuf,
    vbuf,
    sbuf,
    wbuf,
    rbuf,
    hbuf,
    dbuf,
    gates,
    scores,
    stage,
    mine,
    landc,
    landb,
    landa,
    gsend,
    grecv,
    gcore,
    usend,
    urecv,
    wsend,
    wrecv,
    wload,
    hsend,
    hrecv,
    ssem,
    rsem,
    lsem,
    osem,
    esem,
):
    me = Spot()
    f32, bf16 = jnp.float32, jnp.bfloat16
    tokens, packed = parcel_ref.shape
    hidden, width = down_in.shape
    notes_width = packed - width
    count = planes * 4
    half = tokens // 2
    side = width // 2
    slots = sbuf.shape[2]
    own = me.index(me.a, me.b, me.c)
    ours = pl.ds(pl.multiple_of(me.t * half, half), half)
    theirs = pl.ds(pl.multiple_of((1 - me.t) * half, half), half)
    our_side = pl.ds(pl.multiple_of(me.t * side, side), side)
    their_side = pl.ds(pl.multiple_of((1 - me.t) * side, side), side)
    spots = [(sb, sc) for sc in (1 - me.c, me.c) for sb in (1 - me.b, me.b)]

    def near(i):
        return far_first(me.a, planes, planes - 1 - i)


    def carry(idx, kind, src=None):
        who = {
            0: me.at(me.a + 1, me.b, me.c),
            1: me.at(me.a - 1, me.b, me.c),
            2: me.at(me.a, 1 - me.b, me.c),
            3: me.at(me.a, me.b, 1 - me.c),
            4: me.core(),
        }[kind]
        there = all_ref.at[idx, ours]
        landed = gcore if kind == 4 else grecv
        return push(there if src is None else src, there, gsend.at[idx, kind], landed.at[idx], who)

    def relay(sa, act, first):
        idx = me.index(sa, me.b, me.c)
        src = parcel_ref.at[ours] if first else None
        if act and not first:
            carry(idx, 2).wait_recv()
        run = (lambda c: c.start()) if act else (lambda c: c.wait_send())

        @pl.when((sa <= me.a) & (me.a + 1 < planes))
        def _():
            run(carry(idx, 0, src))

        @pl.when((sa >= me.a) & (me.a > 0))
        def _():
            run(carry(idx, 1, src))

        run(carry(idx, 3, src))
        run(carry(idx, 2, src))
        if not first:
            run(carry(idx, 4))
        idx = me.index(sa, 1 - me.b, me.c)
        if act:
            carry(idx, 2).wait_recv()
        run(carry(idx, 3))
        run(carry(idx, 4))

    def across(sa, act):
        for sb in (me.b, 1 - me.b):
            idx = me.index(sa, sb, 1 - me.c)
            if act:
                carry(idx, 2).wait_recv()
                carry(idx, 4).start()
            else:
                carry(idx, 4).wait_send()

    def from_core(sa):
        for sb, sc in spots:
            idx = me.index(sa, sb, sc)

            @pl.when(idx != own)
            def _(idx=idx):
                there = all_ref.at[idx, theirs]
                push(there, there, gsend.at[idx, 4], gcore.at[idx], me.core()).wait_recv()

    def upstream(sa):
        group = pl.ds(sa * 4, 4)
        return push(up_ref.at[group], other_ref.at[group], usend.at[sa], urecv.at[sa], me.core())


    def part(ref, base, size):
        return ref.at[:, pl.ds(pl.multiple_of(base, 128), size)]

    down_rows = down_half.at[pl.ds(pl.multiple_of(me.t * hidden, 128), hidden)]
    wide_cols = [part(wide_half, me.t * 2 * hidden + i * hidden, hidden) for i in range(2)]
    sources = [gate_in, lift_in]
    loads = [pltpu.make_async_copy(sources[i], wide.at[:, i * hidden : (i + 1) * hidden], wload.at[i]) for i in range(2)]
    loads += [pltpu.make_async_copy(sources[i].at[our_side], wide_cols[i], wload.at[2 + i]) for i in range(2)]
    loads += [
        pltpu.make_async_copy(down_in, down, wload.at[4]),
        pltpu.make_async_copy(down_in.at[:, our_side], down_rows, wload.at[5]),
    ]
    pushes = [push(sources[i].at[their_side], wide_cols[i], wsend.at[i], wrecv.at[i], me.core()) for i in range(2)]
    pushes += [push(down_in.at[:, their_side], down_rows, wsend.at[2], wrecv.at[2], me.core())]


    def send_c(sa, sb):
        slot = sa * 2 + sb
        src = mine.at[me.index(sa, sb, 1 - me.c)]
        return push(src, landc.at[slot], ssem.at[0, slot], rsem.at[0, slot], me.at(me.a, me.b, 1 - me.c))

    def send_b(sa):
        src = mine.at[me.index(sa, 1 - me.b, me.c)]
        return push(src, landb.at[sa], ssem.at[1, sa], rsem.at[1, sa], me.at(me.a, 1 - me.b, me.c))

    def send_a(sa, up):
        arrive = me.a + 1 if up else me.a - 1
        slot = sa if up else jnp.where(sa == arrive, planes, sa)
        src = mine.at[me.index(sa, me.b, me.c)]
        return push(src, landa.at[slot], ssem.at[2, sa], rsem.at[2, slot], me.at(arrive, me.b, me.c))

    def from_c(sa):
        for sb in (1 - me.b, me.b):
            slot = sa * 2 + sb
            push(landc.at[slot], landc.at[slot], ssem.at[0, slot], rsem.at[0, slot], me.at(me.a, me.b, 1 - me.c)).wait_recv()
            idx = me.index(sa, sb, me.c)
            add_rows(mine.at[idx], [mine.at[idx], landc.at[slot]])
            if sb is not me.b:
                send_b(sa).start()

    def along(i, sa):
        idx = me.index(sa, me.b, me.c)
        push(landb.at[sa], landb.at[sa], ssem.at[1, sa], rsem.at[1, sa], me.at(me.a, 1 - me.b, me.c)).wait_recv()
        parts = [mine.at[idx], landb.at[sa]]

        def landed(slot):
            push(landa.at[slot], landa.at[slot], ssem.at[2, 0], rsem.at[2, slot], me.at(me.a, me.b, me.c)).wait_recv()

        if i < planes - 1:
            up = sa > me.a
            inner = (up & (me.a > 0)) | (jnp.logical_not(up) & (me.a + 1 < planes))

            @pl.when(inner)
            def _():
                landed(sa)
                add_rows(mine.at[idx], parts + [landa.at[sa]])

            @pl.when(jnp.logical_not(inner))
            def _():
                add_rows(mine.at[idx], parts)

            @pl.when(up)
            def _():
                send_a(sa, True).start()

            @pl.when(jnp.logical_not(up))
            def _():
                send_a(sa, False).start()

        else:
            target = home_ref.at[me.t]

            @pl.when(me.a > 0)
            def _():
                landed(me.a)

            @pl.when(me.a + 1 < planes)
            def _():
                landed(planes)

            @pl.when((me.a > 0) & (me.a + 1 < planes))
            def _():
                add_rows(target, parts + [landa.at[me.a], landa.at[planes]])

            @pl.when(me.a == 0)
            def _():
                add_rows(target, parts + [landa.at[planes]])

            @pl.when(me.a + 1 == planes)
            def _():
                add_rows(target, parts + [landa.at[me.a]])


    def load_rows(sa, q):
        return pltpu.make_async_copy(all_ref.at[sa * 4 + q], pbuf.at[q], lsem.at[q])

    def load_up(sa):
        group = pl.ds(sa * 4, 4)
        return [
            pltpu.make_async_copy(up_ref.at[group], ubuf.at[:, ours], lsem.at[4]),
            pltpu.make_async_copy(other_ref.at[group], ubuf.at[:, theirs], lsem.at[5]),
        ]

    def fetch_up(sa):
        there = other_ref.at[pl.ds(sa * 4, 4)]
        push(there, there, usend.at[sa], urecv.at[sa], me.core()).wait_recv()
        for k in load_up(sa):
            k.start()

    def lanes(rows):
        return lax.broadcasted_iota(jnp.int32, (rows, notes_width), 1)

    def pick_rows(q, sa):
        load_rows(sa, q).wait()
        notes = pbuf[q, :, width:].astype(f32)
        slot_of = jnp.sum(jnp.where(lanes(tokens) == me.e, notes, 0.0), axis=1, keepdims=True)
        chosen = slot_of == lax.broadcasted_iota(jnp.int32, (tokens, slots), 1).astype(f32)
        chosen = jnp.where(chosen, 1.0, 0.0).astype(bf16)
        sbuf[q] = chosen
        at = pl.ds(pl.multiple_of(q * slots, slots), slots)
        there = over(chosen, pbuf[q, :, width:], TN)
        mark = lanes(slots)
        gate = jnp.sum(jnp.where((mark == count + me.e) | (mark == 2 * count + me.e), there, 0.0), axis=1, keepdims=True)
        gates[at, :] = jnp.broadcast_to(gate, (slots, 128))
        for n in range(0, width, 512):
            cut = slice(n, n + 512)
            xbuf[at, cut] = over(chosen, pbuf[q, :, cut], TN).astype(bf16)
            picked = over(chosen, ubuf[q, :, cut], TN)
            gbuf[at, cut] = (picked * gate).astype(bf16)
        for n in range(0, side, 512):
            cut = pl.ds(pl.multiple_of(me.t * side + n, 512), 512)
            vbuf[at, n : n + 512] = over(chosen, ubuf[q, :, cut], TN).astype(bf16)
        return sa

    def hidden_cols(p):
        return pl.ds(pl.multiple_of(p * hidden, 128), hidden)

    def both_cols(p):
        return pl.ds(pl.multiple_of(p * 2 * hidden, 128), 2 * hidden)

    def hidden_rows(r, slot):
        at = pl.ds(pl.multiple_of(r * 256, 256), 256)
        acts = over(xbuf[at, :], wide[...], NN)
        gate_act, up_act = acts[:, :hidden], acts[:, hidden:]
        sig = 1.0 / (1.0 + jnp.exp(-gate_act))
        silu = gate_act * sig
        hbuf[slot, at, hidden_cols(me.t)] = (silu * up_act).astype(bf16)
        back = over(gbuf[at, :], down[...], NT)
        gate_d = (back * up_act * (sig * (1.0 + gate_act * (1.0 - sig)))).astype(bf16)
        dbuf[slot, at, pl.ds(pl.multiple_of(me.t * 2 * hidden, 128), hidden)] = gate_d
        dbuf[slot, at, pl.ds(pl.multiple_of(me.t * 2 * hidden + hidden, 128), hidden)] = (back * silu).astype(bf16)
        return slot

    def trades(slot):
        h_part = hbuf.at[slot, :, hidden_cols(me.t)]
        d_part = dbuf.at[slot, :, both_cols(me.t)]
        return [
            push(h_part, h_part, hsend.at[0], hrecv.at[slot, 0], me.core()),
            push(d_part, d_part, hsend.at[1], hrecv.at[slot, 1], me.core()),
        ]

    def traded(slot):
        h_part = hbuf.at[slot, :, hidden_cols(1 - me.t)]
        d_part = dbuf.at[slot, :, both_cols(1 - me.t)]
        push(h_part, h_part, hsend.at[0], hrecv.at[slot, 0], me.core()).wait_recv()
        push(d_part, d_part, hsend.at[1], hrecv.at[slot, 1], me.core()).wait_recv()

    def weight_sums(n, slot):
        cut = pl.ds(pl.multiple_of(n * 512, 512), 512)
        own_d = dbuf[slot, :, both_cols(me.t)]
        gate_sum[cut, :] += over(xbuf[:, cut], own_d[:, :hidden], TN)
        lift_sum[cut, :] += over(xbuf[:, cut], own_d[:, hidden:], TN)
        down_sum[:, cut] += over(hbuf[slot, :, hidden_cols(me.t)], gbuf[:, cut], TN)
        return slot

    def out_rows(n, slot):
        cut = pl.ds(pl.multiple_of(n * 512, 512), 512)
        for r in range(0, 4 * slots, 256):
            at = slice(r, r + 256)
            out = over(hbuf[slot, at, :], down_half[:, cut], NN)
            wbuf[at, cut] = (out * gates[at, :1]).astype(bf16)
            total = jnp.sum(out * vbuf[at, cut].astype(f32), axis=1, keepdims=True)
            scores[at, :] += jnp.broadcast_to(total, (256, 128))
            rbuf[at, cut] = over(dbuf[slot, at, :], wide_half[cut, :], NT).astype(bf16)
        return slot

    def note_scores():
        mark = lanes(4 * slots)
        total = scores[...]
        high = total.astype(bf16).astype(f32)
        row = jnp.where(mark == me.e, high, jnp.where(mark == me.e + count, total - high, 0.0))
        rbuf[:, side:] = row.astype(bf16)

    def store(idx, q):
        return pltpu.make_async_copy(stage.at[lax.rem(q, 2)], share_ref.at[idx], osem.at[lax.rem(q, 2)])

    def spread_rows(q, sa):
        at = pl.ds(pl.multiple_of(q * slots, slots), slots)
        idx = sa * 4 + q

        @pl.when(q >= 2)
        def _():
            store(idx, q).wait()

        for n in range(0, side, 512):
            cut = slice(n, n + 512)
            mine[idx, :, cut] = over(sbuf[q], rbuf[at, cut], NN).astype(bf16)
            stage[lax.rem(q, 2), :, cut] = over(sbuf[q], wbuf[at, cut], NN).astype(bf16)
        mine[idx, :, side:] = over(sbuf[q], rbuf[at, side:], NN).astype(bf16)
        store(idx, q).start()
        return sa

    local = pltpu.make_async_copy(parcel_ref, all_ref.at[own], lsem.at[6])
    local.start()
    me.greet(planes, True, True, True)
    relay(me.a, True, True)
    for i in list(range(1, planes)) + [0]:
        upstream(near(i)).start()
    for k in loads + pushes:
        k.start()
    relay(near(1), True, False)
    gate_sum[...] = jnp.zeros_like(gate_sum)
    lift_sum[...] = jnp.zeros_like(lift_sum)
    down_sum[...] = jnp.zeros_like(down_sum)
    across(me.a, True)
    fetch_up(near(1))
    for k in loads + pushes:
        k.wait()
    local.wait()

    def step(i, c):
        last = i == planes - 1
        sa = jnp.where(last, me.a, near(i + 1))
        slot = lax.rem(i, 2)

        @pl.when(i + 2 < planes)
        def _():
            relay(near(i + 2), True, False)

        @pl.when(jnp.logical_not(last))
        def _():
            across(sa, True)

        from_core(sa)
        for q in range(4):
            load_rows(sa, q).start()
        for k in load_up(sa):
            k.wait()
        scores[...] = jnp.zeros_like(scores)
        lax.fori_loop(0, 4, pick_rows, sa)

        @pl.when(jnp.logical_not(last))
        def _():
            fetch_up(jnp.where(i + 1 == planes - 1, me.a, near(i + 2)))

        @pl.when(i > 0)
        def _():
            for k in trades(slot):
                k.wait_send()

        lax.fori_loop(0, 4 * slots // 256, hidden_rows, slot)
        for k in trades(slot):
            k.start()
        lax.fori_loop(0, width // 512, weight_sums, slot)
        traded(slot)
        lax.fori_loop(0, side // 512, out_rows, slot)
        note_scores()
        lax.fori_loop(0, 4, spread_rows, sa)
        for sb in (1 - me.b, me.b):
            send_c(sa, sb).start()
        store(0, 0).wait()
        store(0, 1).wait()

        @pl.when(i > 0)
        def _():
            from_c(near(i))

        return c

    lax.fori_loop(0, planes, step, 0)
    for i in range(planes - 1):
        along(i, far_first(me.a, planes, i))
    from_c(me.a)
    along(planes - 1, me.a)
    done = push(home_ref.at[me.t], home_ref.at[me.t], esem.at[0], esem.at[1], me.core())
    done.start()

    relay(me.a, False, True)

    def settle(i, c):
        sa = near(i)

        @pl.when(i > 0)
        def _():
            relay(sa, False, False)
            send_a(sa, False).wait_send()

        across(sa, False)
        for sb in (1 - me.b, me.b):
            send_c(sa, sb).wait_send()
        send_b(sa).wait_send()
        upstream(sa).wait_send()
        return c

    lax.fori_loop(0, planes, settle, 0)
    for k in trades(0):
        k.wait_send()
    done.wait_send()
    other = home_ref.at[1 - me.t]
    push(other, other, esem.at[0], esem.at[1], me.core()).wait_recv()


def run_experts(parcel, upstream, gate, lift_w, down, planes, slots, cid):
    f32, bf16 = jnp.float32, jnp.bfloat16
    tokens, packed = parcel.shape
    hidden, width = down.shape
    count = planes * 4
    half = tokens // 2
    side = width // 2
    block = side + packed - width
    rows = 4 * slots
    anywhere = pl.BlockSpec(memory_space=pl.ANY)
    inside = pl.BlockSpec(memory_space=pltpu.VMEM)
    return pl.pallas_call(
        functools.partial(experts_kernel, planes),
        out_shape=[
            jax.ShapeDtypeStruct((count, tokens, packed), bf16),
            jax.ShapeDtypeStruct((count, half, width), bf16),
            jax.ShapeDtypeStruct((count, tokens, side), bf16),
            jax.ShapeDtypeStruct((2, tokens, block), bf16),
            jax.ShapeDtypeStruct((width, hidden), f32),
            jax.ShapeDtypeStruct((width, hidden), f32),
            jax.ShapeDtypeStruct((hidden, width), f32),
        ],
        in_specs=[anywhere] * 5,
        out_specs=[anywhere] * 3 + [inside] * 4,
        scratch_shapes=[
            pltpu.VMEM((width, 2 * hidden), bf16),
            pltpu.VMEM((hidden, width), bf16),
            pltpu.VMEM((side, 4 * hidden), bf16),
            pltpu.VMEM((2 * hidden, side), bf16),
            pltpu.VMEM((4, tokens, packed), bf16),
            pltpu.VMEM((4, tokens, width), bf16),
            pltpu.VMEM((rows, width), bf16),
            pltpu.VMEM((rows, width), bf16),
            pltpu.VMEM((rows, side), bf16),
            pltpu.VMEM((4, tokens, slots), bf16),
            pltpu.VMEM((rows, side), bf16),
            pltpu.VMEM((rows, block), bf16),
            pltpu.VMEM((2, rows, 2 * hidden), bf16),
            pltpu.VMEM((2, rows, 4 * hidden), bf16),
            pltpu.VMEM((rows, 128), f32),
            pltpu.VMEM((rows, 128), f32),
            pltpu.VMEM((2, tokens, side), bf16),
            pltpu.VMEM((count, tokens, block), bf16),
            pltpu.VMEM((2 * planes, tokens, block), bf16),
            pltpu.VMEM((planes, tokens, block), bf16),
            pltpu.VMEM((planes + 1, tokens, block), bf16),
            pltpu.SemaphoreType.DMA((count, 5)),
            pltpu.SemaphoreType.DMA((count,)),
            pltpu.SemaphoreType.DMA((count,)),
            pltpu.SemaphoreType.DMA((planes,)),
            pltpu.SemaphoreType.DMA((planes,)),
            pltpu.SemaphoreType.DMA((3,)),
            pltpu.SemaphoreType.DMA((3,)),
            pltpu.SemaphoreType.DMA((6,)),
            pltpu.SemaphoreType.DMA((2,)),
            pltpu.SemaphoreType.DMA((2, 2)),
            pltpu.SemaphoreType.DMA((3, 2 * planes)),
            pltpu.SemaphoreType.DMA((3, 2 * planes)),
            pltpu.SemaphoreType.DMA((7,)),
            pltpu.SemaphoreType.DMA((2,)),
            pltpu.SemaphoreType.DMA((2,)),
        ],
        compiler_params=pltpu.CompilerParams(
            collective_id=cid, has_side_effects=True, vmem_limit_bytes=62 * 2**20
        ),
        name="experts",
    )(parcel, upstream, gate, lift_w, down)


def stack_heads(target, source, group):
    items, rows, size = target.shape
    seg = rows // group
    keys = source.shape[1] // (group * size)
    for s in range(items // keys):
        for k in range(keys):
            for h in range(group):
                at = (k * group + h) * size
                part = source[s * seg : (s + 1) * seg, at : at + size]
                target[s * keys + k, h * seg : (h + 1) * seg, :] = part.astype(target.dtype)


def spread_heads(target, item, value, group, keys):
    rows, size = value.shape
    seg = rows // group
    s, k = item // keys, item % keys
    for h in range(group):
        at = (k * group + h) * size
        target[s * seg : (s + 1) * seg, at : at + size] = value[h * seg : (h + 1) * seg, :].astype(target.dtype)


def block_heads(ref, plane, item, keys, size, part):
    seg = BLOCK // 4
    s, k = lax.div(item, keys), lax.rem(item, keys)
    rows = pl.ds(pl.multiple_of(s * seg, seg), seg)
    cols = pl.ds(pl.multiple_of((part * keys + k) * size, size), size)
    return [ref.at[plane * 4 + q, rows, cols] for q in range(4)]


def joined(refs):
    return jnp.concatenate([ref[...] for ref in refs], axis=0)


def attend_kernel(
    planes, group, q_ref, x_ref, context_ref, all_ref, log_ref, qs, top, total, acc, ssem, rsem, lsem
):
    me = Spot()
    f32, bf16 = jnp.float32, jnp.bfloat16
    items, rows, size = qs.shape
    keys = x_ref.shape[1] // (2 * size)
    factor = size ** (-0.5)
    own = me.index(me.a, me.b, me.c)

    def carry(idx, kind, src=None):
        who = {
            0: me.at(me.a + 1, me.b, me.c),
            2: me.at(me.a, 1 - me.b, me.c),
            3: me.at(me.a, me.b, 1 - me.c),
        }[kind]
        there = all_ref.at[idx]
        return push(there if src is None else src, there, ssem.at[idx, kind], rsem.at[idx], who)

    def relay(sa, act, first):
        idx = me.index(sa, me.b, me.c)
        src = x_ref if first else None
        if act and not first:
            carry(idx, 2).wait_recv()
        run = (lambda c: c.start()) if act else (lambda c: c.wait_send())

        @pl.when(me.a + 1 < planes)
        def _():
            run(carry(idx, 0, src))

        run(carry(idx, 3, src))
        run(carry(idx, 2, src))
        idx = me.index(sa, 1 - me.b, me.c)
        if act:
            carry(idx, 2).wait_recv()
        run(carry(idx, 3))

    def block(item, sa):
        scores = over(qs[item], joined(block_heads(all_ref, sa, item, keys, size, 0)), NT) * factor
        values = joined(block_heads(all_ref, sa, item, keys, size, 1))
        before = top[item]
        high = jnp.maximum(before, jnp.broadcast_to(jnp.max(scores, axis=1, keepdims=True), before.shape))
        shrink = jnp.exp(before - high)
        terms = jnp.exp(scores - high[:, :1])
        top[item] = high
        total[item] = total[item] * shrink + jnp.broadcast_to(jnp.sum(terms, axis=1, keepdims=True), before.shape)
        acc[item] = acc[item] * shrink + over(terms.astype(bf16), values, NN)
        return sa

    local = pltpu.make_async_copy(x_ref, all_ref.at[own], lsem)
    local.start()
    me.greet(planes, True, True, False)
    relay(me.a, True, True)
    stack_heads(qs, q_ref, group)
    top[...] = jnp.full(top.shape, far_below, f32)
    total[...] = jnp.zeros_like(total)
    acc[...] = jnp.zeros_like(acc)
    local.wait()

    def step(i, c):
        sa = me.a - i

        @pl.when(sa > 0)
        def _():
            relay(sa - 1, True, False)

        for sb in (me.b, 1 - me.b):
            carry(me.index(sa, sb, 1 - me.c), 2).wait_recv()
        lax.fori_loop(0, items, block, sa)
        return c

    lax.fori_loop(0, me.a + 1, step, 0)
    for item in range(items):
        spread_heads(context_ref, item, acc[item] / total[item], group, keys)
    log_ref[...] = top[...] + jnp.log(total[...])
    relay(me.a, False, True)

    def settle(i, c):
        relay(me.a - i, False, False)
        return c

    lax.fori_loop(1, me.a + 1, settle, 0)


def attend(query, pairs, planes, group, size, cid):
    f32, bf16 = jnp.float32, jnp.bfloat16
    tokens, width = query.shape
    count = planes * 4
    items = (tokens * 4 // BLOCK) * (width // (group * size))
    state = (items, group * BLOCK // 4, size)
    inside = pl.BlockSpec(memory_space=pltpu.VMEM)
    return pl.pallas_call(
        functools.partial(attend_kernel, planes, group),
        out_shape=[
            jax.ShapeDtypeStruct((tokens, width), bf16),
            jax.ShapeDtypeStruct((count,) + pairs.shape, bf16),
            jax.ShapeDtypeStruct(state, f32),
        ],
        in_specs=[inside] * 2,
        out_specs=[inside] * 3,
        scratch_shapes=[
            pltpu.VMEM(state, bf16),
            pltpu.VMEM(state, f32),
            pltpu.VMEM(state, f32),
            pltpu.VMEM(state, f32),
            pltpu.SemaphoreType.DMA((count, 4)),
            pltpu.SemaphoreType.DMA((count,)),
            pltpu.SemaphoreType.DMA,
        ],
        compiler_params=pltpu.CompilerParams(collective_id=cid, has_side_effects=True, vmem_limit_bytes=ROOM),
        name="attend",
    )(query, pairs)


def attend_back_kernel(
    planes,
    group,
    q_ref,
    g_ref,
    o_ref,
    all_ref,
    log_ref,
    cut_ref,
    query_grad,
    pair_grad,
    plane_o,
    plane_cut,
    qs,
    gs,
    delta,
    qacc,
    mine,
    landc,
    landb,
    landa,
    ssem,
    rsem,
    psend,
    precv,
    lsem,
):
    me = Spot()
    f32, bf16 = jnp.float32, jnp.bfloat16
    items, rows, size = qs.shape
    keys = all_ref.shape[2] // (2 * size)
    factor = size ** (-0.5)
    place = lax.rem(me.e, 4)
    base = me.e - place

    def spot(b, c):
        return me.index(0, b, c)

    near = [(1 - me.b, me.c), (me.b, 1 - me.c), (1 - me.b, 1 - me.c)]
    keep = [
        pltpu.make_async_copy(o_ref, plane_o.at[place], lsem.at[0]),
        pltpu.make_async_copy(cut_ref.at[place], plane_cut.at[place], lsem.at[1]),
    ]
    for k in keep:
        k.start()
    barrier = pltpu.get_barrier_semaphore()
    for b, c in near:
        pl.semaphore_signal(barrier, inc=1, device_id=(base + spot(b, c), me.t), device_id_type=MESH)
    up, down = me.a + 1 < planes, me.a > 0

    @pl.when(up)
    def _():
        pl.semaphore_signal(barrier, inc=1, device_id=me.at(me.a + 1, me.b, me.c), device_id_type=MESH)

    @pl.when(down)
    def _():
        pl.semaphore_signal(barrier, inc=1, device_id=me.at(me.a - 1, me.b, me.c), device_id_type=MESH)

    pl.semaphore_wait(barrier, 3 + up.astype(jnp.int32) + down.astype(jnp.int32))
    parts = [
        push(cut_ref.at[spot(*near[i])], plane_cut.at[place], psend.at[3 + i], precv.at[3 + i], (base + spot(*near[i]), me.t))
        for i in range(3)
    ]
    whole = [push(o_ref, plane_o.at[place], psend.at[i], precv.at[i], (base + spot(*near[i]), me.t)) for i in range(2)]
    for k in parts + whole:
        k.start()

    stack_heads(qs, q_ref, group)
    stack_heads(gs, g_ref, group)
    stack_heads(qacc, o_ref, group)

    def prepare(item, c):
        part = jnp.sum(gs[item].astype(f32) * qacc[item], axis=1, keepdims=True)
        delta[item] = jnp.broadcast_to(part, delta.shape[1:])
        qacc[item] = jnp.zeros(qacc.shape[1:], f32)
        return c

    lax.fori_loop(0, items, prepare, 0)

    def block(item, sa):
        keys_here = joined(block_heads(all_ref, sa, item, keys, size, 0))
        values = joined(block_heads(all_ref, sa, item, keys, size, 1))
        queries, grads = qs[item], gs[item]
        scores = over(queries, keys_here, NT) * factor
        probs = jnp.exp(scores - log_ref[item][:, :1])
        prob_grads = over(grads, values, NT)
        score_grads = (probs * (prob_grads - delta[item][:, :1])).astype(bf16)
        qacc[item] += over(score_grads, keys_here, NN)
        key_part = (over(score_grads, queries, TN) * factor).astype(bf16)
        value_part = over(probs.astype(bf16), grads, TN).astype(bf16)
        seg = key_part.shape[0] // 4
        for part, value in ((0, key_part), (1, value_part)):
            for q, ref in enumerate(block_heads(mine, sa, item, keys, size, part)):
                ref[...] = value[q * seg : (q + 1) * seg, :]
        return sa

    def send_c(sa, sb):
        slot = sa * 2 + sb
        src = mine.at[me.index(sa, sb, 1 - me.c)]
        return push(src, landc.at[slot], ssem.at[0, slot], rsem.at[0, slot], me.at(me.a, me.b, 1 - me.c))

    def send_b(sa):
        src = mine.at[me.index(sa, 1 - me.b, me.c)]
        return push(src, landb.at[sa], ssem.at[1, sa], rsem.at[1, sa], me.at(me.a, 1 - me.b, me.c))

    def send_a(sa):
        src = mine.at[me.index(sa, me.b, me.c)]
        return push(src, landa.at[sa], ssem.at[2, sa], rsem.at[2, sa], me.at(me.a - 1, me.b, me.c))

    def from_c(sa):
        for sb in (1 - me.b, me.b):
            slot = sa * 2 + sb
            push(landc.at[slot], landc.at[slot], ssem.at[0, slot], rsem.at[0, slot], me.at(me.a, me.b, 1 - me.c)).wait_recv()
            idx = me.index(sa, sb, me.c)
            add_rows(mine.at[idx], [mine.at[idx], landc.at[slot]])
            if sb is not me.b:
                send_b(sa).start()

    def along(sa):
        idx = me.index(sa, me.b, me.c)
        push(landb.at[sa], landb.at[sa], ssem.at[1, sa], rsem.at[1, sa], me.at(me.a, 1 - me.b, me.c)).wait_recv()

        def finish(target):
            @pl.when(me.a + 1 < planes)
            def _():
                push(landa.at[sa], landa.at[sa], ssem.at[2, sa], rsem.at[2, sa], me.at(me.a, me.b, me.c)).wait_recv()
                add_rows(target, [mine.at[idx], landb.at[sa], landa.at[sa]])

            @pl.when(me.a + 1 == planes)
            def _():
                add_rows(target, [mine.at[idx], landb.at[sa]])

        @pl.when(sa < me.a)
        def _():
            finish(mine.at[idx])
            send_a(sa).start()

        @pl.when(sa == me.a)
        def _():
            finish(pair_grad)

    source = spot(*near[0])
    relay = push(plane_o.at[source], plane_o.at[source], psend.at[2], precv.at[2], (base + spot(*near[1]), me.t))

    def step(sa, c):
        lax.fori_loop(0, items, block, sa)
        for sb in (1 - me.b, me.b):
            send_c(sa, sb).start()

        @pl.when(sa == 0)
        def _():
            whole[0].wait_recv()
            relay.start()

        @pl.when(sa >= 1)
        def _():
            from_c(sa - 1)

        @pl.when(sa >= 2)
        def _():
            along(sa - 2)

        return c

    lax.fori_loop(0, me.a + 1, step, 0)
    for item in range(items):
        spread_heads(query_grad, item, qacc[item] * factor, group, keys)
    from_c(me.a)

    @pl.when(me.a > 0)
    def _():
        along(me.a - 1)

    along(me.a)

    def settle(sa, c):
        for sb in (1 - me.b, me.b):
            send_c(sa, sb).wait_send()
        send_b(sa).wait_send()

        @pl.when(sa < me.a)
        def _():
            send_a(sa).wait_send()

        return c

    lax.fori_loop(0, me.a + 1, settle, 0)
    whole[0].wait_send()
    whole[1].wait()
    for k in parts:
        k.wait()
    relay.wait()
    for k in keep:
        k.wait()


def attend_back(query, grads, context, pairs_all, logs, cut, planes, group, size, cid):
    f32, bf16 = jnp.float32, jnp.bfloat16
    tokens, width = query.shape
    items = logs.shape[0]
    state = logs.shape
    block = pairs_all.shape[1:]
    inside = pl.BlockSpec(memory_space=pltpu.VMEM)
    anywhere = pl.BlockSpec(memory_space=pl.ANY)
    return pl.pallas_call(
        functools.partial(attend_back_kernel, planes, group),
        out_shape=[
            jax.ShapeDtypeStruct((tokens, width), f32),
            jax.ShapeDtypeStruct(block, f32),
            jax.ShapeDtypeStruct((4,) + context.shape, bf16),
            jax.ShapeDtypeStruct(cut.shape, bf16),
        ],
        in_specs=[inside] * 5 + [anywhere],
        out_specs=[inside, inside, anywhere, anywhere],
        scratch_shapes=[
            pltpu.VMEM(state, bf16),
            pltpu.VMEM(state, bf16),
            pltpu.VMEM(state, f32),
            pltpu.VMEM(state, f32),
            pltpu.VMEM((4 * planes,) + block, bf16),
            pltpu.VMEM((2 * planes,) + block, bf16),
            pltpu.VMEM((planes,) + block, bf16),
            pltpu.VMEM((planes,) + block, bf16),
            pltpu.SemaphoreType.DMA((3, 2 * planes)),
            pltpu.SemaphoreType.DMA((3, 2 * planes)),
            pltpu.SemaphoreType.DMA((6,)),
            pltpu.SemaphoreType.DMA((6,)),
            pltpu.SemaphoreType.DMA((2,)),
        ],
        compiler_params=pltpu.CompilerParams(collective_id=cid, has_side_effects=True, vmem_limit_bytes=ROOM),
        name="attend_back",
    )(query, grads, context, pairs_all, logs, cut)


epsilon = 1e-06
rope_base = 1000000.0
far_below = -1e30


def rms_scaled(values, gain_vec):
    return (
        values * lax.rsqrt(jnp.mean(values * values, axis=-1, keepdims=True) + epsilon) * gain_vec
    )


def rotary_tables(positions, head_dim):
    halfway = head_dim // 2
    exponents = jnp.arange(halfway, dtype=jnp.float32) * (2.0 / head_dim)
    inverse = jnp.exp(-exponents * jnp.log(jnp.float32(rope_base)))
    angles = positions.astype(jnp.float32)[:, None] * inverse[None, :]
    return (jnp.cos(angles), jnp.sin(angles))


def rotate(values, cosine, sine_table):
    halfway = values.shape[-1] // 2
    first = values[..., :halfway]
    latter = values[..., halfway:]
    return jnp.concatenate(
        [first * cosine - latter * sine_table, latter * cosine + first * sine_table], axis=-1
    )


def glu_value(gate_act, up_act):
    return jax.nn.silu(gate_act) * up_act


def on_device(
    layer_input,
    norm_first,
    query_weight,
    key_weight,
    value_weight,
    mixing_weight,
    query_gain,
    key_gain,
    norm_second,
    router_weight,
    gate_weight,
    up_weight,
    down_weight,
    routes,
    fill_order,
    cotangent,
):
    seq_count, seg_len, model_width = layer_input.shape
    expert_count = lax.axis_size("expert")
    tensor_count = lax.axis_size("tensor")
    expert_idx = lax.axis_index("expert")
    tensor_idx = lax.axis_index("tensor")
    head_dim = query_gain.shape[0]
    local_queries = query_weight.shape[1] // head_dim
    local_keys = key_weight.shape[1] // head_dim
    group_size = local_queries // local_keys
    seq_length = seg_len * expert_count
    top_count = routes.shape[2]
    token_count = seq_count * seg_len
    capacity = 5 * token_count * top_count // (4 * expert_count)
    half_width = model_width // tensor_count
    factor = head_dim ** (-0.5)
    inputs = layer_input.astype(jnp.float32)
    normed_f, first_back = jax.vjp(rms_scaled, inputs, norm_first)
    normed = normed_f.astype(jnp.bfloat16)
    positions = expert_idx * seg_len + jnp.arange(seg_len, dtype=jnp.int32)
    cosine, sine_table = rotary_tables(positions, head_dim)
    cosine = cosine[:, None, :]
    sine_table = sine_table[:, None, :]

    def rope_norm(raw_heads, gain_vec):
        return rotate(rms_scaled(raw_heads, gain_vec), cosine, sine_table)

    query_raw = jnp.dot(normed, query_weight, preferred_element_type=jnp.float32).reshape(
        seq_count, seg_len, local_queries, head_dim
    )
    key_raw = jnp.dot(normed, key_weight, preferred_element_type=jnp.float32).reshape(
        seq_count, seg_len, local_keys, head_dim
    )
    value_local = jnp.dot(normed, value_weight, preferred_element_type=jnp.float32).astype(
        jnp.bfloat16
    )
    query_rot, query_back = jax.vjp(rope_norm, query_raw, query_gain)
    key_rot, key_back = jax.vjp(rope_norm, key_raw, key_gain)
    key_local = key_rot.astype(jnp.bfloat16).reshape(seq_count, seg_len, local_keys * head_dim)
    key_all, value_all = (
        lax.all_gather(key_local, "expert", axis=1, tiled=True),
        lax.all_gather(value_local, "expert", axis=1, tiled=True),
    )
    key_tiles = key_all.reshape(seq_count, seq_length, local_keys, head_dim)
    value_tiles = value_all.reshape(seq_count, seq_length, local_keys, head_dim)
    query_rows = query_rot.astype(jnp.bfloat16).reshape(
        seq_count, seg_len, local_keys, group_size, head_dim
    )
    query_rows = query_rows.transpose(0, 2, 3, 1, 4).reshape(
        seq_count, local_keys, group_size * seg_len, head_dim
    )
    row_block = (
        expert_idx * seg_len + jnp.arange(group_size * seg_len, dtype=jnp.int32) % seg_len
    ) // BLOCK
    tile_len = min(512, seq_length)
    reach_end = jnp.minimum(((expert_idx + 1) * seg_len - 1) // BLOCK * BLOCK + BLOCK, seq_length)
    tile_count = (reach_end + tile_len - 1) // tile_len

    def tile_scores(tile_idx):
        offset = tile_idx * tile_len
        key_part = lax.dynamic_slice_in_dim(key_tiles, offset, tile_len, 1)
        scores = (
            jnp.einsum("shrd,skhd->shrk", query_rows, key_part, preferred_element_type=jnp.float32)
            * factor
        )
        key_block = (offset + jnp.arange(tile_len, dtype=jnp.int32)) // BLOCK
        allowed = key_block[None, :] <= row_block[:, None]
        return (scores, allowed, offset)

    stat_shape = (seq_count, local_keys, group_size * seg_len)

    def stats_step(tile_idx, state_pair):
        running_max, running_sum = state_pair
        scores, allowed, offset = tile_scores(tile_idx)
        masked = jnp.where(allowed, scores, far_below)
        new_max = jnp.maximum(running_max, jnp.max(masked, axis=-1))
        exp_terms = jnp.where(allowed, jnp.exp(masked - new_max[..., None]), 0.0)
        return (new_max, running_sum * jnp.exp(running_max - new_max) + jnp.sum(exp_terms, axis=-1))

    row_max, row_sum = lax.fori_loop(
        0,
        tile_count,
        stats_step,
        (jnp.full(stat_shape, far_below, jnp.float32), jnp.zeros(stat_shape, jnp.float32)),
    )
    log_total = row_max + jnp.log(row_sum)

    def probabilities(tile_idx):
        scores, allowed, offset = tile_scores(tile_idx)
        return (jnp.where(allowed, jnp.exp(scores - log_total[..., None]), 0.0), offset)

    def context_step(tile_idx, context_sum):
        prob_tile, offset = probabilities(tile_idx)
        value_part = lax.dynamic_slice_in_dim(value_tiles, offset, tile_len, 1)
        return context_sum + jnp.einsum(
            "shrk,skhd->shrd",
            prob_tile.astype(jnp.bfloat16),
            value_part,
            preferred_element_type=jnp.float32,
        )

    context_f = lax.fori_loop(0, tile_count, context_step, jnp.zeros(query_rows.shape, jnp.float32))
    shaped = context_f.reshape(seq_count, local_keys, group_size, seg_len, head_dim).transpose(
        0, 3, 1, 2, 4
    )
    context = shaped.reshape(seq_count, seg_len, local_queries * head_dim).astype(jnp.bfloat16)
    head_part = jnp.dot(context, mixing_weight, preferred_element_type=jnp.float32)
    residual = inputs + lax.psum(head_part.astype(jnp.bfloat16), "tensor").astype(jnp.float32)
    second_f, second_back = jax.vjp(rms_scaled, residual, norm_second)
    second = second_f.astype(jnp.bfloat16).reshape(token_count, model_width)
    logits = jnp.dot(second, router_weight, preferred_element_type=jnp.float32)
    flat_routes = routes.reshape(token_count, top_count)
    picked = (flat_routes[:, :, None] == jnp.arange(expert_count, dtype=jnp.int32)).astype(
        jnp.float32
    )
    gates = jax.nn.softmax(jnp.sum(picked * logits[:, None, :], axis=-1), axis=-1)
    usages = jnp.sum(picked, axis=1)
    ranking = fill_order.reshape(token_count)
    before = (ranking[None, :] < ranking[:, None]).astype(jnp.bfloat16)
    counts = jnp.dot(before, usages.astype(jnp.bfloat16), preferred_element_type=jnp.float32)
    slot_ids = jnp.sum(picked * counts[:, None, :], axis=-1).astype(jnp.int32)
    kept_mask = slot_ids < capacity
    kept_float = kept_mask.astype(jnp.float32)
    weighted = gates * kept_float
    places = jnp.where(kept_mask, flat_routes * capacity + slot_ids, -1)
    slot_grid = jnp.arange(expert_count * capacity, dtype=jnp.int32)
    assign = (places[:, :, None] == slot_grid).astype(jnp.bfloat16)
    placed = jnp.sum(assign, axis=1)
    combine = jnp.sum(weighted[:, :, None] * assign.astype(jnp.float32), axis=1)
    send_rows = jnp.einsum("tp,td->pd", placed, second, preferred_element_type=jnp.float32).astype(
        jnp.bfloat16
    )
    arrived = lax.all_to_all(
        send_rows.reshape(expert_count, capacity, model_width),
        "expert",
        split_axis=0,
        concat_axis=0,
        tiled=True,
    )
    arrived = arrived.reshape(expert_count * capacity, model_width)
    gate_one = gate_weight[0]
    up_one = up_weight[0]
    down_one = down_weight[0]
    gate_act = jnp.dot(arrived, gate_one, preferred_element_type=jnp.float32)
    up_act = jnp.dot(arrived, up_one, preferred_element_type=jnp.float32)
    hidden_val, glu_back = jax.vjp(glu_value, gate_act, up_act)
    hidden = hidden_val.astype(jnp.bfloat16)
    expert_part = jnp.dot(hidden, down_one, preferred_element_type=jnp.float32)
    summed = lax.psum(expert_part.astype(jnp.bfloat16), "tensor")
    returned = lax.all_to_all(
        summed.reshape(expert_count, capacity, model_width),
        "expert",
        split_axis=0,
        concat_axis=0,
        tiled=True,
    )
    returned = returned.reshape(expert_count * capacity, model_width)
    per_route = (
        jnp.take(returned, jnp.maximum(places, 0), axis=0).astype(jnp.float32)
        * kept_float[:, :, None]
    )
    mixture = residual.reshape(token_count, model_width) + jnp.sum(
        weighted[:, :, None] * per_route, axis=1
    )
    layer_output = lax.dynamic_slice_in_dim(mixture, tensor_idx * half_width, half_width, 1)
    layer_output = layer_output.astype(jnp.bfloat16).reshape(seq_count, seg_len, half_width)
    upstream = cotangent.astype(jnp.float32).reshape(token_count, model_width)
    gate_grads = jnp.sum(upstream[:, None, :] * per_route, axis=-1) * kept_float
    send_grads = jnp.einsum(
        "tp,td->pd",
        combine,
        upstream,
        precision=lax.Precision.HIGHEST,
        preferred_element_type=jnp.float32,
    ).astype(jnp.bfloat16)
    grads_in = lax.all_to_all(
        send_grads.reshape(expert_count, capacity, model_width),
        "expert",
        split_axis=0,
        concat_axis=0,
        tiled=True,
    )
    grads_in = grads_in.reshape(expert_count * capacity, model_width)
    hidden_grad = lax.dot_general(
        grads_in, down_one, (((1,), (1,)), ((), ())), preferred_element_type=jnp.float32
    )
    down_grad = jnp.einsum("rf,rd->fd", hidden, grads_in, preferred_element_type=jnp.float32)
    gate_d, up_d = glu_back(hidden_grad)
    gate_d = gate_d.astype(jnp.bfloat16)
    up_d = up_d.astype(jnp.bfloat16)
    gate_grad = jnp.einsum("rd,rf->df", arrived, gate_d, preferred_element_type=jnp.float32)
    up_grad = jnp.einsum("rd,rf->df", arrived, up_d, preferred_element_type=jnp.float32)
    row_part = lax.dot_general(
        gate_d, gate_one, (((1,), (1,)), ((), ())), preferred_element_type=jnp.float32
    )
    row_part = row_part + lax.dot_general(
        up_d, up_one, (((1,), (1,)), ((), ())), preferred_element_type=jnp.float32
    )
    row_share = lax.psum_scatter(
        row_part.reshape(expert_count, capacity, model_width).astype(jnp.bfloat16),
        "tensor",
        scatter_dimension=2,
        tiled=True,
    )
    row_home = lax.all_to_all(row_share, "expert", split_axis=0, concat_axis=0, tiled=True).reshape(
        expert_count * capacity, half_width
    )
    second_half = jnp.dot(placed, row_home, preferred_element_type=jnp.float32)
    route_grads = gates * (gate_grads - jnp.sum(gates * gate_grads, axis=-1, keepdims=True))
    logit_grads = jnp.sum(picked * route_grads[:, :, None], axis=1).astype(jnp.bfloat16)
    router_grad = jnp.einsum("td,te->de", second, logit_grads, preferred_element_type=jnp.float32)
    router_back = lax.dot_general(
        logit_grads, router_weight, (((1,), (1,)), ((), ())), preferred_element_type=jnp.float32
    )
    own_part = second_half + lax.dynamic_slice_in_dim(
        router_back, tensor_idx * half_width, half_width, 1
    )
    second_part = lax.dynamic_update_slice_in_dim(
        jnp.zeros((token_count, model_width), jnp.float32), own_part, tensor_idx * half_width, 1
    )
    residual_part, norm_part = second_back(second_part.reshape(seq_count, seg_len, model_width))
    residual_grad, second_grad = (
        lax.psum(residual_part.astype(jnp.bfloat16), "tensor").astype(jnp.float32),
        lax.psum(norm_part.astype(jnp.bfloat16), "tensor").astype(jnp.float32),
    )
    residual_grad = residual_grad + upstream.reshape(seq_count, seg_len, model_width)
    head_in = residual_grad.astype(jnp.bfloat16)
    mixing_part = jnp.einsum("std,stc->dc", head_in, context, preferred_element_type=jnp.float32)
    context_grad = lax.dot_general(
        head_in, mixing_weight, (((2,), (1,)), ((), ())), preferred_element_type=jnp.float32
    ).astype(jnp.bfloat16)
    grad_rows = context_grad.reshape(
        seq_count, seg_len, local_keys, group_size, head_dim
    ).transpose(0, 2, 3, 1, 4)
    grad_rows = grad_rows.reshape(query_rows.shape)
    delta_rows = jnp.sum(grad_rows.astype(jnp.float32) * context_f, axis=-1)
    key_shape = (seq_count, seq_length, local_keys, head_dim)

    def gradient_step(tile_idx, state_trio):
        query_acc, key_acc, value_acc = state_trio
        prob_tile, offset = probabilities(tile_idx)
        key_part = lax.dynamic_slice_in_dim(key_tiles, offset, tile_len, 1)
        value_part = lax.dynamic_slice_in_dim(value_tiles, offset, tile_len, 1)
        prob_low = prob_tile.astype(jnp.bfloat16)
        prob_grad = jnp.einsum(
            "shrd,skhd->shrk", grad_rows, value_part, preferred_element_type=jnp.float32
        )
        score_grad = (prob_tile * (prob_grad - delta_rows[..., None])).astype(jnp.bfloat16)
        query_acc = query_acc + jnp.einsum(
            "shrk,skhd->shrd", score_grad, key_part, preferred_element_type=jnp.float32
        )
        key_tile = jnp.einsum(
            "shrk,shrd->skhd", score_grad, query_rows, preferred_element_type=jnp.float32
        )
        value_tile = jnp.einsum(
            "shrk,shrd->skhd", prob_low, grad_rows, preferred_element_type=jnp.float32
        )
        key_acc = lax.dynamic_update_slice_in_dim(key_acc, key_tile, offset, 1)
        value_acc = lax.dynamic_update_slice_in_dim(value_acc, value_tile, offset, 1)
        return (query_acc, key_acc, value_acc)

    start_state = (
        jnp.zeros(query_rows.shape, jnp.float32),
        jnp.zeros(key_shape, jnp.float32),
        jnp.zeros(key_shape, jnp.float32),
    )
    query_acc, key_acc, value_acc = lax.fori_loop(0, tile_count, gradient_step, start_state)
    key_grad_all, value_grad_all = (
        lax.psum_scatter(
            (key_acc * factor).reshape(seq_count, seq_length, local_keys * head_dim),
            "expert",
            scatter_dimension=1,
            tiled=True,
        ),
        lax.psum_scatter(
            value_acc.reshape(seq_count, seq_length, local_keys * head_dim),
            "expert",
            scatter_dimension=1,
            tiled=True,
        ),
    )
    key_raw_grad, keygain_part = key_back(
        key_grad_all.reshape(seq_count, seg_len, local_keys, head_dim)
    )
    query_shaped = (
        (query_acc * factor)
        .reshape(seq_count, local_keys, group_size, seg_len, head_dim)
        .transpose(0, 3, 1, 2, 4)
    )
    query_raw_grad, querygain_part = query_back(
        query_shaped.reshape(seq_count, seg_len, local_queries, head_dim)
    )
    query_low = query_raw_grad.astype(jnp.bfloat16).reshape(
        seq_count, seg_len, local_queries * head_dim
    )
    key_low = key_raw_grad.astype(jnp.bfloat16).reshape(seq_count, seg_len, local_keys * head_dim)
    value_low = value_grad_all.astype(jnp.bfloat16)
    query_sum = jnp.einsum("std,stc->dc", normed, query_low, preferred_element_type=jnp.float32)
    keys_sum = jnp.einsum("std,stc->dc", normed, key_low, preferred_element_type=jnp.float32)
    values_sum = jnp.einsum("std,stc->dc", normed, value_low, preferred_element_type=jnp.float32)
    query_grad, key_grad, value_grad, mixing_rows = (
        lax.psum_scatter(query_sum, "expert", scatter_dimension=0, tiled=True),
        lax.psum_scatter(keys_sum, "expert", scatter_dimension=0, tiled=True),
        lax.psum_scatter(values_sum, "expert", scatter_dimension=0, tiled=True),
        lax.psum_scatter(mixing_part, "expert", scatter_dimension=0, tiled=True),
    )
    mixing_grad = mixing_rows.T
    normed_part = lax.dot_general(
        query_low, query_weight, (((2,), (1,)), ((), ())), preferred_element_type=jnp.float32
    )
    normed_part = normed_part + lax.dot_general(
        key_low, key_weight, (((2,), (1,)), ((), ())), preferred_element_type=jnp.float32
    )
    normed_part = normed_part + lax.dot_general(
        value_low, value_weight, (((2,), (1,)), ((), ())), preferred_element_type=jnp.float32
    )
    normed_grad, querygain_grad, keygain_grad = (
        lax.psum(normed_part.astype(jnp.bfloat16), "tensor").astype(jnp.float32),
        lax.psum(querygain_part.astype(jnp.bfloat16), "tensor").astype(jnp.float32),
        lax.psum(keygain_part.astype(jnp.bfloat16), "tensor").astype(jnp.float32),
    )
    input_part, first_grad = first_back(normed_grad)
    input_grad = residual_grad + input_part
    first_grad, second_grad, querygain_grad, keygain_grad, router_grad = lax.psum(
        (first_grad, second_grad, querygain_grad, keygain_grad, router_grad), "expert"
    )
    return (
        layer_output,
        input_grad,
        first_grad,
        query_grad,
        key_grad,
        value_grad,
        mixing_grad,
        querygain_grad,
        keygain_grad,
        second_grad,
        router_grad,
        gate_grad[None],
        up_grad[None],
        down_grad[None],
    )

def lift(values, wide):
    high = lax.reduce_precision(values, 8, 7)
    both = jnp.concatenate([high, values - high], axis=-1).astype(jnp.bfloat16)
    return jnp.pad(both, ((0, 0), (0, wide - both.shape[-1])))


def on_chips(
    layer_input,
    norm_first,
    query_weight,
    key_weight,
    value_weight,
    mixing_weight,
    query_gain,
    key_gain,
    norm_second,
    router_weight,
    gate_weight,
    up_weight,
    down_weight,
    routes,
    fill_order,
    cotangent,
):
    seq_count, seg_len, model_width = layer_input.shape
    expert_count = lax.axis_size("expert")
    planes = expert_count // 4
    expert_idx = lax.axis_index("expert")
    tensor_idx = lax.axis_index("tensor")
    head_dim = query_gain.shape[0]
    local_queries = query_weight.shape[1] // head_dim
    local_keys = key_weight.shape[1] // head_dim
    key_width = local_keys * head_dim
    group_size = local_queries // local_keys
    top_count = routes.shape[2]
    token_count = seq_count * seg_len
    capacity = 5 * token_count * top_count // (4 * expert_count)
    slots = -(-capacity // 32) * 32
    half_width = model_width // 2
    share_width = model_width // expert_count
    f32, bf16 = jnp.float32, jnp.bfloat16
    inputs = layer_input.astype(f32)
    normed_f, first_back = jax.vjp(rms_scaled, inputs, norm_first)
    normed = normed_f.astype(bf16)
    positions = expert_idx * seg_len + jnp.arange(seg_len, dtype=jnp.int32)
    cosine, sine_table = rotary_tables(positions, head_dim)
    cosine = cosine[:, None, :]
    sine_table = sine_table[:, None, :]

    def rope_norm(raw_heads, gain_vec):
        return rotate(rms_scaled(raw_heads, gain_vec), cosine, sine_table)

    query_raw = jnp.dot(normed, query_weight, preferred_element_type=f32).reshape(
        seq_count, seg_len, local_queries, head_dim
    )
    key_raw = jnp.dot(normed, key_weight, preferred_element_type=f32).reshape(
        seq_count, seg_len, local_keys, head_dim
    )
    value_local = jnp.dot(normed, value_weight, preferred_element_type=f32).astype(bf16)
    query_rot, query_back = jax.vjp(rope_norm, query_raw, query_gain)
    key_rot, key_back = jax.vjp(rope_norm, key_raw, key_gain)
    key_local = key_rot.astype(bf16).reshape(token_count, key_width)
    pairs = jnp.concatenate([key_local, value_local.reshape(token_count, key_width)], axis=1)
    upstream_low = cotangent.reshape(token_count, model_width)
    half_tokens = token_count // 2
    upstream_half = lax.dynamic_slice_in_dim(upstream_low, tensor_idx * half_tokens, half_tokens, 0)
    upstream_mine = lax.all_gather(upstream_half, "expert")
    query_rows = query_rot.astype(bf16).reshape(token_count, local_queries * head_dim)
    context, pairs_all, logs = attend(query_rows, pairs, planes, group_size, head_dim, 1)
    head_part = jnp.dot(context, mixing_weight, preferred_element_type=f32)
    head_low = head_part.astype(bf16)
    head_other = swap_cores(head_low, 3, "swap_heads")
    residual = inputs.reshape(token_count, model_width) + (head_low.astype(f32) + head_other.astype(f32))
    second_f, second_back = jax.vjp(rms_scaled, residual, norm_second)
    second = second_f.astype(bf16)
    logits = jnp.dot(second, router_weight, preferred_element_type=f32)
    flat_routes = routes.reshape(token_count, top_count)
    picked = (flat_routes[:, :, None] == jnp.arange(expert_count, dtype=jnp.int32)).astype(f32)
    gates = jax.nn.softmax(jnp.sum(picked * logits[:, None, :], axis=-1), axis=-1)
    usages = jnp.sum(picked, axis=1)
    ranking = fill_order.reshape(token_count)
    before = (ranking[None, :] < ranking[:, None]).astype(bf16)
    counts = jnp.dot(before, usages.astype(bf16), preferred_element_type=f32)
    here = (usages > 0.0) & (counts < capacity)
    slot_table = jnp.where(here, counts, -1.0)
    gate_table = jnp.where(here, jnp.sum(picked * gates[:, :, None], axis=1), 0.0)
    slot_hi = lift(slot_table, 2 * expert_count)[:, :expert_count]
    notes = jnp.concatenate([slot_hi, lift(gate_table, 128 - expert_count)], axis=1)
    parcel = jnp.concatenate([second, notes], axis=1)
    _, _, out_share, row_home, gate_grad, up_grad, down_grad = run_experts(
        parcel, upstream_mine, gate_weight[0], up_weight[0], down_weight[0], planes, slots, 4
    )
    out_home = lax.psum_scatter(out_share, "expert", scatter_dimension=0, tiled=True)[0]
    residual_half = lax.dynamic_slice_in_dim(residual, tensor_idx * half_width, half_width, 1)
    layer_output = (residual_half + out_home.astype(f32)).astype(bf16).reshape(seq_count, seg_len, half_width)
    home_scores = jnp.sum(row_home[:, :, half_width:].astype(f32), axis=0)
    home_scores = home_scores[:, :expert_count] + home_scores[:, expert_count : 2 * expert_count]
    gate_grads = jnp.sum(picked * home_scores[:, None, :], axis=-1)
    route_grads = gates * (gate_grads - jnp.sum(gates * gate_grads, axis=-1, keepdims=True))
    logit_grads = jnp.sum(picked * route_grads[:, :, None], axis=1).astype(bf16)
    router_grad = jnp.einsum("td,te->ed", second, logit_grads, preferred_element_type=f32)
    router_back = lax.dot_general(
        logit_grads, router_weight, (((1,), (1,)), ((), ())), preferred_element_type=f32
    )
    second_rows = jnp.concatenate([row_home[0, :, :half_width], row_home[1, :, :half_width]], axis=1)
    second_in = second_rows.astype(f32) + router_back
    residual_part, second_grad = second_back(second_in)
    residual_grad = residual_part + upstream_low.astype(f32)
    head_in = residual_grad.astype(bf16)

    def slices(rows):
        cut = rows.reshape(token_count, planes, 4, share_width)
        return cut.transpose(2, 0, 1, 3).reshape(4, token_count, planes * share_width)

    context_grad = lax.dot_general(
        head_in, mixing_weight, (((1,), (1,)), ((), ())), preferred_element_type=f32
    ).astype(bf16)
    query_rot_grad, pair_home, context_plane, head_plane = attend_back(
        query_rows, context_grad, context, pairs_all, logs, slices(head_in), planes, group_size, head_dim, 7
    )
    mixing_part = jnp.einsum("gtd,gtc->dc", head_plane, context_plane, preferred_element_type=f32)
    mixing_part = mixing_part.astype(bf16).reshape(planes, share_width, local_queries * head_dim)
    mixing_rows = scatter_sum(mixing_part, planes, False, False, f32, 8, "scatter_mixing")
    mixing_grad = mixing_rows.T
    key_raw_grad, keygain_part = key_back(
        pair_home[:, :key_width].reshape(seq_count, seg_len, local_keys, head_dim)
    )
    query_raw_grad, querygain_part = query_back(
        query_rot_grad.reshape(seq_count, seg_len, local_queries, head_dim)
    )
    query_low = query_raw_grad.astype(bf16).reshape(token_count, local_queries * head_dim)
    key_low = key_raw_grad.astype(bf16).reshape(token_count, key_width)
    value_low = pair_home[:, key_width:].astype(bf16)
    all_low = jnp.concatenate([query_low, key_low, value_low], axis=1)
    flat_normed = normed.reshape(token_count, model_width)
    low_plane, normed_plane = plane_exchange(all_low, slices(flat_normed), 10, "plane_queries")
    weight_part = jnp.einsum("gtd,gtc->dc", normed_plane, low_plane, preferred_element_type=f32)
    weight_part = weight_part.astype(bf16).reshape(planes, share_width, all_low.shape[1])
    weight_rows = scatter_sum(weight_part, planes, False, False, f32, 11, "scatter_queries")
    query_width = local_queries * head_dim
    query_grad = weight_rows[:, :query_width]
    key_grad = weight_rows[:, query_width : query_width + key_width]
    value_grad = weight_rows[:, query_width + key_width :]
    normed_part = lax.dot_general(
        query_low, query_weight, (((1,), (1,)), ((), ())), preferred_element_type=f32
    )
    normed_part = normed_part + lax.dot_general(
        key_low, key_weight, (((1,), (1,)), ((), ())), preferred_element_type=f32
    )
    normed_part = normed_part + lax.dot_general(
        value_low, value_weight, (((1,), (1,)), ((), ())), preferred_element_type=f32
    )
    gain_row = jnp.pad(
        jnp.concatenate([querygain_part, keygain_part])[None], ((0, 15), (0, model_width - 2 * head_dim))
    )
    normed_low = jnp.concatenate([normed_part, gain_row], axis=0).astype(bf16)
    normed_sum = normed_low.astype(f32) + swap_cores(normed_low, 12, "swap_normed").astype(f32)
    normed_grad = normed_sum[:token_count].reshape(seq_count, seg_len, model_width)
    input_part, first_grad = first_back(normed_grad)
    input_grad = residual_grad.reshape(seq_count, seg_len, model_width) + input_part
    small = jnp.concatenate(
        [
            first_grad[None],
            second_grad[None],
            normed_sum[token_count : token_count + 1],
            jnp.zeros((13, model_width), f32),
            router_grad,
        ],
        axis=0,
    )
    small = total_over(small, expert_count, 13, "total_small")
    return (
        layer_output,
        input_grad,
        small[0],
        query_grad,
        key_grad,
        value_grad,
        mixing_grad,
        small[2, :head_dim],
        small[2, head_dim : 2 * head_dim],
        small[1],
        small[16:].T,
        gate_grad[None],
        up_grad[None],
        down_grad[None],
    )


def solution(mesh):
    chips = mesh.shape["expert"] == 16 and mesh.shape["tensor"] == 2
    return jax.shard_map(
        on_chips if chips else on_device,
        mesh=mesh,
        in_specs=(
            P(None, "expert", None),
            P(),
            P(None, "tensor"),
            P(None, "tensor"),
            P(None, "tensor"),
            P("tensor", None),
            P(),
            P(),
            P(),
            P(),
            P("expert", None, "tensor"),
            P("expert", None, "tensor"),
            P("expert", "tensor", None),
            P(None, "expert", None),
            P(None, "expert"),
            P(None, "expert", None),
        ),
        out_specs=(
            P(None, "expert", "tensor"),
            P(None, "expert", None),
            P(),
            P("expert", "tensor"),
            P("expert", "tensor"),
            P("expert", "tensor"),
            P("tensor", "expert"),
            P(),
            P(),
            P(),
            P(),
            P("expert", None, "tensor"),
            P("expert", None, "tensor"),
            P("expert", "tensor", None),
        ),
        check_vma=False,
    )
```

```python
import functools

import jax
import jax.numpy as jnp
from jax import lax
from jax.experimental import pallas as pl
from jax.experimental.pallas import tpu as pltpu
from jax.sharding import PartitionSpec as P

BLOCK = 256
MESH = pl.DeviceIdType.MESH
ROOM = 56 * 2**20


class Spot:
    def __init__(self):
        self.e = lax.axis_index("expert")
        self.t = lax.axis_index("tensor")
        self.a = lax.div(self.e, 4)
        y = lax.rem(lax.div(self.e, 2), 2)
        x = lax.rem(self.e, 2)
        self.b = x + self.t * (y - x)
        self.c = y + self.t * (x - y)

    def index(self, a, b, c):
        y = c + self.t * (b - c)
        x = b + self.t * (c - b)
        return a * 4 + y * 2 + x

    def at(self, a, b, c):
        return (self.index(a, b, c), self.t)

    def core(self):
        return (self.e, 1 - self.t)

    def greet(self, planes, chain, flat, share, far=False, corner=False):
        barrier = pltpu.get_barrier_semaphore()
        total = 0

        def call(who):
            pl.semaphore_signal(barrier, inc=1, device_id=who, device_id_type=MESH)

        if share:
            call(self.core())
            total = total + 1
        if flat:
            call(self.at(self.a, 1 - self.b, self.c))
            call(self.at(self.a, self.b, 1 - self.c))
            total = total + 2
        if corner:
            call(self.at(self.a, 1 - self.b, 1 - self.c))
            total = total + 1
        if far:
            for k in range(1, planes):
                call(self.at(lax.rem(self.a + k, planes), self.b, self.c))
            total = total + planes - 1
        elif chain:
            up = self.a + 1 < planes
            down = self.a > 0

            @pl.when(up)
            def _():
                call(self.at(self.a + 1, self.b, self.c))

            @pl.when(down)
            def _():
                call(self.at(self.a - 1, self.b, self.c))

            total = total + up.astype(jnp.int32) + down.astype(jnp.int32)
        pl.semaphore_wait(barrier, total)


def push(src, dst, send_sem, recv_sem, who):
    return pltpu.make_async_remote_copy(
        src_ref=src, dst_ref=dst, send_sem=send_sem, recv_sem=recv_sem, device_id=who, device_id_type=MESH
    )


def add_rows(target, parts):
    rows = target.shape[0]
    step = 32 if rows % 32 == 0 else 16

    def body(i, carry):
        at = pl.ds(pl.multiple_of(i * step, step), step)
        total = parts[0][at, :].astype(jnp.float32)
        for part in parts[1:]:
            total = total + part[at, :].astype(jnp.float32)
        target[at, :] = total.astype(target.dtype)
        return carry

    lax.fori_loop(0, rows // step, body, 0)


def far_first(a, planes, i):
    last = planes - 1
    low = jnp.where(i < last - a, last - i, jnp.where(i < last, i - (last - a), a))
    high = jnp.where(i < a, i, jnp.where(i < last, last - (i - a), a))
    return jnp.where(2 * a < last, low, high)


def swap_kernel(x_ref, o_ref, sems):
    me = Spot()
    me.greet(1, False, False, True)
    c = push(x_ref, o_ref, sems.at[0], sems.at[1], me.core())
    c.start()
    c.wait()


def swap_cores(x, cid, name):
    return pl.pallas_call(
        swap_kernel,
        out_shape=jax.ShapeDtypeStruct(x.shape, x.dtype),
        in_specs=[pl.BlockSpec(memory_space=pl.ANY)],
        out_specs=pl.BlockSpec(memory_space=pl.ANY),
        scratch_shapes=[pltpu.SemaphoreType.DMA((2,))],
        compiler_params=pltpu.CompilerParams(collective_id=cid, has_side_effects=True),
        name=name,
    )(x)


def over(first, second, contract):
    return lax.dot_general(first, second, (contract, ((), ())), preferred_element_type=jnp.float32)


NN = ((1,), (0,))
NT = ((1,), (1,))
TN = ((0,), (0,))


def experts_kernel(
    planes,
    parcel_ref,
    up_ref,
    gate_in,
    lift_in,
    down_in,
    context_ref,
    cut_ref,
    all_ref,
    other_ref,
    share_ref,
    home_ref,
    column_ref,
    cut_all,
    gate_sum,
    lift_sum,
    down_sum,
    wide,
    down,
    wide_half,
    down_half,
    pbuf,
    ubuf,
    xbuf,
    gbuf,
    vbuf,
    sbuf,
    wbuf,
    rbuf,
    hbuf,
    dbuf,
    gates,
    scores,
    stage,
    mine,
    outgoing,
    partner,
    landc,
    landb,
    landa,
    gsend,
    grecv,
    gcore,
    usend,
    urecv,
    wsend,
    wrecv,
    wload,
    hsend,
    hrecv,
    ssem,
    rsem,
    lsem,
    osem,
    esem,
    xsend,
    xrecv,
    csend,
    crecv,
):
    me = Spot()
    f32, bf16 = jnp.float32, jnp.bfloat16
    tokens, packed = parcel_ref.shape
    hidden, width = down_in.shape
    notes_width = packed - width
    count = planes * 4
    half = tokens // 2
    side = width // 2
    slots = sbuf.shape[2]
    own = me.index(me.a, me.b, me.c)
    ours = pl.ds(pl.multiple_of(me.t * half, half), half)
    theirs = pl.ds(pl.multiple_of((1 - me.t) * half, half), half)
    our_side = pl.ds(pl.multiple_of(me.t * side, side), side)
    their_side = pl.ds(pl.multiple_of((1 - me.t) * side, side), side)
    spots = [(sb, sc) for sc in (1 - me.c, me.c) for sb in (1 - me.b, me.b)]

    def near(i):
        return far_first(me.a, planes, planes - 1 - i)


    def carry(idx, kind, src=None):
        who = {
            0: me.at(me.a + 1, me.b, me.c),
            1: me.at(me.a - 1, me.b, me.c),
            2: me.at(me.a, 1 - me.b, me.c),
            3: me.at(me.a, me.b, 1 - me.c),
            4: me.core(),
        }[kind]
        there = all_ref.at[idx, ours]
        landed = gcore if kind == 4 else grecv
        return push(there if src is None else src, there, gsend.at[idx, kind], landed.at[idx], who)

    def relay_a(sa, act, first):
        idx = me.index(sa, me.b, me.c)
        src = parcel_ref.at[ours] if first else None
        if act and not first:
            carry(idx, 2).wait_recv()
        run = (lambda c: c.start()) if act else (lambda c: c.wait_send())

        @pl.when((sa <= me.a) & (me.a + 1 < planes))
        def _():
            run(carry(idx, 0, src))

        @pl.when((sa >= me.a) & (me.a > 0))
        def _():
            run(carry(idx, 1, src))

        run(carry(idx, 3, src))
        run(carry(idx, 2, src))
        if not first:
            run(carry(idx, 4))

    def relay_b(sa, act):
        idx = me.index(sa, 1 - me.b, me.c)
        run = (lambda c: c.start()) if act else (lambda c: c.wait_send())
        if act:
            carry(idx, 2).wait_recv()
        run(carry(idx, 3))
        run(carry(idx, 4))

    def across(sa, act):
        for sb in (me.b, 1 - me.b):
            idx = me.index(sa, sb, 1 - me.c)
            if act:
                carry(idx, 2).wait_recv()
                carry(idx, 4).start()
            else:
                carry(idx, 4).wait_send()

    def from_core(sa):
        for sb, sc in spots:
            idx = me.index(sa, sb, sc)

            @pl.when(idx != own)
            def _(idx=idx):
                there = all_ref.at[idx, theirs]
                push(there, there, gsend.at[idx, 4], gcore.at[idx], me.core()).wait_recv()

    def upstream(sa):
        group = pl.ds(sa * 4, 4)
        return push(up_ref.at[group], other_ref.at[group], usend.at[sa], urecv.at[sa], me.core())


    def part(ref, base, size):
        return ref.at[:, pl.ds(pl.multiple_of(base, 128), size)]

    down_rows = down_half.at[pl.ds(pl.multiple_of(me.t * hidden, 128), hidden)]
    wide_cols = [part(wide_half, me.t * 2 * hidden + i * hidden, hidden) for i in range(2)]
    sources = [gate_in, lift_in]
    loads = [pltpu.make_async_copy(sources[i], wide.at[:, i * hidden : (i + 1) * hidden], wload.at[i]) for i in range(2)]
    loads += [pltpu.make_async_copy(sources[i].at[our_side], wide_cols[i], wload.at[2 + i]) for i in range(2)]
    loads += [
        pltpu.make_async_copy(down_in, down, wload.at[4]),
        pltpu.make_async_copy(down_in.at[:, our_side], down_rows, wload.at[5]),
    ]
    pushes = [push(sources[i].at[their_side], wide_cols[i], wsend.at[i], wrecv.at[i], me.core()) for i in range(2)]
    pushes += [push(down_in.at[:, their_side], down_rows, wsend.at[2], wrecv.at[2], me.core())]


    def send_c(sa, sb):
        slot = sa * 2 + sb
        there = me.at(me.a, me.b, 1 - me.c)
        return push(outgoing.at[slot], landc.at[slot], ssem.at[0, slot], rsem.at[0, slot], there)

    def send_b(sa):
        src = mine.at[sa * 2 + 1 - me.b]
        return push(src, landb.at[sa], ssem.at[1, sa], rsem.at[1, sa], me.at(me.a, 1 - me.b, me.c))

    def send_a(sa):
        src = mine.at[sa * 2 + me.b]
        return push(src, landa.at[me.a], ssem.at[2, sa], rsem.at[2, me.a], me.at(sa, me.b, me.c))

    def from_c(sa):
        for sb in (1 - me.b, me.b):
            slot = sa * 2 + sb
            push(landc.at[slot], landc.at[slot], ssem.at[0, slot], rsem.at[0, slot], me.at(me.a, me.b, 1 - me.c)).wait_recv()
            for n in range(0, mine.shape[2], 384):
                cut = slice(n, n + 384)
                spread = over(partner[slot], landc[slot, :, cut], NN)
                mine[slot, :, cut] = (mine[slot, :, cut].astype(f32) + spread).astype(bf16)
            if sb is not me.b:
                send_b(sa).start()

    def from_b(sa):
        push(landb.at[sa], landb.at[sa], ssem.at[1, sa], rsem.at[1, sa], me.at(me.a, 1 - me.b, me.c)).wait_recv()
        return [mine.at[sa * 2 + me.b], landb.at[sa]]

    def along(sa):
        parts = from_b(sa)
        add_rows(parts[0], parts)
        send_a(sa).start()

    def finish():
        parts = from_b(me.a)
        for k in range(1, planes):
            far = lax.rem(me.a + k, planes)
            push(landa.at[far], landa.at[far], ssem.at[2, far], rsem.at[2, far], me.at(far, me.b, me.c)).wait_recv()
            parts = parts + [landa.at[far]]
        add_rows(home_ref.at[me.t], parts)


    def context_to(source, up, own_rows):
        there = column_ref.at[source]
        who = me.at(me.a + 1 if up else me.a - 1, me.b, me.c)
        return push(context_ref if own_rows else there, there, xsend.at[source, int(up)], xrecv.at[source], who)

    def context_pass(i, act):
        for up in (True, False):
            source = me.a - i if up else me.a + i
            further = me.a + 1 < planes if up else me.a > 0
            run = (lambda c: c.start()) if act else (lambda c: c.wait_send())

            @pl.when((source >= 0) & (source < planes))
            def _(source=source, up=up, further=further, run=run):
                if act and i > 0:
                    context_to(source, up, False).wait_recv()

                @pl.when(further)
                def _():
                    run(context_to(source, up, i == 0))

    place = lax.rem(me.e, 4)
    peers = [me.index(0, b, c) for b, c in ((1 - me.b, me.c), (me.b, 1 - me.c), (1 - me.b, 1 - me.c))]

    def cut_to(i):
        there = (me.e - place + peers[i], me.t)
        return push(cut_ref.at[peers[i]], cut_all.at[place], csend.at[i], crecv.at[i], there)


    def load_rows(sa, q):
        return pltpu.make_async_copy(all_ref.at[sa * 4 + q], pbuf.at[q], lsem.at[q])

    def fetch_rows(sa):
        from_core(sa)
        for q in range(4):
            mine_here = sa * 4 + q == own

            @pl.when(mine_here)
            def _(q=q):
                pltpu.make_async_copy(parcel_ref, pbuf.at[q], lsem.at[q]).start()

            @pl.when(jnp.logical_not(mine_here))
            def _(q=q):
                load_rows(sa, q).start()

    def load_up(sa):
        group = pl.ds(sa * 4, 4)
        return [
            pltpu.make_async_copy(up_ref.at[group], ubuf.at[:, ours], lsem.at[4]),
            pltpu.make_async_copy(other_ref.at[group], ubuf.at[:, theirs], lsem.at[5]),
        ]

    def fetch_up(sa):
        there = other_ref.at[pl.ds(sa * 4, 4)]
        push(there, there, usend.at[sa], urecv.at[sa], me.core()).wait_recv()
        for k in load_up(sa):
            k.start()

    def lanes(rows):
        return lax.broadcasted_iota(jnp.int32, (rows, notes_width), 1)

    def side_of(q):
        y, x = lax.div(q, 2), lax.rem(q, 2)
        return x + me.t * (y - x), y + me.t * (x - y)

    def chosen_by(expert, notes):
        slot_of = jnp.sum(jnp.where(lanes(tokens) == expert, notes, 0.0), axis=1, keepdims=True)
        chosen = slot_of == lax.broadcasted_iota(jnp.int32, (tokens, slots), 1).astype(f32)
        return jnp.where(chosen, 1.0, 0.0).astype(bf16)

    def pick_rows(q, carried):
        sa, slot = carried
        load_rows(sa, q).wait()
        notes = pbuf[q, :, width:].astype(f32)
        sb, sc = side_of(q)

        @pl.when(sc == me.c)
        def _():
            partner[sa * 2 + sb] = chosen_by(me.index(me.a, me.b, 1 - me.c), notes)

        chosen = chosen_by(me.e, notes)
        sbuf[q] = chosen
        pick = jnp.transpose(chosen.astype(f32)).astype(bf16)
        at = pl.ds(pl.multiple_of(q * slots, slots), slots)
        there = over(pick, pbuf[q, :, width:], NN)
        mark = lanes(slots)
        gate = jnp.sum(jnp.where((mark == count + me.e) | (mark == 2 * count + me.e), there, 0.0), axis=1, keepdims=True)
        gates[at, :] = jnp.broadcast_to(gate, (slots, 128))
        for n in range(0, width, 512):
            cut = slice(n, n + 512)
            xbuf[at, cut] = over(pick, pbuf[q, :, cut], NN).astype(bf16)
            picked = over(pick, ubuf[q, :, cut], NN)
            gbuf[at, cut] = (picked * gate).astype(bf16)
        for n in range(0, side, 512):
            cut = pl.ds(pl.multiple_of(me.t * side + n, 512), 512)
            vbuf[at, n : n + 512] = over(pick, ubuf[q, :, cut], NN).astype(bf16)
        return carried

    def hidden_cols(p):
        return pl.ds(pl.multiple_of(p * hidden, 128), hidden)

    def both_cols(p):
        return pl.ds(pl.multiple_of(p * 2 * hidden, 128), 2 * hidden)

    def hidden_rows(r, slot):
        at = pl.ds(pl.multiple_of(r * 256, 256), 256)
        acts = over(xbuf[at, :], wide[...], NN)
        gate_act, up_act = acts[:, :hidden], acts[:, hidden:]
        sig = 1.0 / (1.0 + jnp.exp(-gate_act))
        silu = gate_act * sig
        hbuf[slot, at, hidden_cols(me.t)] = (silu * up_act).astype(bf16)
        back = over(gbuf[at, :], down[...], NT)
        gate_d = (back * up_act * (sig * (1.0 + gate_act * (1.0 - sig)))).astype(bf16)
        dbuf[slot, at, pl.ds(pl.multiple_of(me.t * 2 * hidden, 128), hidden)] = gate_d
        dbuf[slot, at, pl.ds(pl.multiple_of(me.t * 2 * hidden + hidden, 128), hidden)] = (back * silu).astype(bf16)
        return slot

    def trades(slot):
        h_part = hbuf.at[slot, :, hidden_cols(me.t)]
        d_part = dbuf.at[slot, :, both_cols(me.t)]
        return [
            push(h_part, h_part, hsend.at[0], hrecv.at[slot, 0], me.core()),
            push(d_part, d_part, hsend.at[1], hrecv.at[slot, 1], me.core()),
        ]

    def traded(slot):
        h_part = hbuf.at[slot, :, hidden_cols(1 - me.t)]
        d_part = dbuf.at[slot, :, both_cols(1 - me.t)]
        push(h_part, h_part, hsend.at[0], hrecv.at[slot, 0], me.core()).wait_recv()
        push(d_part, d_part, hsend.at[1], hrecv.at[slot, 1], me.core()).wait_recv()

    def weight_sums(n, slot):
        cut = pl.ds(pl.multiple_of(n * 512, 512), 512)
        own_d = dbuf[slot, :, both_cols(me.t)]
        rows = xbuf[:, cut]
        gate_sum[cut, :] += over(rows, own_d[:, :hidden], TN)
        lift_sum[cut, :] += over(rows, own_d[:, hidden:], TN)
        down_sum[:, cut] += over(hbuf[slot, :, hidden_cols(me.t)], gbuf[:, cut], TN)
        return slot

    def out_rows(n, slot):
        cut = pl.ds(pl.multiple_of(n * 512, 512), 512)
        for r in range(0, 4 * slots, 256):
            at = slice(r, r + 256)
            out = over(hbuf[slot, at, :], down_half[:, cut], NN)
            wbuf[at, cut] = (out * gates[at, :1]).astype(bf16)
            total = jnp.sum(out * vbuf[at, cut].astype(f32), axis=1, keepdims=True)
            scores[at, :] += jnp.broadcast_to(total, (256, 128))
            rbuf[at, cut] = over(dbuf[slot, at, :], wide_half[cut, :], NT).astype(bf16)
        return slot

    def note_scores():
        mark = lanes(4 * slots)
        total = scores[...]
        high = total.astype(bf16).astype(f32)
        row = jnp.where(mark == me.e, high, jnp.where(mark == me.e + count, total - high, 0.0))
        rbuf[:, side:] = row.astype(bf16)

    def store(idx, q):
        return pltpu.make_async_copy(stage.at[lax.rem(q, 2)], share_ref.at[idx], osem.at[lax.rem(q, 2)])

    def spread_rows(q, sa):
        at = pl.ds(pl.multiple_of(q * slots, slots), slots)
        idx = sa * 4 + q

        @pl.when((q >= 2) | (sa != near(1)))
        def _():
            store(idx, q).wait()

        for n in range(0, side, 512):
            cut = slice(n, n + 512)
            stage[lax.rem(q, 2), :, cut] = over(sbuf[q], wbuf[at, cut], NN).astype(bf16)
        sb, sc = side_of(q)
        slot = sa * 2 + sb

        @pl.when(sc == me.c)
        def _():
            for n in range(0, mine.shape[2], 384):
                cut = slice(n, n + 384)
                mine[slot, :, cut] = over(sbuf[q], rbuf[at, cut], NN).astype(bf16)

        @pl.when(sc != me.c)
        def _():
            outgoing[slot] = rbuf[at, :]
            send_c(sa, sb).start()

        store(idx, q).start()
        return sa

    me.greet(planes, True, True, True, True, True)
    relay_a(me.a, True, True)
    for i in range(planes):
        upstream(near(i)).start()
    for k in loads + pushes:
        k.start()
    gate_sum[...] = jnp.zeros_like(gate_sum)
    lift_sum[...] = jnp.zeros_like(lift_sum)
    down_sum[...] = jnp.zeros_like(down_sum)
    fetch_up(near(1))
    relay_b(me.a, True)
    relay_a(near(1), True, False)
    across(me.a, True)
    for i in range(2, planes):
        relay_a(near(i), True, False)
        relay_b(near(i - 1), True)
    across(near(1), True)
    fetch_rows(near(1))
    for k in loads + pushes:
        k.wait()

    def step(i, c):
        last = i == planes - 1
        sa = jnp.where(last, me.a, near(i + 1))
        after = jnp.where(i + 2 < planes, near(i + 2), me.a)
        slot = lax.rem(i, 2)
        for k in load_up(sa):
            k.wait()
        scores[...] = jnp.zeros_like(scores)
        lax.fori_loop(0, 4, pick_rows, (sa, slot))

        @pl.when(i + 1 < planes)
        def _():
            fetch_up(after)

        @pl.when(i > 0)
        def _():
            for k in trades(slot):
                k.wait_send()

        lax.fori_loop(0, 4 * slots // 256, hidden_rows, slot)
        for k in trades(slot):
            k.start()

        @pl.when(i == 0)
        def _():
            relay_b(near(planes - 1), True)
            context_pass(0, True)
            for k in range(3):
                cut_to(k).start()

        @pl.when(i > 0)
        def _():
            from_c(near(i))

        traded(slot)
        lax.fori_loop(0, side // 512, out_rows, slot)
        note_scores()
        lax.fori_loop(0, 4, spread_rows, sa)

        @pl.when(i + 2 < planes)
        def _():
            across(after, True)

        @pl.when(jnp.logical_not(last))
        def _():
            fetch_rows(after)

        lax.fori_loop(0, width // 512, weight_sums, slot)

        @pl.when(i > 0)
        def _():
            along(near(i))

        for k in range(1, planes):

            @pl.when(i == k)
            def _(k=k):
                context_pass(k, True)

        return c

    lax.fori_loop(0, planes, step, 0)
    from_c(me.a)
    finish()
    store(0, 0).wait()
    store(0, 1).wait()
    done = push(home_ref.at[me.t], home_ref.at[me.t], esem.at[0], esem.at[1], me.core())
    done.start()

    relay_a(me.a, False, True)

    def settle(i, c):
        sa = near(i)
        relay_b(sa, False)

        @pl.when(i > 0)
        def _():
            relay_a(sa, False, False)
            send_a(sa).wait_send()

        across(sa, False)
        for sb in (1 - me.b, me.b):
            send_c(sa, sb).wait_send()
        send_b(sa).wait_send()
        upstream(sa).wait_send()
        return c

    lax.fori_loop(0, planes, settle, 0)
    for k in trades(0):
        k.wait_send()
    for k in range(planes):
        context_pass(k, False)
    for k in range(3):
        cut_to(k).wait()
    done.wait_send()
    other = home_ref.at[1 - me.t]
    push(other, other, esem.at[0], esem.at[1], me.core()).wait_recv()


def run_experts(parcel, upstream, gate, lift_w, down, context, cut, planes, slots, cid):
    f32, bf16 = jnp.float32, jnp.bfloat16
    tokens, packed = parcel.shape
    hidden, width = down.shape
    count = planes * 4
    half = tokens // 2
    side = width // 2
    block = side + packed - width
    rows = 4 * slots
    anywhere = pl.BlockSpec(memory_space=pl.ANY)
    inside = pl.BlockSpec(memory_space=pltpu.VMEM)
    return pl.pallas_call(
        functools.partial(experts_kernel, planes),
        out_shape=[
            jax.ShapeDtypeStruct((count, tokens, packed), bf16),
            jax.ShapeDtypeStruct((count, half, width), bf16),
            jax.ShapeDtypeStruct((count, tokens, side), bf16),
            jax.ShapeDtypeStruct((2, tokens, block), bf16),
            jax.ShapeDtypeStruct((planes,) + context.shape, bf16),
            jax.ShapeDtypeStruct(cut.shape, bf16),
            jax.ShapeDtypeStruct((width, hidden), f32),
            jax.ShapeDtypeStruct((width, hidden), f32),
            jax.ShapeDtypeStruct((hidden, width), f32),
        ],
        in_specs=[anywhere] * 7,
        out_specs=[anywhere] * 3 + [inside, anywhere, anywhere] + [inside] * 3,
        scratch_shapes=[
            pltpu.VMEM((width, 2 * hidden), bf16),
            pltpu.VMEM((hidden, width), bf16),
            pltpu.VMEM((side, 4 * hidden), bf16),
            pltpu.VMEM((2 * hidden, side), bf16),
            pltpu.VMEM((4, tokens, packed), bf16),
            pltpu.VMEM((4, tokens, width), bf16),
            pltpu.VMEM((rows, width), bf16),
            pltpu.VMEM((rows, width), bf16),
            pltpu.VMEM((rows, side), bf16),
            pltpu.VMEM((4, tokens, slots), bf16),
            pltpu.VMEM((rows, side), bf16),
            pltpu.VMEM((rows, block), bf16),
            pltpu.VMEM((2, rows, 2 * hidden), bf16),
            pltpu.VMEM((2, rows, 4 * hidden), bf16),
            pltpu.VMEM((rows, 128), f32),
            pltpu.VMEM((rows, 128), f32),
            pltpu.VMEM((2, tokens, side), bf16),
            pltpu.VMEM((2 * planes, tokens, block), bf16),
            pltpu.VMEM((2 * planes, slots, block), bf16),
            pltpu.VMEM((2 * planes, tokens, slots), bf16),
            pltpu.VMEM((2 * planes, slots, block), bf16),
            pltpu.VMEM((planes, tokens, block), bf16),
            pltpu.VMEM((planes, tokens, block), bf16),
            pltpu.SemaphoreType.DMA((count, 5)),
            pltpu.SemaphoreType.DMA((count,)),
            pltpu.SemaphoreType.DMA((count,)),
            pltpu.SemaphoreType.DMA((planes,)),
            pltpu.SemaphoreType.DMA((planes,)),
            pltpu.SemaphoreType.DMA((3,)),
            pltpu.SemaphoreType.DMA((3,)),
            pltpu.SemaphoreType.DMA((6,)),
            pltpu.SemaphoreType.DMA((2,)),
            pltpu.SemaphoreType.DMA((2, 2)),
            pltpu.SemaphoreType.DMA((3, 2 * planes)),
            pltpu.SemaphoreType.DMA((3, 2 * planes)),
            pltpu.SemaphoreType.DMA((7,)),
            pltpu.SemaphoreType.DMA((2,)),
            pltpu.SemaphoreType.DMA((2,)),
            pltpu.SemaphoreType.DMA((planes, 2)),
            pltpu.SemaphoreType.DMA((planes,)),
            pltpu.SemaphoreType.DMA((3,)),
            pltpu.SemaphoreType.DMA((3,)),
        ],
        compiler_params=pltpu.CompilerParams(
            collective_id=cid, has_side_effects=True, vmem_limit_bytes=62 * 2**20
        ),
        name="experts",
    )(parcel, upstream, gate, lift_w, down, context, cut)


def stack_heads(target, source, group):
    items, rows, size = target.shape
    seg = rows // group
    keys = source.shape[1] // (group * size)
    for s in range(items // keys):
        for k in range(keys):
            for h in range(group):
                at = (k * group + h) * size
                part = source[s * seg : (s + 1) * seg, at : at + size]
                target[s * keys + k, h * seg : (h + 1) * seg, :] = part.astype(target.dtype)


def spread_heads(target, item, value, group, keys):
    rows, size = value.shape
    seg = rows // group
    s, k = item // keys, item % keys
    for h in range(group):
        at = (k * group + h) * size
        target[s * seg : (s + 1) * seg, at : at + size] = value[h * seg : (h + 1) * seg, :].astype(target.dtype)


def block_heads(ref, plane, item, keys, size, part):
    seg = BLOCK // 4
    s, k = lax.div(item, keys), lax.rem(item, keys)
    rows = pl.ds(pl.multiple_of(s * seg, seg), seg)
    cols = pl.ds(pl.multiple_of((part * keys + k) * size, size), size)
    return [ref.at[plane * 4 + q, rows, cols] for q in range(4)]


def joined(refs):
    return jnp.concatenate([ref[...] for ref in refs], axis=0)


def attend_kernel(
    planes, group, q_ref, x_ref, context_ref, all_ref, log_ref, qs, top, total, acc, ssem, rsem
):
    me = Spot()
    f32, bf16 = jnp.float32, jnp.bfloat16
    items, rows, size = qs.shape
    keys = x_ref.shape[1] // (2 * size)
    factor = size ** (-0.5)
    own = me.index(me.a, me.b, me.c)

    def carry(idx, kind, src=None):
        who = {
            0: me.at(me.a + 1, me.b, me.c),
            2: me.at(me.a, 1 - me.b, me.c),
            3: me.at(me.a, me.b, 1 - me.c),
        }[kind]
        there = all_ref.at[idx]
        return push(there if src is None else src, there, ssem.at[idx, kind], rsem.at[idx], who)

    def relay(sa, act, first):
        idx = me.index(sa, me.b, me.c)
        src = x_ref if first else None
        if act and not first:
            carry(idx, 2).wait_recv()
        run = (lambda c: c.start()) if act else (lambda c: c.wait_send())

        @pl.when(me.a + 1 < planes)
        def _():
            run(carry(idx, 0, src))

        run(carry(idx, 3, src))
        run(carry(idx, 2, src))
        idx = me.index(sa, 1 - me.b, me.c)
        if act:
            carry(idx, 2).wait_recv()
        run(carry(idx, 3))

    def block(item, sa):
        scores = over(qs[item], joined(block_heads(all_ref, sa, item, keys, size, 0)), NT) * factor
        values = joined(block_heads(all_ref, sa, item, keys, size, 1))
        before = top[item]
        high = jnp.maximum(before, jnp.broadcast_to(jnp.max(scores, axis=1, keepdims=True), before.shape))
        shrink = jnp.exp(before - high)
        terms = jnp.exp(scores - high[:, :1])
        top[item] = high
        total[item] = total[item] * shrink + jnp.broadcast_to(jnp.sum(terms, axis=1, keepdims=True), before.shape)
        acc[item] = acc[item] * shrink + over(terms.astype(bf16), values, NN)
        return sa

    me.greet(planes, True, True, False)
    relay(me.a, True, True)
    all_ref[own] = x_ref[...]

    @pl.when(me.a > 0)
    def _():
        relay(me.a - 1, True, False)

    stack_heads(qs, q_ref, group)
    top[...] = jnp.full(top.shape, far_below, f32)
    total[...] = jnp.zeros_like(total)
    acc[...] = jnp.zeros_like(acc)

    def step(i, c):
        sa = me.a - i

        @pl.when(sa > 1)
        def _():
            relay(sa - 2, True, False)

        for sb in (me.b, 1 - me.b):
            carry(me.index(sa, sb, 1 - me.c), 2).wait_recv()
        lax.fori_loop(0, items, block, sa)
        return c

    lax.fori_loop(0, me.a + 1, step, 0)
    for item in range(items):
        spread_heads(context_ref, item, acc[item] / total[item], group, keys)
    log_ref[...] = top[...] + jnp.log(total[...])
    relay(me.a, False, True)

    def settle(i, c):
        relay(me.a - i, False, False)
        return c

    lax.fori_loop(1, me.a + 1, settle, 0)


def attend(query, pairs, planes, group, size, cid):
    f32, bf16 = jnp.float32, jnp.bfloat16
    tokens, width = query.shape
    count = planes * 4
    items = (tokens * 4 // BLOCK) * (width // (group * size))
    state = (items, group * BLOCK // 4, size)
    inside = pl.BlockSpec(memory_space=pltpu.VMEM)
    return pl.pallas_call(
        functools.partial(attend_kernel, planes, group),
        out_shape=[
            jax.ShapeDtypeStruct((tokens, width), bf16),
            jax.ShapeDtypeStruct((count,) + pairs.shape, bf16),
            jax.ShapeDtypeStruct(state, f32),
        ],
        in_specs=[inside] * 2,
        out_specs=[inside] * 3,
        scratch_shapes=[
            pltpu.VMEM(state, bf16),
            pltpu.VMEM(state, f32),
            pltpu.VMEM(state, f32),
            pltpu.VMEM(state, f32),
            pltpu.SemaphoreType.DMA((count, 4)),
            pltpu.SemaphoreType.DMA((count,)),
        ],
        compiler_params=pltpu.CompilerParams(collective_id=cid, has_side_effects=True, vmem_limit_bytes=ROOM),
        name="attend",
    )(query, pairs)


def attend_back_kernel(
    planes,
    group,
    q_ref,
    g_ref,
    o_ref,
    all_ref,
    log_ref,
    cut_ref,
    column_ref,
    query_grad,
    pair_grad,
    mixing_ref,
    cut_all,
    column,
    qs,
    gs,
    delta,
    qacc,
    mine,
    landc,
    landb,
    landa,
    ssem,
    rsem,
    psend,
    precv,
    lsem,
):
    me = Spot()
    f32, bf16 = jnp.float32, jnp.bfloat16
    items, rows, size = qs.shape
    keys = all_ref.shape[2] // (2 * size)
    factor = size ** (-0.5)
    me.greet(planes, False, True, False, True)

    def cut_to(k):
        far = lax.rem(me.a + k, planes)
        return push(cut_ref.at[far], cut_all.at[me.a], psend.at[k], precv.at[me.a], me.at(far, me.b, me.c))

    def cut_from(k):
        far = lax.rem(me.a + k, planes)
        there = cut_all.at[far]
        push(there, there, psend.at[k], precv.at[far], me.at(far, me.b, me.c)).wait_recv()

    for k in range(1, planes):
        cut_to(k).start()
    keep = pltpu.make_async_copy(cut_ref.at[me.a], cut_all.at[me.a], lsem.at[0])
    keep.start()

    def column_in(k):
        far = lax.rem(me.a + k, planes)
        return pltpu.make_async_copy(column_ref.at[far], column.at[far], lsem.at[k])

    for k in range(1, planes):
        column_in(k).start()
    column[me.a] = o_ref[...]
    stack_heads(qs, q_ref, group)
    stack_heads(gs, g_ref, group)
    stack_heads(qacc, o_ref, group)

    def prepare(item, c):
        part = jnp.sum(gs[item].astype(f32) * qacc[item], axis=1, keepdims=True)
        delta[item] = jnp.broadcast_to(part, delta.shape[1:])
        qacc[item] = jnp.zeros(qacc.shape[1:], f32)
        return c

    lax.fori_loop(0, items, prepare, 0)

    def block(item, sa):
        keys_here = joined(block_heads(all_ref, sa, item, keys, size, 0))
        values = joined(block_heads(all_ref, sa, item, keys, size, 1))
        queries, grads = qs[item], gs[item]
        scores = over(queries, keys_here, NT) * factor
        probs = jnp.exp(scores - log_ref[item][:, :1])
        prob_grads = over(grads, values, NT)
        score_grads = (probs * (prob_grads - delta[item][:, :1])).astype(bf16)
        qacc[item] += over(score_grads, keys_here, NN)
        key_part = (over(score_grads, queries, TN) * factor).astype(bf16)
        value_part = over(probs.astype(bf16), grads, TN).astype(bf16)
        seg = key_part.shape[0] // 4
        for part, value in ((0, key_part), (1, value_part)):
            for q, ref in enumerate(block_heads(mine, sa, item, keys, size, part)):
                ref[...] = value[q * seg : (q + 1) * seg, :]
        return sa

    def send_c(sa, sb):
        slot = sa * 2 + sb
        src = mine.at[me.index(sa, sb, 1 - me.c)]
        return push(src, landc.at[slot], ssem.at[0, slot], rsem.at[0, slot], me.at(me.a, me.b, 1 - me.c))

    def send_b(sa):
        src = mine.at[me.index(sa, 1 - me.b, me.c)]
        return push(src, landb.at[sa], ssem.at[1, sa], rsem.at[1, sa], me.at(me.a, 1 - me.b, me.c))

    def send_a(sa):
        src = mine.at[me.index(sa, me.b, me.c)]
        return push(src, landa.at[me.a], ssem.at[2, sa], rsem.at[2, me.a], me.at(sa, me.b, me.c))

    def from_c(sa):
        for sb in (1 - me.b, me.b):
            slot = sa * 2 + sb
            push(landc.at[slot], landc.at[slot], ssem.at[0, slot], rsem.at[0, slot], me.at(me.a, me.b, 1 - me.c)).wait_recv()
            idx = me.index(sa, sb, me.c)
            add_rows(mine.at[idx], [mine.at[idx], landc.at[slot]])
            if sb is not me.b:
                send_b(sa).start()

    def from_b(sa):
        push(landb.at[sa], landb.at[sa], ssem.at[1, sa], rsem.at[1, sa], me.at(me.a, 1 - me.b, me.c)).wait_recv()
        idx = me.index(sa, me.b, me.c)
        return mine.at[idx], [mine.at[idx], landb.at[sa]]

    def along(sa):
        target, parts = from_b(sa)
        add_rows(target, parts)
        send_a(sa).start()

    def finish():
        target, parts = from_b(me.a)
        add_rows(pair_grad, parts)
        for far in range(1, planes):

            @pl.when(far > me.a)
            def _(far=far):
                push(landa.at[far], landa.at[far], ssem.at[2, far], rsem.at[2, far], me.at(far, me.b, me.c)).wait_recv()
                add_rows(pair_grad, [pair_grad, landa.at[far]])

    def mix():
        share = mixing_ref.shape[1]
        keep.wait()
        for k in range(1, planes):
            cut_from(k)
            column_in(k).wait()
        tokens = column.shape[0] * column.shape[1]
        for n in range(0, column.shape[2], 512):
            rows = column[:, :, n : n + 512].reshape(tokens, 512)
            part = over(cut_all[...].reshape(tokens, 4 * share), rows, TN).astype(bf16)
            for q in range(4):
                mixing_ref[q, :, n : n + 512] = part[q * share : (q + 1) * share]

    def step(sa, c):
        lax.fori_loop(0, items, block, sa)
        for sb in (1 - me.b, me.b):
            send_c(sa, sb).start()

        @pl.when(sa >= 1)
        def _():
            from_c(sa - 1)

        @pl.when(sa >= 2)
        def _():
            along(sa - 2)

        return c

    lax.fori_loop(0, me.a + 1, step, 0)
    for item in range(items):
        spread_heads(query_grad, item, qacc[item] * factor, group, keys)
    mix()
    from_c(me.a)

    @pl.when(me.a > 0)
    def _():
        along(me.a - 1)

    finish()

    def settle(sa, c):
        for sb in (1 - me.b, me.b):
            send_c(sa, sb).wait_send()
        send_b(sa).wait_send()

        @pl.when(sa < me.a)
        def _():
            send_a(sa).wait_send()

        return c

    lax.fori_loop(0, me.a + 1, settle, 0)
    for k in range(1, planes):
        cut_to(k).wait_send()


def attend_back(query, grads, context, pairs_all, logs, cut, column, planes, group, size, cid):
    f32, bf16 = jnp.float32, jnp.bfloat16
    tokens, width = query.shape
    items = logs.shape[0]
    state = logs.shape
    block = pairs_all.shape[1:]
    share = cut.shape[2] // 4
    inside = pl.BlockSpec(memory_space=pltpu.VMEM)
    anywhere = pl.BlockSpec(memory_space=pl.ANY)
    return pl.pallas_call(
        functools.partial(attend_back_kernel, planes, group),
        out_shape=[
            jax.ShapeDtypeStruct((tokens, width), f32),
            jax.ShapeDtypeStruct(block, f32),
            jax.ShapeDtypeStruct((4, share, width), bf16),
        ],
        in_specs=[inside] * 5 + [anywhere] * 2,
        out_specs=[inside] * 3,
        scratch_shapes=[
            pltpu.VMEM(cut.shape, bf16),
            pltpu.VMEM(column.shape, bf16),
            pltpu.VMEM(state, bf16),
            pltpu.VMEM(state, bf16),
            pltpu.VMEM(state, f32),
            pltpu.VMEM(state, f32),
            pltpu.VMEM((4 * planes,) + block, bf16),
            pltpu.VMEM((2 * planes,) + block, bf16),
            pltpu.VMEM((planes,) + block, bf16),
            pltpu.VMEM((planes,) + block, bf16),
            pltpu.SemaphoreType.DMA((3, 2 * planes)),
            pltpu.SemaphoreType.DMA((3, 2 * planes)),
            pltpu.SemaphoreType.DMA((planes,)),
            pltpu.SemaphoreType.DMA((planes,)),
            pltpu.SemaphoreType.DMA((planes,)),
        ],
        compiler_params=pltpu.CompilerParams(collective_id=cid, has_side_effects=True, vmem_limit_bytes=ROOM),
        name="attend_back",
    )(query, grads, context, pairs_all, logs, cut, column)


def weights_kernel(
    planes,
    chunk,
    low_ref,
    cut_ref,
    query_w,
    key_w,
    value_w,
    input_ref,
    gain_ref,
    grad_ref,
    small_ref,
    mixing_part,
    rows_ref,
    input_grad,
    total_ref,
    mixing_rows,
    low_all,
    mixed,
    mixc,
    mixb,
    weights,
    sums,
    landz,
    normed,
    normed_other,
    gains_other,
    send,
    land,
    wload,
    lsend,
    lrecv,
    msend,
    mrecv,
    mload,
    zsend,
    zrecv,
    nsend,
    nrecv,
    tsend,
    trecv,
):
    me = Spot()
    f32, bf16 = jnp.float32, jnp.bfloat16
    tokens, packed = low_ref.shape
    width = input_ref.shape[1]
    chunks = packed // chunk
    assert chunks == 10
    place = lax.rem(me.e, 4)
    base = me.e - place
    share = sums.shape[1] // planes

    def spot(b, c):
        return me.index(0, b, c)

    near = [(1 - me.b, me.c), (me.b, 1 - me.c), (1 - me.b, 1 - me.c)]
    peers = [(base + spot(b, c), me.t) for b, c in near]
    barrier = pltpu.get_barrier_semaphore()
    for who in peers + [me.core()] + [me.at(lax.rem(me.a + k, planes), me.b, me.c) for k in range(1, planes)]:
        pl.semaphore_signal(barrier, inc=1, device_id=who, device_id_type=MESH)
    pl.semaphore_wait(barrier, 3 + planes)

    def cols(k):
        return pl.ds(pl.multiple_of(k * chunk, chunk), chunk)

    def whole(i, k):
        return push(low_ref.at[:, cols(k)], low_all.at[place, :, cols(k)], lsend.at[i, k], lrecv.at[i, k], peers[i])

    first = spot(*near[0])

    def relay(k):
        there = low_all.at[first, :, cols(k)]
        return push(there, there, lsend.at[2, k], lrecv.at[2, k], peers[1])

    quarters = [spot(b, c) for b, c in ((1 - me.b, 1 - me.c), (me.b, 1 - me.c), (1 - me.b, me.c), (me.b, me.c))]

    def mix_c(i):
        return push(mixing_part.at[quarters[i]], mixc.at[i], msend.at[i], mrecv.at[i], peers[1])

    def mix_b():
        return push(mixed.at[0], mixb, msend.at[2], mrecv.at[2], peers[0])

    mix_loads = [pltpu.make_async_copy(mixing_part.at[quarters[2 + i]], mixed.at[i], mload.at[i]) for i in range(2)]

    def mix_round(k):
        if k == chunks - 2:
            for i in range(2):
                mix_c(i).start()
        if k == chunks:
            for i in range(2):
                mix_loads[i].wait()
                mix_c(i).wait_recv()
                add_rows(mixed.at[i], [mixed.at[i], mixc.at[i]])
                if i == 0:
                    mix_b().start()
        if k == chunks + 1:
            mix_b().wait_recv()
            add_rows(mixing_rows, [mixed.at[1], mixb])

    def send_low(k, c):
        whole(0, k).start()
        return c

    lax.fori_loop(0, chunks, send_low, 0)
    whole(1, 0).start()
    whole(1, 1).start()
    for k in mix_loads:
        k.start()
    query_width, key_width = query_w.shape[1], key_w.shape[1]
    loads = [
        pltpu.make_async_copy(query_w, weights.at[:, :query_width], wload.at[0]),
        pltpu.make_async_copy(key_w, weights.at[:, query_width : query_width + key_width], wload.at[1]),
        pltpu.make_async_copy(value_w, weights.at[:, query_width + key_width :], wload.at[2]),
    ]
    for k in loads:
        k.start()
    gains = push(small_ref.at[pl.ds(0, 8)], gains_other, nsend.at[4], nrecv.at[4], me.core())
    gains.start()
    low_all[place] = low_ref[...]
    quarter = width // 4

    def trade(n):
        at = pl.ds(pl.multiple_of(n * quarter, quarter), quarter)
        return push(normed.at[:, at], normed_other.at[:, at], nsend.at[n], nrecv.at[n], me.core())

    def normed_cols(n, c):
        at = pl.ds(pl.multiple_of(n * quarter, quarter), quarter)
        normed[:, at] = over(low_ref[...], weights[at, :], NT).astype(bf16)
        trade(n).start()
        return c

    def await_trade(n, c):
        trade(n).wait_recv()
        return c


    def input_rows(r, total):
        at = pl.ds(pl.multiple_of(r * 16, 16), 16)
        grads = normed[at, :].astype(f32) + normed_other[at, :].astype(f32)
        inputs = input_ref[at, :].astype(f32)
        scale = lax.rsqrt(jnp.mean(inputs * inputs, axis=1, keepdims=True) + epsilon)
        scaled = gain_ref[...] * grads
        level = jnp.mean(scaled * inputs, axis=1, keepdims=True)
        input_grad[at, :] = grad_ref[at, :] + scale * scaled - inputs * (scale * scale * scale * level)
        return total + jnp.sum(grads * inputs * scale, axis=0, keepdims=True)

    def norm_round(k):
        if k == 0:
            for copy in loads:
                copy.wait()
        if k < 4:
            lax.fori_loop(k, k + 1, normed_cols, 0)
        if k == 4:
            gains.wait()
            total_ref[...] = small_ref[...]
            total_ref[0:8, :] += gains_other[...]
            lax.fori_loop(0, 4, await_trade, 0)
            total_ref[8:9, :] = lax.fori_loop(0, tokens // 16, input_rows, jnp.zeros((1, width), f32))
            send[0] = total_ref[ours, :]

    half = total_ref.shape[0] // 2
    ours = pl.ds(pl.multiple_of(me.t * half, half), half)
    others = pl.ds(pl.multiple_of((1 - me.t) * half, half), half)
    bits = [1, 2, 4, 8]

    def small(j):
        bit = bits[j]
        who = (me.e + bit * (1 - 2 * lax.rem(lax.div(me.e, bit), 2)), me.t)
        return push(send.at[j], land.at[j], tsend.at[j], trecv.at[j], who)

    share_back = push(send.at[4], land.at[4], tsend.at[4], trecv.at[4], me.core())

    def small_round(j):
        if j > 0:
            small(j - 1).wait_recv()
            if j < 4:
                send[j] = send[j - 1] + land[j - 1]
            else:
                send[4] = send[3] + land[3]
                share_back.start()
        if j < 4:
            small(j).start()


    def block(k, d):
        return sums.at[k, pl.ds(pl.multiple_of(d * share, share), share)]

    def along(k, d, up):
        arrive = me.a + 1 if up else me.a - 1
        slot = d if up else jnp.where(d == arrive, planes, d)
        return push(block(k, d), landz.at[k, slot], zsend.at[k, d], zrecv.at[k, slot], me.at(arrive, me.b, me.c))

    def landed(k, slot):
        push(landz.at[k, slot], landz.at[k, slot], zsend.at[k, 0], zrecv.at[k, slot], me.core()).wait_recv()

    def chain(k, act, ends):
        for i in range(planes - 1):
            d = far_first(me.a, planes, i)
            up = d > me.a
            inner = (up & (me.a > 0)) | (jnp.logical_not(up) & (me.a + 1 < planes))

            @pl.when(jnp.logical_not(inner) if ends else inner)
            def _(d=d, up=up):
                if act and not ends:
                    landed(k, d)
                    add_rows(block(k, d), [block(k, d), landz.at[k, d]])

                @pl.when(up)
                def _():
                    along(k, d, True).start() if act else along(k, d, True).wait_send()

                @pl.when(jnp.logical_not(up))
                def _():
                    along(k, d, False).start() if act else along(k, d, False).wait_send()

    def finish(k):
        target = rows_ref.at[:, cols(k)]
        own = block(k, me.a)

        @pl.when(me.a > 0)
        def _():
            landed(k, me.a)

        @pl.when(me.a + 1 < planes)
        def _():
            landed(k, planes)

        @pl.when((me.a > 0) & (me.a + 1 < planes))
        def _():
            add_rows(target, [own, landz.at[k, me.a], landz.at[k, planes]])

        @pl.when(me.a == 0)
        def _():
            add_rows(target, [own, landz.at[k, planes]])

        @pl.when(me.a + 1 == planes)
        def _():
            add_rows(target, [own, landz.at[k, me.a]])

    def forward(k):
        whole(0, k).wait_recv()
        relay(k).start()
        if k + 2 < chunks:
            whole(1, k + 2).start()

    for k in range(chunks + 2):
        if k < chunks:
            if k == 0:
                forward(0)
            if k + 1 < chunks:
                forward(k + 1)
            whole(1, k).wait_recv()
            relay(k).wait_recv()
            mixed_rows = low_all[:, :, k * chunk : (k + 1) * chunk].reshape(4 * tokens, chunk)
            sums[k] = over(cut_ref[...], mixed_rows, NN).astype(bf16)
            chain(k, True, True)
        norm_round(k)
        if k in (4, 6, 8, 10, 11):
            small_round((4, 6, 8, 10, 11).index(k))
        if 1 <= k <= chunks:
            chain(k - 1, True, False)
        if k >= 2:
            finish(k - 2)
        mix_round(k)

    def settle(k, c):
        for i in range(2):
            whole(i, k).wait_send()
        relay(k).wait_send()
        chain(k, False, True)
        chain(k, False, False)
        return c

    lax.fori_loop(0, chunks, settle, 0)
    for k in (mix_c(0), mix_c(1), mix_b()):
        k.wait_send()
    for n in range(4):
        trade(n).wait_send()
        small(n).wait_send()
    share_back.wait_send()
    share_back.wait_recv()
    total_ref[ours, :] = send[4]
    total_ref[others, :] = land[4]


def weight_grads(low, cut, query_w, key_w, value_w, inputs, gain, residual_grad, small, mixing, planes, cid):
    f32, bf16 = jnp.float32, jnp.bfloat16
    tokens, packed = low.shape
    width = inputs.shape[1]
    chunk = 256
    chunks = packed // chunk
    share = cut.shape[0] // planes
    quarter = mixing.shape[1:]
    inside = pl.BlockSpec(memory_space=pltpu.VMEM)
    anywhere = pl.BlockSpec(memory_space=pl.ANY)
    half = (small.shape[0] // 2, small.shape[1])
    return pl.pallas_call(
        functools.partial(weights_kernel, planes, chunk),
        out_shape=[
            jax.ShapeDtypeStruct((share, packed), f32),
            jax.ShapeDtypeStruct((tokens, width), f32),
            jax.ShapeDtypeStruct(small.shape, f32),
            jax.ShapeDtypeStruct(quarter, f32),
        ],
        in_specs=[inside, inside, anywhere, anywhere, anywhere, inside, inside, inside, inside, anywhere],
        out_specs=[inside] * 4,
        scratch_shapes=[
            pltpu.VMEM((4, tokens, packed), bf16),
            pltpu.VMEM((2,) + quarter, bf16),
            pltpu.VMEM((2,) + quarter, bf16),
            pltpu.VMEM(quarter, bf16),
            pltpu.VMEM((width, packed), bf16),
            pltpu.VMEM((chunks, planes * share, chunk), bf16),
            pltpu.VMEM((chunks, planes + 1, share, chunk), bf16),
            pltpu.VMEM((tokens, width), bf16),
            pltpu.VMEM((tokens, width), bf16),
            pltpu.VMEM((8, width), f32),
            pltpu.VMEM((5,) + half, f32),
            pltpu.VMEM((5,) + half, f32),
            pltpu.SemaphoreType.DMA((3,)),
            pltpu.SemaphoreType.DMA((3, chunks)),
            pltpu.SemaphoreType.DMA((3, chunks)),
            pltpu.SemaphoreType.DMA((3,)),
            pltpu.SemaphoreType.DMA((3,)),
            pltpu.SemaphoreType.DMA((2,)),
            pltpu.SemaphoreType.DMA((chunks, planes)),
            pltpu.SemaphoreType.DMA((chunks, planes + 1)),
            pltpu.SemaphoreType.DMA((5,)),
            pltpu.SemaphoreType.DMA((5,)),
            pltpu.SemaphoreType.DMA((5,)),
            pltpu.SemaphoreType.DMA((5,)),
        ],
        compiler_params=pltpu.CompilerParams(collective_id=cid, has_side_effects=True, vmem_limit_bytes=ROOM),
        name="weight_grads",
    )(low, cut, query_w, key_w, value_w, inputs, gain, residual_grad, small, mixing)


epsilon = 1e-06
rope_base = 1000000.0
far_below = -1e30


def rms_scaled(values, gain_vec):
    return (
        values * lax.rsqrt(jnp.mean(values * values, axis=-1, keepdims=True) + epsilon) * gain_vec
    )


def rotary_tables(positions, head_dim):
    halfway = head_dim // 2
    exponents = jnp.arange(halfway, dtype=jnp.float32) * (2.0 / head_dim)
    inverse = jnp.exp(-exponents * jnp.log(jnp.float32(rope_base)))
    angles = positions.astype(jnp.float32)[:, None] * inverse[None, :]
    return (jnp.cos(angles), jnp.sin(angles))


def rotate(values, cosine, sine_table):
    halfway = values.shape[-1] // 2
    first = values[..., :halfway]
    latter = values[..., halfway:]
    return jnp.concatenate(
        [first * cosine - latter * sine_table, latter * cosine + first * sine_table], axis=-1
    )


def glu_value(gate_act, up_act):
    return jax.nn.silu(gate_act) * up_act


def on_device(
    layer_input,
    norm_first,
    query_weight,
    key_weight,
    value_weight,
    mixing_weight,
    query_gain,
    key_gain,
    norm_second,
    router_weight,
    gate_weight,
    up_weight,
    down_weight,
    routes,
    fill_order,
    cotangent,
):
    seq_count, seg_len, model_width = layer_input.shape
    expert_count = lax.axis_size("expert")
    tensor_count = lax.axis_size("tensor")
    expert_idx = lax.axis_index("expert")
    tensor_idx = lax.axis_index("tensor")
    head_dim = query_gain.shape[0]
    local_queries = query_weight.shape[1] // head_dim
    local_keys = key_weight.shape[1] // head_dim
    group_size = local_queries // local_keys
    seq_length = seg_len * expert_count
    top_count = routes.shape[2]
    token_count = seq_count * seg_len
    capacity = 5 * token_count * top_count // (4 * expert_count)
    half_width = model_width // tensor_count
    factor = head_dim ** (-0.5)
    inputs = layer_input.astype(jnp.float32)
    normed_f, first_back = jax.vjp(rms_scaled, inputs, norm_first)
    normed = normed_f.astype(jnp.bfloat16)
    positions = expert_idx * seg_len + jnp.arange(seg_len, dtype=jnp.int32)
    cosine, sine_table = rotary_tables(positions, head_dim)
    cosine = cosine[:, None, :]
    sine_table = sine_table[:, None, :]

    def rope_norm(raw_heads, gain_vec):
        return rotate(rms_scaled(raw_heads, gain_vec), cosine, sine_table)

    query_raw = jnp.dot(normed, query_weight, preferred_element_type=jnp.float32).reshape(
        seq_count, seg_len, local_queries, head_dim
    )
    key_raw = jnp.dot(normed, key_weight, preferred_element_type=jnp.float32).reshape(
        seq_count, seg_len, local_keys, head_dim
    )
    value_local = jnp.dot(normed, value_weight, preferred_element_type=jnp.float32).astype(
        jnp.bfloat16
    )
    query_rot, query_back = jax.vjp(rope_norm, query_raw, query_gain)
    key_rot, key_back = jax.vjp(rope_norm, key_raw, key_gain)
    key_local = key_rot.astype(jnp.bfloat16).reshape(seq_count, seg_len, local_keys * head_dim)
    key_all, value_all = (
        lax.all_gather(key_local, "expert", axis=1, tiled=True),
        lax.all_gather(value_local, "expert", axis=1, tiled=True),
    )
    key_tiles = key_all.reshape(seq_count, seq_length, local_keys, head_dim)
    value_tiles = value_all.reshape(seq_count, seq_length, local_keys, head_dim)
    query_rows = query_rot.astype(jnp.bfloat16).reshape(
        seq_count, seg_len, local_keys, group_size, head_dim
    )
    query_rows = query_rows.transpose(0, 2, 3, 1, 4).reshape(
        seq_count, local_keys, group_size * seg_len, head_dim
    )
    row_block = (
        expert_idx * seg_len + jnp.arange(group_size * seg_len, dtype=jnp.int32) % seg_len
    ) // BLOCK
    tile_len = min(512, seq_length)
    reach_end = jnp.minimum(((expert_idx + 1) * seg_len - 1) // BLOCK * BLOCK + BLOCK, seq_length)
    tile_count = (reach_end + tile_len - 1) // tile_len

    def tile_scores(tile_idx):
        offset = tile_idx * tile_len
        key_part = lax.dynamic_slice_in_dim(key_tiles, offset, tile_len, 1)
        scores = (
            jnp.einsum("shrd,skhd->shrk", query_rows, key_part, preferred_element_type=jnp.float32)
            * factor
        )
        key_block = (offset + jnp.arange(tile_len, dtype=jnp.int32)) // BLOCK
        allowed = key_block[None, :] <= row_block[:, None]
        return (scores, allowed, offset)

    stat_shape = (seq_count, local_keys, group_size * seg_len)

    def stats_step(tile_idx, state_pair):
        running_max, running_sum = state_pair
        scores, allowed, offset = tile_scores(tile_idx)
        masked = jnp.where(allowed, scores, far_below)
        new_max = jnp.maximum(running_max, jnp.max(masked, axis=-1))
        exp_terms = jnp.where(allowed, jnp.exp(masked - new_max[..., None]), 0.0)
        return (new_max, running_sum * jnp.exp(running_max - new_max) + jnp.sum(exp_terms, axis=-1))

    row_max, row_sum = lax.fori_loop(
        0,
        tile_count,
        stats_step,
        (jnp.full(stat_shape, far_below, jnp.float32), jnp.zeros(stat_shape, jnp.float32)),
    )
    log_total = row_max + jnp.log(row_sum)

    def probabilities(tile_idx):
        scores, allowed, offset = tile_scores(tile_idx)
        return (jnp.where(allowed, jnp.exp(scores - log_total[..., None]), 0.0), offset)

    def context_step(tile_idx, context_sum):
        prob_tile, offset = probabilities(tile_idx)
        value_part = lax.dynamic_slice_in_dim(value_tiles, offset, tile_len, 1)
        return context_sum + jnp.einsum(
            "shrk,skhd->shrd",
            prob_tile.astype(jnp.bfloat16),
            value_part,
            preferred_element_type=jnp.float32,
        )

    context_f = lax.fori_loop(0, tile_count, context_step, jnp.zeros(query_rows.shape, jnp.float32))
    shaped = context_f.reshape(seq_count, local_keys, group_size, seg_len, head_dim).transpose(
        0, 3, 1, 2, 4
    )
    context = shaped.reshape(seq_count, seg_len, local_queries * head_dim).astype(jnp.bfloat16)
    head_part = jnp.dot(context, mixing_weight, preferred_element_type=jnp.float32)
    residual = inputs + lax.psum(head_part.astype(jnp.bfloat16), "tensor").astype(jnp.float32)
    second_f, second_back = jax.vjp(rms_scaled, residual, norm_second)
    second = second_f.astype(jnp.bfloat16).reshape(token_count, model_width)
    logits = jnp.dot(second, router_weight, preferred_element_type=jnp.float32)
    flat_routes = routes.reshape(token_count, top_count)
    picked = (flat_routes[:, :, None] == jnp.arange(expert_count, dtype=jnp.int32)).astype(
        jnp.float32
    )
    gates = jax.nn.softmax(jnp.sum(picked * logits[:, None, :], axis=-1), axis=-1)
    usages = jnp.sum(picked, axis=1)
    ranking = fill_order.reshape(token_count)
    before = (ranking[None, :] < ranking[:, None]).astype(jnp.bfloat16)
    counts = jnp.dot(before, usages.astype(jnp.bfloat16), preferred_element_type=jnp.float32)
    slot_ids = jnp.sum(picked * counts[:, None, :], axis=-1).astype(jnp.int32)
    kept_mask = slot_ids < capacity
    kept_float = kept_mask.astype(jnp.float32)
    weighted = gates * kept_float
    places = jnp.where(kept_mask, flat_routes * capacity + slot_ids, -1)
    slot_grid = jnp.arange(expert_count * capacity, dtype=jnp.int32)
    assign = (places[:, :, None] == slot_grid).astype(jnp.bfloat16)
    placed = jnp.sum(assign, axis=1)
    combine = jnp.sum(weighted[:, :, None] * assign.astype(jnp.float32), axis=1)
    send_rows = jnp.einsum("tp,td->pd", placed, second, preferred_element_type=jnp.float32).astype(
        jnp.bfloat16
    )
    arrived = lax.all_to_all(
        send_rows.reshape(expert_count, capacity, model_width),
        "expert",
        split_axis=0,
        concat_axis=0,
        tiled=True,
    )
    arrived = arrived.reshape(expert_count * capacity, model_width)
    gate_one = gate_weight[0]
    up_one = up_weight[0]
    down_one = down_weight[0]
    gate_act = jnp.dot(arrived, gate_one, preferred_element_type=jnp.float32)
    up_act = jnp.dot(arrived, up_one, preferred_element_type=jnp.float32)
    hidden_val, glu_back = jax.vjp(glu_value, gate_act, up_act)
    hidden = hidden_val.astype(jnp.bfloat16)
    expert_part = jnp.dot(hidden, down_one, preferred_element_type=jnp.float32)
    summed = lax.psum(expert_part.astype(jnp.bfloat16), "tensor")
    returned = lax.all_to_all(
        summed.reshape(expert_count, capacity, model_width),
        "expert",
        split_axis=0,
        concat_axis=0,
        tiled=True,
    )
    returned = returned.reshape(expert_count * capacity, model_width)
    per_route = (
        jnp.take(returned, jnp.maximum(places, 0), axis=0).astype(jnp.float32)
        * kept_float[:, :, None]
    )
    mixture = residual.reshape(token_count, model_width) + jnp.sum(
        weighted[:, :, None] * per_route, axis=1
    )
    layer_output = lax.dynamic_slice_in_dim(mixture, tensor_idx * half_width, half_width, 1)
    layer_output = layer_output.astype(jnp.bfloat16).reshape(seq_count, seg_len, half_width)
    upstream = cotangent.astype(jnp.float32).reshape(token_count, model_width)
    gate_grads = jnp.sum(upstream[:, None, :] * per_route, axis=-1) * kept_float
    send_grads = jnp.einsum(
        "tp,td->pd",
        combine,
        upstream,
        precision=lax.Precision.HIGHEST,
        preferred_element_type=jnp.float32,
    ).astype(jnp.bfloat16)
    grads_in = lax.all_to_all(
        send_grads.reshape(expert_count, capacity, model_width),
        "expert",
        split_axis=0,
        concat_axis=0,
        tiled=True,
    )
    grads_in = grads_in.reshape(expert_count * capacity, model_width)
    hidden_grad = lax.dot_general(
        grads_in, down_one, (((1,), (1,)), ((), ())), preferred_element_type=jnp.float32
    )
    down_grad = jnp.einsum("rf,rd->fd", hidden, grads_in, preferred_element_type=jnp.float32)
    gate_d, up_d = glu_back(hidden_grad)
    gate_d = gate_d.astype(jnp.bfloat16)
    up_d = up_d.astype(jnp.bfloat16)
    gate_grad = jnp.einsum("rd,rf->df", arrived, gate_d, preferred_element_type=jnp.float32)
    up_grad = jnp.einsum("rd,rf->df", arrived, up_d, preferred_element_type=jnp.float32)
    row_part = lax.dot_general(
        gate_d, gate_one, (((1,), (1,)), ((), ())), preferred_element_type=jnp.float32
    )
    row_part = row_part + lax.dot_general(
        up_d, up_one, (((1,), (1,)), ((), ())), preferred_element_type=jnp.float32
    )
    row_share = lax.psum_scatter(
        row_part.reshape(expert_count, capacity, model_width).astype(jnp.bfloat16),
        "tensor",
        scatter_dimension=2,
        tiled=True,
    )
    row_home = lax.all_to_all(row_share, "expert", split_axis=0, concat_axis=0, tiled=True).reshape(
        expert_count * capacity, half_width
    )
    second_half = jnp.dot(placed, row_home, preferred_element_type=jnp.float32)
    route_grads = gates * (gate_grads - jnp.sum(gates * gate_grads, axis=-1, keepdims=True))
    logit_grads = jnp.sum(picked * route_grads[:, :, None], axis=1).astype(jnp.bfloat16)
    router_grad = jnp.einsum("td,te->de", second, logit_grads, preferred_element_type=jnp.float32)
    router_back = lax.dot_general(
        logit_grads, router_weight, (((1,), (1,)), ((), ())), preferred_element_type=jnp.float32
    )
    own_part = second_half + lax.dynamic_slice_in_dim(
        router_back, tensor_idx * half_width, half_width, 1
    )
    second_part = lax.dynamic_update_slice_in_dim(
        jnp.zeros((token_count, model_width), jnp.float32), own_part, tensor_idx * half_width, 1
    )
    residual_part, norm_part = second_back(second_part.reshape(seq_count, seg_len, model_width))
    residual_grad, second_grad = (
        lax.psum(residual_part.astype(jnp.bfloat16), "tensor").astype(jnp.float32),
        lax.psum(norm_part.astype(jnp.bfloat16), "tensor").astype(jnp.float32),
    )
    residual_grad = residual_grad + upstream.reshape(seq_count, seg_len, model_width)
    head_in = residual_grad.astype(jnp.bfloat16)
    mixing_part = jnp.einsum("std,stc->dc", head_in, context, preferred_element_type=jnp.float32)
    context_grad = lax.dot_general(
        head_in, mixing_weight, (((2,), (1,)), ((), ())), preferred_element_type=jnp.float32
    ).astype(jnp.bfloat16)
    grad_rows = context_grad.reshape(
        seq_count, seg_len, local_keys, group_size, head_dim
    ).transpose(0, 2, 3, 1, 4)
    grad_rows = grad_rows.reshape(query_rows.shape)
    delta_rows = jnp.sum(grad_rows.astype(jnp.float32) * context_f, axis=-1)
    key_shape = (seq_count, seq_length, local_keys, head_dim)

    def gradient_step(tile_idx, state_trio):
        query_acc, key_acc, value_acc = state_trio
        prob_tile, offset = probabilities(tile_idx)
        key_part = lax.dynamic_slice_in_dim(key_tiles, offset, tile_len, 1)
        value_part = lax.dynamic_slice_in_dim(value_tiles, offset, tile_len, 1)
        prob_low = prob_tile.astype(jnp.bfloat16)
        prob_grad = jnp.einsum(
            "shrd,skhd->shrk", grad_rows, value_part, preferred_element_type=jnp.float32
        )
        score_grad = (prob_tile * (prob_grad - delta_rows[..., None])).astype(jnp.bfloat16)
        query_acc = query_acc + jnp.einsum(
            "shrk,skhd->shrd", score_grad, key_part, preferred_element_type=jnp.float32
        )
        key_tile = jnp.einsum(
            "shrk,shrd->skhd", score_grad, query_rows, preferred_element_type=jnp.float32
        )
        value_tile = jnp.einsum(
            "shrk,shrd->skhd", prob_low, grad_rows, preferred_element_type=jnp.float32
        )
        key_acc = lax.dynamic_update_slice_in_dim(key_acc, key_tile, offset, 1)
        value_acc = lax.dynamic_update_slice_in_dim(value_acc, value_tile, offset, 1)
        return (query_acc, key_acc, value_acc)

    start_state = (
        jnp.zeros(query_rows.shape, jnp.float32),
        jnp.zeros(key_shape, jnp.float32),
        jnp.zeros(key_shape, jnp.float32),
    )
    query_acc, key_acc, value_acc = lax.fori_loop(0, tile_count, gradient_step, start_state)
    key_grad_all, value_grad_all = (
        lax.psum_scatter(
            (key_acc * factor).reshape(seq_count, seq_length, local_keys * head_dim),
            "expert",
            scatter_dimension=1,
            tiled=True,
        ),
        lax.psum_scatter(
            value_acc.reshape(seq_count, seq_length, local_keys * head_dim),
            "expert",
            scatter_dimension=1,
            tiled=True,
        ),
    )
    key_raw_grad, keygain_part = key_back(
        key_grad_all.reshape(seq_count, seg_len, local_keys, head_dim)
    )
    query_shaped = (
        (query_acc * factor)
        .reshape(seq_count, local_keys, group_size, seg_len, head_dim)
        .transpose(0, 3, 1, 2, 4)
    )
    query_raw_grad, querygain_part = query_back(
        query_shaped.reshape(seq_count, seg_len, local_queries, head_dim)
    )
    query_low = query_raw_grad.astype(jnp.bfloat16).reshape(
        seq_count, seg_len, local_queries * head_dim
    )
    key_low = key_raw_grad.astype(jnp.bfloat16).reshape(seq_count, seg_len, local_keys * head_dim)
    value_low = value_grad_all.astype(jnp.bfloat16)
    query_sum = jnp.einsum("std,stc->dc", normed, query_low, preferred_element_type=jnp.float32)
    keys_sum = jnp.einsum("std,stc->dc", normed, key_low, preferred_element_type=jnp.float32)
    values_sum = jnp.einsum("std,stc->dc", normed, value_low, preferred_element_type=jnp.float32)
    query_grad, key_grad, value_grad, mixing_rows = (
        lax.psum_scatter(query_sum, "expert", scatter_dimension=0, tiled=True),
        lax.psum_scatter(keys_sum, "expert", scatter_dimension=0, tiled=True),
        lax.psum_scatter(values_sum, "expert", scatter_dimension=0, tiled=True),
        lax.psum_scatter(mixing_part, "expert", scatter_dimension=0, tiled=True),
    )
    mixing_grad = mixing_rows.T
    normed_part = lax.dot_general(
        query_low, query_weight, (((2,), (1,)), ((), ())), preferred_element_type=jnp.float32
    )
    normed_part = normed_part + lax.dot_general(
        key_low, key_weight, (((2,), (1,)), ((), ())), preferred_element_type=jnp.float32
    )
    normed_part = normed_part + lax.dot_general(
        value_low, value_weight, (((2,), (1,)), ((), ())), preferred_element_type=jnp.float32
    )
    normed_grad, querygain_grad, keygain_grad = (
        lax.psum(normed_part.astype(jnp.bfloat16), "tensor").astype(jnp.float32),
        lax.psum(querygain_part.astype(jnp.bfloat16), "tensor").astype(jnp.float32),
        lax.psum(keygain_part.astype(jnp.bfloat16), "tensor").astype(jnp.float32),
    )
    input_part, first_grad = first_back(normed_grad)
    input_grad = residual_grad + input_part
    first_grad, second_grad, querygain_grad, keygain_grad, router_grad = lax.psum(
        (first_grad, second_grad, querygain_grad, keygain_grad, router_grad), "expert"
    )
    return (
        layer_output,
        input_grad,
        first_grad,
        query_grad,
        key_grad,
        value_grad,
        mixing_grad,
        querygain_grad,
        keygain_grad,
        second_grad,
        router_grad,
        gate_grad[None],
        up_grad[None],
        down_grad[None],
    )

def lift(values, wide):
    high = lax.reduce_precision(values, 8, 7)
    both = jnp.concatenate([high, values - high], axis=-1).astype(jnp.bfloat16)
    return jnp.pad(both, ((0, 0), (0, wide - both.shape[-1])))


def on_chips(
    layer_input,
    norm_first,
    query_weight,
    key_weight,
    value_weight,
    mixing_weight,
    query_gain,
    key_gain,
    norm_second,
    router_weight,
    gate_weight,
    up_weight,
    down_weight,
    routes,
    fill_order,
    cotangent,
):
    seq_count, seg_len, model_width = layer_input.shape
    expert_count = lax.axis_size("expert")
    planes = expert_count // 4
    expert_idx = lax.axis_index("expert")
    tensor_idx = lax.axis_index("tensor")
    head_dim = query_gain.shape[0]
    local_queries = query_weight.shape[1] // head_dim
    local_keys = key_weight.shape[1] // head_dim
    key_width = local_keys * head_dim
    group_size = local_queries // local_keys
    top_count = routes.shape[2]
    token_count = seq_count * seg_len
    capacity = 5 * token_count * top_count // (4 * expert_count)
    slots = -(-capacity // 32) * 32
    half_width = model_width // 2
    share_width = model_width // expert_count
    f32, bf16 = jnp.float32, jnp.bfloat16
    inputs = layer_input.astype(f32)
    normed = rms_scaled(inputs, norm_first).astype(bf16)
    positions = expert_idx * seg_len + jnp.arange(seg_len, dtype=jnp.int32)
    cosine, sine_table = rotary_tables(positions, head_dim)
    cosine = cosine[:, None, :]
    sine_table = sine_table[:, None, :]

    def rope_norm(raw_heads, gain_vec):
        return rotate(rms_scaled(raw_heads, gain_vec), cosine, sine_table)

    def slices(rows):
        cut = rows.reshape(token_count, planes, 4, share_width)
        return cut.transpose(2, 0, 1, 3).reshape(4, token_count, planes * share_width)

    query_raw = jnp.dot(normed, query_weight, preferred_element_type=f32).reshape(
        seq_count, seg_len, local_queries, head_dim
    )
    key_raw = jnp.dot(normed, key_weight, preferred_element_type=f32).reshape(
        seq_count, seg_len, local_keys, head_dim
    )
    value_local = jnp.dot(normed, value_weight, preferred_element_type=f32).astype(bf16)
    query_rot, query_back = jax.vjp(rope_norm, query_raw, query_gain)
    key_rot, key_back = jax.vjp(rope_norm, key_raw, key_gain)
    key_local = key_rot.astype(bf16).reshape(token_count, key_width)
    pairs = jnp.concatenate([key_local, value_local.reshape(token_count, key_width)], axis=1)
    upstream_low = cotangent.reshape(token_count, model_width)
    half_tokens = token_count // 2
    upstream_half = lax.dynamic_slice_in_dim(upstream_low, tensor_idx * half_tokens, half_tokens, 0)
    upstream_mine = lax.all_gather(upstream_half, "expert")
    query_rows = query_rot.astype(bf16).reshape(token_count, local_queries * head_dim)
    context, pairs_all, logs = attend(query_rows, pairs, planes, group_size, head_dim, 1)
    head_part = jnp.dot(context, mixing_weight, preferred_element_type=f32)
    head_low = head_part.astype(bf16)
    head_other = swap_cores(head_low, 3, "swap_heads")
    residual = inputs.reshape(token_count, model_width) + (head_low.astype(f32) + head_other.astype(f32))
    second_f, second_back = jax.vjp(rms_scaled, residual, norm_second)
    second = second_f.astype(bf16)
    logits = jnp.dot(second, router_weight, preferred_element_type=f32)
    flat_routes = routes.reshape(token_count, top_count)
    picked = (flat_routes[:, :, None] == jnp.arange(expert_count, dtype=jnp.int32)).astype(f32)
    gates = jax.nn.softmax(jnp.sum(picked * logits[:, None, :], axis=-1), axis=-1)
    usages = jnp.sum(picked, axis=1)
    ranking = fill_order.reshape(token_count)
    before = (ranking[None, :] < ranking[:, None]).astype(bf16)
    counts = jnp.dot(before, usages.astype(bf16), preferred_element_type=f32)
    here = (usages > 0.0) & (counts < capacity)
    slot_table = jnp.where(here, counts, -1.0)
    gate_table = jnp.where(here, jnp.sum(picked * gates[:, :, None], axis=1), 0.0)
    slot_hi = lift(slot_table, 2 * expert_count)[:, :expert_count]
    notes = jnp.concatenate([slot_hi, lift(gate_table, 128 - expert_count)], axis=1)
    parcel = jnp.concatenate([second, notes], axis=1)
    normed_cut = slices(normed.reshape(token_count, model_width))
    _, _, out_share, row_home, context_column, other_cuts, gate_grad, up_grad, down_grad = run_experts(
        parcel, upstream_mine, gate_weight[0], up_weight[0], down_weight[0], context, normed_cut, planes, slots, 4
    )
    place = lax.rem(expert_idx, 4)
    own_cut = lax.dynamic_index_in_dim(normed_cut, place, 0)
    normed_cut = lax.dynamic_update_slice_in_dim(other_cuts, own_cut, place, 0)
    out_home = lax.psum_scatter(out_share, "expert", scatter_dimension=0, tiled=True)[0]
    residual_half = lax.dynamic_slice_in_dim(residual, tensor_idx * half_width, half_width, 1)
    layer_output = (residual_half + out_home.astype(f32)).astype(bf16).reshape(seq_count, seg_len, half_width)
    home_scores = jnp.sum(row_home[:, :, half_width:].astype(f32), axis=0)
    home_scores = home_scores[:, :expert_count] + home_scores[:, expert_count : 2 * expert_count]
    gate_grads = jnp.sum(picked * home_scores[:, None, :], axis=-1)
    route_grads = gates * (gate_grads - jnp.sum(gates * gate_grads, axis=-1, keepdims=True))
    logit_grads = jnp.sum(picked * route_grads[:, :, None], axis=1).astype(bf16)
    router_grad = jnp.einsum("td,te->ed", second, logit_grads, preferred_element_type=f32)
    router_back = lax.dot_general(
        logit_grads, router_weight, (((1,), (1,)), ((), ())), preferred_element_type=f32
    )
    second_rows = jnp.concatenate([row_home[0, :, :half_width], row_home[1, :, :half_width]], axis=1)
    second_in = second_rows.astype(f32) + router_back
    residual_part, second_grad = second_back(second_in)
    residual_grad = residual_part + upstream_low.astype(f32)
    head_in = residual_grad.astype(bf16)

    context_grad = lax.dot_general(
        head_in, mixing_weight, (((1,), (1,)), ((), ())), preferred_element_type=f32
    ).astype(bf16)
    head_cut = head_in.reshape(token_count, planes, 4 * share_width).transpose(1, 0, 2)
    query_rot_grad, pair_home, mixing_part = attend_back(
        query_rows,
        context_grad,
        context,
        pairs_all,
        logs,
        head_cut,
        context_column,
        planes,
        group_size,
        head_dim,
        7,
    )
    key_raw_grad, keygain_part = key_back(
        pair_home[:, :key_width].reshape(seq_count, seg_len, local_keys, head_dim)
    )
    query_raw_grad, querygain_part = query_back(
        query_rot_grad.reshape(seq_count, seg_len, local_queries, head_dim)
    )
    query_low = query_raw_grad.astype(bf16).reshape(token_count, local_queries * head_dim)
    key_low = key_raw_grad.astype(bf16).reshape(token_count, key_width)
    value_low = pair_home[:, key_width:].astype(bf16)
    all_low = jnp.concatenate([query_low, key_low, value_low], axis=1)
    gain_row = jnp.pad(
        jnp.concatenate([querygain_part, keygain_part])[None], ((0, 7), (0, model_width - 2 * head_dim))
    )
    small = jnp.concatenate(
        [gain_row, jnp.pad(second_grad[None], ((1, 6), (0, 0))), router_grad], axis=0
    )
    weight_rows, input_grad, small, mixing_rows = weight_grads(
        all_low,
        normed_cut.reshape(4 * token_count, planes * share_width).T,
        query_weight,
        key_weight,
        value_weight,
        layer_input.reshape(token_count, model_width),
        norm_first[None],
        residual_grad,
        small,
        mixing_part,
        planes,
        10,
    )
    mixing_grad = mixing_rows.T
    query_width = local_queries * head_dim
    query_grad = weight_rows[:, :query_width]
    key_grad = weight_rows[:, query_width : query_width + key_width]
    value_grad = weight_rows[:, query_width + key_width :]
    return (
        layer_output,
        input_grad.reshape(seq_count, seg_len, model_width),
        small[8],
        query_grad,
        key_grad,
        value_grad,
        mixing_grad,
        small[0, :head_dim],
        small[0, head_dim : 2 * head_dim],
        small[9],
        small[16:].T,
        gate_grad[None],
        up_grad[None],
        down_grad[None],
    )


def solution(mesh):
    chips = mesh.shape["expert"] == 16 and mesh.shape["tensor"] == 2
    return jax.shard_map(
        on_chips if chips else on_device,
        mesh=mesh,
        in_specs=(
            P(None, "expert", None),
            P(),
            P(None, "tensor"),
            P(None, "tensor"),
            P(None, "tensor"),
            P("tensor", None),
            P(),
            P(),
            P(),
            P(),
            P("expert", None, "tensor"),
            P("expert", None, "tensor"),
            P("expert", "tensor", None),
            P(None, "expert", None),
            P(None, "expert"),
            P(None, "expert", None),
        ),
        out_specs=(
            P(None, "expert", "tensor"),
            P(None, "expert", None),
            P(),
            P("expert", "tensor"),
            P("expert", "tensor"),
            P("expert", "tensor"),
            P("tensor", "expert"),
            P(),
            P(),
            P(),
            P(),
            P("expert", None, "tensor"),
            P("expert", None, "tensor"),
            P("expert", "tensor", None),
        ),
        check_vma=False,
    )
```

```python
import functools

import jax
import jax.numpy as jnp
from jax import lax
from jax.experimental import pallas as pl
from jax.experimental.pallas import tpu as pltpu
from jax.sharding import PartitionSpec as P

BLOCK = 256
MESH = pl.DeviceIdType.MESH
ROOM = 56 * 2**20


class Spot:
    def __init__(self):
        self.e = lax.axis_index("expert")
        self.t = lax.axis_index("tensor")
        self.a = lax.div(self.e, 4)
        y = lax.rem(lax.div(self.e, 2), 2)
        x = lax.rem(self.e, 2)
        self.b = x + self.t * (y - x)
        self.c = y + self.t * (x - y)

    def index(self, a, b, c):
        y = c + self.t * (b - c)
        x = b + self.t * (c - b)
        return a * 4 + y * 2 + x

    def at(self, a, b, c):
        return (self.index(a, b, c), self.t)

    def core(self):
        return (self.e, 1 - self.t)

    def greet(self, planes, chain, flat, share, far=False, corner=False):
        barrier = pltpu.get_barrier_semaphore()
        total = 0

        def call(who):
            pl.semaphore_signal(barrier, inc=1, device_id=who, device_id_type=MESH)

        if share:
            call(self.core())
            total = total + 1
        if flat:
            call(self.at(self.a, 1 - self.b, self.c))
            call(self.at(self.a, self.b, 1 - self.c))
            total = total + 2
        if corner:
            call(self.at(self.a, 1 - self.b, 1 - self.c))
            total = total + 1
        if far:
            for k in range(1, planes):
                call(self.at(lax.rem(self.a + k, planes), self.b, self.c))
            total = total + planes - 1
        elif chain:
            up = self.a + 1 < planes
            down = self.a > 0

            @pl.when(up)
            def _():
                call(self.at(self.a + 1, self.b, self.c))

            @pl.when(down)
            def _():
                call(self.at(self.a - 1, self.b, self.c))

            total = total + up.astype(jnp.int32) + down.astype(jnp.int32)
        pl.semaphore_wait(barrier, total)


def push(src, dst, send_sem, recv_sem, who):
    return pltpu.make_async_remote_copy(
        src_ref=src, dst_ref=dst, send_sem=send_sem, recv_sem=recv_sem, device_id=who, device_id_type=MESH
    )


def add_rows(target, parts):
    rows = target.shape[0]
    step = 32 if rows % 32 == 0 else 16

    def body(i, carry):
        at = pl.ds(pl.multiple_of(i * step, step), step)
        total = parts[0][at, :].astype(jnp.float32)
        for part in parts[1:]:
            total = total + part[at, :].astype(jnp.float32)
        target[at, :] = total.astype(target.dtype)
        return carry

    lax.fori_loop(0, rows // step, body, 0)


def far_first(a, planes, i):
    last = planes - 1
    low = jnp.where(i < last - a, last - i, jnp.where(i < last, i - (last - a), a))
    high = jnp.where(i < a, i, jnp.where(i < last, last - (i - a), a))
    return jnp.where(2 * a < last, low, high)


def swap_kernel(x_ref, o_ref, sems):
    me = Spot()
    me.greet(1, False, False, True)
    c = push(x_ref, o_ref, sems.at[0], sems.at[1], me.core())
    c.start()
    c.wait()


def swap_cores(x, cid, name):
    return pl.pallas_call(
        swap_kernel,
        out_shape=jax.ShapeDtypeStruct(x.shape, x.dtype),
        in_specs=[pl.BlockSpec(memory_space=pl.ANY)],
        out_specs=pl.BlockSpec(memory_space=pl.ANY),
        scratch_shapes=[pltpu.SemaphoreType.DMA((2,))],
        compiler_params=pltpu.CompilerParams(collective_id=cid, has_side_effects=True),
        name=name,
    )(x)


def over(first, second, contract):
    return lax.dot_general(first, second, (contract, ((), ())), preferred_element_type=jnp.float32)


NN = ((1,), (0,))
NT = ((1,), (1,))
TN = ((0,), (0,))


def experts_kernel(
    planes,
    parcel_ref,
    up_ref,
    gate_in,
    lift_in,
    down_in,
    context_ref,
    cut_ref,
    all_ref,
    other_ref,
    share_ref,
    home_ref,
    column_ref,
    cut_all,
    gate_sum,
    lift_sum,
    down_sum,
    wide,
    down,
    wide_half,
    down_half,
    pbuf,
    ubuf,
    xbuf,
    gbuf,
    vbuf,
    sbuf,
    wbuf,
    rbuf,
    hbuf,
    dbuf,
    gates,
    scores,
    stage,
    mine,
    outgoing,
    partner,
    landc,
    landb,
    landa,
    gsend,
    grecv,
    gcore,
    usend,
    urecv,
    wsend,
    wrecv,
    wload,
    hsend,
    hrecv,
    ssem,
    rsem,
    lsem,
    osem,
    esem,
    xsend,
    xrecv,
    csend,
    crecv,
):
    me = Spot()
    f32, bf16 = jnp.float32, jnp.bfloat16
    tokens, packed = parcel_ref.shape
    hidden, width = down_in.shape
    notes_width = packed - width
    count = planes * 4
    half = tokens // 2
    side = width // 2
    slots = sbuf.shape[2]
    own = me.index(me.a, me.b, me.c)
    ours = pl.ds(pl.multiple_of(me.t * half, half), half)
    theirs = pl.ds(pl.multiple_of((1 - me.t) * half, half), half)
    our_side = pl.ds(pl.multiple_of(me.t * side, side), side)
    their_side = pl.ds(pl.multiple_of((1 - me.t) * side, side), side)
    spots = [(sb, sc) for sc in (1 - me.c, me.c) for sb in (1 - me.b, me.b)]

    def near(i):
        return far_first(me.a, planes, planes - 1 - i)


    def carry(idx, kind, src=None):
        who = {
            0: me.at(me.a + 1, me.b, me.c),
            1: me.at(me.a - 1, me.b, me.c),
            2: me.at(me.a, 1 - me.b, me.c),
            3: me.at(me.a, me.b, 1 - me.c),
            4: me.core(),
        }[kind]
        there = all_ref.at[idx, ours]
        landed = gcore if kind == 4 else grecv
        return push(there if src is None else src, there, gsend.at[idx, kind], landed.at[idx], who)

    def relay_a(sa, act, first):
        idx = me.index(sa, me.b, me.c)
        src = parcel_ref.at[ours] if first else None
        if act and not first:
            carry(idx, 2).wait_recv()
        run = (lambda c: c.start()) if act else (lambda c: c.wait_send())

        @pl.when((sa <= me.a) & (me.a + 1 < planes))
        def _():
            run(carry(idx, 0, src))

        @pl.when((sa >= me.a) & (me.a > 0))
        def _():
            run(carry(idx, 1, src))

        run(carry(idx, 3, src))
        run(carry(idx, 2, src))
        if not first:
            run(carry(idx, 4))

    def relay_b(sa, act):
        idx = me.index(sa, 1 - me.b, me.c)
        run = (lambda c: c.start()) if act else (lambda c: c.wait_send())
        if act:
            carry(idx, 2).wait_recv()
        run(carry(idx, 3))
        run(carry(idx, 4))

    def across(sa, act):
        for sb in (me.b, 1 - me.b):
            idx = me.index(sa, sb, 1 - me.c)
            if act:
                carry(idx, 2).wait_recv()
                carry(idx, 4).start()
            else:
                carry(idx, 4).wait_send()

    def from_core(sa):
        for sb, sc in spots:
            idx = me.index(sa, sb, sc)

            @pl.when(idx != own)
            def _(idx=idx):
                there = all_ref.at[idx, theirs]
                push(there, there, gsend.at[idx, 4], gcore.at[idx], me.core()).wait_recv()

    def upstream(sa):
        group = pl.ds(sa * 4, 4)
        return push(up_ref.at[group], other_ref.at[group], usend.at[sa], urecv.at[sa], me.core())


    def part(ref, base, size):
        return ref.at[:, pl.ds(pl.multiple_of(base, 128), size)]

    down_rows = down_half.at[pl.ds(pl.multiple_of(me.t * hidden, 128), hidden)]
    wide_cols = [part(wide_half, me.t * 2 * hidden + i * hidden, hidden) for i in range(2)]
    sources = [gate_in, lift_in]
    loads = [pltpu.make_async_copy(sources[i], wide.at[:, i * hidden : (i + 1) * hidden], wload.at[i]) for i in range(2)]
    loads += [pltpu.make_async_copy(sources[i].at[our_side], wide_cols[i], wload.at[2 + i]) for i in range(2)]
    loads += [
        pltpu.make_async_copy(down_in, down, wload.at[4]),
        pltpu.make_async_copy(down_in.at[:, our_side], down_rows, wload.at[5]),
    ]
    pushes = [push(sources[i].at[their_side], wide_cols[i], wsend.at[i], wrecv.at[i], me.core()) for i in range(2)]
    pushes += [push(down_in.at[:, their_side], down_rows, wsend.at[2], wrecv.at[2], me.core())]


    def send_c(sa, sb):
        slot = sa * 2 + sb
        there = me.at(me.a, me.b, 1 - me.c)
        return push(outgoing.at[slot], landc.at[slot], ssem.at[0, slot], rsem.at[0, slot], there)

    def send_b(sa):
        src = mine.at[sa * 2 + 1 - me.b]
        return push(src, landb.at[sa], ssem.at[1, sa], rsem.at[1, sa], me.at(me.a, 1 - me.b, me.c))

    def send_a(sa):
        src = mine.at[sa * 2 + me.b]
        return push(src, landa.at[me.a], ssem.at[2, sa], rsem.at[2, me.a], me.at(sa, me.b, me.c))

    def from_c(sa):
        for sb in (1 - me.b, me.b):
            slot = sa * 2 + sb
            push(landc.at[slot], landc.at[slot], ssem.at[0, slot], rsem.at[0, slot], me.at(me.a, me.b, 1 - me.c)).wait_recv()
            for n in range(0, mine.shape[2], 384):
                cut = slice(n, n + 384)
                spread = over(partner[slot], landc[slot, :, cut], NN)
                mine[slot, :, cut] = (mine[slot, :, cut].astype(f32) + spread).astype(bf16)
            if sb is not me.b:
                send_b(sa).start()

    def from_b(sa):
        push(landb.at[sa], landb.at[sa], ssem.at[1, sa], rsem.at[1, sa], me.at(me.a, 1 - me.b, me.c)).wait_recv()
        return [mine.at[sa * 2 + me.b], landb.at[sa]]

    def along(sa):
        parts = from_b(sa)
        add_rows(parts[0], parts)
        send_a(sa).start()

    def finish():
        parts = from_b(me.a)
        for k in range(1, planes):
            far = lax.rem(me.a + k, planes)
            push(landa.at[far], landa.at[far], ssem.at[2, far], rsem.at[2, far], me.at(far, me.b, me.c)).wait_recv()
            parts = parts + [landa.at[far]]
        add_rows(home_ref.at[me.t], parts)


    def context_to(source, up, own_rows):
        there = column_ref.at[source]
        who = me.at(me.a + 1 if up else me.a - 1, me.b, me.c)
        return push(context_ref if own_rows else there, there, xsend.at[source, int(up)], xrecv.at[source], who)

    def context_pass(i, act):
        for up in (True, False):
            source = me.a - i if up else me.a + i
            further = me.a + 1 < planes if up else me.a > 0
            run = (lambda c: c.start()) if act else (lambda c: c.wait_send())

            @pl.when((source >= 0) & (source < planes))
            def _(source=source, up=up, further=further, run=run):
                if act and i > 0:
                    context_to(source, up, False).wait_recv()

                @pl.when(further)
                def _():
                    run(context_to(source, up, i == 0))

    place = lax.rem(me.e, 4)
    peers = [me.index(0, b, c) for b, c in ((1 - me.b, me.c), (me.b, 1 - me.c), (1 - me.b, 1 - me.c))]

    def cut_to(i):
        there = (me.e - place + peers[i], me.t)
        return push(cut_ref.at[peers[i]], cut_all.at[place], csend.at[i], crecv.at[i], there)


    def load_rows(sa, q):
        return pltpu.make_async_copy(all_ref.at[sa * 4 + q], pbuf.at[q], lsem.at[q])

    def fetch_rows(sa):
        from_core(sa)
        for q in range(4):
            mine_here = sa * 4 + q == own

            @pl.when(mine_here)
            def _(q=q):
                pltpu.make_async_copy(parcel_ref, pbuf.at[q], lsem.at[q]).start()

            @pl.when(jnp.logical_not(mine_here))
            def _(q=q):
                load_rows(sa, q).start()

    def load_up(sa):
        group = pl.ds(sa * 4, 4)
        return [
            pltpu.make_async_copy(up_ref.at[group], ubuf.at[:, ours], lsem.at[4]),
            pltpu.make_async_copy(other_ref.at[group], ubuf.at[:, theirs], lsem.at[5]),
        ]

    def fetch_up(sa):
        there = other_ref.at[pl.ds(sa * 4, 4)]
        push(there, there, usend.at[sa], urecv.at[sa], me.core()).wait_recv()
        for k in load_up(sa):
            k.start()

    def lanes(rows):
        return lax.broadcasted_iota(jnp.int32, (rows, notes_width), 1)

    def side_of(q):
        y, x = lax.div(q, 2), lax.rem(q, 2)
        return x + me.t * (y - x), y + me.t * (x - y)

    def chosen_by(expert, notes):
        slot_of = jnp.sum(jnp.where(lanes(tokens) == expert, notes, 0.0), axis=1, keepdims=True)
        chosen = slot_of == lax.broadcasted_iota(jnp.int32, (tokens, slots), 1).astype(f32)
        return jnp.where(chosen, 1.0, 0.0).astype(bf16)

    def pick_rows(q, carried):
        sa, slot = carried
        load_rows(sa, q).wait()
        notes = pbuf[q, :, width:].astype(f32)
        sb, sc = side_of(q)

        @pl.when(sc == me.c)
        def _():
            partner[sa * 2 + sb] = chosen_by(me.index(me.a, me.b, 1 - me.c), notes)

        chosen = chosen_by(me.e, notes)
        sbuf[q] = chosen
        pick = jnp.transpose(chosen.astype(f32)).astype(bf16)
        at = pl.ds(pl.multiple_of(q * slots, slots), slots)
        there = over(pick, pbuf[q, :, width:], NN)
        mark = lanes(slots)
        gate = jnp.sum(jnp.where((mark == count + me.e) | (mark == 2 * count + me.e), there, 0.0), axis=1, keepdims=True)
        gates[at, :] = jnp.broadcast_to(gate, (slots, 128))
        for n in range(0, width, 512):
            cut = slice(n, n + 512)
            xbuf[at, cut] = over(pick, pbuf[q, :, cut], NN).astype(bf16)
            picked = over(pick, ubuf[q, :, cut], NN)
            gbuf[at, cut] = (picked * gate).astype(bf16)
        for n in range(0, side, 512):
            cut = pl.ds(pl.multiple_of(me.t * side + n, 512), 512)
            vbuf[at, n : n + 512] = over(pick, ubuf[q, :, cut], NN).astype(bf16)
        return carried

    def hidden_cols(p):
        return pl.ds(pl.multiple_of(p * hidden, 128), hidden)

    def both_cols(p):
        return pl.ds(pl.multiple_of(p * 2 * hidden, 128), 2 * hidden)

    def hidden_rows(r, slot):
        at = pl.ds(pl.multiple_of(r * 256, 256), 256)
        acts = over(xbuf[at, :], wide[...], NN)
        gate_act, up_act = acts[:, :hidden], acts[:, hidden:]
        sig = 1.0 / (1.0 + jnp.exp(-gate_act))
        silu = gate_act * sig
        hbuf[slot, at, hidden_cols(me.t)] = (silu * up_act).astype(bf16)
        back = over(gbuf[at, :], down[...], NT)
        gate_d = (back * up_act * (sig * (1.0 + gate_act * (1.0 - sig)))).astype(bf16)
        dbuf[slot, at, pl.ds(pl.multiple_of(me.t * 2 * hidden, 128), hidden)] = gate_d
        dbuf[slot, at, pl.ds(pl.multiple_of(me.t * 2 * hidden + hidden, 128), hidden)] = (back * silu).astype(bf16)
        return slot

    def trades(slot):
        h_part = hbuf.at[slot, :, hidden_cols(me.t)]
        d_part = dbuf.at[slot, :, both_cols(me.t)]
        return [
            push(h_part, h_part, hsend.at[0], hrecv.at[slot, 0], me.core()),
            push(d_part, d_part, hsend.at[1], hrecv.at[slot, 1], me.core()),
        ]

    def traded(slot):
        h_part = hbuf.at[slot, :, hidden_cols(1 - me.t)]
        d_part = dbuf.at[slot, :, both_cols(1 - me.t)]
        push(h_part, h_part, hsend.at[0], hrecv.at[slot, 0], me.core()).wait_recv()
        push(d_part, d_part, hsend.at[1], hrecv.at[slot, 1], me.core()).wait_recv()

    def weight_sums(n, slot):
        cut = pl.ds(pl.multiple_of(n * 512, 512), 512)
        own_d = dbuf[slot, :, both_cols(me.t)]
        rows = xbuf[:, cut]
        gate_sum[cut, :] += over(rows, own_d[:, :hidden], TN)
        lift_sum[cut, :] += over(rows, own_d[:, hidden:], TN)
        down_sum[:, cut] += over(hbuf[slot, :, hidden_cols(me.t)], gbuf[:, cut], TN)
        return slot

    def out_rows(n, slot):
        cut = pl.ds(pl.multiple_of(n * 512, 512), 512)
        for r in range(0, 4 * slots, 256):
            at = slice(r, r + 256)
            out = over(hbuf[slot, at, :], down_half[:, cut], NN)
            wbuf[at, cut] = (out * gates[at, :1]).astype(bf16)
            total = jnp.sum(out * vbuf[at, cut].astype(f32), axis=1, keepdims=True)
            scores[at, :] += jnp.broadcast_to(total, (256, 128))
            rbuf[at, cut] = over(dbuf[slot, at, :], wide_half[cut, :], NT).astype(bf16)
        return slot

    def note_scores():
        mark = lanes(4 * slots)
        total = scores[...]
        high = total.astype(bf16).astype(f32)
        row = jnp.where(mark == me.e, high, jnp.where(mark == me.e + count, total - high, 0.0))
        rbuf[:, side:] = row.astype(bf16)

    def store(sa, q):
        sb, sc = side_of(q)
        there = share_ref.at[sc * 2 * planes + sa * 2 + sb]
        return pltpu.make_async_copy(stage.at[lax.rem(q, 2)], there, osem.at[lax.rem(q, 2)])

    def spread_rows(q, sa):
        at = pl.ds(pl.multiple_of(q * slots, slots), slots)

        @pl.when((q >= 2) | (sa != near(1)))
        def _():
            store(sa, q).wait()

        for n in range(0, side, 512):
            cut = slice(n, n + 512)
            stage[lax.rem(q, 2), :, cut] = over(sbuf[q], wbuf[at, cut], NN).astype(bf16)
        sb, sc = side_of(q)
        slot = sa * 2 + sb

        @pl.when(sc == me.c)
        def _():
            for n in range(0, mine.shape[2], 384):
                cut = slice(n, n + 384)
                mine[slot, :, cut] = over(sbuf[q], rbuf[at, cut], NN).astype(bf16)

        @pl.when(sc != me.c)
        def _():
            outgoing[slot] = rbuf[at, :]
            send_c(sa, sb).start()

        store(sa, q).start()
        return sa

    me.greet(planes, True, True, True, True, True)
    relay_a(me.a, True, True)
    for i in range(planes):
        upstream(near(i)).start()
    for k in loads + pushes:
        k.start()
    gate_sum[...] = jnp.zeros_like(gate_sum)
    lift_sum[...] = jnp.zeros_like(lift_sum)
    down_sum[...] = jnp.zeros_like(down_sum)
    fetch_up(near(1))
    relay_b(me.a, True)
    relay_a(near(1), True, False)
    across(me.a, True)
    for i in range(2, planes):
        relay_a(near(i), True, False)
        if i == planes - 1:
            context_pass(0, True)
        relay_b(near(i - 1), True)
    across(near(1), True)
    fetch_rows(near(1))
    for k in loads + pushes:
        k.wait()

    def step(i, c):
        last = i == planes - 1
        sa = jnp.where(last, me.a, near(i + 1))
        after = jnp.where(i + 2 < planes, near(i + 2), me.a)
        slot = lax.rem(i, 2)
        for k in load_up(sa):
            k.wait()
        scores[...] = jnp.zeros_like(scores)
        lax.fori_loop(0, 4, pick_rows, (sa, slot))

        @pl.when(i + 1 < planes)
        def _():
            fetch_up(after)

        @pl.when(i > 0)
        def _():
            for k in trades(slot):
                k.wait_send()

        lax.fori_loop(0, 4 * slots // 256, hidden_rows, slot)
        for k in trades(slot):
            k.start()

        @pl.when(i == 0)
        def _():
            relay_b(near(planes - 1), True)
            for k in range(3):
                cut_to(k).start()

        for k in range(1, planes):

            @pl.when(i == k - 1)
            def _(k=k):
                context_pass(k, True)

        @pl.when(i > 0)
        def _():
            from_c(near(i))

        traded(slot)
        lax.fori_loop(0, side // 512, out_rows, slot)
        note_scores()
        lax.fori_loop(0, 4, spread_rows, sa)

        @pl.when(i + 2 < planes)
        def _():
            across(after, True)

        @pl.when(jnp.logical_not(last))
        def _():
            fetch_rows(after)

        lax.fori_loop(0, width // 512, weight_sums, slot)

        @pl.when(i > 0)
        def _():
            along(near(i))

        return c

    lax.fori_loop(0, planes, step, 0)
    from_c(me.a)
    finish()
    store(me.a, 0).wait()
    store(me.a, 1).wait()
    done = push(home_ref.at[me.t], home_ref.at[me.t], esem.at[0], esem.at[1], me.core())
    done.start()

    relay_a(me.a, False, True)

    def settle(i, c):
        sa = near(i)
        relay_b(sa, False)

        @pl.when(i > 0)
        def _():
            relay_a(sa, False, False)
            send_a(sa).wait_send()

        across(sa, False)
        for sb in (1 - me.b, me.b):
            send_c(sa, sb).wait_send()
        send_b(sa).wait_send()
        upstream(sa).wait_send()
        return c

    lax.fori_loop(0, planes, settle, 0)
    for k in trades(0):
        k.wait_send()
    for k in range(planes):
        context_pass(k, False)
    for k in range(3):
        cut_to(k).wait()
    done.wait_send()
    other = home_ref.at[1 - me.t]
    push(other, other, esem.at[0], esem.at[1], me.core()).wait_recv()


def run_experts(parcel, upstream, gate, lift_w, down, context, cut, planes, slots, cid):
    f32, bf16 = jnp.float32, jnp.bfloat16
    tokens, packed = parcel.shape
    hidden, width = down.shape
    count = planes * 4
    half = tokens // 2
    side = width // 2
    block = side + packed - width
    rows = 4 * slots
    anywhere = pl.BlockSpec(memory_space=pl.ANY)
    inside = pl.BlockSpec(memory_space=pltpu.VMEM)
    return pl.pallas_call(
        functools.partial(experts_kernel, planes),
        out_shape=[
            jax.ShapeDtypeStruct((count, tokens, packed), bf16),
            jax.ShapeDtypeStruct((count, half, width), bf16),
            jax.ShapeDtypeStruct((count, tokens, side), bf16),
            jax.ShapeDtypeStruct((2, tokens, block), bf16),
            jax.ShapeDtypeStruct((planes,) + context.shape, bf16),
            jax.ShapeDtypeStruct(cut.shape, bf16),
            jax.ShapeDtypeStruct((width, hidden), f32),
            jax.ShapeDtypeStruct((width, hidden), f32),
            jax.ShapeDtypeStruct((hidden, width), f32),
        ],
        in_specs=[anywhere] * 7,
        out_specs=[anywhere] * 3 + [inside, anywhere, anywhere] + [inside] * 3,
        scratch_shapes=[
            pltpu.VMEM((width, 2 * hidden), bf16),
            pltpu.VMEM((hidden, width), bf16),
            pltpu.VMEM((side, 4 * hidden), bf16),
            pltpu.VMEM((2 * hidden, side), bf16),
            pltpu.VMEM((4, tokens, packed), bf16),
            pltpu.VMEM((4, tokens, width), bf16),
            pltpu.VMEM((rows, width), bf16),
            pltpu.VMEM((rows, width), bf16),
            pltpu.VMEM((rows, side), bf16),
            pltpu.VMEM((4, tokens, slots), bf16),
            pltpu.VMEM((rows, side), bf16),
            pltpu.VMEM((rows, block), bf16),
            pltpu.VMEM((2, rows, 2 * hidden), bf16),
            pltpu.VMEM((2, rows, 4 * hidden), bf16),
            pltpu.VMEM((rows, 128), f32),
            pltpu.VMEM((rows, 128), f32),
            pltpu.VMEM((2, tokens, side), bf16),
            pltpu.VMEM((2 * planes, tokens, block), bf16),
            pltpu.VMEM((2 * planes, slots, block), bf16),
            pltpu.VMEM((2 * planes, tokens, slots), bf16),
            pltpu.VMEM((2 * planes, slots, block), bf16),
            pltpu.VMEM((planes, tokens, block), bf16),
            pltpu.VMEM((planes, tokens, block), bf16),
            pltpu.SemaphoreType.DMA((count, 5)),
            pltpu.SemaphoreType.DMA((count,)),
            pltpu.SemaphoreType.DMA((count,)),
            pltpu.SemaphoreType.DMA((planes,)),
            pltpu.SemaphoreType.DMA((planes,)),
            pltpu.SemaphoreType.DMA((3,)),
            pltpu.SemaphoreType.DMA((3,)),
            pltpu.SemaphoreType.DMA((6,)),
            pltpu.SemaphoreType.DMA((2,)),
            pltpu.SemaphoreType.DMA((2, 2)),
            pltpu.SemaphoreType.DMA((3, 2 * planes)),
            pltpu.SemaphoreType.DMA((3, 2 * planes)),
            pltpu.SemaphoreType.DMA((7,)),
            pltpu.SemaphoreType.DMA((2,)),
            pltpu.SemaphoreType.DMA((2,)),
            pltpu.SemaphoreType.DMA((planes, 2)),
            pltpu.SemaphoreType.DMA((planes,)),
            pltpu.SemaphoreType.DMA((3,)),
            pltpu.SemaphoreType.DMA((3,)),
        ],
        compiler_params=pltpu.CompilerParams(
            collective_id=cid, has_side_effects=True, vmem_limit_bytes=62 * 2**20
        ),
        name="experts",
    )(parcel, upstream, gate, lift_w, down, context, cut)


def stack_heads(target, source, group):
    items, rows, size = target.shape
    seg = rows // group
    keys = source.shape[1] // (group * size)
    for s in range(items // keys):
        for k in range(keys):
            for h in range(group):
                at = (k * group + h) * size
                part = source[s * seg : (s + 1) * seg, at : at + size]
                target[s * keys + k, h * seg : (h + 1) * seg, :] = part.astype(target.dtype)


def spread_heads(target, item, value, group, keys):
    rows, size = value.shape
    seg = rows // group
    s, k = item // keys, item % keys
    for h in range(group):
        at = (k * group + h) * size
        target[s * seg : (s + 1) * seg, at : at + size] = value[h * seg : (h + 1) * seg, :].astype(target.dtype)


def block_heads(ref, plane, item, keys, size, part):
    seg = BLOCK // 4
    s, k = lax.div(item, keys), lax.rem(item, keys)
    rows = pl.ds(pl.multiple_of(s * seg, seg), seg)
    cols = pl.ds(pl.multiple_of((part * keys + k) * size, size), size)
    return [ref.at[plane * 4 + q, rows, cols] for q in range(4)]


def joined(refs):
    return jnp.concatenate([ref[...] for ref in refs], axis=0)


def attend_kernel(
    planes, group, q_ref, x_ref, context_ref, all_ref, log_ref, qs, top, total, acc, ssem, rsem
):
    me = Spot()
    f32, bf16 = jnp.float32, jnp.bfloat16
    items, rows, size = qs.shape
    keys = x_ref.shape[1] // (2 * size)
    factor = size ** (-0.5)
    own = me.index(me.a, me.b, me.c)

    def carry(idx, kind, src=None):
        who = {
            0: me.at(me.a + 1, me.b, me.c),
            2: me.at(me.a, 1 - me.b, me.c),
            3: me.at(me.a, me.b, 1 - me.c),
        }[kind]
        there = all_ref.at[idx]
        return push(there if src is None else src, there, ssem.at[idx, kind], rsem.at[idx], who)

    def relay(sa, act, first):
        idx = me.index(sa, me.b, me.c)
        src = x_ref if first else None
        if act and not first:
            carry(idx, 2).wait_recv()
        run = (lambda c: c.start()) if act else (lambda c: c.wait_send())

        @pl.when(me.a + 1 < planes)
        def _():
            run(carry(idx, 0, src))

        run(carry(idx, 3, src))
        run(carry(idx, 2, src))
        idx = me.index(sa, 1 - me.b, me.c)
        if act:
            carry(idx, 2).wait_recv()
        run(carry(idx, 3))

    def block(item, sa):
        scores = over(qs[item], joined(block_heads(all_ref, sa, item, keys, size, 0)), NT) * factor
        values = joined(block_heads(all_ref, sa, item, keys, size, 1))
        before = top[item]
        high = jnp.maximum(before, jnp.broadcast_to(jnp.max(scores, axis=1, keepdims=True), before.shape))
        shrink = jnp.exp(before - high)
        terms = jnp.exp(scores - high[:, :1])
        top[item] = high
        total[item] = total[item] * shrink + jnp.broadcast_to(jnp.sum(terms, axis=1, keepdims=True), before.shape)
        acc[item] = acc[item] * shrink + over(terms.astype(bf16), values, NN)
        return sa

    me.greet(planes, True, True, False)
    relay(me.a, True, True)
    all_ref[own] = x_ref[...]

    @pl.when(me.a > 0)
    def _():
        relay(me.a - 1, True, False)

    stack_heads(qs, q_ref, group)
    top[...] = jnp.full(top.shape, far_below, f32)
    total[...] = jnp.zeros_like(total)
    acc[...] = jnp.zeros_like(acc)

    def step(i, c):
        sa = me.a - i

        @pl.when(sa > 1)
        def _():
            relay(sa - 2, True, False)

        for sb in (me.b, 1 - me.b):
            carry(me.index(sa, sb, 1 - me.c), 2).wait_recv()
        lax.fori_loop(0, items, block, sa)
        return c

    lax.fori_loop(0, me.a + 1, step, 0)
    for item in range(items):
        spread_heads(context_ref, item, acc[item] / total[item], group, keys)
    log_ref[...] = top[...] + jnp.log(total[...])
    relay(me.a, False, True)

    def settle(i, c):
        relay(me.a - i, False, False)
        return c

    lax.fori_loop(1, me.a + 1, settle, 0)


def attend(query, pairs, planes, group, size, cid):
    f32, bf16 = jnp.float32, jnp.bfloat16
    tokens, width = query.shape
    count = planes * 4
    items = (tokens * 4 // BLOCK) * (width // (group * size))
    state = (items, group * BLOCK // 4, size)
    inside = pl.BlockSpec(memory_space=pltpu.VMEM)
    return pl.pallas_call(
        functools.partial(attend_kernel, planes, group),
        out_shape=[
            jax.ShapeDtypeStruct((tokens, width), bf16),
            jax.ShapeDtypeStruct((count,) + pairs.shape, bf16),
            jax.ShapeDtypeStruct(state, f32),
        ],
        in_specs=[inside] * 2,
        out_specs=[inside] * 3,
        scratch_shapes=[
            pltpu.VMEM(state, bf16),
            pltpu.VMEM(state, f32),
            pltpu.VMEM(state, f32),
            pltpu.VMEM(state, f32),
            pltpu.SemaphoreType.DMA((count, 4)),
            pltpu.SemaphoreType.DMA((count,)),
        ],
        compiler_params=pltpu.CompilerParams(collective_id=cid, has_side_effects=True, vmem_limit_bytes=ROOM),
        name="attend",
    )(query, pairs)


def attend_back_kernel(
    planes,
    group,
    q_ref,
    g_ref,
    o_ref,
    all_ref,
    log_ref,
    cut_ref,
    column_ref,
    query_raw,
    key_raw,
    gain_ref,
    turn_ref,
    low_ref,
    gain_grad,
    mixing_ref,
    pair_grad,
    cut_all,
    column,
    qs,
    gs,
    delta,
    qacc,
    mine,
    landc,
    landb,
    landa,
    ssem,
    rsem,
    psend,
    precv,
    lsem,
):
    me = Spot()
    f32, bf16 = jnp.float32, jnp.bfloat16
    items, rows, size = qs.shape
    keys = all_ref.shape[2] // (2 * size)
    factor = size ** (-0.5)
    me.greet(planes, False, True, False, True)

    def cut_to(k):
        far = lax.rem(me.a + k, planes)
        return push(cut_ref.at[far], cut_all.at[me.a], psend.at[k], precv.at[me.a], me.at(far, me.b, me.c))

    def cut_from(k):
        far = lax.rem(me.a + k, planes)
        there = cut_all.at[far]
        push(there, there, psend.at[k], precv.at[far], me.at(far, me.b, me.c)).wait_recv()

    for k in range(1, planes):
        cut_to(k).start()
    keep = pltpu.make_async_copy(cut_ref.at[me.a], cut_all.at[me.a], lsem.at[0])
    keep.start()

    def column_in(k):
        far = lax.rem(me.a + k, planes)
        return pltpu.make_async_copy(column_ref.at[far], column.at[far], lsem.at[k])

    for k in range(1, planes):
        column_in(k).start()
    column[me.a] = o_ref[...]
    stack_heads(qs, q_ref, group)
    stack_heads(gs, g_ref, group)
    stack_heads(qacc, o_ref, group)

    def prepare(item, c):
        part = jnp.sum(gs[item].astype(f32) * qacc[item], axis=1, keepdims=True)
        delta[item] = jnp.broadcast_to(part, delta.shape[1:])
        qacc[item] = jnp.zeros(qacc.shape[1:], f32)
        return c

    lax.fori_loop(0, items, prepare, 0)

    def block(item, sa):
        keys_here = joined(block_heads(all_ref, sa, item, keys, size, 0))
        values = joined(block_heads(all_ref, sa, item, keys, size, 1))
        queries, grads = qs[item], gs[item]
        scores = over(queries, keys_here, NT) * factor
        probs = jnp.exp(scores - log_ref[item][:, :1])
        prob_grads = over(grads, values, NT)
        score_grads = (probs * (prob_grads - delta[item][:, :1])).astype(bf16)
        qacc[item] += over(score_grads, keys_here, NN)
        key_part = (over(score_grads, queries, TN) * factor).astype(bf16)
        value_part = over(probs.astype(bf16), grads, TN).astype(bf16)
        seg = key_part.shape[0] // 4
        for part, value in ((0, key_part), (1, value_part)):
            for q, ref in enumerate(block_heads(mine, sa, item, keys, size, part)):
                ref[...] = value[q * seg : (q + 1) * seg, :]
        return sa

    def send_c(sa, sb):
        slot = sa * 2 + sb
        src = mine.at[me.index(sa, sb, 1 - me.c)]
        return push(src, landc.at[slot], ssem.at[0, slot], rsem.at[0, slot], me.at(me.a, me.b, 1 - me.c))

    def send_b(sa):
        src = mine.at[me.index(sa, 1 - me.b, me.c)]
        return push(src, landb.at[sa], ssem.at[1, sa], rsem.at[1, sa], me.at(me.a, 1 - me.b, me.c))

    def send_a(sa):
        src = mine.at[me.index(sa, me.b, me.c)]
        return push(src, landa.at[me.a], ssem.at[2, sa], rsem.at[2, me.a], me.at(sa, me.b, me.c))

    def from_c(sa):
        for sb in (1 - me.b, me.b):
            slot = sa * 2 + sb
            push(landc.at[slot], landc.at[slot], ssem.at[0, slot], rsem.at[0, slot], me.at(me.a, me.b, 1 - me.c)).wait_recv()
            idx = me.index(sa, sb, me.c)
            add_rows(mine.at[idx], [mine.at[idx], landc.at[slot]])
            if sb is not me.b:
                send_b(sa).start()

    def from_b(sa):
        push(landb.at[sa], landb.at[sa], ssem.at[1, sa], rsem.at[1, sa], me.at(me.a, 1 - me.b, me.c)).wait_recv()
        idx = me.index(sa, me.b, me.c)
        return mine.at[idx], [mine.at[idx], landb.at[sa]]

    def along(sa):
        target, parts = from_b(sa)
        add_rows(target, parts)
        send_a(sa).start()

    def finish():
        target, parts = from_b(me.a)
        add_rows(pair_grad, parts)
        for far in range(1, planes):

            @pl.when(far > me.a)
            def _(far=far):
                push(landa.at[far], landa.at[far], ssem.at[2, far], rsem.at[2, far], me.at(far, me.b, me.c)).wait_recv()
                add_rows(pair_grad, [pair_grad, landa.at[far]])

    def mix():
        share = mixing_ref.shape[1]
        keep.wait()
        for k in range(1, planes):
            cut_from(k)
            column_in(k).wait()
        tokens = column.shape[0] * column.shape[1]
        for n in range(0, column.shape[2], 512):
            rows = column[:, :, n : n + 512].reshape(tokens, 512)
            part = over(cut_all[...].reshape(tokens, 4 * share), rows, TN).astype(bf16)
            for q in range(4):
                mixing_ref[q, :, n : n + 512] = part[q * share : (q + 1) * share]

    def step(sa, c):
        lax.fori_loop(0, items, block, sa)
        for sb in (1 - me.b, me.b):
            send_c(sa, sb).start()

        @pl.when(sa >= 1)
        def _():
            from_c(sa - 1)

        @pl.when(sa >= 2)
        def _():
            along(sa - 2)

        return c

    lax.fori_loop(0, me.a + 1, step, 0)
    mix()

    def unturned(grads, raw, gain):
        turned = grads * turn_ref[0] + pltpu.roll(grads, size // 2, 1) * turn_ref[1]
        scale = lax.rsqrt(jnp.mean(raw * raw, axis=1, keepdims=True) + epsilon)
        scaled = gain * turned
        level = jnp.mean(scaled * raw, axis=1, keepdims=True)
        return scale * scaled - raw * (scale * scale * scale * level), jnp.sum(turned * raw * scale, axis=0, keepdims=True)

    seg = rows // group
    gain_grad[...] = jnp.zeros_like(gain_grad)

    def query_item(item, c):
        at = pl.ds(pl.multiple_of(lax.div(item, keys) * seg, seg), seg)
        total = jnp.zeros((1, size), f32)
        for h in range(group):
            cols = pl.ds(pl.multiple_of((lax.rem(item, keys) * group + h) * size, size), size)
            grads = qacc[item, h * seg : (h + 1) * seg, :] * factor
            value, part = unturned(grads, query_raw[at, cols], gain_ref[0:1, :])
            low_ref[at, cols] = value.astype(bf16)
            total = total + part
        gain_grad[0:1, :] += total
        return c

    lax.fori_loop(0, items, query_item, 0)
    from_c(me.a)

    @pl.when(me.a > 0)
    def _():
        along(me.a - 1)

    finish()
    width = query_raw.shape[1]
    for item in range(items):
        s, k = item // keys, item % keys
        at = slice(s * seg, (s + 1) * seg)
        cols = slice(k * size, (k + 1) * size)
        value, part = unturned(pair_grad[at, cols], key_raw[at, cols], gain_ref[1:2, :])
        low_ref[at, width + k * size : width + (k + 1) * size] = value.astype(bf16)
        gain_grad[1:2, :] += part
    low_ref[:, width + keys * size :] = pair_grad[:, keys * size :].astype(bf16)

    def settle(sa, c):
        for sb in (1 - me.b, me.b):
            send_c(sa, sb).wait_send()
        send_b(sa).wait_send()

        @pl.when(sa < me.a)
        def _():
            send_a(sa).wait_send()

        return c

    lax.fori_loop(0, me.a + 1, settle, 0)
    for k in range(1, planes):
        cut_to(k).wait_send()


def attend_back(query, grads, context, pairs_all, logs, cut, column, raws, gains, turns, planes, group, size, cid):
    f32, bf16 = jnp.float32, jnp.bfloat16
    tokens, width = query.shape
    items = logs.shape[0]
    state = logs.shape
    block = pairs_all.shape[1:]
    share = cut.shape[2] // 4
    inside = pl.BlockSpec(memory_space=pltpu.VMEM)
    anywhere = pl.BlockSpec(memory_space=pl.ANY)
    return pl.pallas_call(
        functools.partial(attend_back_kernel, planes, group),
        out_shape=[
            jax.ShapeDtypeStruct((tokens, width + block[1]), bf16),
            jax.ShapeDtypeStruct((8, size), f32),
            jax.ShapeDtypeStruct((4, share, width), bf16),
        ],
        in_specs=[inside] * 5 + [anywhere] * 2 + [inside] * 4,
        out_specs=[inside] * 3,
        scratch_shapes=[
            pltpu.VMEM(block, f32),
            pltpu.VMEM(cut.shape, bf16),
            pltpu.VMEM(column.shape, bf16),
            pltpu.VMEM(state, bf16),
            pltpu.VMEM(state, bf16),
            pltpu.VMEM(state, f32),
            pltpu.VMEM(state, f32),
            pltpu.VMEM((4 * planes,) + block, bf16),
            pltpu.VMEM((2 * planes,) + block, bf16),
            pltpu.VMEM((planes,) + block, bf16),
            pltpu.VMEM((planes,) + block, bf16),
            pltpu.SemaphoreType.DMA((3, 2 * planes)),
            pltpu.SemaphoreType.DMA((3, 2 * planes)),
            pltpu.SemaphoreType.DMA((planes,)),
            pltpu.SemaphoreType.DMA((planes,)),
            pltpu.SemaphoreType.DMA((planes,)),
        ],
        compiler_params=pltpu.CompilerParams(collective_id=cid, has_side_effects=True, vmem_limit_bytes=ROOM),
        name="attend_back",
    )(query, grads, context, pairs_all, logs, cut, column, raws[0], raws[1], gains, turns)


def weights_kernel(
    planes,
    chunk,
    low_ref,
    cut_ref,
    query_w,
    key_w,
    value_w,
    input_ref,
    gain_ref,
    grad_ref,
    small_ref,
    mixing_part,
    rows_ref,
    input_grad,
    total_ref,
    mixing_rows,
    low_all,
    mixed,
    mixc,
    mixb,
    weights,
    sums,
    landz,
    normed,
    normed_other,
    gains_other,
    send,
    land,
    wload,
    lsend,
    lrecv,
    msend,
    mrecv,
    mload,
    zsend,
    zrecv,
    nsend,
    nrecv,
    tsend,
    trecv,
):
    me = Spot()
    f32, bf16 = jnp.float32, jnp.bfloat16
    tokens, packed = low_ref.shape
    width = input_ref.shape[1]
    chunks = packed // chunk
    assert chunks == 10
    place = lax.rem(me.e, 4)
    base = me.e - place
    share = sums.shape[1] // planes

    def spot(b, c):
        return me.index(0, b, c)

    near = [(1 - me.b, me.c), (me.b, 1 - me.c), (1 - me.b, 1 - me.c)]
    peers = [(base + spot(b, c), me.t) for b, c in near]
    barrier = pltpu.get_barrier_semaphore()
    for who in peers + [me.core()] + [me.at(lax.rem(me.a + k, planes), me.b, me.c) for k in range(1, planes)]:
        pl.semaphore_signal(barrier, inc=1, device_id=who, device_id_type=MESH)
    pl.semaphore_wait(barrier, 3 + planes)

    def cols(k):
        return pl.ds(pl.multiple_of(k * chunk, chunk), chunk)

    def whole(i, k):
        return push(low_ref.at[:, cols(k)], low_all.at[place, :, cols(k)], lsend.at[i, k], lrecv.at[i, k], peers[i])

    first = spot(*near[0])

    def relay(k):
        there = low_all.at[first, :, cols(k)]
        return push(there, there, lsend.at[2, k], lrecv.at[2, k], peers[1])

    quarters = [spot(b, c) for b, c in ((1 - me.b, 1 - me.c), (me.b, 1 - me.c), (1 - me.b, me.c), (me.b, me.c))]

    def mix_c(i):
        return push(mixing_part.at[quarters[i]], mixc.at[i], msend.at[i], mrecv.at[i], peers[1])

    def mix_b():
        return push(mixed.at[0], mixb, msend.at[2], mrecv.at[2], peers[0])

    mix_loads = [pltpu.make_async_copy(mixing_part.at[quarters[2 + i]], mixed.at[i], mload.at[i]) for i in range(2)]

    def mix_round(k):
        if k == chunks - 2:
            for i in range(2):
                mix_c(i).start()
        if k == chunks:
            for i in range(2):
                mix_loads[i].wait()
                mix_c(i).wait_recv()
                add_rows(mixed.at[i], [mixed.at[i], mixc.at[i]])
                if i == 0:
                    mix_b().start()
        if k == chunks + 1:
            mix_b().wait_recv()
            add_rows(mixing_rows, [mixed.at[1], mixb])

    def send_low(k, c):
        whole(0, k).start()
        return c

    lax.fori_loop(0, chunks, send_low, 0)
    whole(1, 0).start()
    whole(1, 1).start()
    for k in mix_loads:
        k.start()
    query_width, key_width = query_w.shape[1], key_w.shape[1]
    loads = [
        pltpu.make_async_copy(query_w, weights.at[:, :query_width], wload.at[0]),
        pltpu.make_async_copy(key_w, weights.at[:, query_width : query_width + key_width], wload.at[1]),
        pltpu.make_async_copy(value_w, weights.at[:, query_width + key_width :], wload.at[2]),
    ]
    for k in loads:
        k.start()
    gains = push(small_ref.at[pl.ds(0, 8)], gains_other, nsend.at[4], nrecv.at[4], me.core())
    gains.start()
    low_all[place] = low_ref[...]
    quarter = width // 4

    def trade(n):
        at = pl.ds(pl.multiple_of(n * quarter, quarter), quarter)
        return push(normed.at[:, at], normed_other.at[:, at], nsend.at[n], nrecv.at[n], me.core())

    def normed_cols(n, c):
        at = pl.ds(pl.multiple_of(n * quarter, quarter), quarter)
        normed[:, at] = over(low_ref[...], weights[at, :], NT).astype(bf16)
        trade(n).start()
        return c

    def await_trade(n, c):
        trade(n).wait_recv()
        return c


    def input_rows(r, total):
        at = pl.ds(pl.multiple_of(r * 16, 16), 16)
        grads = normed[at, :].astype(f32) + normed_other[at, :].astype(f32)
        inputs = input_ref[at, :].astype(f32)
        scale = lax.rsqrt(jnp.mean(inputs * inputs, axis=1, keepdims=True) + epsilon)
        scaled = gain_ref[...] * grads
        level = jnp.mean(scaled * inputs, axis=1, keepdims=True)
        input_grad[at, :] = grad_ref[at, :] + scale * scaled - inputs * (scale * scale * scale * level)
        return total + jnp.sum(grads * inputs * scale, axis=0, keepdims=True)

    def norm_round(k):
        if k == 0:
            for copy in loads:
                copy.wait()
        if k < 4:
            lax.fori_loop(k, k + 1, normed_cols, 0)
        if k == 4:
            gains.wait()
            total_ref[...] = small_ref[...]
            total_ref[0:8, :] += gains_other[...]
            lax.fori_loop(0, 4, await_trade, 0)
            total_ref[8:9, :] = lax.fori_loop(0, tokens // 16, input_rows, jnp.zeros((1, width), f32))
            send[0] = total_ref[ours, :]

    half = total_ref.shape[0] // 2
    ours = pl.ds(pl.multiple_of(me.t * half, half), half)
    others = pl.ds(pl.multiple_of((1 - me.t) * half, half), half)
    bits = [1, 2, 4, 8]

    def small(j):
        bit = bits[j]
        who = (me.e + bit * (1 - 2 * lax.rem(lax.div(me.e, bit), 2)), me.t)
        return push(send.at[j], land.at[j], tsend.at[j], trecv.at[j], who)

    share_back = push(send.at[4], land.at[4], tsend.at[4], trecv.at[4], me.core())

    def small_round(j):
        if j > 0:
            small(j - 1).wait_recv()
            if j < 4:
                send[j] = send[j - 1] + land[j - 1]
            else:
                send[4] = send[3] + land[3]
                share_back.start()
        if j < 4:
            small(j).start()


    def block(k, d):
        return sums.at[k, pl.ds(pl.multiple_of(d * share, share), share)]

    def along(k, d, up):
        arrive = me.a + 1 if up else me.a - 1
        slot = d if up else jnp.where(d == arrive, planes, d)
        return push(block(k, d), landz.at[k, slot], zsend.at[k, d], zrecv.at[k, slot], me.at(arrive, me.b, me.c))

    def landed(k, slot):
        push(landz.at[k, slot], landz.at[k, slot], zsend.at[k, 0], zrecv.at[k, slot], me.core()).wait_recv()

    def chain(k, act, ends):
        for i in range(planes - 1):
            d = far_first(me.a, planes, i)
            up = d > me.a
            inner = (up & (me.a > 0)) | (jnp.logical_not(up) & (me.a + 1 < planes))

            @pl.when(jnp.logical_not(inner) if ends else inner)
            def _(d=d, up=up):
                if act and not ends:
                    landed(k, d)
                    add_rows(block(k, d), [block(k, d), landz.at[k, d]])

                @pl.when(up)
                def _():
                    along(k, d, True).start() if act else along(k, d, True).wait_send()

                @pl.when(jnp.logical_not(up))
                def _():
                    along(k, d, False).start() if act else along(k, d, False).wait_send()

    def finish(k):
        target = rows_ref.at[:, cols(k)]
        own = block(k, me.a)

        @pl.when(me.a > 0)
        def _():
            landed(k, me.a)

        @pl.when(me.a + 1 < planes)
        def _():
            landed(k, planes)

        @pl.when((me.a > 0) & (me.a + 1 < planes))
        def _():
            add_rows(target, [own, landz.at[k, me.a], landz.at[k, planes]])

        @pl.when(me.a == 0)
        def _():
            add_rows(target, [own, landz.at[k, planes]])

        @pl.when(me.a + 1 == planes)
        def _():
            add_rows(target, [own, landz.at[k, me.a]])

    def forward(k):
        whole(0, k).wait_recv()
        relay(k).start()
        if k + 2 < chunks:
            whole(1, k + 2).start()

    for k in range(chunks + 2):
        if k < chunks:
            if k == 0:
                forward(0)
            if k + 1 < chunks:
                forward(k + 1)
            whole(1, k).wait_recv()
            relay(k).wait_recv()
            mixed_rows = low_all[:, :, k * chunk : (k + 1) * chunk].reshape(4 * tokens, chunk)
            sums[k] = over(cut_ref[...], mixed_rows, NN).astype(bf16)
            chain(k, True, True)
        norm_round(k)
        if k in (4, 6, 8, 10, 11):
            small_round((4, 6, 8, 10, 11).index(k))
        if 1 <= k <= chunks:
            chain(k - 1, True, False)
        if k >= 2:
            finish(k - 2)
        mix_round(k)

    def settle(k, c):
        for i in range(2):
            whole(i, k).wait_send()
        relay(k).wait_send()
        chain(k, False, True)
        chain(k, False, False)
        return c

    lax.fori_loop(0, chunks, settle, 0)
    for k in (mix_c(0), mix_c(1), mix_b()):
        k.wait_send()
    for n in range(4):
        trade(n).wait_send()
        small(n).wait_send()
    share_back.wait_send()
    share_back.wait_recv()
    total_ref[ours, :] = send[4]
    total_ref[others, :] = land[4]


def weight_grads(low, cut, query_w, key_w, value_w, inputs, gain, residual_grad, small, mixing, planes, cid):
    f32, bf16 = jnp.float32, jnp.bfloat16
    tokens, packed = low.shape
    width = inputs.shape[1]
    chunk = 256
    chunks = packed // chunk
    share = cut.shape[0] // planes
    quarter = mixing.shape[1:]
    inside = pl.BlockSpec(memory_space=pltpu.VMEM)
    anywhere = pl.BlockSpec(memory_space=pl.ANY)
    half = (small.shape[0] // 2, small.shape[1])
    return pl.pallas_call(
        functools.partial(weights_kernel, planes, chunk),
        out_shape=[
            jax.ShapeDtypeStruct((share, packed), f32),
            jax.ShapeDtypeStruct((tokens, width), f32),
            jax.ShapeDtypeStruct(small.shape, f32),
            jax.ShapeDtypeStruct(quarter, f32),
        ],
        in_specs=[inside, inside, anywhere, anywhere, anywhere, inside, inside, inside, inside, anywhere],
        out_specs=[inside] * 4,
        scratch_shapes=[
            pltpu.VMEM((4, tokens, packed), bf16),
            pltpu.VMEM((2,) + quarter, bf16),
            pltpu.VMEM((2,) + quarter, bf16),
            pltpu.VMEM(quarter, bf16),
            pltpu.VMEM((width, packed), bf16),
            pltpu.VMEM((chunks, planes * share, chunk), bf16),
            pltpu.VMEM((chunks, planes + 1, share, chunk), bf16),
            pltpu.VMEM((tokens, width), bf16),
            pltpu.VMEM((tokens, width), bf16),
            pltpu.VMEM((8, width), f32),
            pltpu.VMEM((5,) + half, f32),
            pltpu.VMEM((5,) + half, f32),
            pltpu.SemaphoreType.DMA((3,)),
            pltpu.SemaphoreType.DMA((3, chunks)),
            pltpu.SemaphoreType.DMA((3, chunks)),
            pltpu.SemaphoreType.DMA((3,)),
            pltpu.SemaphoreType.DMA((3,)),
            pltpu.SemaphoreType.DMA((2,)),
            pltpu.SemaphoreType.DMA((chunks, planes)),
            pltpu.SemaphoreType.DMA((chunks, planes + 1)),
            pltpu.SemaphoreType.DMA((5,)),
            pltpu.SemaphoreType.DMA((5,)),
            pltpu.SemaphoreType.DMA((5,)),
            pltpu.SemaphoreType.DMA((5,)),
        ],
        compiler_params=pltpu.CompilerParams(collective_id=cid, has_side_effects=True, vmem_limit_bytes=ROOM),
        name="weight_grads",
    )(low, cut, query_w, key_w, value_w, inputs, gain, residual_grad, small, mixing)


epsilon = 1e-06
rope_base = 1000000.0
far_below = -1e30


def rms_scaled(values, gain_vec):
    return (
        values * lax.rsqrt(jnp.mean(values * values, axis=-1, keepdims=True) + epsilon) * gain_vec
    )


def rotary_tables(positions, head_dim):
    halfway = head_dim // 2
    exponents = jnp.arange(halfway, dtype=jnp.float32) * (2.0 / head_dim)
    inverse = jnp.exp(-exponents * jnp.log(jnp.float32(rope_base)))
    angles = positions.astype(jnp.float32)[:, None] * inverse[None, :]
    return (jnp.cos(angles), jnp.sin(angles))


def rotate(values, cosine, sine_table):
    halfway = values.shape[-1] // 2
    first = values[..., :halfway]
    latter = values[..., halfway:]
    return jnp.concatenate(
        [first * cosine - latter * sine_table, latter * cosine + first * sine_table], axis=-1
    )


def glu_value(gate_act, up_act):
    return jax.nn.silu(gate_act) * up_act


def on_device(
    layer_input,
    norm_first,
    query_weight,
    key_weight,
    value_weight,
    mixing_weight,
    query_gain,
    key_gain,
    norm_second,
    router_weight,
    gate_weight,
    up_weight,
    down_weight,
    routes,
    fill_order,
    cotangent,
):
    seq_count, seg_len, model_width = layer_input.shape
    expert_count = lax.axis_size("expert")
    tensor_count = lax.axis_size("tensor")
    expert_idx = lax.axis_index("expert")
    tensor_idx = lax.axis_index("tensor")
    head_dim = query_gain.shape[0]
    local_queries = query_weight.shape[1] // head_dim
    local_keys = key_weight.shape[1] // head_dim
    group_size = local_queries // local_keys
    seq_length = seg_len * expert_count
    top_count = routes.shape[2]
    token_count = seq_count * seg_len
    capacity = 5 * token_count * top_count // (4 * expert_count)
    half_width = model_width // tensor_count
    factor = head_dim ** (-0.5)
    inputs = layer_input.astype(jnp.float32)
    normed_f, first_back = jax.vjp(rms_scaled, inputs, norm_first)
    normed = normed_f.astype(jnp.bfloat16)
    positions = expert_idx * seg_len + jnp.arange(seg_len, dtype=jnp.int32)
    cosine, sine_table = rotary_tables(positions, head_dim)
    cosine = cosine[:, None, :]
    sine_table = sine_table[:, None, :]

    def rope_norm(raw_heads, gain_vec):
        return rotate(rms_scaled(raw_heads, gain_vec), cosine, sine_table)

    query_raw = jnp.dot(normed, query_weight, preferred_element_type=jnp.float32).reshape(
        seq_count, seg_len, local_queries, head_dim
    )
    key_raw = jnp.dot(normed, key_weight, preferred_element_type=jnp.float32).reshape(
        seq_count, seg_len, local_keys, head_dim
    )
    value_local = jnp.dot(normed, value_weight, preferred_element_type=jnp.float32).astype(
        jnp.bfloat16
    )
    query_rot, query_back = jax.vjp(rope_norm, query_raw, query_gain)
    key_rot, key_back = jax.vjp(rope_norm, key_raw, key_gain)
    key_local = key_rot.astype(jnp.bfloat16).reshape(seq_count, seg_len, local_keys * head_dim)
    key_all, value_all = (
        lax.all_gather(key_local, "expert", axis=1, tiled=True),
        lax.all_gather(value_local, "expert", axis=1, tiled=True),
    )
    key_tiles = key_all.reshape(seq_count, seq_length, local_keys, head_dim)
    value_tiles = value_all.reshape(seq_count, seq_length, local_keys, head_dim)
    query_rows = query_rot.astype(jnp.bfloat16).reshape(
        seq_count, seg_len, local_keys, group_size, head_dim
    )
    query_rows = query_rows.transpose(0, 2, 3, 1, 4).reshape(
        seq_count, local_keys, group_size * seg_len, head_dim
    )
    row_block = (
        expert_idx * seg_len + jnp.arange(group_size * seg_len, dtype=jnp.int32) % seg_len
    ) // BLOCK
    tile_len = min(512, seq_length)
    reach_end = jnp.minimum(((expert_idx + 1) * seg_len - 1) // BLOCK * BLOCK + BLOCK, seq_length)
    tile_count = (reach_end + tile_len - 1) // tile_len

    def tile_scores(tile_idx):
        offset = tile_idx * tile_len
        key_part = lax.dynamic_slice_in_dim(key_tiles, offset, tile_len, 1)
        scores = (
            jnp.einsum("shrd,skhd->shrk", query_rows, key_part, preferred_element_type=jnp.float32)
            * factor
        )
        key_block = (offset + jnp.arange(tile_len, dtype=jnp.int32)) // BLOCK
        allowed = key_block[None, :] <= row_block[:, None]
        return (scores, allowed, offset)

    stat_shape = (seq_count, local_keys, group_size * seg_len)

    def stats_step(tile_idx, state_pair):
        running_max, running_sum = state_pair
        scores, allowed, offset = tile_scores(tile_idx)
        masked = jnp.where(allowed, scores, far_below)
        new_max = jnp.maximum(running_max, jnp.max(masked, axis=-1))
        exp_terms = jnp.where(allowed, jnp.exp(masked - new_max[..., None]), 0.0)
        return (new_max, running_sum * jnp.exp(running_max - new_max) + jnp.sum(exp_terms, axis=-1))

    row_max, row_sum = lax.fori_loop(
        0,
        tile_count,
        stats_step,
        (jnp.full(stat_shape, far_below, jnp.float32), jnp.zeros(stat_shape, jnp.float32)),
    )
    log_total = row_max + jnp.log(row_sum)

    def probabilities(tile_idx):
        scores, allowed, offset = tile_scores(tile_idx)
        return (jnp.where(allowed, jnp.exp(scores - log_total[..., None]), 0.0), offset)

    def context_step(tile_idx, context_sum):
        prob_tile, offset = probabilities(tile_idx)
        value_part = lax.dynamic_slice_in_dim(value_tiles, offset, tile_len, 1)
        return context_sum + jnp.einsum(
            "shrk,skhd->shrd",
            prob_tile.astype(jnp.bfloat16),
            value_part,
            preferred_element_type=jnp.float32,
        )

    context_f = lax.fori_loop(0, tile_count, context_step, jnp.zeros(query_rows.shape, jnp.float32))
    shaped = context_f.reshape(seq_count, local_keys, group_size, seg_len, head_dim).transpose(
        0, 3, 1, 2, 4
    )
    context = shaped.reshape(seq_count, seg_len, local_queries * head_dim).astype(jnp.bfloat16)
    head_part = jnp.dot(context, mixing_weight, preferred_element_type=jnp.float32)
    residual = inputs + lax.psum(head_part.astype(jnp.bfloat16), "tensor").astype(jnp.float32)
    second_f, second_back = jax.vjp(rms_scaled, residual, norm_second)
    second = second_f.astype(jnp.bfloat16).reshape(token_count, model_width)
    logits = jnp.dot(second, router_weight, preferred_element_type=jnp.float32)
    flat_routes = routes.reshape(token_count, top_count)
    picked = (flat_routes[:, :, None] == jnp.arange(expert_count, dtype=jnp.int32)).astype(
        jnp.float32
    )
    gates = jax.nn.softmax(jnp.sum(picked * logits[:, None, :], axis=-1), axis=-1)
    usages = jnp.sum(picked, axis=1)
    ranking = fill_order.reshape(token_count)
    before = (ranking[None, :] < ranking[:, None]).astype(jnp.bfloat16)
    counts = jnp.dot(before, usages.astype(jnp.bfloat16), preferred_element_type=jnp.float32)
    slot_ids = jnp.sum(picked * counts[:, None, :], axis=-1).astype(jnp.int32)
    kept_mask = slot_ids < capacity
    kept_float = kept_mask.astype(jnp.float32)
    weighted = gates * kept_float
    places = jnp.where(kept_mask, flat_routes * capacity + slot_ids, -1)
    slot_grid = jnp.arange(expert_count * capacity, dtype=jnp.int32)
    assign = (places[:, :, None] == slot_grid).astype(jnp.bfloat16)
    placed = jnp.sum(assign, axis=1)
    combine = jnp.sum(weighted[:, :, None] * assign.astype(jnp.float32), axis=1)
    send_rows = jnp.einsum("tp,td->pd", placed, second, preferred_element_type=jnp.float32).astype(
        jnp.bfloat16
    )
    arrived = lax.all_to_all(
        send_rows.reshape(expert_count, capacity, model_width),
        "expert",
        split_axis=0,
        concat_axis=0,
        tiled=True,
    )
    arrived = arrived.reshape(expert_count * capacity, model_width)
    gate_one = gate_weight[0]
    up_one = up_weight[0]
    down_one = down_weight[0]
    gate_act = jnp.dot(arrived, gate_one, preferred_element_type=jnp.float32)
    up_act = jnp.dot(arrived, up_one, preferred_element_type=jnp.float32)
    hidden_val, glu_back = jax.vjp(glu_value, gate_act, up_act)
    hidden = hidden_val.astype(jnp.bfloat16)
    expert_part = jnp.dot(hidden, down_one, preferred_element_type=jnp.float32)
    summed = lax.psum(expert_part.astype(jnp.bfloat16), "tensor")
    returned = lax.all_to_all(
        summed.reshape(expert_count, capacity, model_width),
        "expert",
        split_axis=0,
        concat_axis=0,
        tiled=True,
    )
    returned = returned.reshape(expert_count * capacity, model_width)
    per_route = (
        jnp.take(returned, jnp.maximum(places, 0), axis=0).astype(jnp.float32)
        * kept_float[:, :, None]
    )
    mixture = residual.reshape(token_count, model_width) + jnp.sum(
        weighted[:, :, None] * per_route, axis=1
    )
    layer_output = lax.dynamic_slice_in_dim(mixture, tensor_idx * half_width, half_width, 1)
    layer_output = layer_output.astype(jnp.bfloat16).reshape(seq_count, seg_len, half_width)
    upstream = cotangent.astype(jnp.float32).reshape(token_count, model_width)
    gate_grads = jnp.sum(upstream[:, None, :] * per_route, axis=-1) * kept_float
    send_grads = jnp.einsum(
        "tp,td->pd",
        combine,
        upstream,
        precision=lax.Precision.HIGHEST,
        preferred_element_type=jnp.float32,
    ).astype(jnp.bfloat16)
    grads_in = lax.all_to_all(
        send_grads.reshape(expert_count, capacity, model_width),
        "expert",
        split_axis=0,
        concat_axis=0,
        tiled=True,
    )
    grads_in = grads_in.reshape(expert_count * capacity, model_width)
    hidden_grad = lax.dot_general(
        grads_in, down_one, (((1,), (1,)), ((), ())), preferred_element_type=jnp.float32
    )
    down_grad = jnp.einsum("rf,rd->fd", hidden, grads_in, preferred_element_type=jnp.float32)
    gate_d, up_d = glu_back(hidden_grad)
    gate_d = gate_d.astype(jnp.bfloat16)
    up_d = up_d.astype(jnp.bfloat16)
    gate_grad = jnp.einsum("rd,rf->df", arrived, gate_d, preferred_element_type=jnp.float32)
    up_grad = jnp.einsum("rd,rf->df", arrived, up_d, preferred_element_type=jnp.float32)
    row_part = lax.dot_general(
        gate_d, gate_one, (((1,), (1,)), ((), ())), preferred_element_type=jnp.float32
    )
    row_part = row_part + lax.dot_general(
        up_d, up_one, (((1,), (1,)), ((), ())), preferred_element_type=jnp.float32
    )
    row_share = lax.psum_scatter(
        row_part.reshape(expert_count, capacity, model_width).astype(jnp.bfloat16),
        "tensor",
        scatter_dimension=2,
        tiled=True,
    )
    row_home = lax.all_to_all(row_share, "expert", split_axis=0, concat_axis=0, tiled=True).reshape(
        expert_count * capacity, half_width
    )
    second_half = jnp.dot(placed, row_home, preferred_element_type=jnp.float32)
    route_grads = gates * (gate_grads - jnp.sum(gates * gate_grads, axis=-1, keepdims=True))
    logit_grads = jnp.sum(picked * route_grads[:, :, None], axis=1).astype(jnp.bfloat16)
    router_grad = jnp.einsum("td,te->de", second, logit_grads, preferred_element_type=jnp.float32)
    router_back = lax.dot_general(
        logit_grads, router_weight, (((1,), (1,)), ((), ())), preferred_element_type=jnp.float32
    )
    own_part = second_half + lax.dynamic_slice_in_dim(
        router_back, tensor_idx * half_width, half_width, 1
    )
    second_part = lax.dynamic_update_slice_in_dim(
        jnp.zeros((token_count, model_width), jnp.float32), own_part, tensor_idx * half_width, 1
    )
    residual_part, norm_part = second_back(second_part.reshape(seq_count, seg_len, model_width))
    residual_grad, second_grad = (
        lax.psum(residual_part.astype(jnp.bfloat16), "tensor").astype(jnp.float32),
        lax.psum(norm_part.astype(jnp.bfloat16), "tensor").astype(jnp.float32),
    )
    residual_grad = residual_grad + upstream.reshape(seq_count, seg_len, model_width)
    head_in = residual_grad.astype(jnp.bfloat16)
    mixing_part = jnp.einsum("std,stc->dc", head_in, context, preferred_element_type=jnp.float32)
    context_grad = lax.dot_general(
        head_in, mixing_weight, (((2,), (1,)), ((), ())), preferred_element_type=jnp.float32
    ).astype(jnp.bfloat16)
    grad_rows = context_grad.reshape(
        seq_count, seg_len, local_keys, group_size, head_dim
    ).transpose(0, 2, 3, 1, 4)
    grad_rows = grad_rows.reshape(query_rows.shape)
    delta_rows = jnp.sum(grad_rows.astype(jnp.float32) * context_f, axis=-1)
    key_shape = (seq_count, seq_length, local_keys, head_dim)

    def gradient_step(tile_idx, state_trio):
        query_acc, key_acc, value_acc = state_trio
        prob_tile, offset = probabilities(tile_idx)
        key_part = lax.dynamic_slice_in_dim(key_tiles, offset, tile_len, 1)
        value_part = lax.dynamic_slice_in_dim(value_tiles, offset, tile_len, 1)
        prob_low = prob_tile.astype(jnp.bfloat16)
        prob_grad = jnp.einsum(
            "shrd,skhd->shrk", grad_rows, value_part, preferred_element_type=jnp.float32
        )
        score_grad = (prob_tile * (prob_grad - delta_rows[..., None])).astype(jnp.bfloat16)
        query_acc = query_acc + jnp.einsum(
            "shrk,skhd->shrd", score_grad, key_part, preferred_element_type=jnp.float32
        )
        key_tile = jnp.einsum(
            "shrk,shrd->skhd", score_grad, query_rows, preferred_element_type=jnp.float32
        )
        value_tile = jnp.einsum(
            "shrk,shrd->skhd", prob_low, grad_rows, preferred_element_type=jnp.float32
        )
        key_acc = lax.dynamic_update_slice_in_dim(key_acc, key_tile, offset, 1)
        value_acc = lax.dynamic_update_slice_in_dim(value_acc, value_tile, offset, 1)
        return (query_acc, key_acc, value_acc)

    start_state = (
        jnp.zeros(query_rows.shape, jnp.float32),
        jnp.zeros(key_shape, jnp.float32),
        jnp.zeros(key_shape, jnp.float32),
    )
    query_acc, key_acc, value_acc = lax.fori_loop(0, tile_count, gradient_step, start_state)
    key_grad_all, value_grad_all = (
        lax.psum_scatter(
            (key_acc * factor).reshape(seq_count, seq_length, local_keys * head_dim),
            "expert",
            scatter_dimension=1,
            tiled=True,
        ),
        lax.psum_scatter(
            value_acc.reshape(seq_count, seq_length, local_keys * head_dim),
            "expert",
            scatter_dimension=1,
            tiled=True,
        ),
    )
    key_raw_grad, keygain_part = key_back(
        key_grad_all.reshape(seq_count, seg_len, local_keys, head_dim)
    )
    query_shaped = (
        (query_acc * factor)
        .reshape(seq_count, local_keys, group_size, seg_len, head_dim)
        .transpose(0, 3, 1, 2, 4)
    )
    query_raw_grad, querygain_part = query_back(
        query_shaped.reshape(seq_count, seg_len, local_queries, head_dim)
    )
    query_low = query_raw_grad.astype(jnp.bfloat16).reshape(
        seq_count, seg_len, local_queries * head_dim
    )
    key_low = key_raw_grad.astype(jnp.bfloat16).reshape(seq_count, seg_len, local_keys * head_dim)
    value_low = value_grad_all.astype(jnp.bfloat16)
    query_sum = jnp.einsum("std,stc->dc", normed, query_low, preferred_element_type=jnp.float32)
    keys_sum = jnp.einsum("std,stc->dc", normed, key_low, preferred_element_type=jnp.float32)
    values_sum = jnp.einsum("std,stc->dc", normed, value_low, preferred_element_type=jnp.float32)
    query_grad, key_grad, value_grad, mixing_rows = (
        lax.psum_scatter(query_sum, "expert", scatter_dimension=0, tiled=True),
        lax.psum_scatter(keys_sum, "expert", scatter_dimension=0, tiled=True),
        lax.psum_scatter(values_sum, "expert", scatter_dimension=0, tiled=True),
        lax.psum_scatter(mixing_part, "expert", scatter_dimension=0, tiled=True),
    )
    mixing_grad = mixing_rows.T
    normed_part = lax.dot_general(
        query_low, query_weight, (((2,), (1,)), ((), ())), preferred_element_type=jnp.float32
    )
    normed_part = normed_part + lax.dot_general(
        key_low, key_weight, (((2,), (1,)), ((), ())), preferred_element_type=jnp.float32
    )
    normed_part = normed_part + lax.dot_general(
        value_low, value_weight, (((2,), (1,)), ((), ())), preferred_element_type=jnp.float32
    )
    normed_grad, querygain_grad, keygain_grad = (
        lax.psum(normed_part.astype(jnp.bfloat16), "tensor").astype(jnp.float32),
        lax.psum(querygain_part.astype(jnp.bfloat16), "tensor").astype(jnp.float32),
        lax.psum(keygain_part.astype(jnp.bfloat16), "tensor").astype(jnp.float32),
    )
    input_part, first_grad = first_back(normed_grad)
    input_grad = residual_grad + input_part
    first_grad, second_grad, querygain_grad, keygain_grad, router_grad = lax.psum(
        (first_grad, second_grad, querygain_grad, keygain_grad, router_grad), "expert"
    )
    return (
        layer_output,
        input_grad,
        first_grad,
        query_grad,
        key_grad,
        value_grad,
        mixing_grad,
        querygain_grad,
        keygain_grad,
        second_grad,
        router_grad,
        gate_grad[None],
        up_grad[None],
        down_grad[None],
    )

def partners(planes):
    def number(a, b, c, t):
        y, x = (b, c) if t else (c, b)
        return (a * 4 + y * 2 + x) * 2 + t

    both = (0, 1)
    pairs = [[number(a, b, c, t) for c in both] for t in both for a in range(planes) for b in both]
    groups = [[number(a, b, c, t) for a in range(planes) for b in both] for t in both for c in both]
    return pairs, groups


def lift(values, wide):
    high = lax.reduce_precision(values, 8, 7)
    both = jnp.concatenate([high, values - high], axis=-1).astype(jnp.bfloat16)
    return jnp.pad(both, ((0, 0), (0, wide - both.shape[-1])))


def on_chips(
    layer_input,
    norm_first,
    query_weight,
    key_weight,
    value_weight,
    mixing_weight,
    query_gain,
    key_gain,
    norm_second,
    router_weight,
    gate_weight,
    up_weight,
    down_weight,
    routes,
    fill_order,
    cotangent,
):
    seq_count, seg_len, model_width = layer_input.shape
    expert_count = lax.axis_size("expert")
    planes = expert_count // 4
    expert_idx = lax.axis_index("expert")
    tensor_idx = lax.axis_index("tensor")
    head_dim = query_gain.shape[0]
    local_queries = query_weight.shape[1] // head_dim
    local_keys = key_weight.shape[1] // head_dim
    key_width = local_keys * head_dim
    group_size = local_queries // local_keys
    top_count = routes.shape[2]
    token_count = seq_count * seg_len
    capacity = 5 * token_count * top_count // (4 * expert_count)
    slots = -(-capacity // 32) * 32
    half_width = model_width // 2
    share_width = model_width // expert_count
    f32, bf16 = jnp.float32, jnp.bfloat16
    inputs = layer_input.astype(f32)
    normed = rms_scaled(inputs, norm_first).astype(bf16)
    positions = expert_idx * seg_len + jnp.arange(seg_len, dtype=jnp.int32)
    cosine, sine_table = rotary_tables(positions, head_dim)
    cosine = cosine[:, None, :]
    sine_table = sine_table[:, None, :]

    def rope_norm(raw_heads, gain_vec):
        return rotate(rms_scaled(raw_heads, gain_vec), cosine, sine_table)

    def slices(rows):
        cut = rows.reshape(token_count, planes, 4, share_width)
        return cut.transpose(2, 0, 1, 3).reshape(4, token_count, planes * share_width)

    query_raw = jnp.dot(normed, query_weight, preferred_element_type=f32).reshape(
        seq_count, seg_len, local_queries, head_dim
    )
    key_raw = jnp.dot(normed, key_weight, preferred_element_type=f32).reshape(
        seq_count, seg_len, local_keys, head_dim
    )
    value_local = jnp.dot(normed, value_weight, preferred_element_type=f32).astype(bf16)
    query_rot = rope_norm(query_raw, query_gain)
    key_rot = rope_norm(key_raw, key_gain)
    key_local = key_rot.astype(bf16).reshape(token_count, key_width)
    pairs = jnp.concatenate([key_local, value_local.reshape(token_count, key_width)], axis=1)
    upstream_low = cotangent.reshape(token_count, model_width)
    half_tokens = token_count // 2
    upstream_half = lax.dynamic_slice_in_dim(upstream_low, tensor_idx * half_tokens, half_tokens, 0)
    axes = ("expert", "tensor")
    pairs_of, groups_of = partners(planes)
    upstream_mine = lax.all_gather(upstream_half, "expert")
    query_rows = query_rot.astype(bf16).reshape(token_count, local_queries * head_dim)
    context, pairs_all, logs = attend(query_rows, pairs, planes, group_size, head_dim, 1)
    head_part = jnp.dot(context, mixing_weight, preferred_element_type=f32)
    head_low = head_part.astype(bf16)
    head_other = swap_cores(head_low, 3, "swap_heads")
    residual = inputs.reshape(token_count, model_width) + (head_low.astype(f32) + head_other.astype(f32))
    second_f, second_back = jax.vjp(rms_scaled, residual, norm_second)
    second = second_f.astype(bf16)
    logits = jnp.dot(second, router_weight, preferred_element_type=f32)
    flat_routes = routes.reshape(token_count, top_count)
    picked = (flat_routes[:, :, None] == jnp.arange(expert_count, dtype=jnp.int32)).astype(f32)
    gates = jax.nn.softmax(jnp.sum(picked * logits[:, None, :], axis=-1), axis=-1)
    usages = jnp.sum(picked, axis=1)
    ranking = fill_order.reshape(token_count)
    before = (ranking[None, :] < ranking[:, None]).astype(bf16)
    counts = jnp.dot(before, usages.astype(bf16), preferred_element_type=f32)
    here = (usages > 0.0) & (counts < capacity)
    slot_table = jnp.where(here, counts, -1.0)
    gate_table = jnp.where(here, jnp.sum(picked * gates[:, :, None], axis=1), 0.0)
    slot_hi = lift(slot_table, 2 * expert_count)[:, :expert_count]
    notes = jnp.concatenate([slot_hi, lift(gate_table, 128 - expert_count)], axis=1)
    parcel = jnp.concatenate([second, notes], axis=1)
    normed_cut = slices(normed.reshape(token_count, model_width))
    _, _, out_share, row_home, context_column, other_cuts, gate_grad, up_grad, down_grad = run_experts(
        parcel, upstream_mine, gate_weight[0], up_weight[0], down_weight[0], context, normed_cut, planes, slots, 4
    )
    place = lax.rem(expert_idx, 4)
    own_cut = lax.dynamic_index_in_dim(normed_cut, place, 0)
    normed_cut = lax.dynamic_update_slice_in_dim(other_cuts, own_cut, place, 0)
    out_side = lax.psum_scatter(out_share, axes, scatter_dimension=0, axis_index_groups=pairs_of, tiled=True)
    home_scores = jnp.sum(row_home[:, :, half_width:].astype(f32), axis=0)
    home_scores = home_scores[:, :expert_count] + home_scores[:, expert_count : 2 * expert_count]
    gate_grads = jnp.sum(picked * home_scores[:, None, :], axis=-1)
    route_grads = gates * (gate_grads - jnp.sum(gates * gate_grads, axis=-1, keepdims=True))
    logit_grads = jnp.sum(picked * route_grads[:, :, None], axis=1).astype(bf16)
    router_grad = jnp.einsum("td,te->ed", second, logit_grads, preferred_element_type=f32)
    router_back = lax.dot_general(
        logit_grads, router_weight, (((1,), (1,)), ((), ())), preferred_element_type=f32
    )
    second_rows = jnp.concatenate([row_home[0, :, :half_width], row_home[1, :, :half_width]], axis=1)
    second_in = second_rows.astype(f32) + router_back
    residual_part, second_grad = second_back(second_in)
    residual_grad = residual_part + upstream_low.astype(f32)
    head_in = residual_grad.astype(bf16)

    context_grad = lax.dot_general(
        head_in, mixing_weight, (((1,), (1,)), ((), ())), preferred_element_type=f32
    ).astype(bf16)
    head_cut = head_in.reshape(token_count, planes, 4 * share_width).transpose(1, 0, 2)
    turns = jnp.stack(
        [
            jnp.concatenate([cosine[:, 0], cosine[:, 0]], axis=1),
            jnp.concatenate([sine_table[:, 0], -sine_table[:, 0]], axis=1),
        ]
    )
    all_low, gain_grads, mixing_part = attend_back(
        query_rows,
        context_grad,
        context,
        pairs_all,
        logs,
        head_cut,
        context_column,
        (query_raw.reshape(token_count, -1), key_raw.reshape(token_count, key_width)),
        jnp.stack([query_gain, key_gain]),
        turns,
        planes,
        group_size,
        head_dim,
        7,
    )
    all_low, out_side = lax.optimization_barrier((all_low, out_side))
    out_home = lax.psum_scatter(out_side, axes, scatter_dimension=0, axis_index_groups=groups_of, tiled=True)[0]
    residual_half = lax.dynamic_slice_in_dim(residual, tensor_idx * half_width, half_width, 1)
    layer_output = (residual_half + out_home.astype(f32)).astype(bf16).reshape(seq_count, seg_len, half_width)
    gain_row = jnp.pad(
        gain_grads[:2].reshape(1, 2 * head_dim), ((0, 7), (0, model_width - 2 * head_dim))
    )
    small = jnp.concatenate(
        [gain_row, jnp.pad(second_grad[None], ((1, 6), (0, 0))), router_grad], axis=0
    )
    weight_rows, input_grad, small, mixing_rows = weight_grads(
        all_low,
        normed_cut.reshape(4 * token_count, planes * share_width).T,
        query_weight,
        key_weight,
        value_weight,
        layer_input.reshape(token_count, model_width),
        norm_first[None],
        residual_grad,
        small,
        mixing_part,
        planes,
        10,
    )
    mixing_grad = mixing_rows.T
    query_width = local_queries * head_dim
    query_grad = weight_rows[:, :query_width]
    key_grad = weight_rows[:, query_width : query_width + key_width]
    value_grad = weight_rows[:, query_width + key_width :]
    return (
        layer_output,
        input_grad.reshape(seq_count, seg_len, model_width),
        small[8],
        query_grad,
        key_grad,
        value_grad,
        mixing_grad,
        small[0, :head_dim],
        small[0, head_dim : 2 * head_dim],
        small[9],
        small[16:].T,
        gate_grad[None],
        up_grad[None],
        down_grad[None],
    )


def solution(mesh):
    chips = mesh.shape["expert"] == 16 and mesh.shape["tensor"] == 2
    return jax.shard_map(
        on_chips if chips else on_device,
        mesh=mesh,
        in_specs=(
            P(None, "expert", None),
            P(),
            P(None, "tensor"),
            P(None, "tensor"),
            P(None, "tensor"),
            P("tensor", None),
            P(),
            P(),
            P(),
            P(),
            P("expert", None, "tensor"),
            P("expert", None, "tensor"),
            P("expert", "tensor", None),
            P(None, "expert", None),
            P(None, "expert"),
            P(None, "expert", None),
        ),
        out_specs=(
            P(None, "expert", "tensor"),
            P(None, "expert", None),
            P(),
            P("expert", "tensor"),
            P("expert", "tensor"),
            P("expert", "tensor"),
            P("tensor", "expert"),
            P(),
            P(),
            P(),
            P(),
            P("expert", None, "tensor"),
            P("expert", None, "tensor"),
            P("expert", "tensor", None),
        ),
        check_vma=False,
    )
```

```python
import functools

import jax
import jax.numpy as jnp
from jax import lax
from jax.experimental import pallas as pl
from jax.experimental.pallas import tpu as pltpu
from jax.sharding import PartitionSpec as P

BLOCK = 256
MESH = pl.DeviceIdType.MESH
ROOM = 56 * 2**20


class Spot:
    def __init__(self):
        self.e = lax.axis_index("expert")
        self.t = lax.axis_index("tensor")
        self.a = lax.div(self.e, 4)
        y = lax.rem(lax.div(self.e, 2), 2)
        x = lax.rem(self.e, 2)
        self.b = x + self.t * (y - x)
        self.c = y + self.t * (x - y)

    def index(self, a, b, c):
        y = c + self.t * (b - c)
        x = b + self.t * (c - b)
        return a * 4 + y * 2 + x

    def at(self, a, b, c):
        return (self.index(a, b, c), self.t)

    def core(self):
        return (self.e, 1 - self.t)

    def greet(self, planes, chain, flat, share, far=False, corner=False):
        barrier = pltpu.get_barrier_semaphore()
        total = 0

        def call(who):
            pl.semaphore_signal(barrier, inc=1, device_id=who, device_id_type=MESH)

        if share:
            call(self.core())
            total = total + 1
        if flat:
            call(self.at(self.a, 1 - self.b, self.c))
            call(self.at(self.a, self.b, 1 - self.c))
            total = total + 2
        if corner:
            call(self.at(self.a, 1 - self.b, 1 - self.c))
            total = total + 1
        if far:
            for k in range(1, planes):
                call(self.at(lax.rem(self.a + k, planes), self.b, self.c))
            total = total + planes - 1
        elif chain:
            up = self.a + 1 < planes
            down = self.a > 0

            @pl.when(up)
            def _():
                call(self.at(self.a + 1, self.b, self.c))

            @pl.when(down)
            def _():
                call(self.at(self.a - 1, self.b, self.c))

            total = total + up.astype(jnp.int32) + down.astype(jnp.int32)
        pl.semaphore_wait(barrier, total)


def push(src, dst, send_sem, recv_sem, who):
    return pltpu.make_async_remote_copy(
        src_ref=src, dst_ref=dst, send_sem=send_sem, recv_sem=recv_sem, device_id=who, device_id_type=MESH
    )


def add_rows(target, parts):
    rows = target.shape[0]
    step = 32 if rows % 32 == 0 else 16

    def body(i, carry):
        at = pl.ds(pl.multiple_of(i * step, step), step)
        total = parts[0][at, :].astype(jnp.float32)
        for part in parts[1:]:
            total = total + part[at, :].astype(jnp.float32)
        target[at, :] = total.astype(target.dtype)
        return carry

    lax.fori_loop(0, rows // step, body, 0)


def far_first(a, planes, i):
    last = planes - 1
    low = jnp.where(i < last - a, last - i, jnp.where(i < last, i - (last - a), a))
    high = jnp.where(i < a, i, jnp.where(i < last, last - (i - a), a))
    return jnp.where(2 * a < last, low, high)


def swap_kernel(x_ref, o_ref, sems):
    me = Spot()
    me.greet(1, False, False, True)
    c = push(x_ref, o_ref, sems.at[0], sems.at[1], me.core())
    c.start()
    c.wait()


def swap_cores(x, cid, name):
    return pl.pallas_call(
        swap_kernel,
        out_shape=jax.ShapeDtypeStruct(x.shape, x.dtype),
        in_specs=[pl.BlockSpec(memory_space=pl.ANY)],
        out_specs=pl.BlockSpec(memory_space=pl.ANY),
        scratch_shapes=[pltpu.SemaphoreType.DMA((2,))],
        compiler_params=pltpu.CompilerParams(collective_id=cid, has_side_effects=True),
        name=name,
    )(x)


def over(first, second, contract):
    return lax.dot_general(first, second, (contract, ((), ())), preferred_element_type=jnp.float32)


NN = ((1,), (0,))
NT = ((1,), (1,))
TN = ((0,), (0,))


def experts_kernel(
    planes,
    parcel_ref,
    up_ref,
    gate_in,
    lift_in,
    down_in,
    context_ref,
    cut_ref,
    all_ref,
    other_ref,
    share_ref,
    home_ref,
    column_ref,
    cut_all,
    gate_sum,
    lift_sum,
    down_sum,
    wide,
    down,
    wide_half,
    down_half,
    pbuf,
    ubuf,
    xbuf,
    gbuf,
    vbuf,
    sbuf,
    wbuf,
    rbuf,
    hbuf,
    dbuf,
    gates,
    scores,
    stage,
    given,
    taken,
    mine,
    outgoing,
    partner,
    landc,
    landb,
    landa,
    gsend,
    grecv,
    gcore,
    usend,
    urecv,
    wsend,
    wrecv,
    wload,
    hsend,
    hrecv,
    ssem,
    rsem,
    lsem,
    osem,
    osend,
    orecv,
    esem,
    xsend,
    xrecv,
    csend,
    crecv,
):
    me = Spot()
    f32, bf16 = jnp.float32, jnp.bfloat16
    tokens, packed = parcel_ref.shape
    hidden, width = down_in.shape
    notes_width = packed - width
    count = planes * 4
    half = tokens // 2
    side = width // 2
    slots = sbuf.shape[2]
    own = me.index(me.a, me.b, me.c)
    ours = pl.ds(pl.multiple_of(me.t * half, half), half)
    theirs = pl.ds(pl.multiple_of((1 - me.t) * half, half), half)
    our_side = pl.ds(pl.multiple_of(me.t * side, side), side)
    their_side = pl.ds(pl.multiple_of((1 - me.t) * side, side), side)
    spots = [(sb, sc) for sc in (1 - me.c, me.c) for sb in (1 - me.b, me.b)]

    def near(i):
        return far_first(me.a, planes, planes - 1 - i)


    def carry(idx, kind, src=None):
        who = {
            0: me.at(me.a + 1, me.b, me.c),
            1: me.at(me.a - 1, me.b, me.c),
            2: me.at(me.a, 1 - me.b, me.c),
            3: me.at(me.a, me.b, 1 - me.c),
            4: me.core(),
        }[kind]
        there = all_ref.at[idx, ours]
        landed = gcore if kind == 4 else grecv
        return push(there if src is None else src, there, gsend.at[idx, kind], landed.at[idx], who)

    def relay_a(sa, act, first):
        idx = me.index(sa, me.b, me.c)
        src = parcel_ref.at[ours] if first else None
        if act and not first:
            carry(idx, 2).wait_recv()
        run = (lambda c: c.start()) if act else (lambda c: c.wait_send())

        @pl.when((sa <= me.a) & (me.a + 1 < planes))
        def _():
            run(carry(idx, 0, src))

        @pl.when((sa >= me.a) & (me.a > 0))
        def _():
            run(carry(idx, 1, src))

        run(carry(idx, 3, src))
        run(carry(idx, 2, src))
        if not first:
            run(carry(idx, 4))

    def relay_b(sa, act):
        idx = me.index(sa, 1 - me.b, me.c)
        run = (lambda c: c.start()) if act else (lambda c: c.wait_send())
        if act:
            carry(idx, 2).wait_recv()
        run(carry(idx, 3))
        run(carry(idx, 4))

    def across(sa, act):
        for sb in (me.b, 1 - me.b):
            idx = me.index(sa, sb, 1 - me.c)
            if act:
                carry(idx, 2).wait_recv()
                carry(idx, 4).start()
            else:
                carry(idx, 4).wait_send()

    def from_core(sa):
        for sb, sc in spots:
            idx = me.index(sa, sb, sc)

            @pl.when(idx != own)
            def _(idx=idx):
                there = all_ref.at[idx, theirs]
                push(there, there, gsend.at[idx, 4], gcore.at[idx], me.core()).wait_recv()

    def upstream(sa):
        group = pl.ds(sa * 4, 4)
        return push(up_ref.at[group], other_ref.at[group], usend.at[sa], urecv.at[sa], me.core())


    def part(ref, base, size):
        return ref.at[:, pl.ds(pl.multiple_of(base, 128), size)]

    down_rows = down_half.at[pl.ds(pl.multiple_of(me.t * hidden, 128), hidden)]
    wide_cols = [part(wide_half, me.t * 2 * hidden + i * hidden, hidden) for i in range(2)]
    sources = [gate_in, lift_in]
    loads = [pltpu.make_async_copy(sources[i], wide.at[:, i * hidden : (i + 1) * hidden], wload.at[i]) for i in range(2)]
    loads += [pltpu.make_async_copy(sources[i].at[our_side], wide_cols[i], wload.at[2 + i]) for i in range(2)]
    loads += [
        pltpu.make_async_copy(down_in, down, wload.at[4]),
        pltpu.make_async_copy(down_in.at[:, our_side], down_rows, wload.at[5]),
    ]
    pushes = [push(sources[i].at[their_side], wide_cols[i], wsend.at[i], wrecv.at[i], me.core()) for i in range(2)]
    pushes += [push(down_in.at[:, their_side], down_rows, wsend.at[2], wrecv.at[2], me.core())]


    def send_c(sa, sb):
        slot = sa * 2 + sb
        there = me.at(me.a, me.b, 1 - me.c)
        return push(outgoing.at[slot], landc.at[slot], ssem.at[0, slot], rsem.at[0, slot], there)

    def send_b(sa):
        src = mine.at[sa * 2 + 1 - me.b]
        return push(src, landb.at[sa], ssem.at[1, sa], rsem.at[1, sa], me.at(me.a, 1 - me.b, me.c))

    def send_a(sa):
        src = mine.at[sa * 2 + me.b]
        return push(src, landa.at[me.a], ssem.at[2, sa], rsem.at[2, me.a], me.at(sa, me.b, me.c))

    def from_c(sa):
        for sb in (1 - me.b, me.b):
            slot = sa * 2 + sb
            push(landc.at[slot], landc.at[slot], ssem.at[0, slot], rsem.at[0, slot], me.at(me.a, me.b, 1 - me.c)).wait_recv()
            for n in range(0, mine.shape[2], 384):
                cut = slice(n, n + 384)
                spread = over(partner[slot], landc[slot, :, cut], NN)
                mine[slot, :, cut] = (mine[slot, :, cut].astype(f32) + spread).astype(bf16)
            if sb is not me.b:
                send_b(sa).start()

    def from_b(sa):
        push(landb.at[sa], landb.at[sa], ssem.at[1, sa], rsem.at[1, sa], me.at(me.a, 1 - me.b, me.c)).wait_recv()
        return [mine.at[sa * 2 + me.b], landb.at[sa]]

    def along(sa):
        parts = from_b(sa)
        add_rows(parts[0], parts)
        send_a(sa).start()

    def finish():
        parts = from_b(me.a)
        for k in range(1, planes):
            far = lax.rem(me.a + k, planes)
            push(landa.at[far], landa.at[far], ssem.at[2, far], rsem.at[2, far], me.at(far, me.b, me.c)).wait_recv()
            parts = parts + [landa.at[far]]
        add_rows(home_ref.at[me.t], parts)


    def context_to(source, up, own_rows):
        there = column_ref.at[source]
        who = me.at(me.a + 1 if up else me.a - 1, me.b, me.c)
        return push(context_ref if own_rows else there, there, xsend.at[source, int(up)], xrecv.at[source], who)

    def context_pass(i, act):
        for up in (True, False):
            source = me.a - i if up else me.a + i
            further = me.a + 1 < planes if up else me.a > 0
            run = (lambda c: c.start()) if act else (lambda c: c.wait_send())

            @pl.when((source >= 0) & (source < planes))
            def _(source=source, up=up, further=further, run=run):
                if act and i > 0:
                    context_to(source, up, False).wait_recv()

                @pl.when(further)
                def _():
                    run(context_to(source, up, i == 0))

    place = lax.rem(me.e, 4)
    peers = [me.index(0, b, c) for b, c in ((1 - me.b, me.c), (me.b, 1 - me.c), (1 - me.b, 1 - me.c))]

    def cut_to(i):
        there = (me.e - place + peers[i], me.t)
        return push(cut_ref.at[peers[i]], cut_all.at[place], csend.at[i], crecv.at[i], there)


    def load_rows(sa, q):
        return pltpu.make_async_copy(all_ref.at[sa * 4 + q], pbuf.at[q], lsem.at[q])

    def fetch_rows(sa):
        from_core(sa)
        for q in range(4):
            mine_here = sa * 4 + q == own

            @pl.when(mine_here)
            def _(q=q):
                pltpu.make_async_copy(parcel_ref, pbuf.at[q], lsem.at[q]).start()

            @pl.when(jnp.logical_not(mine_here))
            def _(q=q):
                load_rows(sa, q).start()

    def load_up(sa):
        group = pl.ds(sa * 4, 4)
        return [
            pltpu.make_async_copy(up_ref.at[group], ubuf.at[:, ours], lsem.at[4]),
            pltpu.make_async_copy(other_ref.at[group], ubuf.at[:, theirs], lsem.at[5]),
        ]

    def fetch_up(sa):
        there = other_ref.at[pl.ds(sa * 4, 4)]
        push(there, there, usend.at[sa], urecv.at[sa], me.core()).wait_recv()
        for k in load_up(sa):
            k.start()

    def lanes(rows):
        return lax.broadcasted_iota(jnp.int32, (rows, notes_width), 1)

    def side_of(q):
        y, x = lax.div(q, 2), lax.rem(q, 2)
        return x + me.t * (y - x), y + me.t * (x - y)

    def chosen_by(expert, notes):
        slot_of = jnp.sum(jnp.where(lanes(tokens) == expert, notes, 0.0), axis=1, keepdims=True)
        chosen = slot_of == lax.broadcasted_iota(jnp.int32, (tokens, slots), 1).astype(f32)
        return jnp.where(chosen, 1.0, 0.0).astype(bf16)

    def pick_rows(q, carried):
        sa, slot = carried
        load_rows(sa, q).wait()
        notes = pbuf[q, :, width:].astype(f32)
        sb, sc = side_of(q)

        @pl.when(sc == me.c)
        def _():
            partner[sa * 2 + sb] = chosen_by(me.index(me.a, me.b, 1 - me.c), notes)

        chosen = chosen_by(me.e, notes)
        sbuf[q] = chosen
        pick = jnp.transpose(chosen.astype(f32)).astype(bf16)
        at = pl.ds(pl.multiple_of(q * slots, slots), slots)
        there = over(pick, pbuf[q, :, width:], NN)
        mark = lanes(slots)
        gate = jnp.sum(jnp.where((mark == count + me.e) | (mark == 2 * count + me.e), there, 0.0), axis=1, keepdims=True)
        gates[at, :] = jnp.broadcast_to(gate, (slots, 128))
        for n in range(0, width, 512):
            cut = slice(n, n + 512)
            xbuf[at, cut] = over(pick, pbuf[q, :, cut], NN).astype(bf16)
            picked = over(pick, ubuf[q, :, cut], NN)
            gbuf[at, cut] = (picked * gate).astype(bf16)
        for n in range(0, side, 512):
            cut = pl.ds(pl.multiple_of(me.t * side + n, 512), 512)
            vbuf[at, n : n + 512] = over(pick, ubuf[q, :, cut], NN).astype(bf16)
        return carried

    def hidden_cols(p):
        return pl.ds(pl.multiple_of(p * hidden, 128), hidden)

    def both_cols(p):
        return pl.ds(pl.multiple_of(p * 2 * hidden, 128), 2 * hidden)

    def hidden_rows(r, slot):
        at = pl.ds(pl.multiple_of(r * 256, 256), 256)
        acts = over(xbuf[at, :], wide[...], NN)
        gate_act, up_act = acts[:, :hidden], acts[:, hidden:]
        sig = 1.0 / (1.0 + jnp.exp(-gate_act))
        silu = gate_act * sig
        hbuf[slot, at, hidden_cols(me.t)] = (silu * up_act).astype(bf16)
        back = over(gbuf[at, :], down[...], NT)
        gate_d = (back * up_act * (sig * (1.0 + gate_act * (1.0 - sig)))).astype(bf16)
        dbuf[slot, at, pl.ds(pl.multiple_of(me.t * 2 * hidden, 128), hidden)] = gate_d
        dbuf[slot, at, pl.ds(pl.multiple_of(me.t * 2 * hidden + hidden, 128), hidden)] = (back * silu).astype(bf16)
        return slot

    def trades(slot):
        h_part = hbuf.at[slot, :, hidden_cols(me.t)]
        d_part = dbuf.at[slot, :, both_cols(me.t)]
        return [
            push(h_part, h_part, hsend.at[0], hrecv.at[slot, 0], me.core()),
            push(d_part, d_part, hsend.at[1], hrecv.at[slot, 1], me.core()),
        ]

    def traded(slot):
        h_part = hbuf.at[slot, :, hidden_cols(1 - me.t)]
        d_part = dbuf.at[slot, :, both_cols(1 - me.t)]
        push(h_part, h_part, hsend.at[0], hrecv.at[slot, 0], me.core()).wait_recv()
        push(d_part, d_part, hsend.at[1], hrecv.at[slot, 1], me.core()).wait_recv()

    def weight_sums(n, slot):
        cut = pl.ds(pl.multiple_of(n * 512, 512), 512)
        own_d = dbuf[slot, :, both_cols(me.t)]
        rows = xbuf[:, cut]
        gate_sum[cut, :] += over(rows, own_d[:, :hidden], TN)
        lift_sum[cut, :] += over(rows, own_d[:, hidden:], TN)
        down_sum[:, cut] += over(hbuf[slot, :, hidden_cols(me.t)], gbuf[:, cut], TN)
        return slot

    def out_rows(n, slot):
        cut = pl.ds(pl.multiple_of(n * 512, 512), 512)
        for r in range(0, 4 * slots, 256):
            at = slice(r, r + 256)
            out = over(hbuf[slot, at, :], down_half[:, cut], NN)
            wbuf[at, cut] = (out * gates[at, :1]).astype(bf16)
            total = jnp.sum(out * vbuf[at, cut].astype(f32), axis=1, keepdims=True)
            scores[at, :] += jnp.broadcast_to(total, (256, 128))
            rbuf[at, cut] = over(dbuf[slot, at, :], wide_half[cut, :], NT).astype(bf16)
        return slot

    def note_scores():
        mark = lanes(4 * slots)
        total = scores[...]
        high = total.astype(bf16).astype(f32)
        row = jnp.where(mark == me.e, high, jnp.where(mark == me.e + count, total - high, 0.0))
        rbuf[:, side:] = row.astype(bf16)

    def send_out(sa, sb):
        slot = sa * 2 + sb
        there = me.at(me.a, me.b, 1 - me.c)
        return push(given.at[slot], taken.at[slot], osend.at[slot], orecv.at[slot], there)

    def store(sa, sb):
        slot = sa * 2 + sb
        return pltpu.make_async_copy(stage.at[slot], share_ref.at[slot], osem.at[slot])

    def out_from_c(sa):
        for sb in (0, 1):
            slot = sa * 2 + sb
            send_out(sa, sb).wait_recv()
            for n in range(0, side, 512):
                cut = slice(n, n + 512)
                spread = over(partner[slot], taken[slot, :, cut], NN)
                stage[slot, :, cut] = (stage[slot, :, cut].astype(f32) + spread).astype(bf16)
            store(sa, sb).start()

    def spread_rows(q, sa):
        at = pl.ds(pl.multiple_of(q * slots, slots), slots)
        sb, sc = side_of(q)
        slot = sa * 2 + sb

        @pl.when(sc == me.c)
        def _():
            for n in range(0, mine.shape[2], 384):
                cut = slice(n, n + 384)
                mine[slot, :, cut] = over(sbuf[q], rbuf[at, cut], NN).astype(bf16)
            for n in range(0, side, 512):
                cut = slice(n, n + 512)
                stage[slot, :, cut] = over(sbuf[q], wbuf[at, cut], NN).astype(bf16)

        @pl.when(sc != me.c)
        def _():
            outgoing[slot] = rbuf[at, :]
            send_c(sa, sb).start()
            given[slot] = wbuf[at, :]

        return sa

    me.greet(planes, True, True, True, True, True)
    relay_a(me.a, True, True)
    for i in range(planes):
        upstream(near(i)).start()
    for k in loads + pushes:
        k.start()
    gate_sum[...] = jnp.zeros_like(gate_sum)
    lift_sum[...] = jnp.zeros_like(lift_sum)
    down_sum[...] = jnp.zeros_like(down_sum)
    fetch_up(near(1))
    relay_b(me.a, True)
    relay_a(near(1), True, False)
    across(me.a, True)
    for i in range(2, planes):
        relay_a(near(i), True, False)
        if i == planes - 1:
            context_pass(0, True)
        relay_b(near(i - 1), True)
    across(near(1), True)
    fetch_rows(near(1))
    for k in loads + pushes:
        k.wait()

    def step(i, c):
        last = i == planes - 1
        sa = jnp.where(last, me.a, near(i + 1))
        after = jnp.where(i + 2 < planes, near(i + 2), me.a)
        slot = lax.rem(i, 2)
        for k in load_up(sa):
            k.wait()
        scores[...] = jnp.zeros_like(scores)
        lax.fori_loop(0, 4, pick_rows, (sa, slot))

        @pl.when(i + 1 < planes)
        def _():
            fetch_up(after)

        @pl.when(i > 0)
        def _():
            for k in trades(slot):
                k.wait_send()

        lax.fori_loop(0, 4 * slots // 256, hidden_rows, slot)
        for k in trades(slot):
            k.start()

        @pl.when(i == 0)
        def _():
            relay_b(near(planes - 1), True)
            for k in range(3):
                cut_to(k).start()

        for k in range(1, planes):

            @pl.when(i == k - 1)
            def _(k=k):
                context_pass(k, True)

        @pl.when(i > 0)
        def _():
            from_c(near(i))

        traded(slot)
        lax.fori_loop(0, side // 512, out_rows, slot)
        note_scores()
        lax.fori_loop(0, 4, spread_rows, sa)
        for sb in (0, 1):
            send_out(sa, sb).start()

        @pl.when(i + 2 < planes)
        def _():
            across(after, True)

        @pl.when(jnp.logical_not(last))
        def _():
            fetch_rows(after)

        lax.fori_loop(0, width // 512, weight_sums, slot)

        @pl.when(i > 0)
        def _():
            along(near(i))
            out_from_c(near(i))

        return c

    lax.fori_loop(0, planes, step, 0)
    from_c(me.a)
    out_from_c(me.a)
    finish()
    done = push(home_ref.at[me.t], home_ref.at[me.t], esem.at[0], esem.at[1], me.core())
    done.start()

    relay_a(me.a, False, True)

    def settle(i, c):
        sa = near(i)
        relay_b(sa, False)

        @pl.when(i > 0)
        def _():
            relay_a(sa, False, False)
            send_a(sa).wait_send()

        across(sa, False)
        for sb in (1 - me.b, me.b):
            send_c(sa, sb).wait_send()
            send_out(sa, sb).wait_send()
            store(sa, sb).wait()
        send_b(sa).wait_send()
        upstream(sa).wait_send()
        return c

    lax.fori_loop(0, planes, settle, 0)
    for k in trades(0):
        k.wait_send()
    for k in range(planes):
        context_pass(k, False)
    for k in range(3):
        cut_to(k).wait()
    done.wait_send()
    other = home_ref.at[1 - me.t]
    push(other, other, esem.at[0], esem.at[1], me.core()).wait_recv()


def run_experts(parcel, upstream, gate, lift_w, down, context, cut, planes, slots, cid):
    f32, bf16 = jnp.float32, jnp.bfloat16
    tokens, packed = parcel.shape
    hidden, width = down.shape
    count = planes * 4
    half = tokens // 2
    side = width // 2
    block = side + packed - width
    rows = 4 * slots
    anywhere = pl.BlockSpec(memory_space=pl.ANY)
    inside = pl.BlockSpec(memory_space=pltpu.VMEM)
    return pl.pallas_call(
        functools.partial(experts_kernel, planes),
        out_shape=[
            jax.ShapeDtypeStruct((count, tokens, packed), bf16),
            jax.ShapeDtypeStruct((count, half, width), bf16),
            jax.ShapeDtypeStruct((2 * planes, tokens, side), bf16),
            jax.ShapeDtypeStruct((2, tokens, block), bf16),
            jax.ShapeDtypeStruct((planes,) + context.shape, bf16),
            jax.ShapeDtypeStruct(cut.shape, bf16),
            jax.ShapeDtypeStruct((width, hidden), f32),
            jax.ShapeDtypeStruct((width, hidden), f32),
            jax.ShapeDtypeStruct((hidden, width), f32),
        ],
        in_specs=[anywhere] * 7,
        out_specs=[anywhere] * 3 + [inside, anywhere, anywhere] + [inside] * 3,
        scratch_shapes=[
            pltpu.VMEM((width, 2 * hidden), bf16),
            pltpu.VMEM((hidden, width), bf16),
            pltpu.VMEM((side, 4 * hidden), bf16),
            pltpu.VMEM((2 * hidden, side), bf16),
            pltpu.VMEM((4, tokens, packed), bf16),
            pltpu.VMEM((4, tokens, width), bf16),
            pltpu.VMEM((rows, width), bf16),
            pltpu.VMEM((rows, width), bf16),
            pltpu.VMEM((rows, side), bf16),
            pltpu.VMEM((4, tokens, slots), bf16),
            pltpu.VMEM((rows, side), bf16),
            pltpu.VMEM((rows, block), bf16),
            pltpu.VMEM((2, rows, 2 * hidden), bf16),
            pltpu.VMEM((2, rows, 4 * hidden), bf16),
            pltpu.VMEM((rows, 128), f32),
            pltpu.VMEM((rows, 128), f32),
            pltpu.VMEM((2 * planes, tokens, side), bf16),
            pltpu.VMEM((2 * planes, slots, side), bf16),
            pltpu.VMEM((2 * planes, slots, side), bf16),
            pltpu.VMEM((2 * planes, tokens, block), bf16),
            pltpu.VMEM((2 * planes, slots, block), bf16),
            pltpu.VMEM((2 * planes, tokens, slots), bf16),
            pltpu.VMEM((2 * planes, slots, block), bf16),
            pltpu.VMEM((planes, tokens, block), bf16),
            pltpu.VMEM((planes, tokens, block), bf16),
            pltpu.SemaphoreType.DMA((count, 5)),
            pltpu.SemaphoreType.DMA((count,)),
            pltpu.SemaphoreType.DMA((count,)),
            pltpu.SemaphoreType.DMA((planes,)),
            pltpu.SemaphoreType.DMA((planes,)),
            pltpu.SemaphoreType.DMA((3,)),
            pltpu.SemaphoreType.DMA((3,)),
            pltpu.SemaphoreType.DMA((6,)),
            pltpu.SemaphoreType.DMA((2,)),
            pltpu.SemaphoreType.DMA((2, 2)),
            pltpu.SemaphoreType.DMA((3, 2 * planes)),
            pltpu.SemaphoreType.DMA((3, 2 * planes)),
            pltpu.SemaphoreType.DMA((7,)),
            pltpu.SemaphoreType.DMA((2 * planes,)),
            pltpu.SemaphoreType.DMA((2 * planes,)),
            pltpu.SemaphoreType.DMA((2 * planes,)),
            pltpu.SemaphoreType.DMA((2,)),
            pltpu.SemaphoreType.DMA((planes, 2)),
            pltpu.SemaphoreType.DMA((planes,)),
            pltpu.SemaphoreType.DMA((3,)),
            pltpu.SemaphoreType.DMA((3,)),
        ],
        compiler_params=pltpu.CompilerParams(
            collective_id=cid, has_side_effects=True, vmem_limit_bytes=62 * 2**20
        ),
        name="experts",
    )(parcel, upstream, gate, lift_w, down, context, cut)


def stack_heads(target, source, group):
    items, rows, size = target.shape
    seg = rows // group
    keys = source.shape[1] // (group * size)
    for s in range(items // keys):
        for k in range(keys):
            for h in range(group):
                at = (k * group + h) * size
                part = source[s * seg : (s + 1) * seg, at : at + size]
                target[s * keys + k, h * seg : (h + 1) * seg, :] = part.astype(target.dtype)


def spread_heads(target, item, value, group, keys):
    rows, size = value.shape
    seg = rows // group
    s, k = item // keys, item % keys
    for h in range(group):
        at = (k * group + h) * size
        target[s * seg : (s + 1) * seg, at : at + size] = value[h * seg : (h + 1) * seg, :].astype(target.dtype)


def block_heads(ref, plane, item, keys, size, part):
    seg = BLOCK // 4
    s, k = lax.div(item, keys), lax.rem(item, keys)
    rows = pl.ds(pl.multiple_of(s * seg, seg), seg)
    cols = pl.ds(pl.multiple_of((part * keys + k) * size, size), size)
    return [ref.at[plane * 4 + q, rows, cols] for q in range(4)]


def joined(refs):
    return jnp.concatenate([ref[...] for ref in refs], axis=0)


def attend_kernel(
    planes, group, q_ref, x_ref, context_ref, all_ref, log_ref, qs, top, total, acc, ssem, rsem
):
    me = Spot()
    f32, bf16 = jnp.float32, jnp.bfloat16
    items, rows, size = qs.shape
    keys = x_ref.shape[1] // (2 * size)
    factor = size ** (-0.5)
    own = me.index(me.a, me.b, me.c)

    def carry(idx, kind, src=None):
        who = {
            0: me.at(me.a + 1, me.b, me.c),
            2: me.at(me.a, 1 - me.b, me.c),
            3: me.at(me.a, me.b, 1 - me.c),
        }[kind]
        there = all_ref.at[idx]
        return push(there if src is None else src, there, ssem.at[idx, kind], rsem.at[idx], who)

    def relay(sa, act, first):
        idx = me.index(sa, me.b, me.c)
        src = x_ref if first else None
        if act and not first:
            carry(idx, 2).wait_recv()
        run = (lambda c: c.start()) if act else (lambda c: c.wait_send())

        @pl.when(me.a + 1 < planes)
        def _():
            run(carry(idx, 0, src))

        run(carry(idx, 3, src))
        run(carry(idx, 2, src))
        idx = me.index(sa, 1 - me.b, me.c)
        if act:
            carry(idx, 2).wait_recv()
        run(carry(idx, 3))

    def block(item, sa):
        scores = over(qs[item], joined(block_heads(all_ref, sa, item, keys, size, 0)), NT) * factor
        values = joined(block_heads(all_ref, sa, item, keys, size, 1))
        before = top[item]
        high = jnp.maximum(before, jnp.broadcast_to(jnp.max(scores, axis=1, keepdims=True), before.shape))
        shrink = jnp.exp(before - high)
        terms = jnp.exp(scores - high[:, :1])
        top[item] = high
        total[item] = total[item] * shrink + jnp.broadcast_to(jnp.sum(terms, axis=1, keepdims=True), before.shape)
        acc[item] = acc[item] * shrink + over(terms.astype(bf16), values, NN)
        return sa

    me.greet(planes, True, True, False)
    relay(me.a, True, True)
    all_ref[own] = x_ref[...]

    @pl.when(me.a > 0)
    def _():
        relay(me.a - 1, True, False)

    stack_heads(qs, q_ref, group)
    top[...] = jnp.full(top.shape, far_below, f32)
    total[...] = jnp.zeros_like(total)
    acc[...] = jnp.zeros_like(acc)

    def step(i, c):
        sa = me.a - i

        @pl.when(sa > 1)
        def _():
            relay(sa - 2, True, False)

        for sb in (me.b, 1 - me.b):
            carry(me.index(sa, sb, 1 - me.c), 2).wait_recv()
        lax.fori_loop(0, items, block, sa)
        return c

    lax.fori_loop(0, me.a + 1, step, 0)
    for item in range(items):
        spread_heads(context_ref, item, acc[item] / total[item], group, keys)
    log_ref[...] = top[...] + jnp.log(total[...])
    relay(me.a, False, True)

    def settle(i, c):
        relay(me.a - i, False, False)
        return c

    lax.fori_loop(1, me.a + 1, settle, 0)


def attend(query, pairs, planes, group, size, cid):
    f32, bf16 = jnp.float32, jnp.bfloat16
    tokens, width = query.shape
    count = planes * 4
    items = (tokens * 4 // BLOCK) * (width // (group * size))
    state = (items, group * BLOCK // 4, size)
    inside = pl.BlockSpec(memory_space=pltpu.VMEM)
    return pl.pallas_call(
        functools.partial(attend_kernel, planes, group),
        out_shape=[
            jax.ShapeDtypeStruct((tokens, width), bf16),
            jax.ShapeDtypeStruct((count,) + pairs.shape, bf16),
            jax.ShapeDtypeStruct(state, f32),
        ],
        in_specs=[inside] * 2,
        out_specs=[inside] * 3,
        scratch_shapes=[
            pltpu.VMEM(state, bf16),
            pltpu.VMEM(state, f32),
            pltpu.VMEM(state, f32),
            pltpu.VMEM(state, f32),
            pltpu.SemaphoreType.DMA((count, 4)),
            pltpu.SemaphoreType.DMA((count,)),
        ],
        compiler_params=pltpu.CompilerParams(collective_id=cid, has_side_effects=True, vmem_limit_bytes=ROOM),
        name="attend",
    )(query, pairs)


def attend_back_kernel(
    planes,
    group,
    q_ref,
    g_ref,
    o_ref,
    all_ref,
    log_ref,
    cut_ref,
    column_ref,
    query_raw,
    key_raw,
    gain_ref,
    turn_ref,
    low_ref,
    gain_grad,
    mixing_ref,
    pair_grad,
    cut_all,
    column,
    qs,
    gs,
    delta,
    qacc,
    mine,
    landc,
    landb,
    landa,
    ssem,
    rsem,
    psend,
    precv,
    lsem,
):
    me = Spot()
    f32, bf16 = jnp.float32, jnp.bfloat16
    items, rows, size = qs.shape
    keys = all_ref.shape[2] // (2 * size)
    factor = size ** (-0.5)
    me.greet(planes, False, True, False, True)

    def cut_to(k):
        far = lax.rem(me.a + k, planes)
        return push(cut_ref.at[far], cut_all.at[me.a], psend.at[k], precv.at[me.a], me.at(far, me.b, me.c))

    def cut_from(k):
        far = lax.rem(me.a + k, planes)
        there = cut_all.at[far]
        push(there, there, psend.at[k], precv.at[far], me.at(far, me.b, me.c)).wait_recv()

    for k in range(1, planes):
        cut_to(k).start()
    keep = pltpu.make_async_copy(cut_ref.at[me.a], cut_all.at[me.a], lsem.at[0])
    keep.start()

    def column_in(k):
        far = lax.rem(me.a + k, planes)
        return pltpu.make_async_copy(column_ref.at[far], column.at[far], lsem.at[k])

    for k in range(1, planes):
        column_in(k).start()
    column[me.a] = o_ref[...]
    stack_heads(qs, q_ref, group)
    stack_heads(gs, g_ref, group)
    stack_heads(qacc, o_ref, group)

    def prepare(item, c):
        part = jnp.sum(gs[item].astype(f32) * qacc[item], axis=1, keepdims=True)
        delta[item] = jnp.broadcast_to(part, delta.shape[1:])
        qacc[item] = jnp.zeros(qacc.shape[1:], f32)
        return c

    lax.fori_loop(0, items, prepare, 0)

    def block(item, sa):
        keys_here = joined(block_heads(all_ref, sa, item, keys, size, 0))
        values = joined(block_heads(all_ref, sa, item, keys, size, 1))
        queries, grads = qs[item], gs[item]
        scores = over(queries, keys_here, NT) * factor
        probs = jnp.exp(scores - log_ref[item][:, :1])
        prob_grads = over(grads, values, NT)
        score_grads = (probs * (prob_grads - delta[item][:, :1])).astype(bf16)
        qacc[item] += over(score_grads, keys_here, NN)
        key_part = (over(score_grads, queries, TN) * factor).astype(bf16)
        value_part = over(probs.astype(bf16), grads, TN).astype(bf16)
        seg = key_part.shape[0] // 4
        for part, value in ((0, key_part), (1, value_part)):
            for q, ref in enumerate(block_heads(mine, sa, item, keys, size, part)):
                ref[...] = value[q * seg : (q + 1) * seg, :]
        return sa

    def send_c(sa, sb):
        slot = sa * 2 + sb
        src = mine.at[me.index(sa, sb, 1 - me.c)]
        return push(src, landc.at[slot], ssem.at[0, slot], rsem.at[0, slot], me.at(me.a, me.b, 1 - me.c))

    def send_b(sa):
        src = mine.at[me.index(sa, 1 - me.b, me.c)]
        return push(src, landb.at[sa], ssem.at[1, sa], rsem.at[1, sa], me.at(me.a, 1 - me.b, me.c))

    def send_a(sa):
        src = mine.at[me.index(sa, me.b, me.c)]
        return push(src, landa.at[me.a], ssem.at[2, sa], rsem.at[2, me.a], me.at(sa, me.b, me.c))

    def from_c(sa):
        for sb in (1 - me.b, me.b):
            slot = sa * 2 + sb
            push(landc.at[slot], landc.at[slot], ssem.at[0, slot], rsem.at[0, slot], me.at(me.a, me.b, 1 - me.c)).wait_recv()
            idx = me.index(sa, sb, me.c)
            add_rows(mine.at[idx], [mine.at[idx], landc.at[slot]])
            if sb is not me.b:
                send_b(sa).start()

    def from_b(sa):
        push(landb.at[sa], landb.at[sa], ssem.at[1, sa], rsem.at[1, sa], me.at(me.a, 1 - me.b, me.c)).wait_recv()
        idx = me.index(sa, me.b, me.c)
        return mine.at[idx], [mine.at[idx], landb.at[sa]]

    def along(sa):
        target, parts = from_b(sa)
        add_rows(target, parts)
        send_a(sa).start()

    def finish():
        target, parts = from_b(me.a)
        add_rows(pair_grad, parts)
        for far in range(1, planes):

            @pl.when(far > me.a)
            def _(far=far):
                push(landa.at[far], landa.at[far], ssem.at[2, far], rsem.at[2, far], me.at(far, me.b, me.c)).wait_recv()
                add_rows(pair_grad, [pair_grad, landa.at[far]])

    def mix():
        share = mixing_ref.shape[1]
        keep.wait()
        for k in range(1, planes):
            cut_from(k)
            column_in(k).wait()
        tokens = column.shape[0] * column.shape[1]
        for n in range(0, column.shape[2], 512):
            rows = column[:, :, n : n + 512].reshape(tokens, 512)
            part = over(cut_all[...].reshape(tokens, 4 * share), rows, TN).astype(bf16)
            for q in range(4):
                mixing_ref[q, :, n : n + 512] = part[q * share : (q + 1) * share]

    def step(sa, c):
        lax.fori_loop(0, items, block, sa)
        for sb in (1 - me.b, me.b):
            send_c(sa, sb).start()

        @pl.when(sa >= 1)
        def _():
            from_c(sa - 1)

        @pl.when(sa >= 2)
        def _():
            along(sa - 2)

        return c

    lax.fori_loop(0, me.a + 1, step, 0)
    mix()

    def unturned(grads, raw, gain):
        turned = grads * turn_ref[0] + pltpu.roll(grads, size // 2, 1) * turn_ref[1]
        scale = lax.rsqrt(jnp.mean(raw * raw, axis=1, keepdims=True) + epsilon)
        scaled = gain * turned
        level = jnp.mean(scaled * raw, axis=1, keepdims=True)
        return scale * scaled - raw * (scale * scale * scale * level), jnp.sum(turned * raw * scale, axis=0, keepdims=True)

    seg = rows // group
    gain_grad[...] = jnp.zeros_like(gain_grad)

    def query_item(item, c):
        at = pl.ds(pl.multiple_of(lax.div(item, keys) * seg, seg), seg)
        total = jnp.zeros((1, size), f32)
        for h in range(group):
            cols = pl.ds(pl.multiple_of((lax.rem(item, keys) * group + h) * size, size), size)
            grads = qacc[item, h * seg : (h + 1) * seg, :] * factor
            value, part = unturned(grads, query_raw[at, cols], gain_ref[0:1, :])
            low_ref[at, cols] = value.astype(bf16)
            total = total + part
        gain_grad[0:1, :] += total
        return c

    lax.fori_loop(0, items, query_item, 0)
    from_c(me.a)

    @pl.when(me.a > 0)
    def _():
        along(me.a - 1)

    finish()
    width = query_raw.shape[1]
    for item in range(items):
        s, k = item // keys, item % keys
        at = slice(s * seg, (s + 1) * seg)
        cols = slice(k * size, (k + 1) * size)
        value, part = unturned(pair_grad[at, cols], key_raw[at, cols], gain_ref[1:2, :])
        low_ref[at, width + k * size : width + (k + 1) * size] = value.astype(bf16)
        gain_grad[1:2, :] += part
    low_ref[:, width + keys * size :] = pair_grad[:, keys * size :].astype(bf16)

    def settle(sa, c):
        for sb in (1 - me.b, me.b):
            send_c(sa, sb).wait_send()
        send_b(sa).wait_send()

        @pl.when(sa < me.a)
        def _():
            send_a(sa).wait_send()

        return c

    lax.fori_loop(0, me.a + 1, settle, 0)
    for k in range(1, planes):
        cut_to(k).wait_send()


def attend_back(query, grads, context, pairs_all, logs, cut, column, raws, gains, turns, planes, group, size, cid):
    f32, bf16 = jnp.float32, jnp.bfloat16
    tokens, width = query.shape
    items = logs.shape[0]
    state = logs.shape
    block = pairs_all.shape[1:]
    share = cut.shape[2] // 4
    inside = pl.BlockSpec(memory_space=pltpu.VMEM)
    anywhere = pl.BlockSpec(memory_space=pl.ANY)
    return pl.pallas_call(
        functools.partial(attend_back_kernel, planes, group),
        out_shape=[
            jax.ShapeDtypeStruct((tokens, width + block[1]), bf16),
            jax.ShapeDtypeStruct((8, size), f32),
            jax.ShapeDtypeStruct((4, share, width), bf16),
        ],
        in_specs=[inside] * 5 + [anywhere] * 2 + [inside] * 4,
        out_specs=[inside] * 3,
        scratch_shapes=[
            pltpu.VMEM(block, f32),
            pltpu.VMEM(cut.shape, bf16),
            pltpu.VMEM(column.shape, bf16),
            pltpu.VMEM(state, bf16),
            pltpu.VMEM(state, bf16),
            pltpu.VMEM(state, f32),
            pltpu.VMEM(state, f32),
            pltpu.VMEM((4 * planes,) + block, bf16),
            pltpu.VMEM((2 * planes,) + block, bf16),
            pltpu.VMEM((planes,) + block, bf16),
            pltpu.VMEM((planes,) + block, bf16),
            pltpu.SemaphoreType.DMA((3, 2 * planes)),
            pltpu.SemaphoreType.DMA((3, 2 * planes)),
            pltpu.SemaphoreType.DMA((planes,)),
            pltpu.SemaphoreType.DMA((planes,)),
            pltpu.SemaphoreType.DMA((planes,)),
        ],
        compiler_params=pltpu.CompilerParams(collective_id=cid, has_side_effects=True, vmem_limit_bytes=ROOM),
        name="attend_back",
    )(query, grads, context, pairs_all, logs, cut, column, raws[0], raws[1], gains, turns)


def weights_kernel(
    planes,
    chunk,
    low_ref,
    cut_ref,
    query_w,
    key_w,
    value_w,
    input_ref,
    gain_ref,
    grad_ref,
    small_ref,
    mixing_part,
    rows_ref,
    input_grad,
    total_ref,
    mixing_rows,
    low_all,
    mixed,
    mixc,
    mixb,
    weights,
    sums,
    landz,
    normed,
    normed_other,
    gains_other,
    send,
    land,
    wload,
    lsend,
    lrecv,
    msend,
    mrecv,
    mload,
    zsend,
    zrecv,
    nsend,
    nrecv,
    tsend,
    trecv,
):
    me = Spot()
    f32, bf16 = jnp.float32, jnp.bfloat16
    tokens, packed = low_ref.shape
    width = input_ref.shape[1]
    chunks = packed // chunk
    assert chunks == 10
    place = lax.rem(me.e, 4)
    base = me.e - place
    share = sums.shape[1] // planes

    def spot(b, c):
        return me.index(0, b, c)

    near = [(1 - me.b, me.c), (me.b, 1 - me.c), (1 - me.b, 1 - me.c)]
    peers = [(base + spot(b, c), me.t) for b, c in near]
    barrier = pltpu.get_barrier_semaphore()
    for who in peers + [me.core()] + [me.at(lax.rem(me.a + k, planes), me.b, me.c) for k in range(1, planes)]:
        pl.semaphore_signal(barrier, inc=1, device_id=who, device_id_type=MESH)
    pl.semaphore_wait(barrier, 3 + planes)

    def cols(k):
        return pl.ds(pl.multiple_of(k * chunk, chunk), chunk)

    def whole(i, k):
        return push(low_ref.at[:, cols(k)], low_all.at[place, :, cols(k)], lsend.at[i, k], lrecv.at[i, k], peers[i])

    first = spot(*near[0])

    def relay(k):
        there = low_all.at[first, :, cols(k)]
        return push(there, there, lsend.at[2, k], lrecv.at[2, k], peers[1])

    quarters = [spot(b, c) for b, c in ((1 - me.b, 1 - me.c), (me.b, 1 - me.c), (1 - me.b, me.c), (me.b, me.c))]

    def mix_c(i):
        return push(mixing_part.at[quarters[i]], mixc.at[i], msend.at[i], mrecv.at[i], peers[1])

    def mix_b():
        return push(mixed.at[0], mixb, msend.at[2], mrecv.at[2], peers[0])

    mix_loads = [pltpu.make_async_copy(mixing_part.at[quarters[2 + i]], mixed.at[i], mload.at[i]) for i in range(2)]

    def mix_round(k):
        if k == chunks - 2:
            for i in range(2):
                mix_c(i).start()
        if k == chunks:
            for i in range(2):
                mix_loads[i].wait()
                mix_c(i).wait_recv()
                add_rows(mixed.at[i], [mixed.at[i], mixc.at[i]])
                if i == 0:
                    mix_b().start()
        if k == chunks + 1:
            mix_b().wait_recv()
            add_rows(mixing_rows, [mixed.at[1], mixb])

    def send_low(k, c):
        whole(0, k).start()
        return c

    lax.fori_loop(0, chunks, send_low, 0)
    whole(1, 0).start()
    whole(1, 1).start()
    for k in mix_loads:
        k.start()
    query_width, key_width = query_w.shape[1], key_w.shape[1]
    loads = [
        pltpu.make_async_copy(query_w, weights.at[:, :query_width], wload.at[0]),
        pltpu.make_async_copy(key_w, weights.at[:, query_width : query_width + key_width], wload.at[1]),
        pltpu.make_async_copy(value_w, weights.at[:, query_width + key_width :], wload.at[2]),
    ]
    for k in loads:
        k.start()
    gains = push(small_ref.at[pl.ds(0, 8)], gains_other, nsend.at[4], nrecv.at[4], me.core())
    gains.start()
    low_all[place] = low_ref[...]
    quarter = width // 4

    def trade(n):
        at = pl.ds(pl.multiple_of(n * quarter, quarter), quarter)
        return push(normed.at[:, at], normed_other.at[:, at], nsend.at[n], nrecv.at[n], me.core())

    def normed_cols(n, c):
        at = pl.ds(pl.multiple_of(n * quarter, quarter), quarter)
        normed[:, at] = over(low_ref[...], weights[at, :], NT).astype(bf16)
        trade(n).start()
        return c

    def await_trade(n, c):
        trade(n).wait_recv()
        return c


    def input_rows(r, total):
        at = pl.ds(pl.multiple_of(r * 16, 16), 16)
        grads = normed[at, :].astype(f32) + normed_other[at, :].astype(f32)
        inputs = input_ref[at, :].astype(f32)
        scale = lax.rsqrt(jnp.mean(inputs * inputs, axis=1, keepdims=True) + epsilon)
        scaled = gain_ref[...] * grads
        level = jnp.mean(scaled * inputs, axis=1, keepdims=True)
        input_grad[at, :] = grad_ref[at, :] + scale * scaled - inputs * (scale * scale * scale * level)
        return total + jnp.sum(grads * inputs * scale, axis=0, keepdims=True)

    def norm_round(k):
        if k == 0:
            for copy in loads:
                copy.wait()
        if k < 4:
            lax.fori_loop(k, k + 1, normed_cols, 0)
        if k == 4:
            gains.wait()
            total_ref[...] = small_ref[...]
            total_ref[0:8, :] += gains_other[...]
            lax.fori_loop(0, 4, await_trade, 0)
            total_ref[8:9, :] = lax.fori_loop(0, tokens // 16, input_rows, jnp.zeros((1, width), f32))
            send[0] = total_ref[ours, :]

    half = total_ref.shape[0] // 2
    ours = pl.ds(pl.multiple_of(me.t * half, half), half)
    others = pl.ds(pl.multiple_of((1 - me.t) * half, half), half)
    bits = [1, 2, 4, 8]

    def small(j):
        bit = bits[j]
        who = (me.e + bit * (1 - 2 * lax.rem(lax.div(me.e, bit), 2)), me.t)
        return push(send.at[j], land.at[j], tsend.at[j], trecv.at[j], who)

    share_back = push(send.at[4], land.at[4], tsend.at[4], trecv.at[4], me.core())

    def small_round(j):
        if j > 0:
            small(j - 1).wait_recv()
            if j < 4:
                send[j] = send[j - 1] + land[j - 1]
            else:
                send[4] = send[3] + land[3]
                share_back.start()
        if j < 4:
            small(j).start()


    def block(k, d):
        return sums.at[k, pl.ds(pl.multiple_of(d * share, share), share)]

    def along(k, d, up):
        arrive = me.a + 1 if up else me.a - 1
        slot = d if up else jnp.where(d == arrive, planes, d)
        return push(block(k, d), landz.at[k, slot], zsend.at[k, d], zrecv.at[k, slot], me.at(arrive, me.b, me.c))

    def landed(k, slot):
        push(landz.at[k, slot], landz.at[k, slot], zsend.at[k, 0], zrecv.at[k, slot], me.core()).wait_recv()

    def chain(k, act, ends):
        for i in range(planes - 1):
            d = far_first(me.a, planes, i)
            up = d > me.a
            inner = (up & (me.a > 0)) | (jnp.logical_not(up) & (me.a + 1 < planes))

            @pl.when(jnp.logical_not(inner) if ends else inner)
            def _(d=d, up=up):
                if act and not ends:
                    landed(k, d)
                    add_rows(block(k, d), [block(k, d), landz.at[k, d]])

                @pl.when(up)
                def _():
                    along(k, d, True).start() if act else along(k, d, True).wait_send()

                @pl.when(jnp.logical_not(up))
                def _():
                    along(k, d, False).start() if act else along(k, d, False).wait_send()

    def finish(k):
        target = rows_ref.at[:, cols(k)]
        own = block(k, me.a)

        @pl.when(me.a > 0)
        def _():
            landed(k, me.a)

        @pl.when(me.a + 1 < planes)
        def _():
            landed(k, planes)

        @pl.when((me.a > 0) & (me.a + 1 < planes))
        def _():
            add_rows(target, [own, landz.at[k, me.a], landz.at[k, planes]])

        @pl.when(me.a == 0)
        def _():
            add_rows(target, [own, landz.at[k, planes]])

        @pl.when(me.a + 1 == planes)
        def _():
            add_rows(target, [own, landz.at[k, me.a]])

    def forward(k):
        whole(0, k).wait_recv()
        relay(k).start()
        if k + 2 < chunks:
            whole(1, k + 2).start()

    for k in range(chunks + 2):
        if k < chunks:
            if k == 0:
                forward(0)
            if k + 1 < chunks:
                forward(k + 1)
            whole(1, k).wait_recv()
            relay(k).wait_recv()
            mixed_rows = low_all[:, :, k * chunk : (k + 1) * chunk].reshape(4 * tokens, chunk)
            sums[k] = over(cut_ref[...], mixed_rows, NN).astype(bf16)
            chain(k, True, True)
        norm_round(k)
        if k in (4, 6, 8, 10, 11):
            small_round((4, 6, 8, 10, 11).index(k))
        if 1 <= k <= chunks:
            chain(k - 1, True, False)
        if k >= 2:
            finish(k - 2)
        mix_round(k)

    def settle(k, c):
        for i in range(2):
            whole(i, k).wait_send()
        relay(k).wait_send()
        chain(k, False, True)
        chain(k, False, False)
        return c

    lax.fori_loop(0, chunks, settle, 0)
    for k in (mix_c(0), mix_c(1), mix_b()):
        k.wait_send()
    for n in range(4):
        trade(n).wait_send()
        small(n).wait_send()
    share_back.wait_send()
    share_back.wait_recv()
    total_ref[ours, :] = send[4]
    total_ref[others, :] = land[4]


def weight_grads(low, cut, query_w, key_w, value_w, inputs, gain, residual_grad, small, mixing, planes, cid):
    f32, bf16 = jnp.float32, jnp.bfloat16
    tokens, packed = low.shape
    width = inputs.shape[1]
    chunk = 256
    chunks = packed // chunk
    share = cut.shape[0] // planes
    quarter = mixing.shape[1:]
    inside = pl.BlockSpec(memory_space=pltpu.VMEM)
    anywhere = pl.BlockSpec(memory_space=pl.ANY)
    half = (small.shape[0] // 2, small.shape[1])
    return pl.pallas_call(
        functools.partial(weights_kernel, planes, chunk),
        out_shape=[
            jax.ShapeDtypeStruct((share, packed), f32),
            jax.ShapeDtypeStruct((tokens, width), f32),
            jax.ShapeDtypeStruct(small.shape, f32),
            jax.ShapeDtypeStruct(quarter, f32),
        ],
        in_specs=[inside, inside, anywhere, anywhere, anywhere, inside, inside, inside, inside, anywhere],
        out_specs=[inside] * 4,
        scratch_shapes=[
            pltpu.VMEM((4, tokens, packed), bf16),
            pltpu.VMEM((2,) + quarter, bf16),
            pltpu.VMEM((2,) + quarter, bf16),
            pltpu.VMEM(quarter, bf16),
            pltpu.VMEM((width, packed), bf16),
            pltpu.VMEM((chunks, planes * share, chunk), bf16),
            pltpu.VMEM((chunks, planes + 1, share, chunk), bf16),
            pltpu.VMEM((tokens, width), bf16),
            pltpu.VMEM((tokens, width), bf16),
            pltpu.VMEM((8, width), f32),
            pltpu.VMEM((5,) + half, f32),
            pltpu.VMEM((5,) + half, f32),
            pltpu.SemaphoreType.DMA((3,)),
            pltpu.SemaphoreType.DMA((3, chunks)),
            pltpu.SemaphoreType.DMA((3, chunks)),
            pltpu.SemaphoreType.DMA((3,)),
            pltpu.SemaphoreType.DMA((3,)),
            pltpu.SemaphoreType.DMA((2,)),
            pltpu.SemaphoreType.DMA((chunks, planes)),
            pltpu.SemaphoreType.DMA((chunks, planes + 1)),
            pltpu.SemaphoreType.DMA((5,)),
            pltpu.SemaphoreType.DMA((5,)),
            pltpu.SemaphoreType.DMA((5,)),
            pltpu.SemaphoreType.DMA((5,)),
        ],
        compiler_params=pltpu.CompilerParams(collective_id=cid, has_side_effects=True, vmem_limit_bytes=ROOM),
        name="weight_grads",
    )(low, cut, query_w, key_w, value_w, inputs, gain, residual_grad, small, mixing)


epsilon = 1e-06
rope_base = 1000000.0
far_below = -1e30


def rms_scaled(values, gain_vec):
    return (
        values * lax.rsqrt(jnp.mean(values * values, axis=-1, keepdims=True) + epsilon) * gain_vec
    )


def rotary_tables(positions, head_dim):
    halfway = head_dim // 2
    exponents = jnp.arange(halfway, dtype=jnp.float32) * (2.0 / head_dim)
    inverse = jnp.exp(-exponents * jnp.log(jnp.float32(rope_base)))
    angles = positions.astype(jnp.float32)[:, None] * inverse[None, :]
    return (jnp.cos(angles), jnp.sin(angles))


def rotate(values, cosine, sine_table):
    halfway = values.shape[-1] // 2
    first = values[..., :halfway]
    latter = values[..., halfway:]
    return jnp.concatenate(
        [first * cosine - latter * sine_table, latter * cosine + first * sine_table], axis=-1
    )


def glu_value(gate_act, up_act):
    return jax.nn.silu(gate_act) * up_act


def on_device(
    layer_input,
    norm_first,
    query_weight,
    key_weight,
    value_weight,
    mixing_weight,
    query_gain,
    key_gain,
    norm_second,
    router_weight,
    gate_weight,
    up_weight,
    down_weight,
    routes,
    fill_order,
    cotangent,
):
    seq_count, seg_len, model_width = layer_input.shape
    expert_count = lax.axis_size("expert")
    tensor_count = lax.axis_size("tensor")
    expert_idx = lax.axis_index("expert")
    tensor_idx = lax.axis_index("tensor")
    head_dim = query_gain.shape[0]
    local_queries = query_weight.shape[1] // head_dim
    local_keys = key_weight.shape[1] // head_dim
    group_size = local_queries // local_keys
    seq_length = seg_len * expert_count
    top_count = routes.shape[2]
    token_count = seq_count * seg_len
    capacity = 5 * token_count * top_count // (4 * expert_count)
    half_width = model_width // tensor_count
    factor = head_dim ** (-0.5)
    inputs = layer_input.astype(jnp.float32)
    normed_f, first_back = jax.vjp(rms_scaled, inputs, norm_first)
    normed = normed_f.astype(jnp.bfloat16)
    positions = expert_idx * seg_len + jnp.arange(seg_len, dtype=jnp.int32)
    cosine, sine_table = rotary_tables(positions, head_dim)
    cosine = cosine[:, None, :]
    sine_table = sine_table[:, None, :]

    def rope_norm(raw_heads, gain_vec):
        return rotate(rms_scaled(raw_heads, gain_vec), cosine, sine_table)

    query_raw = jnp.dot(normed, query_weight, preferred_element_type=jnp.float32).reshape(
        seq_count, seg_len, local_queries, head_dim
    )
    key_raw = jnp.dot(normed, key_weight, preferred_element_type=jnp.float32).reshape(
        seq_count, seg_len, local_keys, head_dim
    )
    value_local = jnp.dot(normed, value_weight, preferred_element_type=jnp.float32).astype(
        jnp.bfloat16
    )
    query_rot, query_back = jax.vjp(rope_norm, query_raw, query_gain)
    key_rot, key_back = jax.vjp(rope_norm, key_raw, key_gain)
    key_local = key_rot.astype(jnp.bfloat16).reshape(seq_count, seg_len, local_keys * head_dim)
    key_all, value_all = (
        lax.all_gather(key_local, "expert", axis=1, tiled=True),
        lax.all_gather(value_local, "expert", axis=1, tiled=True),
    )
    key_tiles = key_all.reshape(seq_count, seq_length, local_keys, head_dim)
    value_tiles = value_all.reshape(seq_count, seq_length, local_keys, head_dim)
    query_rows = query_rot.astype(jnp.bfloat16).reshape(
        seq_count, seg_len, local_keys, group_size, head_dim
    )
    query_rows = query_rows.transpose(0, 2, 3, 1, 4).reshape(
        seq_count, local_keys, group_size * seg_len, head_dim
    )
    row_block = (
        expert_idx * seg_len + jnp.arange(group_size * seg_len, dtype=jnp.int32) % seg_len
    ) // BLOCK
    tile_len = min(512, seq_length)
    reach_end = jnp.minimum(((expert_idx + 1) * seg_len - 1) // BLOCK * BLOCK + BLOCK, seq_length)
    tile_count = (reach_end + tile_len - 1) // tile_len

    def tile_scores(tile_idx):
        offset = tile_idx * tile_len
        key_part = lax.dynamic_slice_in_dim(key_tiles, offset, tile_len, 1)
        scores = (
            jnp.einsum("shrd,skhd->shrk", query_rows, key_part, preferred_element_type=jnp.float32)
            * factor
        )
        key_block = (offset + jnp.arange(tile_len, dtype=jnp.int32)) // BLOCK
        allowed = key_block[None, :] <= row_block[:, None]
        return (scores, allowed, offset)

    stat_shape = (seq_count, local_keys, group_size * seg_len)

    def stats_step(tile_idx, state_pair):
        running_max, running_sum = state_pair
        scores, allowed, offset = tile_scores(tile_idx)
        masked = jnp.where(allowed, scores, far_below)
        new_max = jnp.maximum(running_max, jnp.max(masked, axis=-1))
        exp_terms = jnp.where(allowed, jnp.exp(masked - new_max[..., None]), 0.0)
        return (new_max, running_sum * jnp.exp(running_max - new_max) + jnp.sum(exp_terms, axis=-1))

    row_max, row_sum = lax.fori_loop(
        0,
        tile_count,
        stats_step,
        (jnp.full(stat_shape, far_below, jnp.float32), jnp.zeros(stat_shape, jnp.float32)),
    )
    log_total = row_max + jnp.log(row_sum)

    def probabilities(tile_idx):
        scores, allowed, offset = tile_scores(tile_idx)
        return (jnp.where(allowed, jnp.exp(scores - log_total[..., None]), 0.0), offset)

    def context_step(tile_idx, context_sum):
        prob_tile, offset = probabilities(tile_idx)
        value_part = lax.dynamic_slice_in_dim(value_tiles, offset, tile_len, 1)
        return context_sum + jnp.einsum(
            "shrk,skhd->shrd",
            prob_tile.astype(jnp.bfloat16),
            value_part,
            preferred_element_type=jnp.float32,
        )

    context_f = lax.fori_loop(0, tile_count, context_step, jnp.zeros(query_rows.shape, jnp.float32))
    shaped = context_f.reshape(seq_count, local_keys, group_size, seg_len, head_dim).transpose(
        0, 3, 1, 2, 4
    )
    context = shaped.reshape(seq_count, seg_len, local_queries * head_dim).astype(jnp.bfloat16)
    head_part = jnp.dot(context, mixing_weight, preferred_element_type=jnp.float32)
    residual = inputs + lax.psum(head_part.astype(jnp.bfloat16), "tensor").astype(jnp.float32)
    second_f, second_back = jax.vjp(rms_scaled, residual, norm_second)
    second = second_f.astype(jnp.bfloat16).reshape(token_count, model_width)
    logits = jnp.dot(second, router_weight, preferred_element_type=jnp.float32)
    flat_routes = routes.reshape(token_count, top_count)
    picked = (flat_routes[:, :, None] == jnp.arange(expert_count, dtype=jnp.int32)).astype(
        jnp.float32
    )
    gates = jax.nn.softmax(jnp.sum(picked * logits[:, None, :], axis=-1), axis=-1)
    usages = jnp.sum(picked, axis=1)
    ranking = fill_order.reshape(token_count)
    before = (ranking[None, :] < ranking[:, None]).astype(jnp.bfloat16)
    counts = jnp.dot(before, usages.astype(jnp.bfloat16), preferred_element_type=jnp.float32)
    slot_ids = jnp.sum(picked * counts[:, None, :], axis=-1).astype(jnp.int32)
    kept_mask = slot_ids < capacity
    kept_float = kept_mask.astype(jnp.float32)
    weighted = gates * kept_float
    places = jnp.where(kept_mask, flat_routes * capacity + slot_ids, -1)
    slot_grid = jnp.arange(expert_count * capacity, dtype=jnp.int32)
    assign = (places[:, :, None] == slot_grid).astype(jnp.bfloat16)
    placed = jnp.sum(assign, axis=1)
    combine = jnp.sum(weighted[:, :, None] * assign.astype(jnp.float32), axis=1)
    send_rows = jnp.einsum("tp,td->pd", placed, second, preferred_element_type=jnp.float32).astype(
        jnp.bfloat16
    )
    arrived = lax.all_to_all(
        send_rows.reshape(expert_count, capacity, model_width),
        "expert",
        split_axis=0,
        concat_axis=0,
        tiled=True,
    )
    arrived = arrived.reshape(expert_count * capacity, model_width)
    gate_one = gate_weight[0]
    up_one = up_weight[0]
    down_one = down_weight[0]
    gate_act = jnp.dot(arrived, gate_one, preferred_element_type=jnp.float32)
    up_act = jnp.dot(arrived, up_one, preferred_element_type=jnp.float32)
    hidden_val, glu_back = jax.vjp(glu_value, gate_act, up_act)
    hidden = hidden_val.astype(jnp.bfloat16)
    expert_part = jnp.dot(hidden, down_one, preferred_element_type=jnp.float32)
    summed = lax.psum(expert_part.astype(jnp.bfloat16), "tensor")
    returned = lax.all_to_all(
        summed.reshape(expert_count, capacity, model_width),
        "expert",
        split_axis=0,
        concat_axis=0,
        tiled=True,
    )
    returned = returned.reshape(expert_count * capacity, model_width)
    per_route = (
        jnp.take(returned, jnp.maximum(places, 0), axis=0).astype(jnp.float32)
        * kept_float[:, :, None]
    )
    mixture = residual.reshape(token_count, model_width) + jnp.sum(
        weighted[:, :, None] * per_route, axis=1
    )
    layer_output = lax.dynamic_slice_in_dim(mixture, tensor_idx * half_width, half_width, 1)
    layer_output = layer_output.astype(jnp.bfloat16).reshape(seq_count, seg_len, half_width)
    upstream = cotangent.astype(jnp.float32).reshape(token_count, model_width)
    gate_grads = jnp.sum(upstream[:, None, :] * per_route, axis=-1) * kept_float
    send_grads = jnp.einsum(
        "tp,td->pd",
        combine,
        upstream,
        precision=lax.Precision.HIGHEST,
        preferred_element_type=jnp.float32,
    ).astype(jnp.bfloat16)
    grads_in = lax.all_to_all(
        send_grads.reshape(expert_count, capacity, model_width),
        "expert",
        split_axis=0,
        concat_axis=0,
        tiled=True,
    )
    grads_in = grads_in.reshape(expert_count * capacity, model_width)
    hidden_grad = lax.dot_general(
        grads_in, down_one, (((1,), (1,)), ((), ())), preferred_element_type=jnp.float32
    )
    down_grad = jnp.einsum("rf,rd->fd", hidden, grads_in, preferred_element_type=jnp.float32)
    gate_d, up_d = glu_back(hidden_grad)
    gate_d = gate_d.astype(jnp.bfloat16)
    up_d = up_d.astype(jnp.bfloat16)
    gate_grad = jnp.einsum("rd,rf->df", arrived, gate_d, preferred_element_type=jnp.float32)
    up_grad = jnp.einsum("rd,rf->df", arrived, up_d, preferred_element_type=jnp.float32)
    row_part = lax.dot_general(
        gate_d, gate_one, (((1,), (1,)), ((), ())), preferred_element_type=jnp.float32
    )
    row_part = row_part + lax.dot_general(
        up_d, up_one, (((1,), (1,)), ((), ())), preferred_element_type=jnp.float32
    )
    row_share = lax.psum_scatter(
        row_part.reshape(expert_count, capacity, model_width).astype(jnp.bfloat16),
        "tensor",
        scatter_dimension=2,
        tiled=True,
    )
    row_home = lax.all_to_all(row_share, "expert", split_axis=0, concat_axis=0, tiled=True).reshape(
        expert_count * capacity, half_width
    )
    second_half = jnp.dot(placed, row_home, preferred_element_type=jnp.float32)
    route_grads = gates * (gate_grads - jnp.sum(gates * gate_grads, axis=-1, keepdims=True))
    logit_grads = jnp.sum(picked * route_grads[:, :, None], axis=1).astype(jnp.bfloat16)
    router_grad = jnp.einsum("td,te->de", second, logit_grads, preferred_element_type=jnp.float32)
    router_back = lax.dot_general(
        logit_grads, router_weight, (((1,), (1,)), ((), ())), preferred_element_type=jnp.float32
    )
    own_part = second_half + lax.dynamic_slice_in_dim(
        router_back, tensor_idx * half_width, half_width, 1
    )
    second_part = lax.dynamic_update_slice_in_dim(
        jnp.zeros((token_count, model_width), jnp.float32), own_part, tensor_idx * half_width, 1
    )
    residual_part, norm_part = second_back(second_part.reshape(seq_count, seg_len, model_width))
    residual_grad, second_grad = (
        lax.psum(residual_part.astype(jnp.bfloat16), "tensor").astype(jnp.float32),
        lax.psum(norm_part.astype(jnp.bfloat16), "tensor").astype(jnp.float32),
    )
    residual_grad = residual_grad + upstream.reshape(seq_count, seg_len, model_width)
    head_in = residual_grad.astype(jnp.bfloat16)
    mixing_part = jnp.einsum("std,stc->dc", head_in, context, preferred_element_type=jnp.float32)
    context_grad = lax.dot_general(
        head_in, mixing_weight, (((2,), (1,)), ((), ())), preferred_element_type=jnp.float32
    ).astype(jnp.bfloat16)
    grad_rows = context_grad.reshape(
        seq_count, seg_len, local_keys, group_size, head_dim
    ).transpose(0, 2, 3, 1, 4)
    grad_rows = grad_rows.reshape(query_rows.shape)
    delta_rows = jnp.sum(grad_rows.astype(jnp.float32) * context_f, axis=-1)
    key_shape = (seq_count, seq_length, local_keys, head_dim)

    def gradient_step(tile_idx, state_trio):
        query_acc, key_acc, value_acc = state_trio
        prob_tile, offset = probabilities(tile_idx)
        key_part = lax.dynamic_slice_in_dim(key_tiles, offset, tile_len, 1)
        value_part = lax.dynamic_slice_in_dim(value_tiles, offset, tile_len, 1)
        prob_low = prob_tile.astype(jnp.bfloat16)
        prob_grad = jnp.einsum(
            "shrd,skhd->shrk", grad_rows, value_part, preferred_element_type=jnp.float32
        )
        score_grad = (prob_tile * (prob_grad - delta_rows[..., None])).astype(jnp.bfloat16)
        query_acc = query_acc + jnp.einsum(
            "shrk,skhd->shrd", score_grad, key_part, preferred_element_type=jnp.float32
        )
        key_tile = jnp.einsum(
            "shrk,shrd->skhd", score_grad, query_rows, preferred_element_type=jnp.float32
        )
        value_tile = jnp.einsum(
            "shrk,shrd->skhd", prob_low, grad_rows, preferred_element_type=jnp.float32
        )
        key_acc = lax.dynamic_update_slice_in_dim(key_acc, key_tile, offset, 1)
        value_acc = lax.dynamic_update_slice_in_dim(value_acc, value_tile, offset, 1)
        return (query_acc, key_acc, value_acc)

    start_state = (
        jnp.zeros(query_rows.shape, jnp.float32),
        jnp.zeros(key_shape, jnp.float32),
        jnp.zeros(key_shape, jnp.float32),
    )
    query_acc, key_acc, value_acc = lax.fori_loop(0, tile_count, gradient_step, start_state)
    key_grad_all, value_grad_all = (
        lax.psum_scatter(
            (key_acc * factor).reshape(seq_count, seq_length, local_keys * head_dim),
            "expert",
            scatter_dimension=1,
            tiled=True,
        ),
        lax.psum_scatter(
            value_acc.reshape(seq_count, seq_length, local_keys * head_dim),
            "expert",
            scatter_dimension=1,
            tiled=True,
        ),
    )
    key_raw_grad, keygain_part = key_back(
        key_grad_all.reshape(seq_count, seg_len, local_keys, head_dim)
    )
    query_shaped = (
        (query_acc * factor)
        .reshape(seq_count, local_keys, group_size, seg_len, head_dim)
        .transpose(0, 3, 1, 2, 4)
    )
    query_raw_grad, querygain_part = query_back(
        query_shaped.reshape(seq_count, seg_len, local_queries, head_dim)
    )
    query_low = query_raw_grad.astype(jnp.bfloat16).reshape(
        seq_count, seg_len, local_queries * head_dim
    )
    key_low = key_raw_grad.astype(jnp.bfloat16).reshape(seq_count, seg_len, local_keys * head_dim)
    value_low = value_grad_all.astype(jnp.bfloat16)
    query_sum = jnp.einsum("std,stc->dc", normed, query_low, preferred_element_type=jnp.float32)
    keys_sum = jnp.einsum("std,stc->dc", normed, key_low, preferred_element_type=jnp.float32)
    values_sum = jnp.einsum("std,stc->dc", normed, value_low, preferred_element_type=jnp.float32)
    query_grad, key_grad, value_grad, mixing_rows = (
        lax.psum_scatter(query_sum, "expert", scatter_dimension=0, tiled=True),
        lax.psum_scatter(keys_sum, "expert", scatter_dimension=0, tiled=True),
        lax.psum_scatter(values_sum, "expert", scatter_dimension=0, tiled=True),
        lax.psum_scatter(mixing_part, "expert", scatter_dimension=0, tiled=True),
    )
    mixing_grad = mixing_rows.T
    normed_part = lax.dot_general(
        query_low, query_weight, (((2,), (1,)), ((), ())), preferred_element_type=jnp.float32
    )
    normed_part = normed_part + lax.dot_general(
        key_low, key_weight, (((2,), (1,)), ((), ())), preferred_element_type=jnp.float32
    )
    normed_part = normed_part + lax.dot_general(
        value_low, value_weight, (((2,), (1,)), ((), ())), preferred_element_type=jnp.float32
    )
    normed_grad, querygain_grad, keygain_grad = (
        lax.psum(normed_part.astype(jnp.bfloat16), "tensor").astype(jnp.float32),
        lax.psum(querygain_part.astype(jnp.bfloat16), "tensor").astype(jnp.float32),
        lax.psum(keygain_part.astype(jnp.bfloat16), "tensor").astype(jnp.float32),
    )
    input_part, first_grad = first_back(normed_grad)
    input_grad = residual_grad + input_part
    first_grad, second_grad, querygain_grad, keygain_grad, router_grad = lax.psum(
        (first_grad, second_grad, querygain_grad, keygain_grad, router_grad), "expert"
    )
    return (
        layer_output,
        input_grad,
        first_grad,
        query_grad,
        key_grad,
        value_grad,
        mixing_grad,
        querygain_grad,
        keygain_grad,
        second_grad,
        router_grad,
        gate_grad[None],
        up_grad[None],
        down_grad[None],
    )

def partners(planes):
    def number(a, b, c, t):
        y, x = (b, c) if t else (c, b)
        return (a * 4 + y * 2 + x) * 2 + t

    both = (0, 1)
    return [[number(a, b, c, t) for a in range(planes) for b in both] for t in both for c in both]


def lift(values, wide):
    high = lax.reduce_precision(values, 8, 7)
    both = jnp.concatenate([high, values - high], axis=-1).astype(jnp.bfloat16)
    return jnp.pad(both, ((0, 0), (0, wide - both.shape[-1])))


def on_chips(
    layer_input,
    norm_first,
    query_weight,
    key_weight,
    value_weight,
    mixing_weight,
    query_gain,
    key_gain,
    norm_second,
    router_weight,
    gate_weight,
    up_weight,
    down_weight,
    routes,
    fill_order,
    cotangent,
):
    seq_count, seg_len, model_width = layer_input.shape
    expert_count = lax.axis_size("expert")
    planes = expert_count // 4
    expert_idx = lax.axis_index("expert")
    tensor_idx = lax.axis_index("tensor")
    head_dim = query_gain.shape[0]
    local_queries = query_weight.shape[1] // head_dim
    local_keys = key_weight.shape[1] // head_dim
    key_width = local_keys * head_dim
    group_size = local_queries // local_keys
    top_count = routes.shape[2]
    token_count = seq_count * seg_len
    capacity = 5 * token_count * top_count // (4 * expert_count)
    slots = -(-capacity // 32) * 32
    half_width = model_width // 2
    share_width = model_width // expert_count
    f32, bf16 = jnp.float32, jnp.bfloat16
    inputs = layer_input.astype(f32)
    normed = rms_scaled(inputs, norm_first).astype(bf16)
    positions = expert_idx * seg_len + jnp.arange(seg_len, dtype=jnp.int32)
    cosine, sine_table = rotary_tables(positions, head_dim)
    cosine = cosine[:, None, :]
    sine_table = sine_table[:, None, :]

    def rope_norm(raw_heads, gain_vec):
        return rotate(rms_scaled(raw_heads, gain_vec), cosine, sine_table)

    def slices(rows):
        cut = rows.reshape(token_count, planes, 4, share_width)
        return cut.transpose(2, 0, 1, 3).reshape(4, token_count, planes * share_width)

    query_raw = jnp.dot(normed, query_weight, preferred_element_type=f32).reshape(
        seq_count, seg_len, local_queries, head_dim
    )
    key_raw = jnp.dot(normed, key_weight, preferred_element_type=f32).reshape(
        seq_count, seg_len, local_keys, head_dim
    )
    value_local = jnp.dot(normed, value_weight, preferred_element_type=f32).astype(bf16)
    query_rot = rope_norm(query_raw, query_gain)
    key_rot = rope_norm(key_raw, key_gain)
    key_local = key_rot.astype(bf16).reshape(token_count, key_width)
    pairs = jnp.concatenate([key_local, value_local.reshape(token_count, key_width)], axis=1)
    upstream_low = cotangent.reshape(token_count, model_width)
    half_tokens = token_count // 2
    upstream_half = lax.dynamic_slice_in_dim(upstream_low, tensor_idx * half_tokens, half_tokens, 0)
    axes = ("expert", "tensor")
    groups_of = partners(planes)
    upstream_mine = lax.all_gather(upstream_half, "expert")
    query_rows = query_rot.astype(bf16).reshape(token_count, local_queries * head_dim)
    context, pairs_all, logs = attend(query_rows, pairs, planes, group_size, head_dim, 1)
    head_part = jnp.dot(context, mixing_weight, preferred_element_type=f32)
    head_low = head_part.astype(bf16)
    head_other = swap_cores(head_low, 3, "swap_heads")
    residual = inputs.reshape(token_count, model_width) + (head_low.astype(f32) + head_other.astype(f32))
    second_f, second_back = jax.vjp(rms_scaled, residual, norm_second)
    second = second_f.astype(bf16)
    logits = jnp.dot(second, router_weight, preferred_element_type=f32)
    flat_routes = routes.reshape(token_count, top_count)
    picked = (flat_routes[:, :, None] == jnp.arange(expert_count, dtype=jnp.int32)).astype(f32)
    gates = jax.nn.softmax(jnp.sum(picked * logits[:, None, :], axis=-1), axis=-1)
    usages = jnp.sum(picked, axis=1)
    ranking = fill_order.reshape(token_count)
    before = (ranking[None, :] < ranking[:, None]).astype(bf16)
    counts = jnp.dot(before, usages.astype(bf16), preferred_element_type=f32)
    here = (usages > 0.0) & (counts < capacity)
    slot_table = jnp.where(here, counts, -1.0)
    gate_table = jnp.where(here, jnp.sum(picked * gates[:, :, None], axis=1), 0.0)
    slot_hi = lift(slot_table, 2 * expert_count)[:, :expert_count]
    notes = jnp.concatenate([slot_hi, lift(gate_table, 128 - expert_count)], axis=1)
    parcel = jnp.concatenate([second, notes], axis=1)
    normed_cut = slices(normed.reshape(token_count, model_width))
    _, _, out_share, row_home, context_column, other_cuts, gate_grad, up_grad, down_grad = run_experts(
        parcel, upstream_mine, gate_weight[0], up_weight[0], down_weight[0], context, normed_cut, planes, slots, 4
    )
    place = lax.rem(expert_idx, 4)
    own_cut = lax.dynamic_index_in_dim(normed_cut, place, 0)
    normed_cut = lax.dynamic_update_slice_in_dim(other_cuts, own_cut, place, 0)
    out_home = lax.psum_scatter(out_share, axes, scatter_dimension=0, axis_index_groups=groups_of, tiled=True)[0]
    home_scores = jnp.sum(row_home[:, :, half_width:].astype(f32), axis=0)
    home_scores = home_scores[:, :expert_count] + home_scores[:, expert_count : 2 * expert_count]
    gate_grads = jnp.sum(picked * home_scores[:, None, :], axis=-1)
    route_grads = gates * (gate_grads - jnp.sum(gates * gate_grads, axis=-1, keepdims=True))
    logit_grads = jnp.sum(picked * route_grads[:, :, None], axis=1).astype(bf16)
    router_grad = jnp.einsum("td,te->ed", second, logit_grads, preferred_element_type=f32)
    router_back = lax.dot_general(
        logit_grads, router_weight, (((1,), (1,)), ((), ())), preferred_element_type=f32
    )
    second_rows = jnp.concatenate([row_home[0, :, :half_width], row_home[1, :, :half_width]], axis=1)
    second_in = second_rows.astype(f32) + router_back
    residual_part, second_grad = second_back(second_in)
    residual_grad = residual_part + upstream_low.astype(f32)
    head_in = residual_grad.astype(bf16)

    context_grad = lax.dot_general(
        head_in, mixing_weight, (((1,), (1,)), ((), ())), preferred_element_type=f32
    ).astype(bf16)
    head_cut = head_in.reshape(token_count, planes, 4 * share_width).transpose(1, 0, 2)
    turns = jnp.stack(
        [
            jnp.concatenate([cosine[:, 0], cosine[:, 0]], axis=1),
            jnp.concatenate([sine_table[:, 0], -sine_table[:, 0]], axis=1),
        ]
    )
    all_low, gain_grads, mixing_part = attend_back(
        query_rows,
        context_grad,
        context,
        pairs_all,
        logs,
        head_cut,
        context_column,
        (query_raw.reshape(token_count, -1), key_raw.reshape(token_count, key_width)),
        jnp.stack([query_gain, key_gain]),
        turns,
        planes,
        group_size,
        head_dim,
        7,
    )
    residual_half = lax.dynamic_slice_in_dim(residual, tensor_idx * half_width, half_width, 1)
    layer_output = (residual_half + out_home.astype(f32)).astype(bf16).reshape(seq_count, seg_len, half_width)
    gain_row = jnp.pad(
        gain_grads[:2].reshape(1, 2 * head_dim), ((0, 7), (0, model_width - 2 * head_dim))
    )
    small = jnp.concatenate(
        [gain_row, jnp.pad(second_grad[None], ((1, 6), (0, 0))), router_grad], axis=0
    )
    weight_rows, input_grad, small, mixing_rows = weight_grads(
        all_low,
        normed_cut.reshape(4 * token_count, planes * share_width).T,
        query_weight,
        key_weight,
        value_weight,
        layer_input.reshape(token_count, model_width),
        norm_first[None],
        residual_grad,
        small,
        mixing_part,
        planes,
        10,
    )
    mixing_grad = mixing_rows.T
    query_width = local_queries * head_dim
    query_grad = weight_rows[:, :query_width]
    key_grad = weight_rows[:, query_width : query_width + key_width]
    value_grad = weight_rows[:, query_width + key_width :]
    return (
        layer_output,
        input_grad.reshape(seq_count, seg_len, model_width),
        small[8],
        query_grad,
        key_grad,
        value_grad,
        mixing_grad,
        small[0, :head_dim],
        small[0, head_dim : 2 * head_dim],
        small[9],
        small[16:].T,
        gate_grad[None],
        up_grad[None],
        down_grad[None],
    )


def solution(mesh):
    chips = mesh.shape["expert"] == 16 and mesh.shape["tensor"] == 2
    return jax.shard_map(
        on_chips if chips else on_device,
        mesh=mesh,
        in_specs=(
            P(None, "expert", None),
            P(),
            P(None, "tensor"),
            P(None, "tensor"),
            P(None, "tensor"),
            P("tensor", None),
            P(),
            P(),
            P(),
            P(),
            P("expert", None, "tensor"),
            P("expert", None, "tensor"),
            P("expert", "tensor", None),
            P(None, "expert", None),
            P(None, "expert"),
            P(None, "expert", None),
        ),
        out_specs=(
            P(None, "expert", "tensor"),
            P(None, "expert", None),
            P(),
            P("expert", "tensor"),
            P("expert", "tensor"),
            P("expert", "tensor"),
            P("tensor", "expert"),
            P(),
            P(),
            P(),
            P(),
            P("expert", None, "tensor"),
            P("expert", None, "tensor"),
            P("expert", "tensor", None),
        ),
        check_vma=False,
    )
```

```python
import functools

import jax
import jax.numpy as jnp
from jax import lax
from jax.experimental import pallas as pl
from jax.experimental.pallas import tpu as pltpu
from jax.sharding import PartitionSpec as P

BLOCK = 256
MESH = pl.DeviceIdType.MESH
ROOM = 56 * 2**20


class Spot:
    def __init__(self):
        self.e = lax.axis_index("expert")
        self.t = lax.axis_index("tensor")
        self.a = lax.div(self.e, 4)
        y = lax.rem(lax.div(self.e, 2), 2)
        x = lax.rem(self.e, 2)
        self.b = x + self.t * (y - x)
        self.c = y + self.t * (x - y)

    def index(self, a, b, c):
        y = c + self.t * (b - c)
        x = b + self.t * (c - b)
        return a * 4 + y * 2 + x

    def at(self, a, b, c):
        return (self.index(a, b, c), self.t)

    def core(self):
        return (self.e, 1 - self.t)

    def greet(self, planes, chain, flat, share, far=False, corner=False):
        barrier = pltpu.get_barrier_semaphore()
        total = 0

        def call(who):
            pl.semaphore_signal(barrier, inc=1, device_id=who, device_id_type=MESH)

        if share:
            call(self.core())
            total = total + 1
        if flat:
            call(self.at(self.a, 1 - self.b, self.c))
            call(self.at(self.a, self.b, 1 - self.c))
            total = total + 2
        if corner:
            call(self.at(self.a, 1 - self.b, 1 - self.c))
            total = total + 1
        if far:
            for k in range(1, planes):
                call(self.at(lax.rem(self.a + k, planes), self.b, self.c))
            total = total + planes - 1
        elif chain:
            up = self.a + 1 < planes
            down = self.a > 0

            @pl.when(up)
            def _():
                call(self.at(self.a + 1, self.b, self.c))

            @pl.when(down)
            def _():
                call(self.at(self.a - 1, self.b, self.c))

            total = total + up.astype(jnp.int32) + down.astype(jnp.int32)
        pl.semaphore_wait(barrier, total)


def push(src, dst, send_sem, recv_sem, who):
    return pltpu.make_async_remote_copy(
        src_ref=src, dst_ref=dst, send_sem=send_sem, recv_sem=recv_sem, device_id=who, device_id_type=MESH
    )


def add_rows(target, parts):
    rows = target.shape[0]
    step = 32 if rows % 32 == 0 else 16

    def body(i, carry):
        at = pl.ds(pl.multiple_of(i * step, step), step)
        total = parts[0][at, :].astype(jnp.float32)
        for part in parts[1:]:
            total = total + part[at, :].astype(jnp.float32)
        target[at, :] = total.astype(target.dtype)
        return carry

    lax.fori_loop(0, rows // step, body, 0)


def far_first(a, planes, i):
    last = planes - 1
    low = jnp.where(i < last - a, last - i, jnp.where(i < last, i - (last - a), a))
    high = jnp.where(i < a, i, jnp.where(i < last, last - (i - a), a))
    return jnp.where(2 * a < last, low, high)


def swap_kernel(x_ref, o_ref, sems):
    me = Spot()
    me.greet(1, False, False, True)
    c = push(x_ref, o_ref, sems.at[0], sems.at[1], me.core())
    c.start()
    c.wait()


def swap_cores(x, cid, name):
    return pl.pallas_call(
        swap_kernel,
        out_shape=jax.ShapeDtypeStruct(x.shape, x.dtype),
        in_specs=[pl.BlockSpec(memory_space=pl.ANY)],
        out_specs=pl.BlockSpec(memory_space=pl.ANY),
        scratch_shapes=[pltpu.SemaphoreType.DMA((2,))],
        compiler_params=pltpu.CompilerParams(collective_id=cid, has_side_effects=True),
        name=name,
    )(x)


def over(first, second, contract):
    return lax.dot_general(first, second, (contract, ((), ())), preferred_element_type=jnp.float32)


NN = ((1,), (0,))
NT = ((1,), (1,))
TN = ((0,), (0,))


def experts_kernel(
    planes,
    parcel_ref,
    up_ref,
    gate_in,
    lift_in,
    down_in,
    context_ref,
    cut_ref,
    all_ref,
    other_ref,
    share_ref,
    home_ref,
    column_ref,
    cut_all,
    gate_sum,
    lift_sum,
    down_sum,
    wide,
    down,
    wide_half,
    down_half,
    pbuf,
    ubuf,
    xbuf,
    gbuf,
    vbuf,
    sbuf,
    wbuf,
    rbuf,
    hbuf,
    dbuf,
    gates,
    scores,
    stage,
    given,
    taken,
    mine,
    outgoing,
    partner,
    landc,
    landb,
    landa,
    gsend,
    grecv,
    gcore,
    usend,
    urecv,
    wsend,
    wrecv,
    wload,
    hsend,
    hrecv,
    ssem,
    rsem,
    lsem,
    osem,
    osend,
    orecv,
    esem,
    xsend,
    xrecv,
    csend,
    crecv,
):
    me = Spot()
    f32, bf16 = jnp.float32, jnp.bfloat16
    tokens, packed = parcel_ref.shape
    hidden, width = down_in.shape
    notes_width = packed - width
    count = planes * 4
    half = tokens // 2
    side = width // 2
    slots = sbuf.shape[2]
    own = me.index(me.a, me.b, me.c)
    ours = pl.ds(pl.multiple_of(me.t * half, half), half)
    theirs = pl.ds(pl.multiple_of((1 - me.t) * half, half), half)
    our_side = pl.ds(pl.multiple_of(me.t * side, side), side)
    their_side = pl.ds(pl.multiple_of((1 - me.t) * side, side), side)
    spots = [(sb, sc) for sc in (1 - me.c, me.c) for sb in (1 - me.b, me.b)]

    def near(i):
        return far_first(me.a, planes, planes - 1 - i)


    def carry(idx, kind, src=None):
        who = {
            0: me.at(me.a + 1, me.b, me.c),
            1: me.at(me.a - 1, me.b, me.c),
            2: me.at(me.a, 1 - me.b, me.c),
            3: me.at(me.a, me.b, 1 - me.c),
            4: me.core(),
        }[kind]
        there = all_ref.at[idx, ours]
        landed = gcore if kind == 4 else grecv
        return push(there if src is None else src, there, gsend.at[idx, kind], landed.at[idx], who)

    def relay_a(sa, act, first):
        idx = me.index(sa, me.b, me.c)
        src = parcel_ref.at[ours] if first else None
        if act and not first:
            carry(idx, 2).wait_recv()
        run = (lambda c: c.start()) if act else (lambda c: c.wait_send())

        @pl.when((sa <= me.a) & (me.a + 1 < planes))
        def _():
            run(carry(idx, 0, src))

        @pl.when((sa >= me.a) & (me.a > 0))
        def _():
            run(carry(idx, 1, src))

        run(carry(idx, 3, src))
        run(carry(idx, 2, src))
        if not first:
            run(carry(idx, 4))

    def relay_b(sa, act):
        idx = me.index(sa, 1 - me.b, me.c)
        run = (lambda c: c.start()) if act else (lambda c: c.wait_send())
        if act:
            carry(idx, 2).wait_recv()
        run(carry(idx, 3))
        run(carry(idx, 4))

    def across(sa, act):
        for sb in (me.b, 1 - me.b):
            idx = me.index(sa, sb, 1 - me.c)
            if act:
                carry(idx, 2).wait_recv()
                carry(idx, 4).start()
            else:
                carry(idx, 4).wait_send()

    def from_core(sa):
        for sb, sc in spots:
            idx = me.index(sa, sb, sc)

            @pl.when(idx != own)
            def _(idx=idx):
                there = all_ref.at[idx, theirs]
                push(there, there, gsend.at[idx, 4], gcore.at[idx], me.core()).wait_recv()

    def upstream(sa):
        group = pl.ds(sa * 4, 4)
        return push(up_ref.at[group], other_ref.at[group], usend.at[sa], urecv.at[sa], me.core())


    def part(ref, base, size):
        return ref.at[:, pl.ds(pl.multiple_of(base, 128), size)]

    down_rows = down_half.at[pl.ds(pl.multiple_of(me.t * hidden, 128), hidden)]
    wide_cols = [part(wide_half, me.t * 2 * hidden + i * hidden, hidden) for i in range(2)]
    sources = [gate_in, lift_in]
    loads = [pltpu.make_async_copy(sources[i], wide.at[:, i * hidden : (i + 1) * hidden], wload.at[i]) for i in range(2)]
    loads += [pltpu.make_async_copy(sources[i].at[our_side], wide_cols[i], wload.at[2 + i]) for i in range(2)]
    loads += [
        pltpu.make_async_copy(down_in, down, wload.at[4]),
        pltpu.make_async_copy(down_in.at[:, our_side], down_rows, wload.at[5]),
    ]
    pushes = [push(sources[i].at[their_side], wide_cols[i], wsend.at[i], wrecv.at[i], me.core()) for i in range(2)]
    pushes += [push(down_in.at[:, their_side], down_rows, wsend.at[2], wrecv.at[2], me.core())]


    def send_c(sa, sb):
        slot = sa * 2 + sb
        there = me.at(me.a, me.b, 1 - me.c)
        return push(outgoing.at[slot], landc.at[slot], ssem.at[0, slot], rsem.at[0, slot], there)

    def send_b(sa):
        src = mine.at[sa * 2 + 1 - me.b]
        return push(src, landb.at[sa], ssem.at[1, sa], rsem.at[1, sa], me.at(me.a, 1 - me.b, me.c))

    def send_a(sa):
        src = mine.at[sa * 2 + me.b]
        return push(src, landa.at[me.a], ssem.at[2, sa], rsem.at[2, me.a], me.at(sa, me.b, me.c))

    def from_c(sa):
        for sb in (1 - me.b, me.b):
            slot = sa * 2 + sb
            push(landc.at[slot], landc.at[slot], ssem.at[0, slot], rsem.at[0, slot], me.at(me.a, me.b, 1 - me.c)).wait_recv()
            for n in range(0, mine.shape[2], 384):
                cut = slice(n, n + 384)
                spread = over(partner[slot], landc[slot, :, cut], NN)
                mine[slot, :, cut] = (mine[slot, :, cut].astype(f32) + spread).astype(bf16)
            if sb is not me.b:
                send_b(sa).start()

    def from_b(sa):
        push(landb.at[sa], landb.at[sa], ssem.at[1, sa], rsem.at[1, sa], me.at(me.a, 1 - me.b, me.c)).wait_recv()
        return [mine.at[sa * 2 + me.b], landb.at[sa]]

    def along(sa):
        parts = from_b(sa)
        add_rows(parts[0], parts)
        send_a(sa).start()

    def finish():
        parts = from_b(me.a)
        for k in range(1, planes):
            far = lax.rem(me.a + k, planes)
            push(landa.at[far], landa.at[far], ssem.at[2, far], rsem.at[2, far], me.at(far, me.b, me.c)).wait_recv()
            parts = parts + [landa.at[far]]
        add_rows(home_ref.at[me.t], parts)


    def context_to(source, up, own_rows):
        there = column_ref.at[source]
        who = me.at(me.a + 1 if up else me.a - 1, me.b, me.c)
        return push(context_ref if own_rows else there, there, xsend.at[source, int(up)], xrecv.at[source], who)

    def context_pass(i, act):
        for up in (True, False):
            source = me.a - i if up else me.a + i
            further = me.a + 1 < planes if up else me.a > 0
            run = (lambda c: c.start()) if act else (lambda c: c.wait_send())

            @pl.when((source >= 0) & (source < planes))
            def _(source=source, up=up, further=further, run=run):
                if act and i > 0:
                    context_to(source, up, False).wait_recv()

                @pl.when(further)
                def _():
                    run(context_to(source, up, i == 0))

    place = lax.rem(me.e, 4)
    peers = [me.index(0, b, c) for b, c in ((1 - me.b, me.c), (me.b, 1 - me.c), (1 - me.b, 1 - me.c))]

    def cut_to(i):
        there = (me.e - place + peers[i], me.t)
        return push(cut_ref.at[peers[i]], cut_all.at[place], csend.at[i], crecv.at[i], there)


    def load_rows(sa, q):
        return pltpu.make_async_copy(all_ref.at[sa * 4 + q], pbuf.at[q], lsem.at[q])

    def fetch_rows(sa):
        from_core(sa)
        for q in range(4):
            mine_here = sa * 4 + q == own

            @pl.when(mine_here)
            def _(q=q):
                pltpu.make_async_copy(parcel_ref, pbuf.at[q], lsem.at[q]).start()

            @pl.when(jnp.logical_not(mine_here))
            def _(q=q):
                load_rows(sa, q).start()

    def load_up(sa):
        group = pl.ds(sa * 4, 4)
        return [
            pltpu.make_async_copy(up_ref.at[group], ubuf.at[:, ours], lsem.at[4]),
            pltpu.make_async_copy(other_ref.at[group], ubuf.at[:, theirs], lsem.at[5]),
        ]

    def fetch_up(sa):
        there = other_ref.at[pl.ds(sa * 4, 4)]
        push(there, there, usend.at[sa], urecv.at[sa], me.core()).wait_recv()
        for k in load_up(sa):
            k.start()

    def lanes(rows):
        return lax.broadcasted_iota(jnp.int32, (rows, notes_width), 1)

    def side_of(q):
        y, x = lax.div(q, 2), lax.rem(q, 2)
        return x + me.t * (y - x), y + me.t * (x - y)

    def chosen_by(expert, notes):
        slot_of = jnp.sum(jnp.where(lanes(tokens) == expert, notes, 0.0), axis=1, keepdims=True)
        chosen = slot_of == lax.broadcasted_iota(jnp.int32, (tokens, slots), 1).astype(f32)
        return jnp.where(chosen, 1.0, 0.0).astype(bf16)

    def pick_rows(q, carried):
        sa, slot = carried
        load_rows(sa, q).wait()
        notes = pbuf[q, :, width:].astype(f32)
        sb, sc = side_of(q)

        @pl.when(sc == me.c)
        def _():
            partner[sa * 2 + sb] = chosen_by(me.index(me.a, me.b, 1 - me.c), notes)

        chosen = chosen_by(me.e, notes)
        sbuf[q] = chosen
        pick = jnp.transpose(chosen.astype(f32)).astype(bf16)
        at = pl.ds(pl.multiple_of(q * slots, slots), slots)
        there = over(pick, pbuf[q, :, width:], NN)
        mark = lanes(slots)
        gate = jnp.sum(jnp.where((mark == count + me.e) | (mark == 2 * count + me.e), there, 0.0), axis=1, keepdims=True)
        gates[at, :] = jnp.broadcast_to(gate, (slots, 128))
        for n in range(0, width, 512):
            cut = slice(n, n + 512)
            xbuf[at, cut] = over(pick, pbuf[q, :, cut], NN).astype(bf16)
            picked = over(pick, ubuf[q, :, cut], NN)
            gbuf[at, cut] = (picked * gate).astype(bf16)
        for n in range(0, side, 512):
            cut = pl.ds(pl.multiple_of(me.t * side + n, 512), 512)
            vbuf[at, n : n + 512] = over(pick, ubuf[q, :, cut], NN).astype(bf16)
        return carried

    def hidden_cols(p):
        return pl.ds(pl.multiple_of(p * hidden, 128), hidden)

    def both_cols(p):
        return pl.ds(pl.multiple_of(p * 2 * hidden, 128), 2 * hidden)

    def hidden_rows(r, slot):
        at = pl.ds(pl.multiple_of(r * 256, 256), 256)
        acts = over(xbuf[at, :], wide[...], NN)
        gate_act, up_act = acts[:, :hidden], acts[:, hidden:]
        sig = 1.0 / (1.0 + jnp.exp(-gate_act))
        silu = gate_act * sig
        hbuf[slot, at, hidden_cols(me.t)] = (silu * up_act).astype(bf16)
        back = over(gbuf[at, :], down[...], NT)
        gate_d = (back * up_act * (sig * (1.0 + gate_act * (1.0 - sig)))).astype(bf16)
        dbuf[slot, at, pl.ds(pl.multiple_of(me.t * 2 * hidden, 128), hidden)] = gate_d
        dbuf[slot, at, pl.ds(pl.multiple_of(me.t * 2 * hidden + hidden, 128), hidden)] = (back * silu).astype(bf16)
        return slot

    def trades(slot):
        h_part = hbuf.at[slot, :, hidden_cols(me.t)]
        d_part = dbuf.at[slot, :, both_cols(me.t)]
        return [
            push(h_part, h_part, hsend.at[0], hrecv.at[slot, 0], me.core()),
            push(d_part, d_part, hsend.at[1], hrecv.at[slot, 1], me.core()),
        ]

    def traded(slot):
        h_part = hbuf.at[slot, :, hidden_cols(1 - me.t)]
        d_part = dbuf.at[slot, :, both_cols(1 - me.t)]
        push(h_part, h_part, hsend.at[0], hrecv.at[slot, 0], me.core()).wait_recv()
        push(d_part, d_part, hsend.at[1], hrecv.at[slot, 1], me.core()).wait_recv()

    def weight_sums(n, slot):
        cut = pl.ds(pl.multiple_of(n * 512, 512), 512)
        own_d = dbuf[slot, :, both_cols(me.t)]
        rows = xbuf[:, cut]
        gate_sum[cut, :] += over(rows, own_d[:, :hidden], TN)
        lift_sum[cut, :] += over(rows, own_d[:, hidden:], TN)
        down_sum[:, cut] += over(hbuf[slot, :, hidden_cols(me.t)], gbuf[:, cut], TN)
        return slot

    def out_rows(n, slot):
        cut = pl.ds(pl.multiple_of(n * 512, 512), 512)
        for r in range(0, 4 * slots, 256):
            at = slice(r, r + 256)
            out = over(hbuf[slot, at, :], down_half[:, cut], NN)
            wbuf[at, cut] = (out * gates[at, :1]).astype(bf16)
            total = jnp.sum(out * vbuf[at, cut].astype(f32), axis=1, keepdims=True)
            scores[at, :] += jnp.broadcast_to(total, (256, 128))
            rbuf[at, cut] = over(dbuf[slot, at, :], wide_half[cut, :], NT).astype(bf16)
        return slot

    def note_scores():
        mark = lanes(4 * slots)
        total = scores[...]
        high = total.astype(bf16).astype(f32)
        row = jnp.where(mark == me.e, high, jnp.where(mark == me.e + count, total - high, 0.0))
        rbuf[:, side:] = row.astype(bf16)

    def send_out(sa, sb):
        slot = sa * 2 + sb
        there = me.at(me.a, me.b, 1 - me.c)
        return push(given.at[slot], taken.at[slot], osend.at[slot], orecv.at[slot], there)

    def store(sa, sb):
        slot = sa * 2 + sb
        return pltpu.make_async_copy(stage.at[slot], share_ref.at[slot], osem.at[slot])

    def out_from_c(sa):
        for sb in (0, 1):
            slot = sa * 2 + sb
            send_out(sa, sb).wait_recv()
            for n in range(0, side, 512):
                cut = slice(n, n + 512)
                spread = over(partner[slot], taken[slot, :, cut], NN)
                stage[slot, :, cut] = (stage[slot, :, cut].astype(f32) + spread).astype(bf16)
            store(sa, sb).start()

    def spread_rows(j, sa):
        sb, sc = lax.rem(j, 2), jnp.where(j < 2, 1 - me.c, me.c)
        q = 2 * (sc + me.t * (sb - sc)) + sb + me.t * (sc - sb)
        at = pl.ds(pl.multiple_of(q * slots, slots), slots)
        slot = sa * 2 + sb

        @pl.when(sc == me.c)
        def _():
            for n in range(0, mine.shape[2], 384):
                cut = slice(n, n + 384)
                mine[slot, :, cut] = over(sbuf[q], rbuf[at, cut], NN).astype(bf16)
            for n in range(0, side, 512):
                cut = slice(n, n + 512)
                stage[slot, :, cut] = over(sbuf[q], wbuf[at, cut], NN).astype(bf16)

        @pl.when(sc != me.c)
        def _():
            outgoing[slot] = rbuf[at, :]
            send_c(sa, sb).start()
            given[slot] = wbuf[at, :]

        return sa

    me.greet(planes, True, True, True, True, True)
    relay_a(me.a, True, True)
    for i in range(planes):
        upstream(near(i)).start()
    for k in loads + pushes:
        k.start()
    gate_sum[...] = jnp.zeros_like(gate_sum)
    lift_sum[...] = jnp.zeros_like(lift_sum)
    down_sum[...] = jnp.zeros_like(down_sum)
    fetch_up(near(1))
    relay_b(me.a, True)
    relay_a(near(1), True, False)
    across(me.a, True)
    for i in range(2, planes):
        relay_a(near(i), True, False)
        if i == planes - 1:
            context_pass(0, True)
        relay_b(near(i - 1), True)
    across(near(1), True)
    fetch_rows(near(1))
    for k in loads + pushes:
        k.wait()

    def step(i, c):
        last = i == planes - 1
        sa = jnp.where(last, me.a, near(i + 1))
        after = jnp.where(i + 2 < planes, near(i + 2), me.a)
        slot = lax.rem(i, 2)
        for k in load_up(sa):
            k.wait()
        scores[...] = jnp.zeros_like(scores)
        lax.fori_loop(0, 4, pick_rows, (sa, slot))

        @pl.when(i + 1 < planes)
        def _():
            fetch_up(after)

        @pl.when(i > 0)
        def _():
            for k in trades(slot):
                k.wait_send()

        lax.fori_loop(0, 4 * slots // 256, hidden_rows, slot)
        for k in trades(slot):
            k.start()

        @pl.when(i == 0)
        def _():
            relay_b(near(planes - 1), True)
            for k in range(3):
                cut_to(k).start()

        for k in range(1, planes):

            @pl.when(i == k - 1)
            def _(k=k):
                context_pass(k, True)

        @pl.when(i > 0)
        def _():
            from_c(near(i))

        traded(slot)
        lax.fori_loop(0, side // 512, out_rows, slot)
        note_scores()
        lax.fori_loop(0, 4, spread_rows, sa)
        for sb in (0, 1):
            send_out(sa, sb).start()

        @pl.when(i + 2 < planes)
        def _():
            across(after, True)

        @pl.when(jnp.logical_not(last))
        def _():
            fetch_rows(after)

        @pl.when(i > 0)
        def _():
            along(near(i))

        lax.fori_loop(0, width // 512, weight_sums, slot)

        @pl.when(i > 0)
        def _():
            out_from_c(near(i))

        return c

    lax.fori_loop(0, planes, step, 0)
    from_c(me.a)
    out_from_c(me.a)
    finish()
    done = push(home_ref.at[me.t], home_ref.at[me.t], esem.at[0], esem.at[1], me.core())
    done.start()

    relay_a(me.a, False, True)

    def settle(i, c):
        sa = near(i)
        relay_b(sa, False)

        @pl.when(i > 0)
        def _():
            relay_a(sa, False, False)
            send_a(sa).wait_send()

        across(sa, False)
        for sb in (1 - me.b, me.b):
            send_c(sa, sb).wait_send()
            send_out(sa, sb).wait_send()
            store(sa, sb).wait()
        send_b(sa).wait_send()
        upstream(sa).wait_send()
        return c

    lax.fori_loop(0, planes, settle, 0)
    for k in trades(0):
        k.wait_send()
    for k in range(planes):
        context_pass(k, False)
    for k in range(3):
        cut_to(k).wait()
    done.wait_send()
    other = home_ref.at[1 - me.t]
    push(other, other, esem.at[0], esem.at[1], me.core()).wait_recv()


def run_experts(parcel, upstream, gate, lift_w, down, context, cut, planes, slots, cid):
    f32, bf16 = jnp.float32, jnp.bfloat16
    tokens, packed = parcel.shape
    hidden, width = down.shape
    count = planes * 4
    half = tokens // 2
    side = width // 2
    block = side + packed - width
    rows = 4 * slots
    anywhere = pl.BlockSpec(memory_space=pl.ANY)
    inside = pl.BlockSpec(memory_space=pltpu.VMEM)
    return pl.pallas_call(
        functools.partial(experts_kernel, planes),
        out_shape=[
            jax.ShapeDtypeStruct((count, tokens, packed), bf16),
            jax.ShapeDtypeStruct((count, half, width), bf16),
            jax.ShapeDtypeStruct((2 * planes, tokens, side), bf16),
            jax.ShapeDtypeStruct((2, tokens, block), bf16),
            jax.ShapeDtypeStruct((planes,) + context.shape, bf16),
            jax.ShapeDtypeStruct(cut.shape, bf16),
            jax.ShapeDtypeStruct((width, hidden), f32),
            jax.ShapeDtypeStruct((width, hidden), f32),
            jax.ShapeDtypeStruct((hidden, width), f32),
        ],
        in_specs=[anywhere] * 7,
        out_specs=[anywhere] * 3 + [inside, anywhere, anywhere] + [inside] * 3,
        scratch_shapes=[
            pltpu.VMEM((width, 2 * hidden), bf16),
            pltpu.VMEM((hidden, width), bf16),
            pltpu.VMEM((side, 4 * hidden), bf16),
            pltpu.VMEM((2 * hidden, side), bf16),
            pltpu.VMEM((4, tokens, packed), bf16),
            pltpu.VMEM((4, tokens, width), bf16),
            pltpu.VMEM((rows, width), bf16),
            pltpu.VMEM((rows, width), bf16),
            pltpu.VMEM((rows, side), bf16),
            pltpu.VMEM((4, tokens, slots), bf16),
            pltpu.VMEM((rows, side), bf16),
            pltpu.VMEM((rows, block), bf16),
            pltpu.VMEM((2, rows, 2 * hidden), bf16),
            pltpu.VMEM((2, rows, 4 * hidden), bf16),
            pltpu.VMEM((rows, 128), f32),
            pltpu.VMEM((rows, 128), f32),
            pltpu.VMEM((2 * planes, tokens, side), bf16),
            pltpu.VMEM((2 * planes, slots, side), bf16),
            pltpu.VMEM((2 * planes, slots, side), bf16),
            pltpu.VMEM((2 * planes, tokens, block), bf16),
            pltpu.VMEM((2 * planes, slots, block), bf16),
            pltpu.VMEM((2 * planes, tokens, slots), bf16),
            pltpu.VMEM((2 * planes, slots, block), bf16),
            pltpu.VMEM((planes, tokens, block), bf16),
            pltpu.VMEM((planes, tokens, block), bf16),
            pltpu.SemaphoreType.DMA((count, 5)),
            pltpu.SemaphoreType.DMA((count,)),
            pltpu.SemaphoreType.DMA((count,)),
            pltpu.SemaphoreType.DMA((planes,)),
            pltpu.SemaphoreType.DMA((planes,)),
            pltpu.SemaphoreType.DMA((3,)),
            pltpu.SemaphoreType.DMA((3,)),
            pltpu.SemaphoreType.DMA((6,)),
            pltpu.SemaphoreType.DMA((2,)),
            pltpu.SemaphoreType.DMA((2, 2)),
            pltpu.SemaphoreType.DMA((3, 2 * planes)),
            pltpu.SemaphoreType.DMA((3, 2 * planes)),
            pltpu.SemaphoreType.DMA((7,)),
            pltpu.SemaphoreType.DMA((2 * planes,)),
            pltpu.SemaphoreType.DMA((2 * planes,)),
            pltpu.SemaphoreType.DMA((2 * planes,)),
            pltpu.SemaphoreType.DMA((2,)),
            pltpu.SemaphoreType.DMA((planes, 2)),
            pltpu.SemaphoreType.DMA((planes,)),
            pltpu.SemaphoreType.DMA((3,)),
            pltpu.SemaphoreType.DMA((3,)),
        ],
        compiler_params=pltpu.CompilerParams(
            collective_id=cid, has_side_effects=True, vmem_limit_bytes=62 * 2**20
        ),
        name="experts",
    )(parcel, upstream, gate, lift_w, down, context, cut)


def stack_heads(target, source, group):
    items, rows, size = target.shape
    seg = rows // group
    keys = source.shape[1] // (group * size)
    for s in range(items // keys):
        for k in range(keys):
            for h in range(group):
                at = (k * group + h) * size
                part = source[s * seg : (s + 1) * seg, at : at + size]
                target[s * keys + k, h * seg : (h + 1) * seg, :] = part.astype(target.dtype)


def spread_heads(target, item, value, group, keys):
    rows, size = value.shape
    seg = rows // group
    s, k = item // keys, item % keys
    for h in range(group):
        at = (k * group + h) * size
        target[s * seg : (s + 1) * seg, at : at + size] = value[h * seg : (h + 1) * seg, :].astype(target.dtype)


def block_heads(ref, plane, item, keys, size, part):
    seg = BLOCK // 4
    s, k = lax.div(item, keys), lax.rem(item, keys)
    rows = pl.ds(pl.multiple_of(s * seg, seg), seg)
    cols = pl.ds(pl.multiple_of((part * keys + k) * size, size), size)
    return [ref.at[plane * 4 + q, rows, cols] for q in range(4)]


def joined(refs):
    return jnp.concatenate([ref[...] for ref in refs], axis=0)


def attend_kernel(
    planes, group, q_ref, x_ref, context_ref, all_ref, log_ref, qs, top, total, acc, ssem, rsem
):
    me = Spot()
    f32, bf16 = jnp.float32, jnp.bfloat16
    items, rows, size = qs.shape
    keys = x_ref.shape[1] // (2 * size)
    factor = size ** (-0.5)
    own = me.index(me.a, me.b, me.c)

    def carry(idx, kind, src=None):
        who = {
            0: me.at(me.a + 1, me.b, me.c),
            2: me.at(me.a, 1 - me.b, me.c),
            3: me.at(me.a, me.b, 1 - me.c),
        }[kind]
        there = all_ref.at[idx]
        return push(there if src is None else src, there, ssem.at[idx, kind], rsem.at[idx], who)

    def relay(sa, act, first):
        idx = me.index(sa, me.b, me.c)
        src = x_ref if first else None
        if act and not first:
            carry(idx, 2).wait_recv()
        run = (lambda c: c.start()) if act else (lambda c: c.wait_send())

        @pl.when(me.a + 1 < planes)
        def _():
            run(carry(idx, 0, src))

        run(carry(idx, 3, src))
        run(carry(idx, 2, src))
        idx = me.index(sa, 1 - me.b, me.c)
        if act:
            carry(idx, 2).wait_recv()
        run(carry(idx, 3))

    def block(item, sa):
        scores = over(qs[item], joined(block_heads(all_ref, sa, item, keys, size, 0)), NT) * factor
        values = joined(block_heads(all_ref, sa, item, keys, size, 1))
        before = top[item]
        high = jnp.maximum(before, jnp.broadcast_to(jnp.max(scores, axis=1, keepdims=True), before.shape))
        shrink = jnp.exp(before - high)
        terms = jnp.exp(scores - high[:, :1])
        top[item] = high
        total[item] = total[item] * shrink + jnp.broadcast_to(jnp.sum(terms, axis=1, keepdims=True), before.shape)
        acc[item] = acc[item] * shrink + over(terms.astype(bf16), values, NN)
        return sa

    me.greet(planes, True, True, False)
    relay(me.a, True, True)
    all_ref[own] = x_ref[...]

    @pl.when(me.a > 0)
    def _():
        relay(me.a - 1, True, False)

    stack_heads(qs, q_ref, group)
    top[...] = jnp.full(top.shape, far_below, f32)
    total[...] = jnp.zeros_like(total)
    acc[...] = jnp.zeros_like(acc)

    def step(i, c):
        sa = me.a - i

        @pl.when(sa > 1)
        def _():
            relay(sa - 2, True, False)

        for sb in (me.b, 1 - me.b):
            carry(me.index(sa, sb, 1 - me.c), 2).wait_recv()
        lax.fori_loop(0, items, block, sa)
        return c

    lax.fori_loop(0, me.a + 1, step, 0)
    for item in range(items):
        spread_heads(context_ref, item, acc[item] / total[item], group, keys)
    log_ref[...] = top[...] + jnp.log(total[...])
    relay(me.a, False, True)

    def settle(i, c):
        relay(me.a - i, False, False)
        return c

    lax.fori_loop(1, me.a + 1, settle, 0)


def attend(query, pairs, planes, group, size, cid):
    f32, bf16 = jnp.float32, jnp.bfloat16
    tokens, width = query.shape
    count = planes * 4
    items = (tokens * 4 // BLOCK) * (width // (group * size))
    state = (items, group * BLOCK // 4, size)
    inside = pl.BlockSpec(memory_space=pltpu.VMEM)
    return pl.pallas_call(
        functools.partial(attend_kernel, planes, group),
        out_shape=[
            jax.ShapeDtypeStruct((tokens, width), bf16),
            jax.ShapeDtypeStruct((count,) + pairs.shape, bf16),
            jax.ShapeDtypeStruct(state, f32),
        ],
        in_specs=[inside] * 2,
        out_specs=[inside] * 3,
        scratch_shapes=[
            pltpu.VMEM(state, bf16),
            pltpu.VMEM(state, f32),
            pltpu.VMEM(state, f32),
            pltpu.VMEM(state, f32),
            pltpu.SemaphoreType.DMA((count, 4)),
            pltpu.SemaphoreType.DMA((count,)),
        ],
        compiler_params=pltpu.CompilerParams(collective_id=cid, has_side_effects=True, vmem_limit_bytes=ROOM),
        name="attend",
    )(query, pairs)


def attend_back_kernel(
    planes,
    group,
    q_ref,
    g_ref,
    o_ref,
    all_ref,
    log_ref,
    cut_ref,
    column_ref,
    query_raw,
    key_raw,
    gain_ref,
    turn_ref,
    low_ref,
    gain_grad,
    mixing_ref,
    pair_grad,
    cut_all,
    column,
    qs,
    gs,
    delta,
    qacc,
    mine,
    landc,
    landb,
    landa,
    ssem,
    rsem,
    psend,
    precv,
    lsem,
):
    me = Spot()
    f32, bf16 = jnp.float32, jnp.bfloat16
    items, rows, size = qs.shape
    keys = all_ref.shape[2] // (2 * size)
    factor = size ** (-0.5)
    me.greet(planes, False, True, False, True)

    def cut_to(k):
        far = lax.rem(me.a + k, planes)
        return push(cut_ref.at[far], cut_all.at[me.a], psend.at[k], precv.at[me.a], me.at(far, me.b, me.c))

    def cut_from(k):
        far = lax.rem(me.a + k, planes)
        there = cut_all.at[far]
        push(there, there, psend.at[k], precv.at[far], me.at(far, me.b, me.c)).wait_recv()

    for k in range(1, planes):
        cut_to(k).start()
    keep = pltpu.make_async_copy(cut_ref.at[me.a], cut_all.at[me.a], lsem.at[0])
    keep.start()

    def column_in(k):
        far = lax.rem(me.a + k, planes)
        return pltpu.make_async_copy(column_ref.at[far], column.at[far], lsem.at[k])

    for k in range(1, planes):
        column_in(k).start()
    column[me.a] = o_ref[...]
    stack_heads(qs, q_ref, group)
    stack_heads(gs, g_ref, group)
    stack_heads(qacc, o_ref, group)

    def prepare(item, c):
        part = jnp.sum(gs[item].astype(f32) * qacc[item], axis=1, keepdims=True)
        delta[item] = jnp.broadcast_to(part, delta.shape[1:])
        qacc[item] = jnp.zeros(qacc.shape[1:], f32)
        return c

    lax.fori_loop(0, items, prepare, 0)

    def block(item, sa):
        keys_here = joined(block_heads(all_ref, sa, item, keys, size, 0))
        values = joined(block_heads(all_ref, sa, item, keys, size, 1))
        queries, grads = qs[item], gs[item]
        scores = over(queries, keys_here, NT) * factor
        probs = jnp.exp(scores - log_ref[item][:, :1])
        prob_grads = over(grads, values, NT)
        score_grads = (probs * (prob_grads - delta[item][:, :1])).astype(bf16)
        qacc[item] += over(score_grads, keys_here, NN)
        key_part = (over(score_grads, queries, TN) * factor).astype(bf16)
        value_part = over(probs.astype(bf16), grads, TN).astype(bf16)
        seg = key_part.shape[0] // 4
        for part, value in ((0, key_part), (1, value_part)):
            for q, ref in enumerate(block_heads(mine, sa, item, keys, size, part)):
                ref[...] = value[q * seg : (q + 1) * seg, :]
        return sa

    def send_c(sa, sb):
        slot = sa * 2 + sb
        src = mine.at[me.index(sa, sb, 1 - me.c)]
        return push(src, landc.at[slot], ssem.at[0, slot], rsem.at[0, slot], me.at(me.a, me.b, 1 - me.c))

    def send_b(sa):
        src = mine.at[me.index(sa, 1 - me.b, me.c)]
        return push(src, landb.at[sa], ssem.at[1, sa], rsem.at[1, sa], me.at(me.a, 1 - me.b, me.c))

    def send_a(sa):
        src = mine.at[me.index(sa, me.b, me.c)]
        return push(src, landa.at[me.a], ssem.at[2, sa], rsem.at[2, me.a], me.at(sa, me.b, me.c))

    def from_c(sa):
        for sb in (1 - me.b, me.b):
            slot = sa * 2 + sb
            push(landc.at[slot], landc.at[slot], ssem.at[0, slot], rsem.at[0, slot], me.at(me.a, me.b, 1 - me.c)).wait_recv()
            idx = me.index(sa, sb, me.c)
            add_rows(mine.at[idx], [mine.at[idx], landc.at[slot]])
            if sb is not me.b:
                send_b(sa).start()

    def from_b(sa):
        push(landb.at[sa], landb.at[sa], ssem.at[1, sa], rsem.at[1, sa], me.at(me.a, 1 - me.b, me.c)).wait_recv()
        idx = me.index(sa, me.b, me.c)
        return mine.at[idx], [mine.at[idx], landb.at[sa]]

    def along(sa):
        target, parts = from_b(sa)
        add_rows(target, parts)
        send_a(sa).start()

    def finish():
        target, parts = from_b(me.a)
        add_rows(pair_grad, parts)
        for far in range(1, planes):

            @pl.when(far > me.a)
            def _(far=far):
                push(landa.at[far], landa.at[far], ssem.at[2, far], rsem.at[2, far], me.at(far, me.b, me.c)).wait_recv()
                add_rows(pair_grad, [pair_grad, landa.at[far]])

    def mix():
        share = mixing_ref.shape[1]
        keep.wait()
        for k in range(1, planes):
            cut_from(k)
            column_in(k).wait()
        tokens = column.shape[0] * column.shape[1]
        for n in range(0, column.shape[2], 512):
            rows = column[:, :, n : n + 512].reshape(tokens, 512)
            part = over(cut_all[...].reshape(tokens, 4 * share), rows, TN).astype(bf16)
            for q in range(4):
                mixing_ref[q, :, n : n + 512] = part[q * share : (q + 1) * share]

    def step(sa, c):
        lax.fori_loop(0, items, block, sa)
        for sb in (1 - me.b, me.b):
            send_c(sa, sb).start()

        @pl.when(sa >= 1)
        def _():
            from_c(sa - 1)

        @pl.when(sa >= 2)
        def _():
            along(sa - 2)

        return c

    lax.fori_loop(0, me.a + 1, step, 0)
    mix()

    def unturned(grads, raw, gain):
        turned = grads * turn_ref[0] + pltpu.roll(grads, size // 2, 1) * turn_ref[1]
        scale = lax.rsqrt(jnp.mean(raw * raw, axis=1, keepdims=True) + epsilon)
        scaled = gain * turned
        level = jnp.mean(scaled * raw, axis=1, keepdims=True)
        return scale * scaled - raw * (scale * scale * scale * level), jnp.sum(turned * raw * scale, axis=0, keepdims=True)

    seg = rows // group
    gain_grad[...] = jnp.zeros_like(gain_grad)

    def query_item(item, c):
        at = pl.ds(pl.multiple_of(lax.div(item, keys) * seg, seg), seg)
        total = jnp.zeros((1, size), f32)
        for h in range(group):
            cols = pl.ds(pl.multiple_of((lax.rem(item, keys) * group + h) * size, size), size)
            grads = qacc[item, h * seg : (h + 1) * seg, :] * factor
            value, part = unturned(grads, query_raw[at, cols], gain_ref[0:1, :])
            low_ref[at, cols] = value.astype(bf16)
            total = total + part
        gain_grad[0:1, :] += total
        return c

    lax.fori_loop(0, items, query_item, 0)
    from_c(me.a)

    @pl.when(me.a > 0)
    def _():
        along(me.a - 1)

    finish()
    width = query_raw.shape[1]
    for item in range(items):
        s, k = item // keys, item % keys
        at = slice(s * seg, (s + 1) * seg)
        cols = slice(k * size, (k + 1) * size)
        value, part = unturned(pair_grad[at, cols], key_raw[at, cols], gain_ref[1:2, :])
        low_ref[at, width + k * size : width + (k + 1) * size] = value.astype(bf16)
        gain_grad[1:2, :] += part
    low_ref[:, width + keys * size :] = pair_grad[:, keys * size :].astype(bf16)

    def settle(sa, c):
        for sb in (1 - me.b, me.b):
            send_c(sa, sb).wait_send()
        send_b(sa).wait_send()

        @pl.when(sa < me.a)
        def _():
            send_a(sa).wait_send()

        return c

    lax.fori_loop(0, me.a + 1, settle, 0)
    for k in range(1, planes):
        cut_to(k).wait_send()


def attend_back(query, grads, context, pairs_all, logs, cut, column, raws, gains, turns, planes, group, size, cid):
    f32, bf16 = jnp.float32, jnp.bfloat16
    tokens, width = query.shape
    items = logs.shape[0]
    state = logs.shape
    block = pairs_all.shape[1:]
    share = cut.shape[2] // 4
    inside = pl.BlockSpec(memory_space=pltpu.VMEM)
    anywhere = pl.BlockSpec(memory_space=pl.ANY)
    return pl.pallas_call(
        functools.partial(attend_back_kernel, planes, group),
        out_shape=[
            jax.ShapeDtypeStruct((tokens, width + block[1]), bf16),
            jax.ShapeDtypeStruct((8, size), f32),
            jax.ShapeDtypeStruct((4, share, width), bf16),
        ],
        in_specs=[inside] * 5 + [anywhere] * 2 + [inside] * 4,
        out_specs=[inside] * 3,
        scratch_shapes=[
            pltpu.VMEM(block, f32),
            pltpu.VMEM(cut.shape, bf16),
            pltpu.VMEM(column.shape, bf16),
            pltpu.VMEM(state, bf16),
            pltpu.VMEM(state, bf16),
            pltpu.VMEM(state, f32),
            pltpu.VMEM(state, f32),
            pltpu.VMEM((4 * planes,) + block, bf16),
            pltpu.VMEM((2 * planes,) + block, bf16),
            pltpu.VMEM((planes,) + block, bf16),
            pltpu.VMEM((planes,) + block, bf16),
            pltpu.SemaphoreType.DMA((3, 2 * planes)),
            pltpu.SemaphoreType.DMA((3, 2 * planes)),
            pltpu.SemaphoreType.DMA((planes,)),
            pltpu.SemaphoreType.DMA((planes,)),
            pltpu.SemaphoreType.DMA((planes,)),
        ],
        compiler_params=pltpu.CompilerParams(collective_id=cid, has_side_effects=True, vmem_limit_bytes=ROOM),
        name="attend_back",
    )(query, grads, context, pairs_all, logs, cut, column, raws[0], raws[1], gains, turns)


def weights_kernel(
    planes,
    chunk,
    low_ref,
    cut_ref,
    query_w,
    key_w,
    value_w,
    input_ref,
    gain_ref,
    grad_ref,
    small_ref,
    mixing_part,
    rows_ref,
    input_grad,
    total_ref,
    mixing_rows,
    low_all,
    mixed,
    mixc,
    mixb,
    weights,
    sums,
    landz,
    normed,
    normed_other,
    gains_other,
    send,
    land,
    wload,
    lsend,
    lrecv,
    msend,
    mrecv,
    mload,
    zsend,
    zrecv,
    nsend,
    nrecv,
    tsend,
    trecv,
):
    me = Spot()
    f32, bf16 = jnp.float32, jnp.bfloat16
    tokens, packed = low_ref.shape
    width = input_ref.shape[1]
    chunks = packed // chunk
    assert chunks == 10
    place = lax.rem(me.e, 4)
    base = me.e - place
    share = sums.shape[1] // planes

    def spot(b, c):
        return me.index(0, b, c)

    near = [(1 - me.b, me.c), (me.b, 1 - me.c), (1 - me.b, 1 - me.c)]
    peers = [(base + spot(b, c), me.t) for b, c in near]
    barrier = pltpu.get_barrier_semaphore()
    for who in peers + [me.core()] + [me.at(lax.rem(me.a + k, planes), me.b, me.c) for k in range(1, planes)]:
        pl.semaphore_signal(barrier, inc=1, device_id=who, device_id_type=MESH)
    pl.semaphore_wait(barrier, 3 + planes)

    def cols(k):
        return pl.ds(pl.multiple_of(k * chunk, chunk), chunk)

    def whole(i, k):
        return push(low_ref.at[:, cols(k)], low_all.at[place, :, cols(k)], lsend.at[i, k], lrecv.at[i, k], peers[i])

    first = spot(*near[0])

    def relay(k):
        there = low_all.at[first, :, cols(k)]
        return push(there, there, lsend.at[2, k], lrecv.at[2, k], peers[1])

    quarters = [spot(b, c) for b, c in ((1 - me.b, 1 - me.c), (me.b, 1 - me.c), (1 - me.b, me.c), (me.b, me.c))]

    def mix_c(i):
        return push(mixing_part.at[quarters[i]], mixc.at[i], msend.at[i], mrecv.at[i], peers[1])

    def mix_b():
        return push(mixed.at[0], mixb, msend.at[2], mrecv.at[2], peers[0])

    mix_loads = [pltpu.make_async_copy(mixing_part.at[quarters[2 + i]], mixed.at[i], mload.at[i]) for i in range(2)]

    def mix_round(k):
        if k == chunks - 2:
            for i in range(2):
                mix_c(i).start()
        if k == chunks:
            for i in range(2):
                mix_loads[i].wait()
                mix_c(i).wait_recv()
                add_rows(mixed.at[i], [mixed.at[i], mixc.at[i]])
                if i == 0:
                    mix_b().start()
        if k == chunks + 1:
            mix_b().wait_recv()
            add_rows(mixing_rows, [mixed.at[1], mixb])

    def send_low(k, c):
        whole(0, k).start()
        return c

    lax.fori_loop(0, chunks, send_low, 0)
    whole(1, 0).start()
    whole(1, 1).start()
    for k in mix_loads:
        k.start()
    query_width, key_width = query_w.shape[1], key_w.shape[1]
    loads = [
        pltpu.make_async_copy(query_w, weights.at[:, :query_width], wload.at[0]),
        pltpu.make_async_copy(key_w, weights.at[:, query_width : query_width + key_width], wload.at[1]),
        pltpu.make_async_copy(value_w, weights.at[:, query_width + key_width :], wload.at[2]),
    ]
    for k in loads:
        k.start()
    gains = push(small_ref.at[pl.ds(0, 8)], gains_other, nsend.at[4], nrecv.at[4], me.core())
    gains.start()
    low_all[place] = low_ref[...]
    quarter = width // 4

    def trade(n):
        at = pl.ds(pl.multiple_of(n * quarter, quarter), quarter)
        return push(normed.at[:, at], normed_other.at[:, at], nsend.at[n], nrecv.at[n], me.core())

    def normed_cols(n, c):
        at = pl.ds(pl.multiple_of(n * quarter, quarter), quarter)
        normed[:, at] = over(low_ref[...], weights[at, :], NT).astype(bf16)
        trade(n).start()
        return c

    def await_trade(n, c):
        trade(n).wait_recv()
        return c


    def input_rows(r, total):
        at = pl.ds(pl.multiple_of(r * 16, 16), 16)
        grads = normed[at, :].astype(f32) + normed_other[at, :].astype(f32)
        inputs = input_ref[at, :].astype(f32)
        scale = lax.rsqrt(jnp.mean(inputs * inputs, axis=1, keepdims=True) + epsilon)
        scaled = gain_ref[...] * grads
        level = jnp.mean(scaled * inputs, axis=1, keepdims=True)
        input_grad[at, :] = grad_ref[at, :] + scale * scaled - inputs * (scale * scale * scale * level)
        return total + jnp.sum(grads * inputs * scale, axis=0, keepdims=True)

    def norm_round(k):
        if k == 0:
            for copy in loads:
                copy.wait()
        if k < 4:
            lax.fori_loop(k, k + 1, normed_cols, 0)
        if k == 4:
            gains.wait()
            total_ref[...] = small_ref[...]
            total_ref[0:8, :] += gains_other[...]
            lax.fori_loop(0, 4, await_trade, 0)
            total_ref[8:9, :] = lax.fori_loop(0, tokens // 16, input_rows, jnp.zeros((1, width), f32))
            send[0] = total_ref[ours, :]

    half = total_ref.shape[0] // 2
    ours = pl.ds(pl.multiple_of(me.t * half, half), half)
    others = pl.ds(pl.multiple_of((1 - me.t) * half, half), half)
    bits = [1, 2, 4, 8]

    def small(j):
        bit = bits[j]
        who = (me.e + bit * (1 - 2 * lax.rem(lax.div(me.e, bit), 2)), me.t)
        return push(send.at[j], land.at[j], tsend.at[j], trecv.at[j], who)

    share_back = push(send.at[4], land.at[4], tsend.at[4], trecv.at[4], me.core())

    def small_round(j):
        if j > 0:
            small(j - 1).wait_recv()
            if j < 4:
                send[j] = send[j - 1] + land[j - 1]
            else:
                send[4] = send[3] + land[3]
                share_back.start()
        if j < 4:
            small(j).start()


    def block(k, d):
        return sums.at[k, pl.ds(pl.multiple_of(d * share, share), share)]

    def along(k, d, up):
        arrive = me.a + 1 if up else me.a - 1
        slot = d if up else jnp.where(d == arrive, planes, d)
        return push(block(k, d), landz.at[k, slot], zsend.at[k, d], zrecv.at[k, slot], me.at(arrive, me.b, me.c))

    def landed(k, slot):
        push(landz.at[k, slot], landz.at[k, slot], zsend.at[k, 0], zrecv.at[k, slot], me.core()).wait_recv()

    def chain(k, act, ends):
        for i in range(planes - 1):
            d = far_first(me.a, planes, i)
            up = d > me.a
            inner = (up & (me.a > 0)) | (jnp.logical_not(up) & (me.a + 1 < planes))

            @pl.when(jnp.logical_not(inner) if ends else inner)
            def _(d=d, up=up):
                if act and not ends:
                    landed(k, d)
                    add_rows(block(k, d), [block(k, d), landz.at[k, d]])

                @pl.when(up)
                def _():
                    along(k, d, True).start() if act else along(k, d, True).wait_send()

                @pl.when(jnp.logical_not(up))
                def _():
                    along(k, d, False).start() if act else along(k, d, False).wait_send()

    def finish(k):
        target = rows_ref.at[:, cols(k)]
        own = block(k, me.a)

        @pl.when(me.a > 0)
        def _():
            landed(k, me.a)

        @pl.when(me.a + 1 < planes)
        def _():
            landed(k, planes)

        @pl.when((me.a > 0) & (me.a + 1 < planes))
        def _():
            add_rows(target, [own, landz.at[k, me.a], landz.at[k, planes]])

        @pl.when(me.a == 0)
        def _():
            add_rows(target, [own, landz.at[k, planes]])

        @pl.when(me.a + 1 == planes)
        def _():
            add_rows(target, [own, landz.at[k, me.a]])

    def forward(k):
        whole(0, k).wait_recv()
        relay(k).start()
        if k + 2 < chunks:
            whole(1, k + 2).start()

    for k in range(chunks + 2):
        if k < chunks:
            if k == 0:
                forward(0)
            if k + 1 < chunks:
                forward(k + 1)
            whole(1, k).wait_recv()
            relay(k).wait_recv()
            mixed_rows = low_all[:, :, k * chunk : (k + 1) * chunk].reshape(4 * tokens, chunk)
            sums[k] = over(cut_ref[...], mixed_rows, NN).astype(bf16)
            chain(k, True, True)
        norm_round(k)
        if k in (4, 6, 8, 10, 11):
            small_round((4, 6, 8, 10, 11).index(k))
        if 1 <= k <= chunks:
            chain(k - 1, True, False)
        if k >= 2:
            finish(k - 2)
        mix_round(k)

    def settle(k, c):
        for i in range(2):
            whole(i, k).wait_send()
        relay(k).wait_send()
        chain(k, False, True)
        chain(k, False, False)
        return c

    lax.fori_loop(0, chunks, settle, 0)
    for k in (mix_c(0), mix_c(1), mix_b()):
        k.wait_send()
    for n in range(4):
        trade(n).wait_send()
        small(n).wait_send()
    share_back.wait_send()
    share_back.wait_recv()
    total_ref[ours, :] = send[4]
    total_ref[others, :] = land[4]


def weight_grads(low, cut, query_w, key_w, value_w, inputs, gain, residual_grad, small, mixing, planes, cid):
    f32, bf16 = jnp.float32, jnp.bfloat16
    tokens, packed = low.shape
    width = inputs.shape[1]
    chunk = 256
    chunks = packed // chunk
    share = cut.shape[0] // planes
    quarter = mixing.shape[1:]
    inside = pl.BlockSpec(memory_space=pltpu.VMEM)
    anywhere = pl.BlockSpec(memory_space=pl.ANY)
    half = (small.shape[0] // 2, small.shape[1])
    return pl.pallas_call(
        functools.partial(weights_kernel, planes, chunk),
        out_shape=[
            jax.ShapeDtypeStruct((share, packed), f32),
            jax.ShapeDtypeStruct((tokens, width), f32),
            jax.ShapeDtypeStruct(small.shape, f32),
            jax.ShapeDtypeStruct(quarter, f32),
        ],
        in_specs=[inside, inside, anywhere, anywhere, anywhere, inside, inside, inside, inside, anywhere],
        out_specs=[inside] * 4,
        scratch_shapes=[
            pltpu.VMEM((4, tokens, packed), bf16),
            pltpu.VMEM((2,) + quarter, bf16),
            pltpu.VMEM((2,) + quarter, bf16),
            pltpu.VMEM(quarter, bf16),
            pltpu.VMEM((width, packed), bf16),
            pltpu.VMEM((chunks, planes * share, chunk), bf16),
            pltpu.VMEM((chunks, planes + 1, share, chunk), bf16),
            pltpu.VMEM((tokens, width), bf16),
            pltpu.VMEM((tokens, width), bf16),
            pltpu.VMEM((8, width), f32),
            pltpu.VMEM((5,) + half, f32),
            pltpu.VMEM((5,) + half, f32),
            pltpu.SemaphoreType.DMA((3,)),
            pltpu.SemaphoreType.DMA((3, chunks)),
            pltpu.SemaphoreType.DMA((3, chunks)),
            pltpu.SemaphoreType.DMA((3,)),
            pltpu.SemaphoreType.DMA((3,)),
            pltpu.SemaphoreType.DMA((2,)),
            pltpu.SemaphoreType.DMA((chunks, planes)),
            pltpu.SemaphoreType.DMA((chunks, planes + 1)),
            pltpu.SemaphoreType.DMA((5,)),
            pltpu.SemaphoreType.DMA((5,)),
            pltpu.SemaphoreType.DMA((5,)),
            pltpu.SemaphoreType.DMA((5,)),
        ],
        compiler_params=pltpu.CompilerParams(collective_id=cid, has_side_effects=True, vmem_limit_bytes=ROOM),
        name="weight_grads",
    )(low, cut, query_w, key_w, value_w, inputs, gain, residual_grad, small, mixing)


epsilon = 1e-06
rope_base = 1000000.0
far_below = -1e30


def rms_scaled(values, gain_vec):
    return (
        values * lax.rsqrt(jnp.mean(values * values, axis=-1, keepdims=True) + epsilon) * gain_vec
    )


def rotary_tables(positions, head_dim):
    halfway = head_dim // 2
    exponents = jnp.arange(halfway, dtype=jnp.float32) * (2.0 / head_dim)
    inverse = jnp.exp(-exponents * jnp.log(jnp.float32(rope_base)))
    angles = positions.astype(jnp.float32)[:, None] * inverse[None, :]
    return (jnp.cos(angles), jnp.sin(angles))


def rotate(values, cosine, sine_table):
    halfway = values.shape[-1] // 2
    first = values[..., :halfway]
    latter = values[..., halfway:]
    return jnp.concatenate(
        [first * cosine - latter * sine_table, latter * cosine + first * sine_table], axis=-1
    )


def glu_value(gate_act, up_act):
    return jax.nn.silu(gate_act) * up_act


def on_device(
    layer_input,
    norm_first,
    query_weight,
    key_weight,
    value_weight,
    mixing_weight,
    query_gain,
    key_gain,
    norm_second,
    router_weight,
    gate_weight,
    up_weight,
    down_weight,
    routes,
    fill_order,
    cotangent,
):
    seq_count, seg_len, model_width = layer_input.shape
    expert_count = lax.axis_size("expert")
    tensor_count = lax.axis_size("tensor")
    expert_idx = lax.axis_index("expert")
    tensor_idx = lax.axis_index("tensor")
    head_dim = query_gain.shape[0]
    local_queries = query_weight.shape[1] // head_dim
    local_keys = key_weight.shape[1] // head_dim
    group_size = local_queries // local_keys
    seq_length = seg_len * expert_count
    top_count = routes.shape[2]
    token_count = seq_count * seg_len
    capacity = 5 * token_count * top_count // (4 * expert_count)
    half_width = model_width // tensor_count
    factor = head_dim ** (-0.5)
    inputs = layer_input.astype(jnp.float32)
    normed_f, first_back = jax.vjp(rms_scaled, inputs, norm_first)
    normed = normed_f.astype(jnp.bfloat16)
    positions = expert_idx * seg_len + jnp.arange(seg_len, dtype=jnp.int32)
    cosine, sine_table = rotary_tables(positions, head_dim)
    cosine = cosine[:, None, :]
    sine_table = sine_table[:, None, :]

    def rope_norm(raw_heads, gain_vec):
        return rotate(rms_scaled(raw_heads, gain_vec), cosine, sine_table)

    query_raw = jnp.dot(normed, query_weight, preferred_element_type=jnp.float32).reshape(
        seq_count, seg_len, local_queries, head_dim
    )
    key_raw = jnp.dot(normed, key_weight, preferred_element_type=jnp.float32).reshape(
        seq_count, seg_len, local_keys, head_dim
    )
    value_local = jnp.dot(normed, value_weight, preferred_element_type=jnp.float32).astype(
        jnp.bfloat16
    )
    query_rot, query_back = jax.vjp(rope_norm, query_raw, query_gain)
    key_rot, key_back = jax.vjp(rope_norm, key_raw, key_gain)
    key_local = key_rot.astype(jnp.bfloat16).reshape(seq_count, seg_len, local_keys * head_dim)
    key_all, value_all = (
        lax.all_gather(key_local, "expert", axis=1, tiled=True),
        lax.all_gather(value_local, "expert", axis=1, tiled=True),
    )
    key_tiles = key_all.reshape(seq_count, seq_length, local_keys, head_dim)
    value_tiles = value_all.reshape(seq_count, seq_length, local_keys, head_dim)
    query_rows = query_rot.astype(jnp.bfloat16).reshape(
        seq_count, seg_len, local_keys, group_size, head_dim
    )
    query_rows = query_rows.transpose(0, 2, 3, 1, 4).reshape(
        seq_count, local_keys, group_size * seg_len, head_dim
    )
    row_block = (
        expert_idx * seg_len + jnp.arange(group_size * seg_len, dtype=jnp.int32) % seg_len
    ) // BLOCK
    tile_len = min(512, seq_length)
    reach_end = jnp.minimum(((expert_idx + 1) * seg_len - 1) // BLOCK * BLOCK + BLOCK, seq_length)
    tile_count = (reach_end + tile_len - 1) // tile_len

    def tile_scores(tile_idx):
        offset = tile_idx * tile_len
        key_part = lax.dynamic_slice_in_dim(key_tiles, offset, tile_len, 1)
        scores = (
            jnp.einsum("shrd,skhd->shrk", query_rows, key_part, preferred_element_type=jnp.float32)
            * factor
        )
        key_block = (offset + jnp.arange(tile_len, dtype=jnp.int32)) // BLOCK
        allowed = key_block[None, :] <= row_block[:, None]
        return (scores, allowed, offset)

    stat_shape = (seq_count, local_keys, group_size * seg_len)

    def stats_step(tile_idx, state_pair):
        running_max, running_sum = state_pair
        scores, allowed, offset = tile_scores(tile_idx)
        masked = jnp.where(allowed, scores, far_below)
        new_max = jnp.maximum(running_max, jnp.max(masked, axis=-1))
        exp_terms = jnp.where(allowed, jnp.exp(masked - new_max[..., None]), 0.0)
        return (new_max, running_sum * jnp.exp(running_max - new_max) + jnp.sum(exp_terms, axis=-1))

    row_max, row_sum = lax.fori_loop(
        0,
        tile_count,
        stats_step,
        (jnp.full(stat_shape, far_below, jnp.float32), jnp.zeros(stat_shape, jnp.float32)),
    )
    log_total = row_max + jnp.log(row_sum)

    def probabilities(tile_idx):
        scores, allowed, offset = tile_scores(tile_idx)
        return (jnp.where(allowed, jnp.exp(scores - log_total[..., None]), 0.0), offset)

    def context_step(tile_idx, context_sum):
        prob_tile, offset = probabilities(tile_idx)
        value_part = lax.dynamic_slice_in_dim(value_tiles, offset, tile_len, 1)
        return context_sum + jnp.einsum(
            "shrk,skhd->shrd",
            prob_tile.astype(jnp.bfloat16),
            value_part,
            preferred_element_type=jnp.float32,
        )

    context_f = lax.fori_loop(0, tile_count, context_step, jnp.zeros(query_rows.shape, jnp.float32))
    shaped = context_f.reshape(seq_count, local_keys, group_size, seg_len, head_dim).transpose(
        0, 3, 1, 2, 4
    )
    context = shaped.reshape(seq_count, seg_len, local_queries * head_dim).astype(jnp.bfloat16)
    head_part = jnp.dot(context, mixing_weight, preferred_element_type=jnp.float32)
    residual = inputs + lax.psum(head_part.astype(jnp.bfloat16), "tensor").astype(jnp.float32)
    second_f, second_back = jax.vjp(rms_scaled, residual, norm_second)
    second = second_f.astype(jnp.bfloat16).reshape(token_count, model_width)
    logits = jnp.dot(second, router_weight, preferred_element_type=jnp.float32)
    flat_routes = routes.reshape(token_count, top_count)
    picked = (flat_routes[:, :, None] == jnp.arange(expert_count, dtype=jnp.int32)).astype(
        jnp.float32
    )
    gates = jax.nn.softmax(jnp.sum(picked * logits[:, None, :], axis=-1), axis=-1)
    usages = jnp.sum(picked, axis=1)
    ranking = fill_order.reshape(token_count)
    before = (ranking[None, :] < ranking[:, None]).astype(jnp.bfloat16)
    counts = jnp.dot(before, usages.astype(jnp.bfloat16), preferred_element_type=jnp.float32)
    slot_ids = jnp.sum(picked * counts[:, None, :], axis=-1).astype(jnp.int32)
    kept_mask = slot_ids < capacity
    kept_float = kept_mask.astype(jnp.float32)
    weighted = gates * kept_float
    places = jnp.where(kept_mask, flat_routes * capacity + slot_ids, -1)
    slot_grid = jnp.arange(expert_count * capacity, dtype=jnp.int32)
    assign = (places[:, :, None] == slot_grid).astype(jnp.bfloat16)
    placed = jnp.sum(assign, axis=1)
    combine = jnp.sum(weighted[:, :, None] * assign.astype(jnp.float32), axis=1)
    send_rows = jnp.einsum("tp,td->pd", placed, second, preferred_element_type=jnp.float32).astype(
        jnp.bfloat16
    )
    arrived = lax.all_to_all(
        send_rows.reshape(expert_count, capacity, model_width),
        "expert",
        split_axis=0,
        concat_axis=0,
        tiled=True,
    )
    arrived = arrived.reshape(expert_count * capacity, model_width)
    gate_one = gate_weight[0]
    up_one = up_weight[0]
    down_one = down_weight[0]
    gate_act = jnp.dot(arrived, gate_one, preferred_element_type=jnp.float32)
    up_act = jnp.dot(arrived, up_one, preferred_element_type=jnp.float32)
    hidden_val, glu_back = jax.vjp(glu_value, gate_act, up_act)
    hidden = hidden_val.astype(jnp.bfloat16)
    expert_part = jnp.dot(hidden, down_one, preferred_element_type=jnp.float32)
    summed = lax.psum(expert_part.astype(jnp.bfloat16), "tensor")
    returned = lax.all_to_all(
        summed.reshape(expert_count, capacity, model_width),
        "expert",
        split_axis=0,
        concat_axis=0,
        tiled=True,
    )
    returned = returned.reshape(expert_count * capacity, model_width)
    per_route = (
        jnp.take(returned, jnp.maximum(places, 0), axis=0).astype(jnp.float32)
        * kept_float[:, :, None]
    )
    mixture = residual.reshape(token_count, model_width) + jnp.sum(
        weighted[:, :, None] * per_route, axis=1
    )
    layer_output = lax.dynamic_slice_in_dim(mixture, tensor_idx * half_width, half_width, 1)
    layer_output = layer_output.astype(jnp.bfloat16).reshape(seq_count, seg_len, half_width)
    upstream = cotangent.astype(jnp.float32).reshape(token_count, model_width)
    gate_grads = jnp.sum(upstream[:, None, :] * per_route, axis=-1) * kept_float
    send_grads = jnp.einsum(
        "tp,td->pd",
        combine,
        upstream,
        precision=lax.Precision.HIGHEST,
        preferred_element_type=jnp.float32,
    ).astype(jnp.bfloat16)
    grads_in = lax.all_to_all(
        send_grads.reshape(expert_count, capacity, model_width),
        "expert",
        split_axis=0,
        concat_axis=0,
        tiled=True,
    )
    grads_in = grads_in.reshape(expert_count * capacity, model_width)
    hidden_grad = lax.dot_general(
        grads_in, down_one, (((1,), (1,)), ((), ())), preferred_element_type=jnp.float32
    )
    down_grad = jnp.einsum("rf,rd->fd", hidden, grads_in, preferred_element_type=jnp.float32)
    gate_d, up_d = glu_back(hidden_grad)
    gate_d = gate_d.astype(jnp.bfloat16)
    up_d = up_d.astype(jnp.bfloat16)
    gate_grad = jnp.einsum("rd,rf->df", arrived, gate_d, preferred_element_type=jnp.float32)
    up_grad = jnp.einsum("rd,rf->df", arrived, up_d, preferred_element_type=jnp.float32)
    row_part = lax.dot_general(
        gate_d, gate_one, (((1,), (1,)), ((), ())), preferred_element_type=jnp.float32
    )
    row_part = row_part + lax.dot_general(
        up_d, up_one, (((1,), (1,)), ((), ())), preferred_element_type=jnp.float32
    )
    row_share = lax.psum_scatter(
        row_part.reshape(expert_count, capacity, model_width).astype(jnp.bfloat16),
        "tensor",
        scatter_dimension=2,
        tiled=True,
    )
    row_home = lax.all_to_all(row_share, "expert", split_axis=0, concat_axis=0, tiled=True).reshape(
        expert_count * capacity, half_width
    )
    second_half = jnp.dot(placed, row_home, preferred_element_type=jnp.float32)
    route_grads = gates * (gate_grads - jnp.sum(gates * gate_grads, axis=-1, keepdims=True))
    logit_grads = jnp.sum(picked * route_grads[:, :, None], axis=1).astype(jnp.bfloat16)
    router_grad = jnp.einsum("td,te->de", second, logit_grads, preferred_element_type=jnp.float32)
    router_back = lax.dot_general(
        logit_grads, router_weight, (((1,), (1,)), ((), ())), preferred_element_type=jnp.float32
    )
    own_part = second_half + lax.dynamic_slice_in_dim(
        router_back, tensor_idx * half_width, half_width, 1
    )
    second_part = lax.dynamic_update_slice_in_dim(
        jnp.zeros((token_count, model_width), jnp.float32), own_part, tensor_idx * half_width, 1
    )
    residual_part, norm_part = second_back(second_part.reshape(seq_count, seg_len, model_width))
    residual_grad, second_grad = (
        lax.psum(residual_part.astype(jnp.bfloat16), "tensor").astype(jnp.float32),
        lax.psum(norm_part.astype(jnp.bfloat16), "tensor").astype(jnp.float32),
    )
    residual_grad = residual_grad + upstream.reshape(seq_count, seg_len, model_width)
    head_in = residual_grad.astype(jnp.bfloat16)
    mixing_part = jnp.einsum("std,stc->dc", head_in, context, preferred_element_type=jnp.float32)
    context_grad = lax.dot_general(
        head_in, mixing_weight, (((2,), (1,)), ((), ())), preferred_element_type=jnp.float32
    ).astype(jnp.bfloat16)
    grad_rows = context_grad.reshape(
        seq_count, seg_len, local_keys, group_size, head_dim
    ).transpose(0, 2, 3, 1, 4)
    grad_rows = grad_rows.reshape(query_rows.shape)
    delta_rows = jnp.sum(grad_rows.astype(jnp.float32) * context_f, axis=-1)
    key_shape = (seq_count, seq_length, local_keys, head_dim)

    def gradient_step(tile_idx, state_trio):
        query_acc, key_acc, value_acc = state_trio
        prob_tile, offset = probabilities(tile_idx)
        key_part = lax.dynamic_slice_in_dim(key_tiles, offset, tile_len, 1)
        value_part = lax.dynamic_slice_in_dim(value_tiles, offset, tile_len, 1)
        prob_low = prob_tile.astype(jnp.bfloat16)
        prob_grad = jnp.einsum(
            "shrd,skhd->shrk", grad_rows, value_part, preferred_element_type=jnp.float32
        )
        score_grad = (prob_tile * (prob_grad - delta_rows[..., None])).astype(jnp.bfloat16)
        query_acc = query_acc + jnp.einsum(
            "shrk,skhd->shrd", score_grad, key_part, preferred_element_type=jnp.float32
        )
        key_tile = jnp.einsum(
            "shrk,shrd->skhd", score_grad, query_rows, preferred_element_type=jnp.float32
        )
        value_tile = jnp.einsum(
            "shrk,shrd->skhd", prob_low, grad_rows, preferred_element_type=jnp.float32
        )
        key_acc = lax.dynamic_update_slice_in_dim(key_acc, key_tile, offset, 1)
        value_acc = lax.dynamic_update_slice_in_dim(value_acc, value_tile, offset, 1)
        return (query_acc, key_acc, value_acc)

    start_state = (
        jnp.zeros(query_rows.shape, jnp.float32),
        jnp.zeros(key_shape, jnp.float32),
        jnp.zeros(key_shape, jnp.float32),
    )
    query_acc, key_acc, value_acc = lax.fori_loop(0, tile_count, gradient_step, start_state)
    key_grad_all, value_grad_all = (
        lax.psum_scatter(
            (key_acc * factor).reshape(seq_count, seq_length, local_keys * head_dim),
            "expert",
            scatter_dimension=1,
            tiled=True,
        ),
        lax.psum_scatter(
            value_acc.reshape(seq_count, seq_length, local_keys * head_dim),
            "expert",
            scatter_dimension=1,
            tiled=True,
        ),
    )
    key_raw_grad, keygain_part = key_back(
        key_grad_all.reshape(seq_count, seg_len, local_keys, head_dim)
    )
    query_shaped = (
        (query_acc * factor)
        .reshape(seq_count, local_keys, group_size, seg_len, head_dim)
        .transpose(0, 3, 1, 2, 4)
    )
    query_raw_grad, querygain_part = query_back(
        query_shaped.reshape(seq_count, seg_len, local_queries, head_dim)
    )
    query_low = query_raw_grad.astype(jnp.bfloat16).reshape(
        seq_count, seg_len, local_queries * head_dim
    )
    key_low = key_raw_grad.astype(jnp.bfloat16).reshape(seq_count, seg_len, local_keys * head_dim)
    value_low = value_grad_all.astype(jnp.bfloat16)
    query_sum = jnp.einsum("std,stc->dc", normed, query_low, preferred_element_type=jnp.float32)
    keys_sum = jnp.einsum("std,stc->dc", normed, key_low, preferred_element_type=jnp.float32)
    values_sum = jnp.einsum("std,stc->dc", normed, value_low, preferred_element_type=jnp.float32)
    query_grad, key_grad, value_grad, mixing_rows = (
        lax.psum_scatter(query_sum, "expert", scatter_dimension=0, tiled=True),
        lax.psum_scatter(keys_sum, "expert", scatter_dimension=0, tiled=True),
        lax.psum_scatter(values_sum, "expert", scatter_dimension=0, tiled=True),
        lax.psum_scatter(mixing_part, "expert", scatter_dimension=0, tiled=True),
    )
    mixing_grad = mixing_rows.T
    normed_part = lax.dot_general(
        query_low, query_weight, (((2,), (1,)), ((), ())), preferred_element_type=jnp.float32
    )
    normed_part = normed_part + lax.dot_general(
        key_low, key_weight, (((2,), (1,)), ((), ())), preferred_element_type=jnp.float32
    )
    normed_part = normed_part + lax.dot_general(
        value_low, value_weight, (((2,), (1,)), ((), ())), preferred_element_type=jnp.float32
    )
    normed_grad, querygain_grad, keygain_grad = (
        lax.psum(normed_part.astype(jnp.bfloat16), "tensor").astype(jnp.float32),
        lax.psum(querygain_part.astype(jnp.bfloat16), "tensor").astype(jnp.float32),
        lax.psum(keygain_part.astype(jnp.bfloat16), "tensor").astype(jnp.float32),
    )
    input_part, first_grad = first_back(normed_grad)
    input_grad = residual_grad + input_part
    first_grad, second_grad, querygain_grad, keygain_grad, router_grad = lax.psum(
        (first_grad, second_grad, querygain_grad, keygain_grad, router_grad), "expert"
    )
    return (
        layer_output,
        input_grad,
        first_grad,
        query_grad,
        key_grad,
        value_grad,
        mixing_grad,
        querygain_grad,
        keygain_grad,
        second_grad,
        router_grad,
        gate_grad[None],
        up_grad[None],
        down_grad[None],
    )

def partners(planes):
    def number(a, b, c, t):
        y, x = (b, c) if t else (c, b)
        return (a * 4 + y * 2 + x) * 2 + t

    both = (0, 1)
    return [[number(a, b, c, t) for a in range(planes) for b in both] for t in both for c in both]


def lift(values, wide):
    high = lax.reduce_precision(values, 8, 7)
    both = jnp.concatenate([high, values - high], axis=-1).astype(jnp.bfloat16)
    return jnp.pad(both, ((0, 0), (0, wide - both.shape[-1])))


def on_chips(
    layer_input,
    norm_first,
    query_weight,
    key_weight,
    value_weight,
    mixing_weight,
    query_gain,
    key_gain,
    norm_second,
    router_weight,
    gate_weight,
    up_weight,
    down_weight,
    routes,
    fill_order,
    cotangent,
):
    seq_count, seg_len, model_width = layer_input.shape
    expert_count = lax.axis_size("expert")
    planes = expert_count // 4
    expert_idx = lax.axis_index("expert")
    tensor_idx = lax.axis_index("tensor")
    head_dim = query_gain.shape[0]
    local_queries = query_weight.shape[1] // head_dim
    local_keys = key_weight.shape[1] // head_dim
    key_width = local_keys * head_dim
    group_size = local_queries // local_keys
    top_count = routes.shape[2]
    token_count = seq_count * seg_len
    capacity = 5 * token_count * top_count // (4 * expert_count)
    slots = -(-capacity // 32) * 32
    half_width = model_width // 2
    share_width = model_width // expert_count
    f32, bf16 = jnp.float32, jnp.bfloat16
    inputs = layer_input.astype(f32)
    normed = rms_scaled(inputs, norm_first).astype(bf16)
    positions = expert_idx * seg_len + jnp.arange(seg_len, dtype=jnp.int32)
    cosine, sine_table = rotary_tables(positions, head_dim)
    cosine = cosine[:, None, :]
    sine_table = sine_table[:, None, :]

    def rope_norm(raw_heads, gain_vec):
        return rotate(rms_scaled(raw_heads, gain_vec), cosine, sine_table)

    def slices(rows):
        cut = rows.reshape(token_count, planes, 4, share_width)
        return cut.transpose(2, 0, 1, 3).reshape(4, token_count, planes * share_width)

    query_raw = jnp.dot(normed, query_weight, preferred_element_type=f32).reshape(
        seq_count, seg_len, local_queries, head_dim
    )
    key_raw = jnp.dot(normed, key_weight, preferred_element_type=f32).reshape(
        seq_count, seg_len, local_keys, head_dim
    )
    value_local = jnp.dot(normed, value_weight, preferred_element_type=f32).astype(bf16)
    query_rot = rope_norm(query_raw, query_gain)
    key_rot = rope_norm(key_raw, key_gain)
    key_local = key_rot.astype(bf16).reshape(token_count, key_width)
    pairs = jnp.concatenate([key_local, value_local.reshape(token_count, key_width)], axis=1)
    upstream_low = cotangent.reshape(token_count, model_width)
    half_tokens = token_count // 2
    upstream_half = lax.dynamic_slice_in_dim(upstream_low, tensor_idx * half_tokens, half_tokens, 0)
    axes = ("expert", "tensor")
    groups_of = partners(planes)
    upstream_mine = lax.all_gather(upstream_half, "expert")
    query_rows = query_rot.astype(bf16).reshape(token_count, local_queries * head_dim)
    context, pairs_all, logs = attend(query_rows, pairs, planes, group_size, head_dim, 1)
    head_part = jnp.dot(context, mixing_weight, preferred_element_type=f32)
    head_low = head_part.astype(bf16)
    head_other = swap_cores(head_low, 3, "swap_heads")
    residual = inputs.reshape(token_count, model_width) + (head_low.astype(f32) + head_other.astype(f32))
    second_f, second_back = jax.vjp(rms_scaled, residual, norm_second)
    second = second_f.astype(bf16)
    logits = jnp.dot(second, router_weight, preferred_element_type=f32)
    flat_routes = routes.reshape(token_count, top_count)
    picked = (flat_routes[:, :, None] == jnp.arange(expert_count, dtype=jnp.int32)).astype(f32)
    gates = jax.nn.softmax(jnp.sum(picked * logits[:, None, :], axis=-1), axis=-1)
    usages = jnp.sum(picked, axis=1)
    ranking = fill_order.reshape(token_count)
    before = (ranking[None, :] < ranking[:, None]).astype(bf16)
    counts = jnp.dot(before, usages.astype(bf16), preferred_element_type=f32)
    here = (usages > 0.0) & (counts < capacity)
    slot_table = jnp.where(here, counts, -1.0)
    gate_table = jnp.where(here, jnp.sum(picked * gates[:, :, None], axis=1), 0.0)
    slot_hi = lift(slot_table, 2 * expert_count)[:, :expert_count]
    notes = jnp.concatenate([slot_hi, lift(gate_table, 128 - expert_count)], axis=1)
    parcel = jnp.concatenate([second, notes], axis=1)
    normed_cut = slices(normed.reshape(token_count, model_width))
    _, _, out_share, row_home, context_column, other_cuts, gate_grad, up_grad, down_grad = run_experts(
        parcel, upstream_mine, gate_weight[0], up_weight[0], down_weight[0], context, normed_cut, planes, slots, 4
    )
    place = lax.rem(expert_idx, 4)
    own_cut = lax.dynamic_index_in_dim(normed_cut, place, 0)
    normed_cut = lax.dynamic_update_slice_in_dim(other_cuts, own_cut, place, 0)
    out_home = lax.psum_scatter(out_share, axes, scatter_dimension=0, axis_index_groups=groups_of, tiled=True)[0]
    home_scores = jnp.sum(row_home[:, :, half_width:].astype(f32), axis=0)
    home_scores = home_scores[:, :expert_count] + home_scores[:, expert_count : 2 * expert_count]
    gate_grads = jnp.sum(picked * home_scores[:, None, :], axis=-1)
    route_grads = gates * (gate_grads - jnp.sum(gates * gate_grads, axis=-1, keepdims=True))
    logit_grads = jnp.sum(picked * route_grads[:, :, None], axis=1).astype(bf16)
    router_grad = jnp.einsum("td,te->ed", second, logit_grads, preferred_element_type=f32)
    router_back = lax.dot_general(
        logit_grads, router_weight, (((1,), (1,)), ((), ())), preferred_element_type=f32
    )
    second_rows = jnp.concatenate([row_home[0, :, :half_width], row_home[1, :, :half_width]], axis=1)
    second_in = second_rows.astype(f32) + router_back
    residual_part, second_grad = second_back(second_in)
    residual_grad = residual_part + upstream_low.astype(f32)
    head_in = residual_grad.astype(bf16)

    context_grad = lax.dot_general(
        head_in, mixing_weight, (((1,), (1,)), ((), ())), preferred_element_type=f32
    ).astype(bf16)
    head_cut = head_in.reshape(token_count, planes, 4 * share_width).transpose(1, 0, 2)
    turns = jnp.stack(
        [
            jnp.concatenate([cosine[:, 0], cosine[:, 0]], axis=1),
            jnp.concatenate([sine_table[:, 0], -sine_table[:, 0]], axis=1),
        ]
    )
    all_low, gain_grads, mixing_part = attend_back(
        query_rows,
        context_grad,
        context,
        pairs_all,
        logs,
        head_cut,
        context_column,
        (query_raw.reshape(token_count, -1), key_raw.reshape(token_count, key_width)),
        jnp.stack([query_gain, key_gain]),
        turns,
        planes,
        group_size,
        head_dim,
        7,
    )
    residual_half = lax.dynamic_slice_in_dim(residual, tensor_idx * half_width, half_width, 1)
    layer_output = (residual_half + out_home.astype(f32)).astype(bf16).reshape(seq_count, seg_len, half_width)
    gain_row = jnp.pad(
        gain_grads[:2].reshape(1, 2 * head_dim), ((0, 7), (0, model_width - 2 * head_dim))
    )
    small = jnp.concatenate(
        [gain_row, jnp.pad(second_grad[None], ((1, 6), (0, 0))), router_grad], axis=0
    )
    weight_rows, input_grad, small, mixing_rows = weight_grads(
        all_low,
        normed_cut.reshape(4 * token_count, planes * share_width).T,
        query_weight,
        key_weight,
        value_weight,
        layer_input.reshape(token_count, model_width),
        norm_first[None],
        residual_grad,
        small,
        mixing_part,
        planes,
        10,
    )
    mixing_grad = mixing_rows.T
    query_width = local_queries * head_dim
    query_grad = weight_rows[:, :query_width]
    key_grad = weight_rows[:, query_width : query_width + key_width]
    value_grad = weight_rows[:, query_width + key_width :]
    return (
        layer_output,
        input_grad.reshape(seq_count, seg_len, model_width),
        small[8],
        query_grad,
        key_grad,
        value_grad,
        mixing_grad,
        small[0, :head_dim],
        small[0, head_dim : 2 * head_dim],
        small[9],
        small[16:].T,
        gate_grad[None],
        up_grad[None],
        down_grad[None],
    )


def solution(mesh):
    chips = mesh.shape["expert"] == 16 and mesh.shape["tensor"] == 2
    return jax.shard_map(
        on_chips if chips else on_device,
        mesh=mesh,
        in_specs=(
            P(None, "expert", None),
            P(),
            P(None, "tensor"),
            P(None, "tensor"),
            P(None, "tensor"),
            P("tensor", None),
            P(),
            P(),
            P(),
            P(),
            P("expert", None, "tensor"),
            P("expert", None, "tensor"),
            P("expert", "tensor", None),
            P(None, "expert", None),
            P(None, "expert"),
            P(None, "expert", None),
        ),
        out_specs=(
            P(None, "expert", "tensor"),
            P(None, "expert", None),
            P(),
            P("expert", "tensor"),
            P("expert", "tensor"),
            P("expert", "tensor"),
            P("tensor", "expert"),
            P(),
            P(),
            P(),
            P(),
            P("expert", None, "tensor"),
            P("expert", None, "tensor"),
            P("expert", "tensor", None),
        ),
        check_vma=False,
    )
```
